32 devices in a mesh: width: 4 (over y, x), seq: 8 (over z, core).
Axes of the slice: x: 2, y: 2, z: 4, core: 2. Of those that a mesh axis runs over, the one named last changes fastest.
Arguments:
- tokens: bfloat16 [8192, 2048], P(('width', 'seq')), may hold values from -6 to 6
- cotangent: bfloat16 [8192, 2048], P(('width', 'seq')), may hold values from -6 to 6
- starts: int32 [32, 2], P(('width', 'seq')), may hold values from 0 to 1, as said below
- valid: int32 [32, 2], P(('width', 'seq')), may hold values from 1 to 128, as said below
- norm_gain: float32 [2048], replicated, may hold values from 0.5 to 1.5
- w_zx: bfloat16 [2048, 8192], P('seq'), may hold values from -0.125 to 0.125
- w_bc: bfloat16 [2048, 256], P('seq'), may hold values from -0.125 to 0.125
- w_dt: bfloat16 [2048, 64], P('seq'), may hold values from -0.125 to 0.125
- conv_w: float32 [4352, 4], replicated, may hold values from -3 to 3
- conv_b: float32 [4352], replicated, may hold values from -3 to 3
- dt_bias: float32 [64], replicated, may hold values from -2 to 0.5
- a_log: float32 [64], replicated
- d_skip: float32 [64], replicated, may hold values from 0.5 to 1.5
- gate_gain: float32 [4096], replicated, may hold values from 0.5 to 1.5
- w_out: bfloat16 [4096, 2048], P('seq'), may hold values from -0.125 to 0.125
Outputs:
- output: bfloat16 [8192, 2048], P(('width', 'seq'))
- input_grad: float32 [8192, 2048], P(('width', 'seq'))
- grad_norm_gain: float32 [2048], P('seq')
- grad_w_zx: float32 [2048, 8192], P('seq')
- grad_w_bc: float32 [2048, 256], P('seq')
- grad_w_dt: float32 [2048, 64], P('seq')
- grad_conv_w: float32 [4352, 4], P('seq')
- grad_conv_b: float32 [4352], P('seq')
- grad_dt_bias: float32 [64], P('seq')
- grad_a_log: float32 [64], P('seq')
- grad_d_skip: float32 [64], P('seq')
- grad_gate_gain: float32 [4096], P('seq')
- grad_w_out: float32 [4096, 2048], P('seq')
The draws below stay inside these ranges and needn't reach their ends.
Inputs may be any that keep to these rules, and one draw needn't show every extreme that they name: `starts`: block 0 of every lane begins a sequence; in each group one lane holds a single sequence over all 8 blocks; in the other lanes no sequence spans more than 4 blocks and one spans exactly 4. `valid`: below 128 only in a block after which a new sequence begins or the lane ends.
All inputs are finite; a program needn't handle non-finite values.
Results may differ from the reference program's by a relative error of at most 0.012.
The reference program's roundings to bfloat16 on the way count: a program that leaves them out, or rounds other values in their place, can miss the bound.
Values may be sent and summed in bfloat16 or wider, within the bound.
A program may use at most 576 MiB of HBM per device.

```python
import jax
import jax.numpy as jnp
from jax import lax

D = 2048
H = 64
HEAD_DIM = 64
N = 128
KCONV = 4
BLOCK = 128
LANES = 2
E = 4096
CONV_CH = 4352
TOKENS = 8192
SEQ_MOST = 4
N_WIDTH = 4
N_SEQ = 8


def block_layout(key):
    flag_key, start_key, lane_key = jax.random.split(key, 3)
    position = jnp.arange(N_SEQ)[None, None, :]
    flag_bits = jax.random.randint(flag_key, (N_WIDTH, LANES, N_SEQ), 0, 100) < 35
    block_start = jax.random.randint(start_key, (N_WIDTH, LANES, 1), 0, N_SEQ // SEQ_MOST) * SEQ_MOST
    inside = (position > block_start) & (position < block_start + SEQ_MOST)
    flag_bits = jnp.where(inside, False, flag_bits) | (position % SEQ_MOST == 0)
    chosen = jax.random.randint(lane_key, (N_WIDTH, 1, 1), 0, LANES)
    lane_index = jnp.arange(LANES)[None, :, None]
    flag_bits = jnp.where(lane_index == chosen, position == 0, flag_bits)
    return flag_bits.astype(jnp.int32)


def draw_starts(key, part):
    layout = block_layout(key)
    return jnp.transpose(layout, (0, 2, 1)).reshape(N_WIDTH * N_SEQ, LANES)


def draw_valid(key, part):
    own_key = jax.random.fold_in(key, 5)
    layout = block_layout(key)
    next_start = jnp.concatenate([layout[..., 1:], jnp.ones_like(layout[..., :1])], axis=-1)
    counts = jax.random.randint(own_key, layout.shape, 1, BLOCK + 1)
    filled = jnp.where(next_start == 1, counts, BLOCK).astype(jnp.int32)
    return jnp.transpose(filled, (0, 2, 1)).reshape(N_WIDTH * N_SEQ, LANES)


def draw_a_log(key, part):
    key = jax.random.fold_in(key, 7)
    pick_key, slow_key, fast_key = jax.random.split(key, 3)
    fast_share = 50
    fast_heads = jax.random.randint(pick_key, (H,), 0, 100) < fast_share
    slow_rate = jax.random.uniform(slow_key, (H,), jnp.float32, 0.1, 0.5) / (N_SEQ * BLOCK)
    fast_rate = jax.random.uniform(fast_key, (H,), jnp.float32, 1.0 / 40.0, 1.0 / 15.0)
    return jnp.log(jnp.where(fast_heads, fast_rate, slow_rate)).astype(jnp.float32)


def steps_of(stream_key, dims, cuts, low, high):
    loudness, own = 1.0, jax.random.fold_in(stream_key, 6)
    for dim, blocks in cuts:
        draws = jnp.exp(jax.random.uniform(jax.random.fold_in(own, dim), (blocks,), jnp.float32, low / len(cuts), high / len(cuts)))
        loudness = loudness * jnp.repeat(draws, dims[dim] // blocks).reshape([-1 if axis == dim else 1 for axis in range(len(dims))])
    return loudness


def noise(rng, shape, width, most, cuts=(), dtype=jnp.bfloat16):
    drawn = width * jax.random.normal(rng, shape, jnp.float32)
    if cuts:
        drawn = drawn * steps_of(rng, shape, cuts, -0.22, 0.18)
    return jnp.clip(drawn, -most, most).astype(dtype)


def setup_inputs(seed: int = 0) -> dict:
    streams_of = jax.random.split(jax.random.key(seed), 16)
    return {
        "tokens": noise(streams_of[0], (TOKENS, D), 1.0, 6.0, ((0, 32),)),
        "cotangent": noise(streams_of[1], (TOKENS, D), 1.0, 6.0, ((0, 32),)),
        "starts": draw_starts(jax.random.fold_in(streams_of[15], 71), 0),
        "valid": draw_valid(jax.random.fold_in(streams_of[15], 71), 0),
        "norm_gain": jnp.clip(1.0 + 0.1 * jax.random.normal(streams_of[4], (D,), jnp.float32), 0.5, 1.5),
        "w_zx": noise(streams_of[5], (D, 2 * E), D ** -0.5, 0.125, ((0, 8),)),
        "w_bc": noise(streams_of[6], (D, 2 * N), D ** -0.5, 0.125, ((0, 8),)),
        "w_dt": noise(streams_of[7], (D, H), D ** -0.5, 0.125, ((0, 8),)),
        "conv_w": noise(streams_of[8], (CONV_CH, KCONV), KCONV ** -0.5, 3.0, (), jnp.float32),
        "conv_b": noise(streams_of[9], (CONV_CH,), 0.3, 3.0, (), jnp.float32),
        "dt_bias": jnp.clip(jax.random.uniform(streams_of[10], (H,), jnp.float32, -2.0, 0.5), -2.0, 0.5),
        "a_log": draw_a_log(jax.random.fold_in(streams_of[15], 71), 0),
        "d_skip": jnp.clip(jax.random.uniform(streams_of[12], (H,), jnp.float32, 0.5, 1.5), 0.5, 1.5),
        "gate_gain": jnp.clip(1.0 + 0.1 * jax.random.normal(streams_of[13], (E,), jnp.float32), 0.5, 1.5),
        "w_out": noise(streams_of[14], (E, D), (E // 2) ** -0.5, 0.125, ((0, 8),)),
    }


@jax.custom_vjp
def low(v):
    return lax.optimization_barrier(v.astype(jnp.bfloat16)).astype(jnp.float32)

@jax.custom_vjp
def low_back(v):
    return v

def low_keep(v):
    return (low(v), None)

def low_pass(kept, grad):
    return (grad,)

def back_keep(v):
    return (v, None)

def back_low(kept, grad):
    return (low(grad),)
low.defvjp(low_keep, low_pass)
low_back.defvjp(back_keep, back_low)
epsilon = 1e-05
highest = lax.Precision.HIGHEST

def rms_front(x_rows, norm_gain):
    mean_square = lax.optimization_barrier(jnp.mean(x_rows * x_rows, axis=-1, keepdims=True))
    return x_rows * lax.rsqrt(mean_square + epsilon) * norm_gain

def rim_of(zx_pre, bc_pre, chan_mask):
    return jnp.concatenate([zx_pre[:, BLOCK - KCONV + 1:, E:] * chan_mask, bc_pre[:, BLOCK - KCONV + 1:, :]], axis=-1)

def piece_front(zx_pre, bc_pre, dt_raw, rim_rows, conv_w, conv_b, dt_bias, a_log, chan_mask, head_mask, keep_rows):
    z_gate = zx_pre[..., :E] * chan_mask
    pre_conv = jnp.concatenate([zx_pre[..., E:] * chan_mask, bc_pre], axis=-1)
    padded = jnp.concatenate([rim_rows * keep_rows[:, None, None], pre_conv], axis=1)
    conv_out = conv_b + padded[:, 0:BLOCK, :] * conv_w[:, 0]
    for offset in range(1, KCONV):
        conv_out = conv_out + padded[:, offset:offset + BLOCK, :] * conv_w[:, offset]
    active = jax.nn.silu(conv_out)
    x_conv = low(active[..., :E] * chan_mask)
    b_conv = low(active[..., E:E + N])
    c_conv = low(active[..., E + N:])
    dt_step = jax.nn.softplus(dt_raw + dt_bias) * head_mask
    log_step = -jnp.exp(a_log) * dt_step
    return (z_gate, x_conv, b_conv, c_conv, dt_step, log_step)

def block_state(x_conv, b_conv, dt_step, log_step):
    cumulative = jnp.cumsum(log_step, axis=1)
    to_end = jnp.exp(cumulative[:, -1:, :] - cumulative) * dt_step
    weighted = low(x_conv.reshape(x_conv.shape[0], BLOCK, H, HEAD_DIM) * to_end[..., None])
    state_sum = jnp.einsum('lqhp,lqn->lhpn', weighted, b_conv, precision=highest)
    return (state_sum, cumulative[:, -1, :])

def piece_mix(z_gate, x_conv, b_conv, c_conv, dt_step, log_step, state_in, d_skip, gate_gain, chan_count):
    lane_count = x_conv.shape[0]
    cumulative = jnp.cumsum(log_step, axis=1)
    cum_heads = jnp.swapaxes(cumulative, 1, 2)
    causal = jnp.arange(BLOCK)[:, None] >= jnp.arange(BLOCK)[None, :]
    spread = cum_heads[:, :, :, None] - cum_heads[:, :, None, :]
    decays = jnp.where(causal, jnp.exp(jnp.where(causal, spread, 0.0)), 0.0)
    inner_cb = jnp.einsum('lqn,lsn->lqs', c_conv, b_conv, precision=highest)
    scores = low(inner_cb[:, None] * decays * jnp.swapaxes(dt_step, 1, 2)[:, :, None, :])
    x_heads = x_conv.reshape(lane_count, BLOCK, H, HEAD_DIM)
    within = jnp.einsum('lhqs,lshp->lqhp', scores, x_heads, precision=highest)
    carried = jnp.einsum('lqn,lhpn->lqhp', c_conv, state_in, precision=highest) * jnp.exp(cumulative)[..., None]
    mixed_sum = low_back(within + carried) + d_skip[:, None] * x_heads
    gated_rows = mixed_sum.reshape(lane_count, BLOCK, E) * jax.nn.silu(z_gate)
    mean_square = lax.optimization_barrier(jnp.sum(gated_rows * gated_rows, axis=-1, keepdims=True)) / chan_count
    return low(gated_rows * lax.rsqrt(mean_square + epsilon) * gate_gain)

def group_forward(width_group, x_group, keep_group, rows_group, norm_gain, w_zx, w_bc, w_dt, conv_w, conv_b, dt_bias, a_log, d_skip, gate_gain, w_out):
    active_heads = H // 2 ** (N_WIDTH - 1 - width_group)
    chan_mask = (jnp.arange(E) // HEAD_DIM < active_heads).astype(jnp.float32)
    head_mask = (jnp.arange(H) < active_heads).astype(jnp.float32)
    chan_count = jnp.float32(active_heads * HEAD_DIM)
    flat_rows = x_group.reshape(-1, D)
    normed_low = low(rms_front(flat_rows, norm_gain))
    zx_pre = low_back(jnp.dot(normed_low, w_zx, precision=highest)).reshape(N_SEQ, LANES, BLOCK, 2 * E)
    bc_pre = low_back(jnp.dot(normed_low, w_bc, precision=highest)).reshape(N_SEQ, LANES, BLOCK, 2 * N)
    dt_raw = low_back(jnp.dot(normed_low, w_dt, precision=highest)).reshape(N_SEQ, LANES, BLOCK, H)

    def block_step(carry, inputs):
        state_prev, rim_rows = carry
        zx_block, bc_block, dt_block, keep_rows = inputs
        z_gate, x_conv, b_conv, c_conv, dt_step, log_step = piece_front(zx_block, bc_block, dt_block, rim_rows, conv_w, conv_b, dt_bias, a_log, chan_mask, head_mask, keep_rows)
        state_sum, log_total = block_state(x_conv, b_conv, dt_step, log_step)
        state_in = state_prev * keep_rows[:, None, None, None]
        mixed_low = piece_mix(z_gate, x_conv, b_conv, c_conv, dt_step, log_step, state_in, d_skip, gate_gain, chan_count)
        state_out = jnp.exp(log_total)[:, :, None, None] * state_in + state_sum
        return ((state_out, rim_of(zx_block, bc_block, chan_mask)), mixed_low)
    initial = (jnp.zeros((LANES, H, HEAD_DIM, N), jnp.float32), jnp.zeros((LANES, KCONV - 1, CONV_CH), jnp.float32))
    final_carry, mixed_all = lax.scan(jax.checkpoint(block_step), initial, (zx_pre, bc_pre, dt_raw, keep_group))
    branch = low_back(jnp.dot(mixed_all.reshape(-1, E), w_out, precision=highest))
    return x_group + rows_group[..., None] * branch.reshape(x_group.shape)

def reference(tokens, cotangent, starts, valid, norm_gain, w_zx, w_bc, w_dt, conv_w, conv_b, dt_bias, a_log, d_skip, gate_gain, w_out):
    x_all = tokens.astype(jnp.float32).reshape(N_WIDTH, N_SEQ, LANES, BLOCK, D)
    keep_all = 1.0 - starts.astype(jnp.float32).reshape(N_WIDTH, N_SEQ, LANES)
    rows_all = (jnp.arange(BLOCK)[None, None, None, :] < valid.reshape(N_WIDTH, N_SEQ, LANES)[..., None]).astype(jnp.float32)

    def forward(x_inputs, norm_gain, w_zx, w_bc, w_dt, conv_w, conv_b, dt_bias, a_log, d_skip, gate_gain, w_out):
        return jnp.stack([group_forward(width_group, x_inputs[width_group], keep_all[width_group], rows_all[width_group], norm_gain, w_zx, w_bc, w_dt, conv_w, conv_b, dt_bias, a_log, d_skip, gate_gain, w_out) for width_group in range(N_WIDTH)])
    outputs, pullback = jax.vjp(forward, x_all, norm_gain.astype(jnp.float32), w_zx.astype(jnp.float32), w_bc.astype(jnp.float32), w_dt.astype(jnp.float32), conv_w.astype(jnp.float32), conv_b.astype(jnp.float32), dt_bias.astype(jnp.float32), a_log.astype(jnp.float32), d_skip.astype(jnp.float32), gate_gain.astype(jnp.float32), w_out.astype(jnp.float32))
    gradients = pullback(cotangent.astype(jnp.float32).reshape(x_all.shape))
    return (outputs.reshape(TOKENS, D).astype(jnp.bfloat16), gradients[0].reshape(TOKENS, D), gradients[1], gradients[2], gradients[3], gradients[4], gradients[5], gradients[6], gradients[7], gradients[8], gradients[9], gradients[10], gradients[11])
```

```python
from functools import partial

import jax
import jax.numpy as jnp
from jax import lax
from jax.experimental import pallas as pl
from jax.experimental.pallas import tpu as pltpu
from jax.sharding import PartitionSpec as P

H = 64
HEAD_DIM = 64
N = 128
KCONV = 4
BLOCK = 128
E = 4096
SUB = 8

epsilon = 1e-05
highest = lax.Precision.HIGHEST
f32 = jnp.float32
bf16 = jnp.bfloat16

NN = ((1,), (0,))
NT = ((1,), (1,))
TN = ((0,), (0,))


def mm(left, right, dims=NN, precision=None):
    return lax.dot_general(left, right, (dims, ((), ())), precision=precision, preferred_element_type=f32)


def split2(value):
    high = value.astype(bf16)
    return high, (value - high.astype(f32)).astype(bf16)


def mm_right(left, right, dims=NN):
    high, low = split2(right)
    return mm(left, high, dims) + mm(left, low, dims)


def mm_left(left, right, dims=NN):
    high, low = split2(left)
    return mm(high, right, dims) + mm(low, right, dims)


def softplus(v):
    small = jnp.exp(-jnp.abs(v))
    log1p = jnp.where(small < 1e-4, small - 0.5 * small * small, jnp.log(1.0 + small))
    return jnp.maximum(v, 0.0) + log1p


def sigmoid(v):
    return 1.0 / (1.0 + jnp.exp(-v))


def grids():
    row = lax.broadcasted_iota(jnp.int32, (BLOCK, BLOCK), 0)
    col = lax.broadcasted_iota(jnp.int32, (BLOCK, BLOCK), 1)
    return row, col


def halves(pair, lane):
    zero = jnp.zeros_like(pair)
    return jnp.where(lane < HEAD_DIM, pair, zero), jnp.where(lane < HEAD_DIM, zero, pair)


def decay_of(cum, cum_t, head, causal):
    return jnp.exp(jnp.where(causal, cum[:, head : head + 1] - cum_t[head : head + 1, :], -1e30))


TAP, BIAS, SKIP, GAIN, MASK = 0, 4, 5, 6, 7
DT_BIAS, NEG_A, HEAD_MASK = 0, 1, 2


def forward_kernel(
    keep_ref, zx_ref, bcd_ref, grad_ref, chan_ref, bc_par_ref, head_ref, spread_ref,
    conv_ref, mix_ref, bc_ref, step_ref, state_ref, tail_ref, sums_ref,
    state, tail_x, tail_b, pad_x, pad_b,
    *, lanes, heads,
):
    c = pl.program_id(0)
    width = heads * HEAD_DIM
    row, col = grids()
    causal = row >= col
    tril = causal.astype(f32)
    spread = spread_ref[...]

    @pl.when(c == 0)
    def _():
        state[...] = jnp.zeros_like(state)
        tail_x[...] = jnp.zeros_like(tail_x)
        tail_b[...] = jnp.zeros_like(tail_b)

    for lane in range(lanes):
        rows = pl.ds(lane * BLOCK, BLOCK)
        keep = keep_ref[c, lane]
        pre = zx_ref[rows, width:]
        pad_x[lane, 0:SUB] = tail_x[lane] * keep
        pad_x[lane, SUB:] = pre
        tail_ref[0, lane] = tail_x[lane] * keep
        tail_x[lane] = pre[BLOCK - SUB :, :]
        conv = chan_ref[BIAS : BIAS + 1, :]
        for k in range(KCONV):
            conv = conv + pad_x[lane, SUB - KCONV + 1 + k : SUB - KCONV + 1 + k + BLOCK, :] * chan_ref[k : k + 1, :]
        conv_ref[rows, :] = conv
        x_low = (conv * sigmoid(conv) * chan_ref[MASK : MASK + 1, :]).astype(bf16)

        pre_b = bcd_ref[rows, : 2 * N]
        pad_b[lane, 0:SUB] = tail_b[lane] * keep
        pad_b[lane, SUB:] = pre_b
        tail_b[lane] = pre_b[BLOCK - SUB :, :]
        conv_b = bc_par_ref[BIAS : BIAS + 1, :]
        for k in range(KCONV):
            conv_b = conv_b + pad_b[lane, SUB - KCONV + 1 + k : SUB - KCONV + 1 + k + BLOCK, :] * bc_par_ref[k : k + 1, :]
        bc_low = (conv_b * sigmoid(conv_b)).astype(bf16)
        bc_ref[rows, :] = bc_low
        b_low, c_low = bc_low[:, :N], bc_low[:, N:]

        raw = bcd_ref[rows, 2 * N :] + head_ref[DT_BIAS : DT_BIAS + 1, :]
        dt = softplus(raw) * head_ref[HEAD_MASK : HEAD_MASK + 1, :]
        cum = mm(tril, head_ref[NEG_A : NEG_A + 1, :] * dt, precision=highest)
        step_ref[rows, :BLOCK] = cum
        step_ref[rows, BLOCK:] = dt
        cum_t, dt_t = cum.T, dt.T
        last = cum[BLOCK - 1 :, :]
        carry_x = mm_left(jnp.exp(cum), spread)
        end_x = mm_left(jnp.exp(last - cum) * dt, spread)
        last_x = carry_x[BLOCK - 1 :, :]

        inner = mm(c_low, b_low, NT)
        parts = []
        for j in range(heads // 2):
            pair = x_low[:, 2 * HEAD_DIM * j : 2 * HEAD_DIM * (j + 1)]
            scores = [
                (inner * decay_of(cum, cum_t, h, causal) * dt_t[h : h + 1, :]).astype(bf16)
                for h in (2 * j, 2 * j + 1)
            ]
            parts.append(mm(jnp.concatenate(scores, axis=1), jnp.concatenate(halves(pair, col), axis=0)))
        within = jnp.concatenate(parts, axis=1)

        state_in = state[lane] * keep
        state_ref[0, lane] = state_in
        carried = mm_right(c_low, state_in) * carry_x
        x_f = x_low.astype(f32)
        mixed = within + carried + chan_ref[SKIP : SKIP + 1, :] * x_f
        mix_ref[rows, :] = mixed
        weighted = (x_f * end_x).astype(bf16)
        state[lane] = last_x * state_in + mm(b_low, weighted, TN)

        z = zx_ref[rows, :width]
        gated = mixed * (z * sigmoid(z))
        ones = jnp.ones((SUB, width), bf16)
        square = mm_right(ones, gated * gated, NT)
        cross = mm_right(ones, grad_ref[rows, :] * chan_ref[GAIN : GAIN + 1, :] * gated, NT)
        sub = lax.broadcasted_iota(jnp.int32, (SUB, BLOCK), 0)
        sums_ref[0, lane] = jnp.where(sub == 0, square, jnp.where(sub == 1, cross, 0.0))


def backward_kernel(
    keep_ref, zx_ref, bcd_ref, grad_ref, chan_ref, head_ref, spread_ref,
    conv_ref, mix_ref, bc_ref, step_ref, state_ref, tail_ref, scale_ref,
    dzx_ref, ddt_ref, dbc_ref, dchan_ref, dhead_ref,
    state_grad, next_conv, pad_x, pad_d,
    *, lanes, heads, blocks,
):
    lap = pl.program_id(0)
    c = blocks - 1 - lap
    width = heads * HEAD_DIM
    row, col = grids()
    causal = row >= col
    triu = (col >= row).astype(f32)
    spread = spread_ref[...]

    @pl.when(lap == 0)
    def _():
        state_grad[...] = jnp.zeros_like(state_grad)
        next_conv[...] = jnp.zeros_like(next_conv)
        dchan_ref[...] = jnp.zeros_like(dchan_ref)
        dhead_ref[...] = jnp.zeros_like(dhead_ref)

    def total(value):
        return jnp.sum(value, axis=0, keepdims=True)

    for lane in range(lanes):
        rows = pl.ds(lane * BLOCK, BLOCK)
        keep = keep_ref[c, lane]
        z = zx_ref[rows, :width]
        conv = conv_ref[rows, :]
        mixed = mix_ref[rows, :]
        grad = grad_ref[rows, :]
        gain = chan_ref[GAIN : GAIN + 1, :]
        skip = chan_ref[SKIP : SKIP + 1, :]
        rate = scale_ref[rows, 0:1]
        pull = scale_ref[rows, 1:2]
        gate = sigmoid(z)
        silu = z * gate
        gated = mixed * silu
        dgated = grad * gain * rate - gated * pull
        dzx_ref[rows, :width] = (dgated * mixed * (gate * (1.0 + z * (1.0 - gate)))).astype(bf16)
        dmixed = dgated * silu
        act = sigmoid(conv)
        x_low = (conv * act * chan_ref[MASK : MASK + 1, :]).astype(bf16)
        x_f = x_low.astype(f32)
        dchan_ref[GAIN : GAIN + 1, :] += total(grad * gated * rate)
        dchan_ref[SKIP : SKIP + 1, :] += total(dmixed * x_f)
        dlow = dmixed.astype(bf16)
        dlow_f = dlow.astype(f32)

        b_low, c_low = bc_ref[rows, :N], bc_ref[rows, N:]
        cum, dt = step_ref[rows, :BLOCK], step_ref[rows, BLOCK:]
        cum_t, dt_t = cum.T, dt.T
        last = cum[BLOCK - 1 :, :]
        to_last = jnp.exp(last - cum)
        carry_x = mm_left(jnp.exp(cum), spread)
        end_x = mm_left(to_last * dt, spread)
        last_x = carry_x[BLOCK - 1 :, :]

        inner = mm(c_low, b_low, NT)
        dinner = jnp.zeros((BLOCK, BLOCK), f32)
        parts, dt_rows = [], []
        for j in range(heads // 2):
            lanes_j = slice(2 * HEAD_DIM * j, 2 * HEAD_DIM * (j + 1))
            pair, dpair = x_low[:, lanes_j], dlow[:, lanes_j]
            dstack = jnp.concatenate(halves(dpair, col), axis=0)
            dscores = mm(dstack, pair, NT)
            scores = []
            for i, h in enumerate((2 * j, 2 * j + 1)):
                decay = decay_of(cum, cum_t, h, causal)
                step = dt_t[h : h + 1, :]
                scores.append((inner * decay * step).astype(bf16))
                part = dscores[i * BLOCK : (i + 1) * BLOCK] * decay
                dinner = dinner + part * step
                dt_rows.append(total(part * inner))
            parts.append(mm(jnp.concatenate(scores, axis=0), dstack, TN))
        dx_within = jnp.concatenate(parts, axis=1)
        dt_rows.append(jnp.zeros((BLOCK - heads, BLOCK), f32))
        ddt_within = jnp.concatenate(dt_rows, axis=0).T

        state_in = state_ref[0, lane]
        sgrad = state_grad[lane]
        in_high, in_low = split2(state_in)
        sg_high, sg_low = split2(sgrad)
        dcarry = dlow_f * carry_x
        dc_high, dc_low = split2(dcarry)
        di_high, di_low = split2(dinner)
        dc = mm(dc_high, in_high, NT) + mm(dc_high, in_low, NT) + mm(dc_low, in_high, NT)
        dc = dc + mm(di_high, b_low) + mm(di_low, b_low)
        weighted = (x_f * end_x).astype(bf16)
        db = mm(weighted, sg_high, NT) + mm(weighted, sg_low, NT)
        db = db + mm(di_high, c_low, TN) + mm(di_low, c_low, TN)
        dbc_ref[rows, :N] = db
        dbc_ref[rows, N:] = dc
        dweighted = mm(b_low, sg_high) + mm(b_low, sg_low)
        dx = dx_within + dweighted * end_x
        dcum = mm_left(dlow_f * (mixed - skip * x_f) - x_f * dx, spread, NT)
        dend = mm_left(dweighted * x_f, spread, NT)
        touch = jnp.broadcast_to(total(sgrad * state_in), (SUB, width))
        dlast = total(dend * to_last * dt) + jnp.exp(last) * mm_left(touch, spread, NT)[0:1]
        dlog = mm(triu, dcum, precision=highest) + dlast
        neg_a = head_ref[NEG_A : NEG_A + 1, :]
        ddt = ddt_within + dend * to_last + dlog * neg_a
        raw = bcd_ref[rows, 2 * N :] + head_ref[DT_BIAS : DT_BIAS + 1, :]
        draw = ddt * sigmoid(raw) * head_ref[HEAD_MASK : HEAD_MASK + 1, :]
        ddt_ref[rows, :] = draw.astype(bf16)
        dhead_ref[0:1, :] += total(draw)
        dhead_ref[1:2, :] += total(dlog * neg_a * dt)
        state_grad[lane] = keep * (mm(c_low, dc_high, TN) + mm(c_low, dc_low, TN) + last_x * sgrad)

        dx = dx + skip * dmixed
        dconv = dx * chan_ref[MASK : MASK + 1, :] * (act * (1.0 + conv * (1.0 - act)))
        pad_d[lane, :BLOCK] = dconv
        pad_d[lane, BLOCK:] = next_conv[lane]
        next_conv[lane] = dconv[:SUB] * keep
        pad_x[lane, :SUB] = tail_ref[0, lane]
        pad_x[lane, SUB:] = zx_ref[rows, width:]
        dpre = jnp.zeros((BLOCK, width), f32)
        for k in range(KCONV):
            dpre = dpre + pad_d[lane, KCONV - 1 - k : KCONV - 1 - k + BLOCK, :] * chan_ref[k : k + 1, :]
            dchan_ref[k : k + 1, :] += total(dconv * pad_x[lane, SUB - KCONV + 1 + k : SUB - KCONV + 1 + k + BLOCK, :])
        dchan_ref[BIAS : BIAS + 1, :] += total(dconv)
        dzx_ref[rows, width:] = dpre.astype(bf16)


def run_forward(keep, zx, bcd, grad, chan, bc_par, head, spread, lanes, heads):
    rows, width = grad.shape
    step = lanes * BLOCK
    blocks = rows // step
    by_block = lambda cols: pl.BlockSpec((step, cols), lambda c: (c, 0))
    whole = lambda a: pl.BlockSpec(a.shape, lambda c: (0,) * a.ndim)
    per_lane = lambda r, cols: pl.BlockSpec((1, lanes, r, cols), lambda c: (c, 0, 0, 0))
    return pl.pallas_call(
        partial(forward_kernel, lanes=lanes, heads=heads),
        grid=(blocks,),
        in_specs=[
            pl.BlockSpec(memory_space=pltpu.SMEM), by_block(2 * width), by_block(2 * N + BLOCK), by_block(width),
            whole(chan), whole(bc_par), whole(head), whole(spread),
        ],
        out_specs=[
            by_block(width), by_block(width), by_block(2 * N), by_block(2 * BLOCK),
            per_lane(N, width), per_lane(SUB, width), per_lane(SUB, BLOCK),
        ],
        out_shape=[
            jax.ShapeDtypeStruct((rows, width), f32), jax.ShapeDtypeStruct((rows, width), f32),
            jax.ShapeDtypeStruct((rows, 2 * N), bf16), jax.ShapeDtypeStruct((rows, 2 * BLOCK), f32),
            jax.ShapeDtypeStruct((blocks, lanes, N, width), f32), jax.ShapeDtypeStruct((blocks, lanes, SUB, width), f32),
            jax.ShapeDtypeStruct((blocks, lanes, SUB, BLOCK), f32),
        ],
        scratch_shapes=[
            pltpu.VMEM((lanes, N, width), f32), pltpu.VMEM((lanes, SUB, width), f32), pltpu.VMEM((lanes, SUB, 2 * N), f32),
            pltpu.VMEM((lanes, BLOCK + SUB, width), f32), pltpu.VMEM((lanes, BLOCK + SUB, 2 * N), f32),
        ],
        compiler_params=pltpu.CompilerParams(vmem_limit_bytes=40 << 20, dimension_semantics=("arbitrary",)),
        cost_estimate=pl.CostEstimate(flops=rows * width * 2048, bytes_accessed=rows * width * 32, transcendentals=rows * width * 4),
        name="mix_forward",
    )(keep, zx, bcd, grad, chan, bc_par, head, spread)


def run_backward(keep, zx, bcd, grad, chan, head, spread, conv, mix, bc, step_arr, state, tail, scale, lanes, heads):
    rows, width = grad.shape
    step = lanes * BLOCK
    blocks = rows // step
    by_block = lambda cols: pl.BlockSpec((step, cols), lambda c: (blocks - 1 - c, 0))
    whole = lambda a: pl.BlockSpec(a.shape, lambda c: (0,) * a.ndim)
    fixed = lambda shape: pl.BlockSpec(shape, lambda c: (0,) * len(shape))
    per_lane = lambda r, cols: pl.BlockSpec((1, lanes, r, cols), lambda c: (blocks - 1 - c, 0, 0, 0))
    return pl.pallas_call(
        partial(backward_kernel, lanes=lanes, heads=heads, blocks=blocks),
        grid=(blocks,),
        in_specs=[
            pl.BlockSpec(memory_space=pltpu.SMEM), by_block(2 * width), by_block(2 * N + BLOCK), by_block(width),
            whole(chan), whole(head), whole(spread),
            by_block(width), by_block(width), by_block(2 * N), by_block(2 * BLOCK),
            per_lane(N, width), per_lane(SUB, width), by_block(SUB),
        ],
        out_specs=[by_block(2 * width), by_block(BLOCK), by_block(2 * N), fixed((SUB, width)), fixed((SUB, BLOCK))],
        out_shape=[
            jax.ShapeDtypeStruct((rows, 2 * width), bf16), jax.ShapeDtypeStruct((rows, BLOCK), bf16),
            jax.ShapeDtypeStruct((rows, 2 * N), f32), jax.ShapeDtypeStruct((SUB, width), f32),
            jax.ShapeDtypeStruct((SUB, BLOCK), f32),
        ],
        scratch_shapes=[
            pltpu.VMEM((lanes, N, width), f32), pltpu.VMEM((lanes, SUB, width), f32),
            pltpu.VMEM((lanes, BLOCK + SUB, width), f32), pltpu.VMEM((lanes, BLOCK + SUB, width), f32),
        ],
        compiler_params=pltpu.CompilerParams(vmem_limit_bytes=48 << 20, dimension_semantics=("arbitrary",)),
        cost_estimate=pl.CostEstimate(flops=rows * width * 6144, bytes_accessed=rows * width * 40, transcendentals=rows * width * 6),
        name="mix_backward",
    )(keep, zx, bcd, grad, chan, head, spread, conv, mix, bc, step_arr, state, tail, scale)


def bc_front(bc_pre, taps, bias, keep):
    rim = bc_pre[:, :, BLOCK - KCONV + 1 :, :]
    before = jnp.concatenate([jnp.zeros_like(rim[:1]), rim[:-1]], axis=0) * keep[:, :, None, None]
    padded = jnp.concatenate([before, bc_pre], axis=2)
    out = bias
    for k in range(KCONV):
        out = out + padded[:, :, k : k + BLOCK, :] * taps[k]
    return jax.nn.silu(out)


def packed_rows(rows, count):
    flat = jnp.stack(rows)
    return jnp.pad(flat, ((0, count - len(rows)), (0, 0)))


def heads_body(
    tokens, cotangent, starts, valid, norm_gain, w_zx, w_bc, w_dt, conv_w, conv_b, dt_bias, a_log, d_skip, gate_gain, w_out
):
    peers = lax.axis_size("seq")
    widths = lax.axis_size("width")
    place = lax.axis_index("seq")
    lanes = starts.shape[1]
    heads = H // peers
    chans = heads * HEAD_DIM
    own, model = tokens.shape
    rows = own * peers
    active = jnp.right_shift(jnp.int32(H), widths - 1 - lax.axis_index("width"))
    count = (active * HEAD_DIM).astype(f32)
    first = place * heads

    x_rows = tokens.astype(f32)
    rate = lax.rsqrt(jnp.mean(x_rows * x_rows, axis=-1, keepdims=True) + epsilon)
    normed_own = (x_rows * rate * norm_gain).astype(bf16)
    row_mask = (jnp.arange(BLOCK)[None, :] < valid[0][:, None]).astype(f32).reshape(-1, 1)
    cot_rows = cotangent.astype(f32)
    bgrad_own = (cot_rows * row_mask).astype(bf16)

    weights = lax.all_to_all(w_zx.reshape(-1, 2, peers, chans), "seq", 2, 0, tiled=True).reshape(model, 2 * chans)
    normed = lax.all_gather(normed_own, "seq", axis=0, tiled=True)
    bgrad = lax.all_gather(bgrad_own, "seq", axis=0, tiled=True)
    bc_dt = lax.all_gather(jnp.concatenate([w_bc, w_dt], axis=1), "seq", axis=0, tiled=True)
    keep = 1.0 - lax.all_gather(starts, "seq", axis=0, tiled=True).astype(f32)
    weights_bc = bc_dt[:, : 2 * N]
    weights_dt = jnp.pad(lax.dynamic_slice_in_dim(bc_dt, 2 * N + first, heads, 1), ((0, 0), (0, BLOCK - heads)))

    taps_x = lax.dynamic_slice_in_dim(conv_w, first * HEAD_DIM, chans, 0).T
    of_chans = lambda a: lax.dynamic_slice_in_dim(a, first * HEAD_DIM, chans, 0)
    of_heads = lambda a: jnp.pad(lax.dynamic_slice_in_dim(a, first, heads, 0), (0, BLOCK - heads))
    head_on = (jnp.arange(BLOCK) < jnp.minimum(active - first, heads)).astype(f32)
    chan_on = (jnp.arange(chans) // HEAD_DIM < active - first).astype(f32)
    skip_x = jnp.repeat(lax.dynamic_slice_in_dim(d_skip, first, heads, 0), HEAD_DIM)
    chan = packed_rows([*taps_x, of_chans(conv_b), skip_x, of_chans(gate_gain), chan_on], SUB)
    bc_par = packed_rows([*conv_w[E:].T, conv_b[E:]], SUB)
    head = packed_rows([of_heads(dt_bias), of_heads(-jnp.exp(a_log)), head_on], SUB)
    spread = (jnp.arange(chans)[None, :] // HEAD_DIM == jnp.arange(BLOCK)[:, None]).astype(bf16)

    zx = mm(normed, weights)
    bcd = mm(normed, jnp.concatenate([weights_bc, weights_dt], axis=1))
    mixed_grad = mm(bgrad, w_out, NT)
    conv, mix, bc, steps, state, tail, sums = run_forward(
        keep, zx, bcd, mixed_grad, chan, bc_par, head, spread, lanes, heads
    )
    sums = lax.psum(sums[:, :, :2, :], "seq")
    gate_rate = lax.rsqrt(sums[:, :, 0] / count + epsilon).reshape(rows, 1)
    gate_pull = gate_rate * gate_rate * gate_rate * sums[:, :, 1].reshape(rows, 1) / count
    scale = jnp.pad(jnp.concatenate([gate_rate, gate_pull], axis=1), ((0, 0), (0, SUB - 2)))
    mixed_low = lax.optimization_barrier(
        (mix * jax.nn.silu(zx[:, :chans]) * gate_rate * chan[GAIN]).astype(bf16)
    )
    branch = lax.psum_scatter(mm(mixed_low, w_out).astype(bf16), "seq", scatter_dimension=0, tiled=True).astype(f32)
    output = (x_rows + row_mask * branch).astype(bf16)
    out_grad = lax.psum(mm(mixed_low, bgrad, TN).astype(bf16), "width").astype(f32)

    dzx, ddt, dbc, dchan, dhead = run_backward(
        keep, zx, bcd, mixed_grad, chan, head, spread, conv, mix, bc, steps, state, tail, scale, lanes, heads
    )

    dbc = lax.psum(dbc, "seq").reshape(peers, lanes, BLOCK, 2 * N)
    bc_pre = bcd[:, : 2 * N].reshape(peers, lanes, BLOCK, 2 * N)
    unused, bc_back = jax.vjp(partial(bc_front, keep=keep), bc_pre, conv_w[E:].T, conv_b[E:])
    dbc_pre, dtaps_bc, dbias_bc = bc_back(dbc)
    bc_grad = lax.optimization_barrier(dbc_pre.reshape(rows, 2 * N).astype(bf16))

    wide = jnp.concatenate([mm(normed, dzx, TN).astype(bf16), mm(normed, ddt, TN).astype(bf16)], axis=1)
    wide = wide.reshape(peers, widths, own // widths, -1)
    wide = lax.psum_scatter(wide, "width", scatter_dimension=1, tiled=True)[:, 0]
    wide = lax.all_to_all(wide, "seq", 0, 0, tiled=True)
    wide = lax.all_gather(wide, "width", axis=1, tiled=True).astype(f32)
    grad_zx = wide[:, :, : 2 * chans].reshape(peers, own, 2, chans).transpose(1, 2, 0, 3).reshape(own, 2 * E)
    grad_dt = wide[:, :, 2 * chans : 2 * chans + heads].transpose(1, 0, 2).reshape(own, H)
    normed_cols = lax.dynamic_slice_in_dim(normed, place * own, own, 1)
    grad_bc = lax.psum(mm(normed_cols, bc_grad, TN), "width")

    wide_grad = mm(dzx, weights, NT) + mm(ddt, weights_dt, NT)
    normed_grad = lax.psum_scatter(wide_grad.astype(bf16), "seq", scatter_dimension=0, tiled=True).astype(f32)
    normed_grad = normed_grad + mm(lax.dynamic_slice_in_dim(bc_grad, place * own, own, 0), weights_bc, NT)
    unit = x_rows * rate
    pulled = normed_grad * norm_gain
    input_grad = cot_rows + rate * (pulled - unit * jnp.mean(pulled * unit, axis=-1, keepdims=True))
    grad_norm = jnp.sum(w_zx.astype(f32) * grad_zx, axis=1) + jnp.sum(w_bc.astype(f32) * grad_bc, axis=1)
    grad_norm = grad_norm + jnp.sum(w_dt.astype(f32) * grad_dt, axis=1)
    grad_norm = grad_norm / lax.dynamic_slice_in_dim(norm_gain, place * own, own, 0)

    once = (place == 0).astype(f32)
    at_heads = lambda a: lax.dynamic_update_slice_in_dim(jnp.zeros((H,), f32), a, first, 0)
    at_chans = lambda a: lax.dynamic_update_slice_in_dim(jnp.zeros((E,), f32), a, first * HEAD_DIM, 0)
    taps = [jnp.concatenate([at_chans(dchan[k]), dtaps_bc[k] * once]) for k in range(KCONV)]
    bias = jnp.concatenate([at_chans(dchan[BIAS]), dbias_bc * once])
    skip = jnp.sum(dchan[SKIP].reshape(heads, HEAD_DIM), axis=1)
    small = [*taps, bias, at_chans(dchan[GAIN]), at_heads(dhead[0, :heads]), at_heads(dhead[1, :heads]), at_heads(skip)]
    sizes = [a.shape[0] for a in small]
    summed = lax.psum(jnp.concatenate(small), ("width", "seq"))
    pieces = []
    for size in sizes:
        pieces.append(lax.dynamic_slice_in_dim(summed, sum(a.shape[0] * peers for a in pieces) + place * (size // peers), size // peers, 0))
    grad_taps = jnp.stack(pieces[:KCONV], axis=1)
    grad_bias, grad_gain, grad_dtb, grad_alog, grad_skip = pieces[KCONV:]
    return (
        output, input_grad, grad_norm, grad_zx, grad_bc, grad_dt, grad_taps, grad_bias, grad_dtb, grad_alog, grad_skip,
        grad_gain, out_grad,
    )


def passed_along(array, axis, by):
    peers = lax.axis_size(axis)
    pairs = [(i, i + by) for i in range(peers) if 0 <= i + by < peers]
    return lax.ppermute(array, axis, pairs)


def carried_in(part, axis, combine, identity, reverse):
    count = lax.axis_size(axis)
    place = lax.axis_index(axis)
    at = count - 1 - place if reverse else place
    by = -1 if reverse else 1
    state = jax.tree.map(lambda a, e: jnp.zeros_like(a) + jnp.asarray(e, a.dtype), part, identity)

    def one(lap, state):
        sent = combine(state, part)
        got = jax.tree.map(lambda a: passed_along(a, axis, by), sent)
        return jax.tree.map(lambda old, new: jnp.where(at == lap + 1, new, old), state, got)

    return lax.fori_loop(0, count - 1, one, state)


def round_value(v):
    return lax.optimization_barrier(v.astype(jnp.bfloat16)).astype(jnp.float32)


def keep_round(v):
    return (round_value(v), None)


def pass_grad(kept, grad):
    return (grad,)


def same_value(v):
    return v


def keep_same(v):
    return (v, None)


def round_grad(kept, grad):
    return (round_value(grad),)


def low(v):
    wrapped = jax.custom_vjp(round_value)
    wrapped.defvjp(keep_round, pass_grad)
    return wrapped(v)


def low_back(v):
    wrapped = jax.custom_vjp(same_value)
    wrapped.defvjp(keep_same, round_grad)
    return wrapped(v)


def rms_front(x_rows, norm_gain):
    mean_square = jnp.mean(x_rows * x_rows, axis=-1, keepdims=True)
    return x_rows * lax.rsqrt(mean_square + epsilon) * norm_gain


def rim_of(zx_pre, bc_pre, chan_mask):
    return jnp.concatenate(
        [zx_pre[:, BLOCK - KCONV + 1 :, E:] * chan_mask, bc_pre[:, BLOCK - KCONV + 1 :, :]], axis=-1
    )


def piece_front(
    zx_pre,
    bc_pre,
    dt_raw,
    rim_rows,
    conv_w,
    conv_b,
    dt_bias,
    a_log,
    chan_mask,
    head_mask,
    keep_rows,
):
    z_gate = zx_pre[..., :E] * chan_mask
    pre_conv = jnp.concatenate([zx_pre[..., E:] * chan_mask, bc_pre], axis=-1)
    padded = jnp.concatenate([rim_rows * keep_rows[:, None, None], pre_conv], axis=1)
    conv_out = conv_b + padded[:, 0:BLOCK, :] * conv_w[:, 0]
    for offset in range(1, KCONV):
        conv_out = conv_out + padded[:, offset : offset + BLOCK, :] * conv_w[:, offset]
    active = jax.nn.silu(conv_out)
    x_conv = low(active[..., :E] * chan_mask)
    b_conv = low(active[..., E : E + N])
    c_conv = low(active[..., E + N :])
    dt_step = jax.nn.softplus(dt_raw + dt_bias) * head_mask
    log_step = -jnp.exp(a_log) * dt_step
    return (z_gate, x_conv, b_conv, c_conv, dt_step, log_step)


def block_state(x_conv, b_conv, dt_step, log_step):
    cumulative = jnp.cumsum(log_step, axis=1)
    to_end = jnp.exp(cumulative[:, -1:, :] - cumulative) * dt_step
    weighted = low(x_conv.reshape(x_conv.shape[0], BLOCK, H, HEAD_DIM) * to_end[..., None])
    state_sum = jnp.einsum("lqhp,lqn->lhpn", weighted, b_conv, precision=highest)
    return (state_sum, cumulative[:, -1, :])


def piece_mix(
    z_gate, x_conv, b_conv, c_conv, dt_step, log_step, state_in, d_skip, gate_gain, chan_count
):
    lane_count = x_conv.shape[0]
    cumulative = jnp.cumsum(log_step, axis=1)
    cum_heads = jnp.swapaxes(cumulative, 1, 2)
    causal = jnp.arange(BLOCK)[:, None] >= jnp.arange(BLOCK)[None, :]
    spread = cum_heads[:, :, :, None] - cum_heads[:, :, None, :]
    decays = jnp.where(causal, jnp.exp(jnp.where(causal, spread, 0.0)), 0.0)
    inner_cb = jnp.einsum("lqn,lsn->lqs", c_conv, b_conv, precision=highest)
    scores = low(inner_cb[:, None] * decays * jnp.swapaxes(dt_step, 1, 2)[:, :, None, :])
    x_heads = x_conv.reshape(lane_count, BLOCK, H, HEAD_DIM)
    within = jnp.einsum("lhqs,lshp->lqhp", scores, x_heads, precision=highest)
    carried = (
        jnp.einsum("lqn,lhpn->lqhp", c_conv, state_in, precision=highest)
        * jnp.exp(cumulative)[..., None]
    )
    mixed_sum = low_back(within + carried) + d_skip[:, None] * x_heads
    gated_rows = mixed_sum.reshape(lane_count, BLOCK, E) * jax.nn.silu(z_gate)
    mean_square = jnp.sum(gated_rows * gated_rows, axis=-1, keepdims=True) / chan_count
    return low(gated_rows * lax.rsqrt(mean_square + epsilon) * gate_gain)


def mix_lanes(lane_inputs, d_skip, gate_gain, chan_count):

    def one_lane(pieces):
        lane_gate, lane_xconv, lane_bconv, lane_cconv, lane_step, lane_decay, lane_state = pieces
        return piece_mix(
            lane_gate[None],
            lane_xconv[None],
            lane_bconv[None],
            lane_cconv[None],
            lane_step[None],
            lane_decay[None],
            lane_state[None],
            d_skip,
            gate_gain,
            chan_count,
        )[0]

    return lax.map(one_lane, lane_inputs)


def mix_back_lanes(lane_inputs, mixed_grad, d_skip, gate_gain, chan_count):

    def lane_mix(z_gate, x_conv, b_conv, c_conv, dt_step, log_step, state_in, skip_coef, gain_coef):
        return piece_mix(
            z_gate[None],
            x_conv[None],
            b_conv[None],
            c_conv[None],
            dt_step[None],
            log_step[None],
            state_in[None],
            skip_coef,
            gain_coef,
            chan_count,
        )[0]

    def one_lane(pieces):
        (
            lane_gate,
            lane_xconv,
            lane_bconv,
            lane_cconv,
            lane_step,
            lane_decay,
            lane_state,
            lane_grad,
        ) = pieces
        unused, pull_lane = jax.vjp(
            lane_mix,
            lane_gate,
            lane_xconv,
            lane_bconv,
            lane_cconv,
            lane_step,
            lane_decay,
            lane_state,
            d_skip,
            gate_gain,
        )
        return pull_lane(lane_grad)

    lane_grads = lax.map(one_lane, lane_inputs + (mixed_grad,))
    return (lane_grads[:7], jnp.sum(lane_grads[7], axis=0), jnp.sum(lane_grads[8], axis=0))


def chain_combine(earlier, latter):
    return (earlier[0] * latter[0], latter[0][:, :, None, None] * earlier[1] + latter[1])


def share_out(out_grad):
    return lax.psum_scatter(out_grad, "seq", scatter_dimension=0, tiled=True)


def contract_rows(left, right):
    return lax.dot_general(
        left, right, (((0,), (0,)), ((), ())), preferred_element_type=jnp.float32
    )


def contract_cols(left, right):
    return lax.dot_general(
        left, right, (((1,), (1,)), ((), ())), preferred_element_type=jnp.float32
    )


def rows_body(
    tokens,
    cotangent,
    starts,
    valid,
    norm_gain,
    w_zx,
    w_bc,
    w_dt,
    conv_w,
    conv_b,
    dt_bias,
    a_log,
    d_skip,
    gate_gain,
    w_out,
):
    lane_count = starts.shape[1]
    width_index = lax.axis_index("width")
    shift_bits = lax.axis_size("width") - 1 - width_index
    active_heads = jnp.right_shift(jnp.int32(H), shift_bits)
    chan_mask = (jnp.arange(E) // HEAD_DIM < active_heads).astype(jnp.float32)
    head_mask = (jnp.arange(H) < active_heads).astype(jnp.float32)
    chan_count = (active_heads * HEAD_DIM).astype(jnp.float32)
    keep_rows = 1.0 - starts[0].astype(jnp.float32)
    row_mask = (jnp.arange(BLOCK)[None, :] < valid[0][:, None]).astype(jnp.float32).reshape(-1, 1)
    x_rows = tokens.astype(jnp.float32)
    normed, norm_back = jax.vjp(rms_front, x_rows, norm_gain)
    normed_low = normed.astype(jnp.bfloat16)
    zx_full, bc_full, dt_full, out_full = (
        lax.all_gather(w_zx, "seq", axis=0, tiled=True),
        lax.all_gather(w_bc, "seq", axis=0, tiled=True),
        lax.all_gather(w_dt, "seq", axis=0, tiled=True),
        lax.all_gather(w_out, "seq", axis=0, tiled=True),
    )
    zx_pre = jnp.dot(normed_low, zx_full, preferred_element_type=jnp.float32).reshape(
        lane_count, BLOCK, 2 * E
    )
    bc_pre = jnp.dot(normed_low, bc_full, preferred_element_type=jnp.float32).reshape(
        lane_count, BLOCK, 2 * N
    )
    dt_raw = jnp.dot(normed_low, dt_full, preferred_element_type=jnp.float32).reshape(
        lane_count, BLOCK, H
    )
    rim_rows = passed_along(rim_of(zx_pre, bc_pre, chan_mask), "seq", 1)
    front_fn = partial(piece_front, chan_mask=chan_mask, head_mask=head_mask, keep_rows=keep_rows)
    front_out, front_back = jax.vjp(
        front_fn, zx_pre, bc_pre, dt_raw, rim_rows, conv_w, conv_b, dt_bias, a_log
    )
    z_gate, x_conv, b_conv, c_conv, dt_step, log_step = front_out
    (state_sum, log_total), state_back = jax.vjp(block_state, x_conv, b_conv, dt_step, log_step)
    carry_rate = jnp.exp(log_total) * keep_rows[:, None]
    identity = (jnp.ones_like(carry_rate), jnp.zeros_like(state_sum))
    prefix_pair = carried_in((carry_rate, state_sum), "seq", chain_combine, identity, False)
    state_in = prefix_pair[1] * keep_rows[:, None, None, None]
    lane_inputs = (z_gate, x_conv, b_conv, c_conv, dt_step, log_step, state_in)
    mixed_low = mix_lanes(lane_inputs, d_skip, gate_gain, chan_count)
    mixed_flat = mixed_low.reshape(-1, E).astype(jnp.bfloat16)
    branch = jnp.dot(mixed_flat, out_full, preferred_element_type=jnp.float32)
    output = (x_rows + row_mask * branch).astype(jnp.bfloat16)
    cot_rows = cotangent.astype(jnp.float32)
    branch_grad = (cot_rows * row_mask).astype(jnp.bfloat16)
    out_grad = contract_rows(mixed_flat, branch_grad)
    mixed_grad = contract_cols(branch_grad, out_full).reshape(lane_count, BLOCK, E)
    lane_grads, grad_skip, grad_gain = mix_back_lanes(
        lane_inputs, mixed_grad, d_skip, gate_gain, chan_count
    )
    grad_gate, grad_x, grad_b, grad_c, grad_dt, grad_log, grad_state = lane_grads
    later_pair = carried_in(
        (carry_rate, grad_state * keep_rows[:, None, None, None]),
        "seq",
        chain_combine,
        identity,
        True,
    )
    later_grad = later_pair[1]
    grad_total = jnp.exp(log_total) * jnp.sum(later_grad * state_in, axis=(2, 3))
    grad_x_more, grad_b_more, grad_dt_more, grad_log_more = state_back((later_grad, grad_total))
    grad_zx, grad_bc, grad_dtraw, grad_rim, grad_convw, grad_convb, grad_dtbias, grad_alog = (
        front_back(
            (
                grad_gate,
                grad_x + grad_x_more,
                grad_b + grad_b_more,
                grad_c,
                grad_dt + grad_dt_more,
                grad_log + grad_log_more,
            )
        )
    )
    rim_grad = passed_along(grad_rim.astype(jnp.bfloat16), "seq", -1).astype(grad_rim.dtype)
    grad_zx = grad_zx.at[:, BLOCK - KCONV + 1 :, E:].add(rim_grad[..., :E] * chan_mask)
    grad_bc = grad_bc.at[:, BLOCK - KCONV + 1 :, :].add(rim_grad[..., E:])
    zx_low = grad_zx.reshape(-1, 2 * E).astype(jnp.bfloat16)
    bc_low = grad_bc.reshape(-1, 2 * N).astype(jnp.bfloat16)
    dt_low = grad_dtraw.reshape(-1, H).astype(jnp.bfloat16)
    zx_weight_grad = contract_rows(normed_low, zx_low)
    bc_weight_grad = contract_rows(normed_low, bc_low)
    dt_weight_grad = contract_rows(normed_low, dt_low)
    normed_grad = (
        contract_cols(zx_low, zx_full)
        + contract_cols(bc_low, bc_full)
        + contract_cols(dt_low, dt_full)
    )
    grad_x_rows, grad_norm = norm_back(normed_grad)
    input_grad = cot_rows + grad_x_rows
    out_shard = share_out(out_grad)
    row_shards = (
        lax.psum_scatter(grad_norm, "seq", scatter_dimension=0, tiled=True),
        lax.psum_scatter(zx_weight_grad, "seq", scatter_dimension=0, tiled=True),
        lax.psum_scatter(bc_weight_grad, "seq", scatter_dimension=0, tiled=True),
        lax.psum_scatter(dt_weight_grad, "seq", scatter_dimension=0, tiled=True),
        lax.psum_scatter(grad_convw, "seq", scatter_dimension=0, tiled=True),
        lax.psum_scatter(grad_convb, "seq", scatter_dimension=0, tiled=True),
        lax.psum_scatter(grad_dtbias, "seq", scatter_dimension=0, tiled=True),
        lax.psum_scatter(grad_alog, "seq", scatter_dimension=0, tiled=True),
        lax.psum_scatter(grad_skip, "seq", scatter_dimension=0, tiled=True),
        lax.psum_scatter(grad_gain, "seq", scatter_dimension=0, tiled=True),
    )
    summed = lax.psum(
        (
            row_shards[0],
            row_shards[1],
            row_shards[2],
            row_shards[3],
            row_shards[4],
            row_shards[5],
            row_shards[6],
            row_shards[7],
            row_shards[8],
            row_shards[9],
            out_shard,
        ),
        "width",
    )
    return (
        output,
        input_grad,
        summed[0],
        summed[1],
        summed[2],
        summed[3],
        summed[4],
        summed[5],
        summed[6],
        summed[7],
        summed[8],
        summed[9],
        summed[10],
    )


def solution(mesh):
    in_specs = (
        P(("width", "seq"), None),
        P(("width", "seq"), None),
        P(("width", "seq"), None),
        P(("width", "seq"), None),
        P(),
        P("seq", None),
        P("seq", None),
        P("seq", None),
        P(),
        P(),
        P(),
        P(),
        P(),
        P(),
        P("seq", None),
    )
    out_specs = (
        P(("width", "seq"), None),
        P(("width", "seq"), None),
        P("seq"),
        P("seq", None),
        P("seq", None),
        P("seq", None),
        P("seq", None),
        P("seq"),
        P("seq"),
        P("seq"),
        P("seq"),
        P("seq"),
        P("seq", None),
    )
    body = heads_body if H % (2 * mesh.shape["seq"]) == 0 else rows_body
    return jax.shard_map(body, mesh=mesh, in_specs=in_specs, out_specs=out_specs, check_vma=False)
```

```python
from functools import partial

import jax
import jax.numpy as jnp
from jax import lax
from jax.experimental import pallas as pl
from jax.experimental.pallas import tpu as pltpu
from jax.sharding import PartitionSpec as P

H = 64
HEAD_DIM = 64
N = 128
KCONV = 4
BLOCK = 128
E = 4096
SUB = 8

epsilon = 1e-05
highest = lax.Precision.HIGHEST
f32 = jnp.float32
bf16 = jnp.bfloat16

NN = ((1,), (0,))
NT = ((1,), (1,))
TN = ((0,), (0,))


def mm(left, right, dims=NN, precision=None):
    return lax.dot_general(left, right, (dims, ((), ())), precision=precision, preferred_element_type=f32)


def split2(value):
    high = value.astype(bf16)
    return high, (value - high.astype(f32)).astype(bf16)


def mm_right(left, right, dims=NN):
    high, low = split2(right)
    return mm(left, high, dims) + mm(left, low, dims)


def mm_left(left, right, dims=NN):
    high, low = split2(left)
    return mm(high, right, dims) + mm(low, right, dims)


def softplus(v):
    small = jnp.exp(-jnp.abs(v))
    log1p = jnp.where(small < 1e-4, small - 0.5 * small * small, jnp.log(1.0 + small))
    return jnp.maximum(v, 0.0) + log1p


def sigmoid(v):
    return 1.0 / (1.0 + jnp.exp(-v))


def grids():
    row = lax.broadcasted_iota(jnp.int32, (BLOCK, BLOCK), 0)
    col = lax.broadcasted_iota(jnp.int32, (BLOCK, BLOCK), 1)
    return row, col


def halves(pair, lane):
    zero = jnp.zeros_like(pair)
    return jnp.where(lane < HEAD_DIM, pair, zero), jnp.where(lane < HEAD_DIM, zero, pair)


def decay_of(cum, cum_t, head, causal):
    return jnp.exp(jnp.where(causal, cum[:, head : head + 1] - cum_t[head : head + 1, :], -1e30))


TAP, BIAS, SKIP, GAIN, MASK = 0, 4, 5, 6, 7
DT_BIAS, NEG_A, HEAD_MASK = 0, 1, 2


def forward_kernel(
    keep_ref, zx_ref, grad_ref, chan_ref, bc_par_ref, head_ref, spread_ref,
    conv_ref, mix_ref, bc_ref, step_ref, state_ref, tail_ref, sums_ref,
    state, tail_x, tail_b, pad_x, pad_b,
    *, lanes, heads,
):
    c = pl.program_id(0)
    width = heads * HEAD_DIM
    row, col = grids()
    causal = row >= col
    tril = causal.astype(f32)
    spread = spread_ref[...]

    @pl.when(c == 0)
    def _():
        state[...] = jnp.zeros_like(state)
        tail_x[...] = jnp.zeros_like(tail_x)
        tail_b[...] = jnp.zeros_like(tail_b)

    for lane in range(lanes):
        rows = pl.ds(lane * BLOCK, BLOCK)
        keep = keep_ref[c, lane]
        pre = zx_ref[rows, width : 2 * width]
        pad_x[lane, 0:SUB] = tail_x[lane] * keep
        pad_x[lane, SUB:] = pre
        tail_ref[0, lane] = tail_x[lane] * keep
        tail_x[lane] = pre[BLOCK - SUB :, :]
        conv = chan_ref[BIAS : BIAS + 1, :]
        for k in range(KCONV):
            conv = conv + pad_x[lane, SUB - KCONV + 1 + k : SUB - KCONV + 1 + k + BLOCK, :] * chan_ref[k : k + 1, :]
        conv_ref[rows, :] = conv
        x_low = (conv * sigmoid(conv) * chan_ref[MASK : MASK + 1, :]).astype(bf16)

        pre_b = zx_ref[rows, 2 * width + BLOCK :]
        pad_b[lane, 0:SUB] = tail_b[lane] * keep
        pad_b[lane, SUB:] = pre_b
        tail_b[lane] = pre_b[BLOCK - SUB :, :]
        conv_b = bc_par_ref[BIAS : BIAS + 1, :]
        for k in range(KCONV):
            conv_b = conv_b + pad_b[lane, SUB - KCONV + 1 + k : SUB - KCONV + 1 + k + BLOCK, :] * bc_par_ref[k : k + 1, :]
        bc_low = (conv_b * sigmoid(conv_b)).astype(bf16)
        bc_ref[rows, :] = bc_low
        b_low, c_low = bc_low[:, :N], bc_low[:, N:]

        raw = zx_ref[rows, 2 * width : 2 * width + BLOCK] + head_ref[DT_BIAS : DT_BIAS + 1, :]
        dt = softplus(raw) * head_ref[HEAD_MASK : HEAD_MASK + 1, :]
        cum = mm(tril, head_ref[NEG_A : NEG_A + 1, :] * dt, precision=highest)
        step_ref[rows, :BLOCK] = cum
        step_ref[rows, BLOCK:] = dt
        cum_t, dt_t = cum.T, dt.T
        last = cum[BLOCK - 1 :, :]
        carry_x = mm_left(jnp.exp(cum), spread)
        end_x = mm_left(jnp.exp(last - cum) * dt, spread)
        last_x = carry_x[BLOCK - 1 :, :]

        inner = mm(c_low, b_low, NT)
        parts = []
        for j in range(heads // 2):
            pair = x_low[:, 2 * HEAD_DIM * j : 2 * HEAD_DIM * (j + 1)]
            scores = [
                (inner * decay_of(cum, cum_t, h, causal) * dt_t[h : h + 1, :]).astype(bf16)
                for h in (2 * j, 2 * j + 1)
            ]
            parts.append(mm(jnp.concatenate(scores, axis=1), jnp.concatenate(halves(pair, col), axis=0)))
        within = jnp.concatenate(parts, axis=1)

        state_in = state[lane] * keep
        state_ref[0, lane] = state_in
        carried = mm_right(c_low, state_in) * carry_x
        x_f = x_low.astype(f32)
        mixed = within + carried + chan_ref[SKIP : SKIP + 1, :] * x_f
        mix_ref[rows, :] = mixed
        weighted = (x_f * end_x).astype(bf16)
        state[lane] = last_x * state_in + mm(b_low, weighted, TN)

        z = zx_ref[rows, :width]
        gated = mixed * (z * sigmoid(z))
        ones = jnp.ones((SUB, width), bf16)
        square = mm_right(ones, gated * gated, NT)
        cross = mm_right(ones, grad_ref[rows, :] * chan_ref[GAIN : GAIN + 1, :] * gated, NT)
        sub = lax.broadcasted_iota(jnp.int32, (SUB, BLOCK), 0)
        sums_ref[0, lane] = jnp.where(sub == 0, square, jnp.where(sub == 1, cross, 0.0))


def backward_kernel(
    keep_ref, zx_ref, grad_ref, chan_ref, head_ref, spread_ref,
    conv_ref, mix_ref, bc_ref, step_ref, state_ref, tail_ref, scale_ref,
    dzx_ref, dbc_ref, dchan_ref, dhead_ref,
    state_grad, next_conv, pad_x, pad_d,
    *, lanes, heads, blocks,
):
    lap = pl.program_id(0)
    c = blocks - 1 - lap
    width = heads * HEAD_DIM
    row, col = grids()
    causal = row >= col
    triu = (col >= row).astype(f32)
    spread = spread_ref[...]

    @pl.when(lap == 0)
    def _():
        state_grad[...] = jnp.zeros_like(state_grad)
        next_conv[...] = jnp.zeros_like(next_conv)
        dchan_ref[...] = jnp.zeros_like(dchan_ref)
        dhead_ref[...] = jnp.zeros_like(dhead_ref)

    def total(value):
        return jnp.sum(value, axis=0, keepdims=True)

    for lane in range(lanes):
        rows = pl.ds(lane * BLOCK, BLOCK)
        keep = keep_ref[c, lane]
        z = zx_ref[rows, :width]
        conv = conv_ref[rows, :]
        mixed = mix_ref[rows, :]
        grad = grad_ref[rows, :]
        gain = chan_ref[GAIN : GAIN + 1, :]
        skip = chan_ref[SKIP : SKIP + 1, :]
        rate = scale_ref[rows, 0:1]
        pull = scale_ref[rows, 1:2]
        gate = sigmoid(z)
        silu = z * gate
        gated = mixed * silu
        dgated = grad * gain * rate - gated * pull
        dzx_ref[rows, :width] = (dgated * mixed * (gate * (1.0 + z * (1.0 - gate)))).astype(bf16)
        dmixed = dgated * silu
        act = sigmoid(conv)
        x_low = (conv * act * chan_ref[MASK : MASK + 1, :]).astype(bf16)
        x_f = x_low.astype(f32)
        dchan_ref[GAIN : GAIN + 1, :] += total(grad * gated * rate)
        dchan_ref[SKIP : SKIP + 1, :] += total(dmixed * x_f)
        dlow = dmixed.astype(bf16)
        dlow_f = dlow.astype(f32)

        b_low, c_low = bc_ref[rows, :N], bc_ref[rows, N:]
        cum, dt = step_ref[rows, :BLOCK], step_ref[rows, BLOCK:]
        cum_t, dt_t = cum.T, dt.T
        last = cum[BLOCK - 1 :, :]
        to_last = jnp.exp(last - cum)
        carry_x = mm_left(jnp.exp(cum), spread)
        end_x = mm_left(to_last * dt, spread)
        last_x = carry_x[BLOCK - 1 :, :]

        inner = mm(c_low, b_low, NT)
        dinner = jnp.zeros((BLOCK, BLOCK), f32)
        parts, dt_rows = [], []
        for j in range(heads // 2):
            lanes_j = slice(2 * HEAD_DIM * j, 2 * HEAD_DIM * (j + 1))
            pair, dpair = x_low[:, lanes_j], dlow[:, lanes_j]
            dstack = jnp.concatenate(halves(dpair, col), axis=0)
            dscores = mm(dstack, pair, NT)
            scores = []
            for i, h in enumerate((2 * j, 2 * j + 1)):
                decay = decay_of(cum, cum_t, h, causal)
                step = dt_t[h : h + 1, :]
                scores.append((inner * decay * step).astype(bf16))
                part = dscores[i * BLOCK : (i + 1) * BLOCK] * decay
                dinner = dinner + part * step
                dt_rows.append(total(part * inner))
            parts.append(mm(jnp.concatenate(scores, axis=0), dstack, TN))
        dx_within = jnp.concatenate(parts, axis=1)
        dt_rows.append(jnp.zeros((BLOCK - heads, BLOCK), f32))
        ddt_within = jnp.concatenate(dt_rows, axis=0).T

        state_in = state_ref[0, lane]
        sgrad = state_grad[lane]
        in_high, in_low = split2(state_in)
        sg_high, sg_low = split2(sgrad)
        dcarry = dlow_f * carry_x
        dc_high, dc_low = split2(dcarry)
        di_high, di_low = split2(dinner)
        dc = mm(dc_high, in_high, NT) + mm(dc_high, in_low, NT) + mm(dc_low, in_high, NT)
        dc = dc + mm(di_high, b_low) + mm(di_low, b_low)
        weighted = (x_f * end_x).astype(bf16)
        db = mm(weighted, sg_high, NT) + mm(weighted, sg_low, NT)
        db = db + mm(di_high, c_low, TN) + mm(di_low, c_low, TN)
        dbc_ref[:N, rows] = db.T.astype(bf16)
        dbc_ref[N:, rows] = dc.T.astype(bf16)
        dweighted = mm(b_low, sg_high) + mm(b_low, sg_low)
        dx = dx_within + dweighted * end_x
        dcum = mm_left(dlow_f * (mixed - skip * x_f) - x_f * dx, spread, NT)
        dend = mm_left(dweighted * x_f, spread, NT)
        touch = jnp.broadcast_to(total(sgrad * state_in), (SUB, width))
        dlast = total(dend * to_last * dt) + jnp.exp(last) * mm_left(touch, spread, NT)[0:1]
        dlog = mm(triu, dcum, precision=highest) + dlast
        neg_a = head_ref[NEG_A : NEG_A + 1, :]
        ddt = ddt_within + dend * to_last + dlog * neg_a
        raw = zx_ref[rows, 2 * width : 2 * width + BLOCK] + head_ref[DT_BIAS : DT_BIAS + 1, :]
        draw = ddt * sigmoid(raw) * head_ref[HEAD_MASK : HEAD_MASK + 1, :]
        dzx_ref[rows, 2 * width :] = draw.astype(bf16)
        dhead_ref[0:1, :] += total(draw)
        dhead_ref[1:2, :] += total(dlog * neg_a * dt)
        state_grad[lane] = keep * (mm(c_low, dc_high, TN) + mm(c_low, dc_low, TN) + last_x * sgrad)

        dx = dx + skip * dmixed
        dconv = dx * chan_ref[MASK : MASK + 1, :] * (act * (1.0 + conv * (1.0 - act)))
        pad_d[lane, :BLOCK] = dconv
        pad_d[lane, BLOCK:] = next_conv[lane]
        next_conv[lane] = dconv[:SUB] * keep
        pad_x[lane, :SUB] = tail_ref[0, lane]
        pad_x[lane, SUB:] = zx_ref[rows, width : 2 * width]
        dpre = jnp.zeros((BLOCK, width), f32)
        for k in range(KCONV):
            dpre = dpre + pad_d[lane, KCONV - 1 - k : KCONV - 1 - k + BLOCK, :] * chan_ref[k : k + 1, :]
            dchan_ref[k : k + 1, :] += total(dconv * pad_x[lane, SUB - KCONV + 1 + k : SUB - KCONV + 1 + k + BLOCK, :])
        dchan_ref[BIAS : BIAS + 1, :] += total(dconv)
        dzx_ref[rows, width : 2 * width] = dpre.astype(bf16)


def entry_kernel(valid_ref, start_ref, x_ref, cot_ref, gain_ref, bc_ref, dt_ref, normed_ref, bgrad_ref, third_ref, starts_ref, *, peers):
    rows = x_ref.shape[0]
    lanes = rows // BLOCK
    x = x_ref[...].astype(f32)
    normed_ref[...] = (x * lax.rsqrt(jnp.mean(x * x, axis=-1, keepdims=True) + epsilon) * gain_ref[...]).astype(bf16)
    row = lax.broadcasted_iota(jnp.int32, (BLOCK, 1), 0)
    for lane in range(lanes):
        at = slice(lane * BLOCK, (lane + 1) * BLOCK)
        mask = (row < valid_ref[0, lane]).astype(f32)
        bgrad_ref[at, :] = (cot_ref[at, :].astype(f32) * mask).astype(bf16)
    bc, dt = bc_ref[...].astype(f32), dt_ref[...].astype(f32)
    share, heads = bc.shape[1] // peers, dt.shape[1] // peers
    rest = jnp.zeros((rows, BLOCK - share - heads), f32)
    for s in range(peers):
        tile = [dt[:, s * heads : (s + 1) * heads], bc[:, s * share : (s + 1) * share], rest]
        third_ref[s] = jnp.concatenate(tile, axis=1).astype(bf16)
    lane = lax.broadcasted_iota(jnp.int32, (SUB, BLOCK), 1)
    tile = jnp.zeros((SUB, BLOCK), f32)
    for l in range(lanes):
        tile = jnp.where(lane == l, start_ref[0, l].astype(f32), tile)
    starts_ref[...] = tile


def entry(valid, starts, tokens, cotangent, gain, w_bc, w_dt, peers):
    smem, vmem = pl.BlockSpec(memory_space=pltpu.SMEM), pl.BlockSpec(memory_space=pltpu.VMEM)
    return pl.pallas_call(
        partial(entry_kernel, peers=peers),
        in_specs=[smem] * 2 + [vmem] * 5,
        out_specs=[vmem] * 4,
        out_shape=[
            jax.ShapeDtypeStruct(tokens.shape, bf16), jax.ShapeDtypeStruct(tokens.shape, bf16),
            jax.ShapeDtypeStruct((peers, w_bc.shape[0], BLOCK), bf16), jax.ShapeDtypeStruct((SUB, BLOCK), f32),
        ],
        compiler_params=pltpu.CompilerParams(vmem_limit_bytes=32 << 20),
        name="entry",
    )(valid, starts, tokens, cotangent, gain[None], w_bc, w_dt)


def run_forward(keep, zx, grad, chan, bc_par, head, spread, lanes, heads):
    rows, width = grad.shape
    step = lanes * BLOCK
    blocks = rows // step
    by_block = lambda cols: pl.BlockSpec((step, cols), lambda c: (c, 0))
    whole = lambda a: pl.BlockSpec(a.shape, lambda c: (0,) * a.ndim)
    per_lane = lambda r, cols: pl.BlockSpec((1, lanes, r, cols), lambda c: (c, 0, 0, 0))
    return pl.pallas_call(
        partial(forward_kernel, lanes=lanes, heads=heads),
        grid=(blocks,),
        in_specs=[
            pl.BlockSpec(memory_space=pltpu.SMEM), by_block(zx.shape[1]), by_block(width),
            whole(chan), whole(bc_par), whole(head), whole(spread),
        ],
        out_specs=[
            by_block(width), by_block(width), by_block(2 * N), by_block(2 * BLOCK),
            per_lane(N, width), per_lane(SUB, width), per_lane(SUB, BLOCK),
        ],
        out_shape=[
            jax.ShapeDtypeStruct((rows, width), f32), jax.ShapeDtypeStruct((rows, width), f32),
            jax.ShapeDtypeStruct((rows, 2 * N), bf16), jax.ShapeDtypeStruct((rows, 2 * BLOCK), f32),
            jax.ShapeDtypeStruct((blocks, lanes, N, width), f32), jax.ShapeDtypeStruct((blocks, lanes, SUB, width), f32),
            jax.ShapeDtypeStruct((blocks, lanes, SUB, BLOCK), f32),
        ],
        scratch_shapes=[
            pltpu.VMEM((lanes, N, width), f32), pltpu.VMEM((lanes, SUB, width), f32), pltpu.VMEM((lanes, SUB, 2 * N), f32),
            pltpu.VMEM((lanes, BLOCK + SUB, width), f32), pltpu.VMEM((lanes, BLOCK + SUB, 2 * N), f32),
        ],
        compiler_params=pltpu.CompilerParams(vmem_limit_bytes=40 << 20, dimension_semantics=("arbitrary",)),
        cost_estimate=pl.CostEstimate(flops=rows * width * 2048, bytes_accessed=rows * width * 32, transcendentals=rows * width * 4),
        name="mix_forward",
    )(keep, zx, grad, chan, bc_par, head, spread)


def run_backward(keep, zx, grad, chan, head, spread, conv, mix, bc, step_arr, state, tail, scale, lanes, heads):
    rows, width = grad.shape
    step = lanes * BLOCK
    blocks = rows // step
    by_block = lambda cols: pl.BlockSpec((step, cols), lambda c: (blocks - 1 - c, 0))
    whole = lambda a: pl.BlockSpec(a.shape, lambda c: (0,) * a.ndim)
    fixed = lambda shape: pl.BlockSpec(shape, lambda c: (0,) * len(shape))
    per_lane = lambda r, cols: pl.BlockSpec((1, lanes, r, cols), lambda c: (blocks - 1 - c, 0, 0, 0))
    return pl.pallas_call(
        partial(backward_kernel, lanes=lanes, heads=heads, blocks=blocks),
        grid=(blocks,),
        in_specs=[
            pl.BlockSpec(memory_space=pltpu.SMEM), by_block(2 * width + BLOCK), by_block(width),
            whole(chan), whole(head), whole(spread),
            by_block(width), by_block(width), by_block(2 * N), by_block(2 * BLOCK),
            per_lane(N, width), per_lane(SUB, width), by_block(SUB),
        ],
        out_specs=[
            by_block(2 * width + BLOCK), pl.BlockSpec((2 * N, step), lambda c: (0, blocks - 1 - c)),
            fixed((SUB, width)), fixed((SUB, BLOCK)),
        ],
        out_shape=[
            jax.ShapeDtypeStruct((rows, 2 * width + BLOCK), bf16),
            jax.ShapeDtypeStruct((2 * N, rows), bf16), jax.ShapeDtypeStruct((SUB, width), f32),
            jax.ShapeDtypeStruct((SUB, BLOCK), f32),
        ],
        scratch_shapes=[
            pltpu.VMEM((lanes, N, width), f32), pltpu.VMEM((lanes, SUB, width), f32),
            pltpu.VMEM((lanes, BLOCK + SUB, width), f32), pltpu.VMEM((lanes, BLOCK + SUB, width), f32),
        ],
        compiler_params=pltpu.CompilerParams(vmem_limit_bytes=48 << 20, dimension_semantics=("arbitrary",)),
        cost_estimate=pl.CostEstimate(flops=rows * width * 6144, bytes_accessed=rows * width * 40, transcendentals=rows * width * 6),
        name="mix_backward",
    )(keep, zx, grad, chan, head, spread, conv, mix, bc, step_arr, state, tail, scale)


MESH = pl.DeviceIdType.MESH


def greet(others):
    barrier = pltpu.get_barrier_semaphore()
    for other in others:
        pl.semaphore_signal(barrier, inc=1, device_id=other, device_id_type=MESH)
    pl.semaphore_wait(barrier, len(others))


def gather_kernel(
    zx_ref, third_ref, bc_ref, own_ref, start_ref, w_ref, rows_ref, starts_ref,
    w_send, w_recv, st_send, st_recv, own_sem, wide_send, wide_recv,
    up_send, up_recv, down_send, down_recv, mate_send, mate_recv,
    *, peers, widths, chans,
):
    width, place = lax.axis_index("width"), lax.axis_index("seq")
    chips = peers // 2
    chip = place // 2
    quarter = zx_ref.shape[0] // widths
    ring = [lax.rem(place + by, peers) for by in range(1, peers)]
    cross = [jnp.bitwise_xor(width, m) for m in range(1, widths)]
    greet([(width, s) for s in ring] + [(w, place) for w in cross])
    mine = pl.ds(pl.multiple_of(width * quarter, quarter), quarter)

    def remote(src, dst, send, recv, device):
        return pltpu.make_async_remote_copy(
            src_ref=src, dst_ref=dst, send_sem=send, recv_sem=recv, device_id=device, device_id_type=MESH
        )

    def columns(half, s):
        return pl.ds(pl.multiple_of(half * peers * chans + s * chans, 128), chans)

    wide = 2 * chans
    spots = [pl.ds(0, chans), pl.ds(chans, chans), pl.ds(wide, BLOCK), pl.ds(wide + BLOCK, 2 * N)]

    def parts(s):
        return [zx_ref.at[mine, columns(0, s)], zx_ref.at[mine, columns(1, s)], third_ref.at[s, mine], bc_ref.at[mine]]

    pushes = []
    for i, s in enumerate(ring):
        for k, (part, spot) in enumerate(zip(parts(s), spots)):
            pushes.append(remote(part, w_ref.at[place, width, :, spot], w_send.at[k, i], w_recv.at[k, i], (width, s)))
        pushes.append(remote(start_ref, starts_ref.at[place], st_send.at[i], st_recv.at[i], (width, s)))
    for push in pushes:
        push.start()
    keeps = [
        pltpu.make_async_copy(part, w_ref.at[place, width, :, spot], own_sem.at[k])
        for k, (part, spot) in enumerate(zip(parts(place), spots))
    ]
    keeps.append(pltpu.make_async_copy(start_ref, starts_ref.at[place], own_sem.at[4]))
    keeps.append(pltpu.make_async_copy(own_ref, rows_ref.at[place], own_sem.at[5]))
    for keep in keeps:
        keep.start()

    def hop(ref, s, step, by):
        send, recv = (up_send, up_recv) if by > 0 else (down_send, down_recv)
        return remote(ref, rows_ref.at[s], send.at[step], recv.at[step], (width, jnp.clip(place + 2 * by, 0, peers - 1)))

    def over(ref, s, slot):
        return remote(ref, rows_ref.at[s], mate_send.at[slot], mate_recv.at[slot], (width, jnp.bitwise_xor(place, 1)))

    def inside(by):
        return chip + 1 < chips if by > 0 else chip > 0

    def reached(by, step):
        return chip >= step if by > 0 else chip + step < chips

    for by in (1, -1):
        @pl.when(inside(by))
        def _():
            hop(own_ref, place, 0, by).start()
    over(own_ref, place, 0).start()

    for push in pushes:
        push.wait_recv()
    for keep in keeps:
        keep.wait()
    shares = []
    for m, w in enumerate(cross):
        shares.append(remote(w_ref.at[:, width], w_ref.at[:, width], wide_send.at[m], wide_recv.at[m], (w, place)))
    for share in shares:
        share.start()

    for step in range(1, chips):
        for by in (1, -1):
            @pl.when(reached(by, step))
            def _():
                s = jnp.clip(place - 2 * by * step, 0, peers - 1)
                ref = rows_ref.at[s]
                hop(ref, s, step - 1, by).wait_recv()

                @pl.when(inside(by))
                def _():
                    hop(ref, s, step, by).start()
                over(ref, s, 2 * step - (by > 0)).start()

    for share in shares:
        share.wait()
    for push in pushes:
        push.wait_send()
    over(own_ref, place, 0).wait()
    for step in range(chips):
        for by in (1, -1):
            if step:
                @pl.when(reached(by, step))
                def _():
                    s = jnp.clip(place - 2 * by * step, 0, peers - 1)
                    over(rows_ref.at[s], s, 2 * step - (by > 0)).wait()

            @pl.when(inside(by) & reached(by, step))
            def _():
                s = jnp.clip(place - 2 * by * step, 0, peers - 1)
                hop(rows_ref.at[s], s, step, by).wait_send()


def gathered_in(w_zx, third, w_bc, own_rows, start_tile, chans):
    peers, widths = lax.axis_size("seq"), lax.axis_size("width")
    own, model = own_rows.shape
    quarter = own // widths
    dma = pltpu.SemaphoreType.DMA
    chips = peers // 2
    anywhere = pl.BlockSpec(memory_space=pl.ANY)
    return pl.pallas_call(
        partial(gather_kernel, peers=peers, widths=widths, chans=chans),
        in_specs=[anywhere] * 5,
        out_specs=[anywhere] * 3,
        out_shape=[
            jax.ShapeDtypeStruct((peers, widths, quarter, 2 * chans + BLOCK + 2 * N), bf16),
            jax.ShapeDtypeStruct((peers, own, model), bf16),
            jax.ShapeDtypeStruct((peers,) + start_tile.shape, f32),
        ],
        scratch_shapes=[
            dma((4, peers - 1)), dma((4, peers - 1)), dma((peers - 1,)), dma((peers - 1,)),
            dma((6,)), dma((widths - 1,)), dma((widths - 1,)),
            dma((chips,)), dma((chips,)), dma((chips,)), dma((chips,)), dma((2 * chips,)), dma((2 * chips,)),
        ],
        compiler_params=pltpu.CompilerParams(collective_id=1, has_side_effects=True),
        name="gather_in",
    )(w_zx, third, w_bc, own_rows, start_tile)


ROWS_AT_ONCE = 16


def add_into(dst, others, rows):
    @pl.loop(0, rows // ROWS_AT_ONCE)
    def _(i):
        at = pl.ds(pl.multiple_of(i * ROWS_AT_ONCE, ROWS_AT_ONCE), ROWS_AT_ONCE)
        value = dst[at].astype(f32)
        for other in others:
            value = value + other[at].astype(f32)
        dst[at] = value.astype(dst.dtype)


def scatter_kernel(
    part_ref, wide_ref, third_ref, x_ref, cot_ref, gain_ref, rows_ref, out_ref, out_third_ref,
    mine, from_core, up, down, own0, own1, own2, got0, got1, got2, piece0, piece1, piece2,
    local_sem, core_send, core_recv, up_send, up_recv, down_send, down_recv,
    own_sem, q_send, q_recv, p_send, p_recv, o_send, o_recv,
    *, peers, widths,
):
    width, place = lax.axis_index("width"), lax.axis_index("seq")
    chips = peers // 2
    chip, core = place // 2, lax.rem(place, 2)
    mate = (width, jnp.bitwise_xor(place, 1))
    ring = [lax.rem(place + by, peers) for by in range(1, peers)]
    cross = [jnp.bitwise_xor(width, m) for m in range(1, widths)]
    greet([(width, s) for s in ring] + [(w, place) for w in cross])
    half = wide_ref.shape[3] // 2
    sets = [
        (wide_ref, out_ref, pl.ds(0, half), own0, got0, piece0),
        (wide_ref, out_ref, pl.ds(half, half), own1, got1, piece1),
        (third_ref, out_third_ref, pl.ds(0, BLOCK), own2, got2, piece2),
    ]

    def remote(src, dst, send, recv, device):
        return pltpu.make_async_remote_copy(
            src_ref=src, dst_ref=dst, send_sem=send, recv_sem=recv, device_id=device, device_id_type=MESH
        )

    locals_ = [pltpu.make_async_copy(part_ref.at[2 * q + core], mine.at[q], local_sem.at[q]) for q in range(chips)]
    to_core = [
        remote(part_ref.at[2 * q + 1 - core], from_core.at[q], core_send.at[q], core_recv.at[q], mate) for q in range(chips)
    ]
    own_in, to_width = [], []
    for k, (src, dst, cols, own, got, piece) in enumerate(sets):
        own_in.append(pltpu.make_async_copy(src.at[:, width, :, cols], own, own_sem.at[0, k]))
        to_width.append([
            remote(src.at[:, w, :, cols], got.at[m], q_send.at[k, m], q_recv.at[k, m], (w, place)) for m, w in enumerate(cross)
        ])
    for copy in locals_ + to_core + own_in + to_width[0] + to_width[1] + to_width[2]:
        copy.start()
    rows = mine.shape[1]
    for q in range(chips):
        locals_[q].wait()
        to_core[q].wait_recv()
        add_into(mine.at[q], [from_core.at[q]], rows)

    def flow(by):
        return (up, up_send, up_recv) if by > 0 else (down, down_send, down_recv)

    def sends(by, step):
        far = chips - step
        return chip + far < chips if by > 0 else chip >= far

    def later(by):
        return chip > 0 if by > 0 else chip + 1 < chips

    def hop(src, by, step):
        buffer, send, recv = flow(by)
        return remote(
            src, buffer.at[step - 1], send.at[step - 1], recv.at[step - 1], (width, jnp.clip(place + 2 * by, 0, peers - 1))
        )

    def staged(by, step):
        return flow(by)[0].at[step - 2]

    def run_hops(step):
        for by in (1, -1):
            owner = jnp.clip(chip + by * (chips - step), 0, chips - 1)

            def direct():
                hop(mine.at[owner], by, step).start()

            def relayed():
                hop(staged(by, step), by, step - 1).wait_recv()
                add_into(staged(by, step), [mine.at[owner]], rows)
                hop(staged(by, step), by, step).start()

            if step == 1:
                pl.when(sends(by, step))(direct)
            else:
                pl.when(sends(by, step) & jnp.logical_not(later(by)))(direct)
                pl.when(sends(by, step) & later(by))(relayed)

    to_owner, to_all, kept = [None] * 3, [None] * 3, []

    def exchange(k):
        src, dst, cols, own, got, piece = sets[k]
        own_in[k].wait()
        for copy in to_width[k]:
            copy.wait_recv()
        for s in range(peers):
            add_into(own.at[s], [got.at[m, s] for m in range(widths - 1)], own.shape[1])
        to_owner[k] = [
            remote(own.at[s], piece.at[place], p_send.at[k, i], p_recv.at[k, i], (width, s)) for i, s in enumerate(ring)
        ]
        keep = pltpu.make_async_copy(own.at[place], piece.at[place], own_sem.at[1, k])
        for copy in to_owner[k] + [keep]:
            copy.start()
        kept.append(keep)

    def spread(k):
        src, dst, cols, own, got, piece = sets[k]
        for copy in to_owner[k]:
            copy.wait_recv()
        kept[k].wait()
        to_all[k] = [
            remote(piece, dst.at[:, width, :, cols], o_send.at[k, m], o_recv.at[k, m], (w, place)) for m, w in enumerate(cross)
        ]
        to_all[k].append(pltpu.make_async_copy(piece, dst.at[:, width, :, cols], own_sem.at[2, k]))
        for copy in to_all[k]:
            copy.start()

    run_hops(1)
    exchange(0)
    if chips > 2:
        run_hops(2)
    spread(0)
    exchange(1)
    exchange(2)
    for step in range(3, chips):
        run_hops(step)
    spread(1)
    spread(2)

    for by in (1, -1):
        @pl.when(later(by))
        def _():
            buffer = flow(by)[0].at[chips - 2]
            hop(buffer, by, chips - 1).wait_recv()
            add_into(mine.at[chip], [buffer], rows)

    gain = gain_ref[...]

    @pl.loop(0, rows // ROWS_AT_ONCE)
    def _(i):
        at = pl.ds(pl.multiple_of(i * ROWS_AT_ONCE, ROWS_AT_ONCE), ROWS_AT_ONCE)
        x = x_ref[at, :].astype(f32)
        rate = lax.rsqrt(jnp.mean(x * x, axis=-1, keepdims=True) + epsilon)
        unit = x * rate
        pulled = mine[chip, at].astype(f32) * gain
        inner = jnp.mean(pulled * unit, axis=-1, keepdims=True)
        rows_ref[at, :] = cot_ref[at, :].astype(f32) + rate * (pulled - unit * inner)

    for step in range(1, chips):
        for by in (1, -1):
            @pl.when(sends(by, step))
            def _():
                hop(mine.at[0], by, step).wait_send()
    for copy in to_core:
        copy.wait_send()
    for k in range(len(sets)):
        for copy in to_width[k] + to_owner[k]:
            copy.wait_send()
        for copy in to_all[k]:
            copy.wait()


def scattered_out(part, wide, third, x_rows, cotangent, gain):
    peers, widths = lax.axis_size("seq"), lax.axis_size("width")
    chips = peers // 2
    dma = pltpu.SemaphoreType.DMA
    anywhere = pl.BlockSpec(memory_space=pl.ANY)
    vmem = pl.BlockSpec(memory_space=pltpu.VMEM)
    block = part.shape[1:]
    half = wide.shape[3] // 2
    pieces = [(peers, wide.shape[2], cols) for cols in (half, half, third.shape[3])]
    return pl.pallas_call(
        partial(scatter_kernel, peers=peers, widths=widths),
        in_specs=[anywhere] * 3 + [vmem] * 3,
        out_specs=[vmem, anywhere, anywhere],
        out_shape=[
            jax.ShapeDtypeStruct(block, f32), jax.ShapeDtypeStruct(wide.shape, bf16), jax.ShapeDtypeStruct(third.shape, bf16)
        ],
        scratch_shapes=[
            pltpu.VMEM((chips,) + block, bf16), pltpu.VMEM((chips,) + block, bf16),
            pltpu.VMEM((chips - 1,) + block, bf16), pltpu.VMEM((chips - 1,) + block, bf16),
            *[pltpu.VMEM(piece, bf16) for piece in pieces],
            *[pltpu.VMEM((widths - 1,) + piece, bf16) for piece in pieces],
            *[pltpu.VMEM(piece, bf16) for piece in pieces],
            dma((chips,)), dma((chips,)), dma((chips,)),
            dma((chips - 1,)), dma((chips - 1,)), dma((chips - 1,)), dma((chips - 1,)),
            dma((3, 3)), dma((3, widths - 1)), dma((3, widths - 1)), dma((3, peers - 1)), dma((3, peers - 1)),
            dma((3, widths - 1)), dma((3, widths - 1)),
        ],
        compiler_params=pltpu.CompilerParams(collective_id=2, has_side_effects=True, vmem_limit_bytes=48 << 20),
        name="scatter_out",
    )(part, wide, third, x_rows, cotangent, gain)


def bc_kernel(got_ref, pre_ref, par_ref, keep_ref, ddt_ref, third_ref, dpar_ref, pre_t, *, at):
    chans, times = pre_t.shape
    for i in range(times // BLOCK):
        rows = slice(i * BLOCK, (i + 1) * BLOCK)
        pre_t[:, rows] = pre_ref[rows, :].T[at : at + chans]
    dbc = got_ref[0].astype(f32)
    for s in range(1, got_ref.shape[0]):
        dbc = dbc + got_ref[s].astype(f32)
    pre = pre_t[...]
    in_block = lax.rem(lax.broadcasted_iota(jnp.int32, (chans, times), 1), BLOCK)
    keep, keep_next = keep_ref[0:1, :], keep_ref[1:2, :]
    conv = jnp.broadcast_to(par_ref[:, BIAS : BIAS + 1], (chans, times))
    shifted = []
    for j in range(KCONV):
        moved = pre
        if j:
            moved = jnp.where(in_block >= j, pltpu.roll(pre, j, 1), keep * pltpu.roll(pre, BLOCK + j, 1))
        shifted.append(moved)
        conv = conv + moved * par_ref[:, KCONV - 1 - j : KCONV - j]
    act = sigmoid(conv)
    dconv = dbc * (act * (1.0 + conv * (1.0 - act)))
    dpre = dconv * par_ref[:, KCONV - 1 : KCONV]
    lane = lax.broadcasted_iota(jnp.int32, (chans, BLOCK), 1)
    dpar = jnp.where(lane == BIAS, jnp.sum(dconv, axis=1, keepdims=True), 0.0)
    for j in range(KCONV):
        dpar = dpar + jnp.where(lane == KCONV - 1 - j, jnp.sum(dconv * shifted[j], axis=1, keepdims=True), 0.0)
        if j:
            back = jnp.where(
                in_block < BLOCK - j, pltpu.roll(dconv, times - j, 1), keep_next * pltpu.roll(dconv, times - BLOCK - j, 1)
            )
            dpre = dpre + back * par_ref[:, KCONV - 1 - j : KCONV - j]
    dpar_ref[...] = dpar
    for i in range(times // BLOCK):
        tile = dpre[:, i * BLOCK : (i + 1) * BLOCK]
        below = jnp.zeros((BLOCK - at - chans, BLOCK), f32)
        tile = jnp.concatenate([jnp.zeros((at, BLOCK), f32), tile, below], axis=0).T
        rows = slice(i * BLOCK, (i + 1) * BLOCK)
        third_ref[rows, :] = (tile + ddt_ref[rows, :].astype(f32)).astype(bf16)


def bc_backward(got, zx, par, keep, dzx, at, chans):
    rows = dzx.shape[0]
    share = got.shape[1]
    third = pl.BlockSpec((rows, BLOCK), lambda i: (0, 2 * chans // BLOCK))
    whole = lambda a: pl.BlockSpec(a.shape, lambda i: (0,) * a.ndim)
    return pl.pallas_call(
        partial(bc_kernel, at=at),
        grid=(1,),
        in_specs=[whole(got), third, whole(par), whole(keep), third],
        out_specs=[pl.BlockSpec((rows, BLOCK), lambda i: (0, 0)), pl.BlockSpec((share, BLOCK), lambda i: (0, 0))],
        out_shape=[jax.ShapeDtypeStruct((rows, BLOCK), bf16), jax.ShapeDtypeStruct((share, BLOCK), f32)],
        scratch_shapes=[pltpu.VMEM((share, rows), f32)],
        compiler_params=pltpu.CompilerParams(vmem_limit_bytes=32 << 20),
        name="bc_backward",
    )(got, zx, par, keep, dzx)


def sum_kernel(own_ref, out_ref, got, send_sem, recv_sem, *, peers):
    place = lax.axis_index("seq")
    width = lax.axis_index("width")
    barrier = pltpu.get_barrier_semaphore()
    for by in range(1, peers):
        pl.semaphore_signal(
            barrier, inc=1, device_id=(width, lax.rem(place + by, peers)), device_id_type=pl.DeviceIdType.MESH
        )
    pl.semaphore_wait(barrier, peers - 1)
    copies = []
    for by in range(1, peers):
        copies.append(
            pltpu.make_async_remote_copy(
                src_ref=own_ref, dst_ref=got.at[by - 1], send_sem=send_sem.at[by - 1], recv_sem=recv_sem.at[by - 1],
                device_id=(width, lax.rem(place + by, peers)), device_id_type=pl.DeviceIdType.MESH,
            )
        )
        copies[-1].start()
    total = own_ref[...]
    for by in range(1, peers):
        copies[by - 1].wait()
        total = total + got[by - 1]
    out_ref[...] = total


def summed_small(value):
    peers = lax.axis_size("seq")
    return pl.pallas_call(
        partial(sum_kernel, peers=peers),
        out_shape=jax.ShapeDtypeStruct(value.shape, f32),
        in_specs=[pl.BlockSpec(memory_space=pltpu.VMEM)],
        out_specs=pl.BlockSpec(memory_space=pltpu.VMEM),
        scratch_shapes=[
            pltpu.VMEM((peers - 1,) + value.shape, f32),
            pltpu.SemaphoreType.DMA((peers - 1,)), pltpu.SemaphoreType.DMA((peers - 1,)),
        ],
        compiler_params=pltpu.CompilerParams(collective_id=0, has_side_effects=True),
        name="row_sums",
    )(value)


def laid_kernel(in_ref, third_ref, w_ref, bc_ref, dt_ref, gain_ref, out_ref, out_bc_ref, out_dt_ref, norm_ref, *, heads, share):
    peers, rows, wide = in_ref.shape[0], in_ref.shape[2], in_ref.shape[3]
    chans = wide // 2
    lane = jnp.zeros((rows, BLOCK), f32)
    for s in range(peers):
        for half in (0, 1):
            at = (half * peers + s) * chans
            value = in_ref[s, 0, :, half * chans : (half + 1) * chans].astype(f32)
            out_ref[:, at : at + chans] = value
            value = value * w_ref[:, at : at + chans].astype(f32)
            for j in range(chans // BLOCK):
                lane = lane + value[:, j * BLOCK : (j + 1) * BLOCK]
    third = [third_ref[s, 0].astype(f32) for s in range(peers)]
    bc = jnp.concatenate([t[:, heads : heads + share] for t in third], axis=1)
    dt = jnp.concatenate([t[:, :heads] for t in third], axis=1)
    out_bc_ref[...] = bc
    out_dt_ref[...] = dt
    total = jnp.sum(lane, axis=1, keepdims=True) + jnp.sum(bc * bc_ref[...].astype(f32), axis=1, keepdims=True)
    total = total + jnp.sum(dt * dt_ref[...].astype(f32), axis=1, keepdims=True)
    norm_ref[...] = total / gain_ref[...]


def laid_out(wide, third, w_zx, w_bc, w_dt, gain, heads):
    peers, widths, quarter, cols = wide.shape
    rows = widths * quarter
    steps = 2 * widths
    cut = rows // steps
    share = w_bc.shape[1] // peers
    by_rows = lambda a: pl.BlockSpec((cut, a.shape[1]), lambda i: (i, 0))
    by_piece = lambda a: pl.BlockSpec((peers, 1, cut, a.shape[3]), lambda i: (0, i // 2, i % 2, 0))
    shapes = [jax.ShapeDtypeStruct(a.shape, f32) for a in (w_zx, w_bc, w_dt, gain)]
    return pl.pallas_call(
        partial(laid_kernel, heads=heads, share=share),
        grid=(steps,),
        in_specs=[by_piece(wide), by_piece(third)] + [by_rows(a) for a in (w_zx, w_bc, w_dt, gain)],
        out_specs=[by_rows(a) for a in shapes],
        out_shape=shapes,
        compiler_params=pltpu.CompilerParams(vmem_limit_bytes=32 << 20),
        name="lay_out",
    )(wide, third, w_zx, w_bc, w_dt, gain)


def crossed(value, axis, mask):
    return lax.ppermute(value, axis, [(i, i ^ mask) for i in range(lax.axis_size(axis))])


def pick(value, index):
    return lax.dynamic_index_in_dim(value, index, 0, False)


def quarters_sent(value):
    widths, width = lax.axis_size("width"), lax.axis_index("width")
    value = value.reshape((widths, value.shape[0] // widths) + value.shape[1:])
    sent = [crossed(pick(value, jnp.bitwise_xor(width, m)), "width", m) for m in range(1, widths)]
    return [pick(value, width)] + sent


def quarters_back(total):
    widths = lax.axis_size("width")
    return [total] + [crossed(total, "width", m) for m in range(1, widths)]


def quarters_joined(pieces):
    width = lax.axis_index("width")
    stacked = jnp.stack(pieces)
    whole = jnp.stack([pick(stacked, jnp.bitwise_xor(width, j)) for j in range(len(pieces))])
    return whole.reshape((-1,) + whole.shape[2:]).astype(f32)


def packed_rows(rows, count):
    flat = jnp.stack(rows)
    return jnp.pad(flat, ((0, count - len(rows)), (0, 0)))


def heads_body(
    tokens, cotangent, starts, valid, norm_gain, w_zx, w_bc, w_dt, conv_w, conv_b, dt_bias, a_log, d_skip, gate_gain, w_out
):
    peers = lax.axis_size("seq")
    widths = lax.axis_size("width")
    place = lax.axis_index("seq")
    lanes = starts.shape[1]
    heads = H // peers
    chans = heads * HEAD_DIM
    own, model = tokens.shape
    rows = own * peers
    active = jnp.right_shift(jnp.int32(H), widths - 1 - lax.axis_index("width"))
    count = (active * HEAD_DIM).astype(f32)
    first = place * heads

    share = 2 * N // peers
    used = heads + share
    normed_own, bgrad_own, third_src, start_tile = entry(valid, starts, tokens, cotangent, norm_gain, w_bc, w_dt, peers)
    row_mask = (jnp.arange(BLOCK)[None, :] < valid[0][:, None]).astype(f32).reshape(-1, 1)
    weights, normed, starts_all = gathered_in(w_zx, third_src, w_bc, normed_own, start_tile, chans)
    weights = weights.reshape(model, -1)
    normed = normed.reshape(rows, model)
    bgrad = lax.all_gather(bgrad_own, "seq", axis=0, tiled=True)
    keep = 1.0 - starts_all[:, 0, :lanes]

    taps_x = lax.dynamic_slice_in_dim(conv_w, first * HEAD_DIM, chans, 0).T
    of_chans = lambda a: lax.dynamic_slice_in_dim(a, first * HEAD_DIM, chans, 0)
    of_heads = lambda a: jnp.pad(lax.dynamic_slice_in_dim(a, first, heads, 0), (0, BLOCK - heads))
    head_on = (jnp.arange(BLOCK) < jnp.minimum(active - first, heads)).astype(f32)
    chan_on = (jnp.arange(chans) // HEAD_DIM < active - first).astype(f32)
    skip_x = jnp.repeat(lax.dynamic_slice_in_dim(d_skip, first, heads, 0), HEAD_DIM)
    chan = packed_rows([*taps_x, of_chans(conv_b), skip_x, of_chans(gate_gain), chan_on], SUB)
    bc_par = packed_rows([*conv_w[E:].T, conv_b[E:]], SUB)
    head = packed_rows([of_heads(dt_bias), of_heads(-jnp.exp(a_log)), head_on], SUB)
    spread = (jnp.arange(chans)[None, :] // HEAD_DIM == jnp.arange(BLOCK)[:, None]).astype(bf16)

    zx = mm(normed, weights)
    mixed_grad = mm(bgrad, w_out, NT)
    conv, mix, bc, steps, state, tail, sums = run_forward(
        keep, zx, mixed_grad, chan, bc_par, head, spread, lanes, heads
    )
    sums = summed_small(sums[:, :, :2, :].reshape(-1, BLOCK)).reshape(peers, lanes, 2, BLOCK)
    gate_rate = lax.rsqrt(sums[:, :, 0] / count + epsilon).reshape(rows, 1)
    gate_pull = gate_rate * gate_rate * gate_rate * sums[:, :, 1].reshape(rows, 1) / count
    scale = jnp.pad(jnp.concatenate([gate_rate, gate_pull], axis=1), ((0, 0), (0, SUB - 2)))
    mixed_low = lax.optimization_barrier(
        (mix * jax.nn.silu(zx[:, :chans]) * gate_rate * chan[GAIN]).astype(bf16)
    )
    branch = lax.psum_scatter(mm(mixed_low, w_out).astype(bf16), "seq", scatter_dimension=0, tiled=True).astype(f32)
    output = (tokens.astype(f32) + row_mask * branch).astype(bf16)
    out_part = mm(mixed_low, bgrad, TN).astype(bf16)
    scale, out_part = lax.optimization_barrier((scale, out_part))
    out_quarters = quarters_sent(out_part)

    dzx, dbc, dchan, dhead = run_backward(
        keep, zx, mixed_grad, chan, head, spread, conv, mix, bc, steps, state, tail, scale, lanes, heads
    )
    dzx, dbc, out_quarters = lax.optimization_barrier((dzx, dbc, out_quarters))
    out_pieces = quarters_back(sum(q.astype(f32) for q in out_quarters).astype(bf16))

    got = lax.all_to_all(dbc.reshape(peers, share, rows), "seq", 0, 0, tiled=True)
    of_share = lambda a: lax.dynamic_slice_in_dim(a, E + place * share, share, 0)
    share_par = jnp.pad(jnp.concatenate([of_share(conv_w), of_share(conv_b)[:, None]], axis=1), ((0, 0), (0, BLOCK - BIAS - 1)))
    over_time = lambda a: jnp.repeat(a.reshape(-1), BLOCK)
    keep_next = jnp.concatenate([keep[1:], jnp.zeros_like(keep[:1])], axis=0)
    third, dshare = bc_backward(
        got, zx, share_par, packed_rows([over_time(keep), over_time(keep_next)], SUB), dzx, heads, chans
    )

    at_heads = lambda a: lax.dynamic_update_slice_in_dim(jnp.zeros((H,), f32), a, first, 0)
    at_chans = lambda a: lax.dynamic_update_slice_in_dim(jnp.zeros((E,), f32), a, first * HEAD_DIM, 0)
    at_share = lambda a: lax.dynamic_update_slice_in_dim(jnp.zeros((2 * N,), f32), a, place * share, 0)
    skip = jnp.sum(dchan[SKIP].reshape(heads, HEAD_DIM), axis=1)
    small = [jnp.concatenate([at_chans(dchan[k]), at_share(dshare[:, k])]) for k in range(KCONV + 1)]
    small += [at_chans(dchan[GAIN]), at_heads(dhead[0, :heads]), at_heads(dhead[1, :heads]), at_heads(skip)]
    sizes = [a.shape[0] // peers for a in small]
    small = jnp.concatenate([a.reshape(peers, -1) for a in small], axis=1)
    per_row = -(-small.shape[1] // own)
    small = jnp.pad(small, ((0, 0), (0, own * per_row - small.shape[1]))).reshape(model, per_row)

    wide = mm(normed, dzx[:, : 2 * chans], TN).astype(bf16)
    wide, out_pieces = lax.optimization_barrier((wide, out_pieces))
    out_grad = quarters_joined(out_pieces)
    wide_third = jnp.concatenate(
        [mm(normed, third, TN)[:, :used], small, jnp.zeros((model, BLOCK - used - per_row), f32)], axis=1
    ).astype(bf16)
    part = mm(lax.dynamic_update_slice(dzx, third, (0, 2 * chans)), weights[:, : 2 * chans + BLOCK], NT).astype(bf16)
    by_owner = lambda a: a.reshape(peers, widths, own // widths, -1)
    part, output, out_grad = lax.optimization_barrier((part, output, out_grad))
    input_grad, wide, wide_third = scattered_out(
        part.reshape(peers, own, model), by_owner(wide), by_owner(wide_third), tokens, cotangent, norm_gain[None]
    )
    gain_rows = lax.dynamic_slice_in_dim(norm_gain, place * own, own, 0)[:, None]
    grad_zx, grad_bc, grad_dt, grad_norm = laid_out(wide, wide_third, w_zx, w_bc, w_dt, gain_rows, heads)
    grad_norm = grad_norm[:, 0]
    summed = jnp.sum(wide_third.reshape(peers, own, BLOCK)[:, :, used : used + per_row].astype(f32), axis=0).reshape(-1)
    pieces = [summed[sum(sizes[:i]) : sum(sizes[: i + 1])] for i in range(len(sizes))]
    grad_taps = jnp.stack(pieces[:KCONV], axis=1)
    grad_bias, grad_gain, grad_dtb, grad_alog, grad_skip = pieces[KCONV:]
    return (
        output, input_grad, grad_norm, grad_zx, grad_bc, grad_dt, grad_taps, grad_bias, grad_dtb, grad_alog, grad_skip,
        grad_gain, out_grad,
    )


def passed_along(array, axis, by):
    peers = lax.axis_size(axis)
    pairs = [(i, i + by) for i in range(peers) if 0 <= i + by < peers]
    return lax.ppermute(array, axis, pairs)


def carried_in(part, axis, combine, identity, reverse):
    count = lax.axis_size(axis)
    place = lax.axis_index(axis)
    at = count - 1 - place if reverse else place
    by = -1 if reverse else 1
    state = jax.tree.map(lambda a, e: jnp.zeros_like(a) + jnp.asarray(e, a.dtype), part, identity)

    def one(lap, state):
        sent = combine(state, part)
        got = jax.tree.map(lambda a: passed_along(a, axis, by), sent)
        return jax.tree.map(lambda old, new: jnp.where(at == lap + 1, new, old), state, got)

    return lax.fori_loop(0, count - 1, one, state)


def round_value(v):
    return lax.optimization_barrier(v.astype(jnp.bfloat16)).astype(jnp.float32)


def keep_round(v):
    return (round_value(v), None)


def pass_grad(kept, grad):
    return (grad,)


def same_value(v):
    return v


def keep_same(v):
    return (v, None)


def round_grad(kept, grad):
    return (round_value(grad),)


def low(v):
    wrapped = jax.custom_vjp(round_value)
    wrapped.defvjp(keep_round, pass_grad)
    return wrapped(v)


def low_back(v):
    wrapped = jax.custom_vjp(same_value)
    wrapped.defvjp(keep_same, round_grad)
    return wrapped(v)


def rms_front(x_rows, norm_gain):
    mean_square = jnp.mean(x_rows * x_rows, axis=-1, keepdims=True)
    return x_rows * lax.rsqrt(mean_square + epsilon) * norm_gain


def rim_of(zx_pre, bc_pre, chan_mask):
    return jnp.concatenate(
        [zx_pre[:, BLOCK - KCONV + 1 :, E:] * chan_mask, bc_pre[:, BLOCK - KCONV + 1 :, :]], axis=-1
    )


def piece_front(
    zx_pre,
    bc_pre,
    dt_raw,
    rim_rows,
    conv_w,
    conv_b,
    dt_bias,
    a_log,
    chan_mask,
    head_mask,
    keep_rows,
):
    z_gate = zx_pre[..., :E] * chan_mask
    pre_conv = jnp.concatenate([zx_pre[..., E:] * chan_mask, bc_pre], axis=-1)
    padded = jnp.concatenate([rim_rows * keep_rows[:, None, None], pre_conv], axis=1)
    conv_out = conv_b + padded[:, 0:BLOCK, :] * conv_w[:, 0]
    for offset in range(1, KCONV):
        conv_out = conv_out + padded[:, offset : offset + BLOCK, :] * conv_w[:, offset]
    active = jax.nn.silu(conv_out)
    x_conv = low(active[..., :E] * chan_mask)
    b_conv = low(active[..., E : E + N])
    c_conv = low(active[..., E + N :])
    dt_step = jax.nn.softplus(dt_raw + dt_bias) * head_mask
    log_step = -jnp.exp(a_log) * dt_step
    return (z_gate, x_conv, b_conv, c_conv, dt_step, log_step)


def block_state(x_conv, b_conv, dt_step, log_step):
    cumulative = jnp.cumsum(log_step, axis=1)
    to_end = jnp.exp(cumulative[:, -1:, :] - cumulative) * dt_step
    weighted = low(x_conv.reshape(x_conv.shape[0], BLOCK, H, HEAD_DIM) * to_end[..., None])
    state_sum = jnp.einsum("lqhp,lqn->lhpn", weighted, b_conv, precision=highest)
    return (state_sum, cumulative[:, -1, :])


def piece_mix(
    z_gate, x_conv, b_conv, c_conv, dt_step, log_step, state_in, d_skip, gate_gain, chan_count
):
    lane_count = x_conv.shape[0]
    cumulative = jnp.cumsum(log_step, axis=1)
    cum_heads = jnp.swapaxes(cumulative, 1, 2)
    causal = jnp.arange(BLOCK)[:, None] >= jnp.arange(BLOCK)[None, :]
    spread = cum_heads[:, :, :, None] - cum_heads[:, :, None, :]
    decays = jnp.where(causal, jnp.exp(jnp.where(causal, spread, 0.0)), 0.0)
    inner_cb = jnp.einsum("lqn,lsn->lqs", c_conv, b_conv, precision=highest)
    scores = low(inner_cb[:, None] * decays * jnp.swapaxes(dt_step, 1, 2)[:, :, None, :])
    x_heads = x_conv.reshape(lane_count, BLOCK, H, HEAD_DIM)
    within = jnp.einsum("lhqs,lshp->lqhp", scores, x_heads, precision=highest)
    carried = (
        jnp.einsum("lqn,lhpn->lqhp", c_conv, state_in, precision=highest)
        * jnp.exp(cumulative)[..., None]
    )
    mixed_sum = low_back(within + carried) + d_skip[:, None] * x_heads
    gated_rows = mixed_sum.reshape(lane_count, BLOCK, E) * jax.nn.silu(z_gate)
    mean_square = jnp.sum(gated_rows * gated_rows, axis=-1, keepdims=True) / chan_count
    return low(gated_rows * lax.rsqrt(mean_square + epsilon) * gate_gain)


def mix_lanes(lane_inputs, d_skip, gate_gain, chan_count):

    def one_lane(pieces):
        lane_gate, lane_xconv, lane_bconv, lane_cconv, lane_step, lane_decay, lane_state = pieces
        return piece_mix(
            lane_gate[None],
            lane_xconv[None],
            lane_bconv[None],
            lane_cconv[None],
            lane_step[None],
            lane_decay[None],
            lane_state[None],
            d_skip,
            gate_gain,
            chan_count,
        )[0]

    return lax.map(one_lane, lane_inputs)


def mix_back_lanes(lane_inputs, mixed_grad, d_skip, gate_gain, chan_count):

    def lane_mix(z_gate, x_conv, b_conv, c_conv, dt_step, log_step, state_in, skip_coef, gain_coef):
        return piece_mix(
            z_gate[None],
            x_conv[None],
            b_conv[None],
            c_conv[None],
            dt_step[None],
            log_step[None],
            state_in[None],
            skip_coef,
            gain_coef,
            chan_count,
        )[0]

    def one_lane(pieces):
        (
            lane_gate,
            lane_xconv,
            lane_bconv,
            lane_cconv,
            lane_step,
            lane_decay,
            lane_state,
            lane_grad,
        ) = pieces
        unused, pull_lane = jax.vjp(
            lane_mix,
            lane_gate,
            lane_xconv,
            lane_bconv,
            lane_cconv,
            lane_step,
            lane_decay,
            lane_state,
            d_skip,
            gate_gain,
        )
        return pull_lane(lane_grad)

    lane_grads = lax.map(one_lane, lane_inputs + (mixed_grad,))
    return (lane_grads[:7], jnp.sum(lane_grads[7], axis=0), jnp.sum(lane_grads[8], axis=0))


def chain_combine(earlier, latter):
    return (earlier[0] * latter[0], latter[0][:, :, None, None] * earlier[1] + latter[1])


def share_out(out_grad):
    return lax.psum_scatter(out_grad, "seq", scatter_dimension=0, tiled=True)


def contract_rows(left, right):
    return lax.dot_general(
        left, right, (((0,), (0,)), ((), ())), preferred_element_type=jnp.float32
    )


def contract_cols(left, right):
    return lax.dot_general(
        left, right, (((1,), (1,)), ((), ())), preferred_element_type=jnp.float32
    )


def rows_body(
    tokens,
    cotangent,
    starts,
    valid,
    norm_gain,
    w_zx,
    w_bc,
    w_dt,
    conv_w,
    conv_b,
    dt_bias,
    a_log,
    d_skip,
    gate_gain,
    w_out,
):
    lane_count = starts.shape[1]
    width_index = lax.axis_index("width")
    shift_bits = lax.axis_size("width") - 1 - width_index
    active_heads = jnp.right_shift(jnp.int32(H), shift_bits)
    chan_mask = (jnp.arange(E) // HEAD_DIM < active_heads).astype(jnp.float32)
    head_mask = (jnp.arange(H) < active_heads).astype(jnp.float32)
    chan_count = (active_heads * HEAD_DIM).astype(jnp.float32)
    keep_rows = 1.0 - starts[0].astype(jnp.float32)
    row_mask = (jnp.arange(BLOCK)[None, :] < valid[0][:, None]).astype(jnp.float32).reshape(-1, 1)
    x_rows = tokens.astype(jnp.float32)
    normed, norm_back = jax.vjp(rms_front, x_rows, norm_gain)
    normed_low = normed.astype(jnp.bfloat16)
    zx_full, bc_full, dt_full, out_full = (
        lax.all_gather(w_zx, "seq", axis=0, tiled=True),
        lax.all_gather(w_bc, "seq", axis=0, tiled=True),
        lax.all_gather(w_dt, "seq", axis=0, tiled=True),
        lax.all_gather(w_out, "seq", axis=0, tiled=True),
    )
    zx_pre = jnp.dot(normed_low, zx_full, preferred_element_type=jnp.float32).reshape(
        lane_count, BLOCK, 2 * E
    )
    bc_pre = jnp.dot(normed_low, bc_full, preferred_element_type=jnp.float32).reshape(
        lane_count, BLOCK, 2 * N
    )
    dt_raw = jnp.dot(normed_low, dt_full, preferred_element_type=jnp.float32).reshape(
        lane_count, BLOCK, H
    )
    rim_rows = passed_along(rim_of(zx_pre, bc_pre, chan_mask), "seq", 1)
    front_fn = partial(piece_front, chan_mask=chan_mask, head_mask=head_mask, keep_rows=keep_rows)
    front_out, front_back = jax.vjp(
        front_fn, zx_pre, bc_pre, dt_raw, rim_rows, conv_w, conv_b, dt_bias, a_log
    )
    z_gate, x_conv, b_conv, c_conv, dt_step, log_step = front_out
    (state_sum, log_total), state_back = jax.vjp(block_state, x_conv, b_conv, dt_step, log_step)
    carry_rate = jnp.exp(log_total) * keep_rows[:, None]
    identity = (jnp.ones_like(carry_rate), jnp.zeros_like(state_sum))
    prefix_pair = carried_in((carry_rate, state_sum), "seq", chain_combine, identity, False)
    state_in = prefix_pair[1] * keep_rows[:, None, None, None]
    lane_inputs = (z_gate, x_conv, b_conv, c_conv, dt_step, log_step, state_in)
    mixed_low = mix_lanes(lane_inputs, d_skip, gate_gain, chan_count)
    mixed_flat = mixed_low.reshape(-1, E).astype(jnp.bfloat16)
    branch = jnp.dot(mixed_flat, out_full, preferred_element_type=jnp.float32)
    output = (x_rows + row_mask * branch).astype(jnp.bfloat16)
    cot_rows = cotangent.astype(jnp.float32)
    branch_grad = (cot_rows * row_mask).astype(jnp.bfloat16)
    out_grad = contract_rows(mixed_flat, branch_grad)
    mixed_grad = contract_cols(branch_grad, out_full).reshape(lane_count, BLOCK, E)
    lane_grads, grad_skip, grad_gain = mix_back_lanes(
        lane_inputs, mixed_grad, d_skip, gate_gain, chan_count
    )
    grad_gate, grad_x, grad_b, grad_c, grad_dt, grad_log, grad_state = lane_grads
    later_pair = carried_in(
        (carry_rate, grad_state * keep_rows[:, None, None, None]),
        "seq",
        chain_combine,
        identity,
        True,
    )
    later_grad = later_pair[1]
    grad_total = jnp.exp(log_total) * jnp.sum(later_grad * state_in, axis=(2, 3))
    grad_x_more, grad_b_more, grad_dt_more, grad_log_more = state_back((later_grad, grad_total))
    grad_zx, grad_bc, grad_dtraw, grad_rim, grad_convw, grad_convb, grad_dtbias, grad_alog = (
        front_back(
            (
                grad_gate,
                grad_x + grad_x_more,
                grad_b + grad_b_more,
                grad_c,
                grad_dt + grad_dt_more,
                grad_log + grad_log_more,
            )
        )
    )
    rim_grad = passed_along(grad_rim.astype(jnp.bfloat16), "seq", -1).astype(grad_rim.dtype)
    grad_zx = grad_zx.at[:, BLOCK - KCONV + 1 :, E:].add(rim_grad[..., :E] * chan_mask)
    grad_bc = grad_bc.at[:, BLOCK - KCONV + 1 :, :].add(rim_grad[..., E:])
    zx_low = grad_zx.reshape(-1, 2 * E).astype(jnp.bfloat16)
    bc_low = grad_bc.reshape(-1, 2 * N).astype(jnp.bfloat16)
    dt_low = grad_dtraw.reshape(-1, H).astype(jnp.bfloat16)
    zx_weight_grad = contract_rows(normed_low, zx_low)
    bc_weight_grad = contract_rows(normed_low, bc_low)
    dt_weight_grad = contract_rows(normed_low, dt_low)
    normed_grad = (
        contract_cols(zx_low, zx_full)
        + contract_cols(bc_low, bc_full)
        + contract_cols(dt_low, dt_full)
    )
    grad_x_rows, grad_norm = norm_back(normed_grad)
    input_grad = cot_rows + grad_x_rows
    out_shard = share_out(out_grad)
    row_shards = (
        lax.psum_scatter(grad_norm, "seq", scatter_dimension=0, tiled=True),
        lax.psum_scatter(zx_weight_grad, "seq", scatter_dimension=0, tiled=True),
        lax.psum_scatter(bc_weight_grad, "seq", scatter_dimension=0, tiled=True),
        lax.psum_scatter(dt_weight_grad, "seq", scatter_dimension=0, tiled=True),
        lax.psum_scatter(grad_convw, "seq", scatter_dimension=0, tiled=True),
        lax.psum_scatter(grad_convb, "seq", scatter_dimension=0, tiled=True),
        lax.psum_scatter(grad_dtbias, "seq", scatter_dimension=0, tiled=True),
        lax.psum_scatter(grad_alog, "seq", scatter_dimension=0, tiled=True),
        lax.psum_scatter(grad_skip, "seq", scatter_dimension=0, tiled=True),
        lax.psum_scatter(grad_gain, "seq", scatter_dimension=0, tiled=True),
    )
    summed = lax.psum(
        (
            row_shards[0],
            row_shards[1],
            row_shards[2],
            row_shards[3],
            row_shards[4],
            row_shards[5],
            row_shards[6],
            row_shards[7],
            row_shards[8],
            row_shards[9],
            out_shard,
        ),
        "width",
    )
    return (
        output,
        input_grad,
        summed[0],
        summed[1],
        summed[2],
        summed[3],
        summed[4],
        summed[5],
        summed[6],
        summed[7],
        summed[8],
        summed[9],
        summed[10],
    )


def solution(mesh):
    in_specs = (
        P(("width", "seq"), None),
        P(("width", "seq"), None),
        P(("width", "seq"), None),
        P(("width", "seq"), None),
        P(),
        P("seq", None),
        P("seq", None),
        P("seq", None),
        P(),
        P(),
        P(),
        P(),
        P(),
        P(),
        P("seq", None),
    )
    out_specs = (
        P(("width", "seq"), None),
        P(("width", "seq"), None),
        P("seq"),
        P("seq", None),
        P("seq", None),
        P("seq", None),
        P("seq", None),
        P("seq"),
        P("seq"),
        P("seq"),
        P("seq"),
        P("seq"),
        P("seq", None),
    )
    body = heads_body if H % (2 * mesh.shape["seq"]) == 0 else rows_body
    return jax.shard_map(body, mesh=mesh, in_specs=in_specs, out_specs=out_specs, check_vma=False)
```

```python
from functools import partial

import jax
import jax.numpy as jnp
from jax import lax
from jax.experimental import pallas as pl
from jax.experimental.pallas import tpu as pltpu
from jax.sharding import PartitionSpec as P

H = 64
HEAD_DIM = 64
N = 128
KCONV = 4
BLOCK = 128
E = 4096
SUB = 8

epsilon = 1e-05
highest = lax.Precision.HIGHEST
f32 = jnp.float32
bf16 = jnp.bfloat16

NN = ((1,), (0,))
NT = ((1,), (1,))
TN = ((0,), (0,))


def mm(left, right, dims=NN, precision=None):
    return lax.dot_general(left, right, (dims, ((), ())), precision=precision, preferred_element_type=f32)


def split2(value):
    high = value.astype(bf16)
    return high, (value - high.astype(f32)).astype(bf16)


def mm_right(left, right, dims=NN):
    high, low = split2(right)
    return mm(left, high, dims) + mm(left, low, dims)


def mm_left(left, right, dims=NN):
    high, low = split2(left)
    return mm(high, right, dims) + mm(low, right, dims)


def softplus(v):
    small = jnp.exp(-jnp.abs(v))
    log1p = jnp.where(small < 1e-4, small - 0.5 * small * small, jnp.log(1.0 + small))
    return jnp.maximum(v, 0.0) + log1p


def sigmoid(v):
    return 1.0 / (1.0 + jnp.exp(-v))


def grids():
    row = lax.broadcasted_iota(jnp.int32, (BLOCK, BLOCK), 0)
    col = lax.broadcasted_iota(jnp.int32, (BLOCK, BLOCK), 1)
    return row, col


def halves(pair, lane):
    zero = jnp.zeros_like(pair)
    return jnp.where(lane < HEAD_DIM, pair, zero), jnp.where(lane < HEAD_DIM, zero, pair)


def decay_of(cum, cum_t, head, causal):
    return jnp.exp(jnp.where(causal, cum[:, head : head + 1] - cum_t[head : head + 1, :], -1e30))


TAP, BIAS, SKIP, GAIN, MASK = 0, 4, 5, 6, 7
DT_BIAS, NEG_A, HEAD_MASK = 0, 1, 2


def forward_block(
    keep_row, zx_ref, chan_ref, bc_par_ref, head_ref, spread,
    conv_ref, mix_ref, bc_ref, step_ref, state_ref, tail_ref,
    state, tail_x, tail_b, pad_x, pad_b,
    *, lane, heads,
):
    width = heads * HEAD_DIM
    row, col = grids()
    causal = row >= col
    tril = causal.astype(f32)
    rows = pl.ds(lane * BLOCK, BLOCK)
    keep = jnp.concatenate([keep_row] * (width // BLOCK), axis=1)
    keep_b = jnp.concatenate([keep_row] * (2 * N // BLOCK), axis=1)

    pre = zx_ref[rows, width : 2 * width]
    before = tail_x[lane] * keep
    pad_x[lane, 0:SUB] = before
    pad_x[lane, SUB:] = pre
    tail_ref[lane] = before
    tail_x[lane] = pre[BLOCK - SUB :, :]
    conv = chan_ref[BIAS : BIAS + 1, :]
    for k in range(KCONV):
        conv = conv + pad_x[lane, SUB - KCONV + 1 + k : SUB - KCONV + 1 + k + BLOCK, :] * chan_ref[k : k + 1, :]
    conv_ref[rows, :] = conv
    x_low = (conv * sigmoid(conv) * chan_ref[MASK : MASK + 1, :]).astype(bf16)

    pre_b = zx_ref[rows, 2 * width + BLOCK :]
    pad_b[lane, 0:SUB] = tail_b[lane] * keep_b
    pad_b[lane, SUB:] = pre_b
    tail_b[lane] = pre_b[BLOCK - SUB :, :]
    conv_b = bc_par_ref[BIAS : BIAS + 1, :]
    for k in range(KCONV):
        conv_b = conv_b + pad_b[lane, SUB - KCONV + 1 + k : SUB - KCONV + 1 + k + BLOCK, :] * bc_par_ref[k : k + 1, :]
    bc_low = (conv_b * sigmoid(conv_b)).astype(bf16)
    bc_ref[rows, :] = bc_low
    b_low, c_low = bc_low[:, :N], bc_low[:, N:]

    raw = zx_ref[rows, 2 * width : 2 * width + BLOCK] + head_ref[DT_BIAS : DT_BIAS + 1, :]
    dt = softplus(raw) * head_ref[HEAD_MASK : HEAD_MASK + 1, :]
    cum = mm(tril, head_ref[NEG_A : NEG_A + 1, :] * dt, precision=highest)
    step_ref[rows, :BLOCK] = cum
    step_ref[rows, BLOCK:] = dt
    cum_t, dt_t = cum.T, dt.T
    last = cum[BLOCK - 1 :, :]
    carry_x = mm_left(jnp.exp(cum), spread)
    end_x = mm_left(jnp.exp(last - cum) * dt, spread)
    last_x = carry_x[BLOCK - 1 :, :]

    inner = mm(c_low, b_low, NT)
    parts = []
    for j in range(heads // 2):
        pair = x_low[:, 2 * HEAD_DIM * j : 2 * HEAD_DIM * (j + 1)]
        scores = [
            (inner * decay_of(cum, cum_t, h, causal) * dt_t[h : h + 1, :]).astype(bf16)
            for h in (2 * j, 2 * j + 1)
        ]
        parts.append(mm(jnp.concatenate(scores, axis=1), jnp.concatenate(halves(pair, col), axis=0)))
    within = jnp.concatenate(parts, axis=1)

    state_in = state[lane] * keep
    state_ref[lane] = state_in
    carried = mm_right(c_low, state_in) * carry_x
    x_f = x_low.astype(f32)
    mix_ref[rows, :] = within + carried + chan_ref[SKIP : SKIP + 1, :] * x_f
    weighted = (x_f * end_x).astype(bf16)
    state[lane] = last_x * state_in + mm(b_low, weighted, TN)


def grad_kernel(bgrad_ref, w_ref, zx_ref, mix_ref, chan_ref, grad_ref, sums_ref):
    grad = mm(bgrad_ref[...], w_ref[...], NT)
    grad_ref[...] = grad
    z = zx_ref[...]
    gated = mix_ref[...] * (z * sigmoid(z))
    ones = jnp.ones((SUB, gated.shape[1]), bf16)
    square = mm_right(ones, gated * gated, NT)
    cross = mm_right(ones, grad * chan_ref[GAIN : GAIN + 1, :] * gated, NT)
    sub = lax.broadcasted_iota(jnp.int32, (SUB, BLOCK), 0)
    for lane in range(gated.shape[0] // BLOCK):
        at = slice(lane * BLOCK, (lane + 1) * BLOCK)
        sums_ref[0, lane] = jnp.where(sub == 0, square[:, at], jnp.where(sub == 1, cross[:, at], 0.0))


def run_grad(bgrad, w_out, zx, mix, chan, lanes):
    rows, width = mix.shape
    step = lanes * BLOCK
    blocks = rows // step
    by_block = lambda cols: pl.BlockSpec((step, cols), lambda c: (c, 0))
    whole = lambda a: pl.BlockSpec(a.shape, lambda c: (0,) * a.ndim)
    return pl.pallas_call(
        grad_kernel,
        grid=(blocks,),
        in_specs=[by_block(bgrad.shape[1]), whole(w_out), by_block(width), by_block(width), whole(chan)],
        out_specs=[by_block(width), pl.BlockSpec((1, lanes, SUB, BLOCK), lambda c: (c, 0, 0, 0))],
        out_shape=[jax.ShapeDtypeStruct((rows, width), f32), jax.ShapeDtypeStruct((blocks, lanes, SUB, BLOCK), f32)],
        compiler_params=pltpu.CompilerParams(vmem_limit_bytes=32 << 20),
        cost_estimate=pl.CostEstimate(flops=2 * rows * width * bgrad.shape[1], bytes_accessed=rows * width * 24, transcendentals=rows * width),
        name="mixed_grad",
    )(bgrad, w_out, zx, mix, chan)


def backward_kernel(
    keep_ref, zx_ref, grad_ref, chan_ref, head_ref, spread_ref,
    conv_ref, mix_ref, bc_ref, step_ref, state_ref, tail_ref, scale_ref,
    dzx_ref, dbc_ref, dchan_ref, dhead_ref,
    state_grad, next_conv, pad_x, pad_d,
    *, lanes, heads, blocks,
):
    lap = pl.program_id(0)
    c = blocks - 1 - lap
    width = heads * HEAD_DIM
    row, col = grids()
    causal = row >= col
    triu = (col >= row).astype(f32)
    spread = spread_ref[...]

    @pl.when(lap == 0)
    def _():
        state_grad[...] = jnp.zeros_like(state_grad)
        next_conv[...] = jnp.zeros_like(next_conv)
        dchan_ref[...] = jnp.zeros_like(dchan_ref)
        dhead_ref[...] = jnp.zeros_like(dhead_ref)

    def total(value):
        return jnp.sum(value, axis=0, keepdims=True)

    for lane in range(lanes):
        rows = pl.ds(lane * BLOCK, BLOCK)
        keep = keep_ref[c, lane]
        z = zx_ref[rows, :width]
        conv = conv_ref[rows, :]
        mixed = mix_ref[rows, :]
        grad = grad_ref[rows, :]
        gain = chan_ref[GAIN : GAIN + 1, :]
        skip = chan_ref[SKIP : SKIP + 1, :]
        rate = scale_ref[rows, 0:1]
        pull = scale_ref[rows, 1:2]
        gate = sigmoid(z)
        silu = z * gate
        gated = mixed * silu
        dgated = grad * gain * rate - gated * pull
        dzx_ref[rows, :width] = (dgated * mixed * (gate * (1.0 + z * (1.0 - gate)))).astype(bf16)
        dmixed = dgated * silu
        act = sigmoid(conv)
        x_low = (conv * act * chan_ref[MASK : MASK + 1, :]).astype(bf16)
        x_f = x_low.astype(f32)
        dchan_ref[GAIN : GAIN + 1, :] += total(grad * gated * rate)
        dchan_ref[SKIP : SKIP + 1, :] += total(dmixed * x_f)
        dlow = dmixed.astype(bf16)
        dlow_f = dlow.astype(f32)

        b_low, c_low = bc_ref[rows, :N], bc_ref[rows, N:]
        cum, dt = step_ref[rows, :BLOCK], step_ref[rows, BLOCK:]
        cum_t, dt_t = cum.T, dt.T
        last = cum[BLOCK - 1 :, :]
        to_last = jnp.exp(last - cum)
        carry_x = mm_left(jnp.exp(cum), spread)
        end_x = mm_left(to_last * dt, spread)
        last_x = carry_x[BLOCK - 1 :, :]

        inner = mm(c_low, b_low, NT)
        dinner = jnp.zeros((BLOCK, BLOCK), f32)
        parts, dt_rows = [], []
        for j in range(heads // 2):
            lanes_j = slice(2 * HEAD_DIM * j, 2 * HEAD_DIM * (j + 1))
            pair, dpair = x_low[:, lanes_j], dlow[:, lanes_j]
            dstack = jnp.concatenate(halves(dpair, col), axis=0)
            dscores = mm(dstack, pair, NT)
            scores = []
            for i, h in enumerate((2 * j, 2 * j + 1)):
                decay = decay_of(cum, cum_t, h, causal)
                step = dt_t[h : h + 1, :]
                scores.append((inner * decay * step).astype(bf16))
                part = dscores[i * BLOCK : (i + 1) * BLOCK] * decay
                dinner = dinner + part * step
                dt_rows.append(total(part * inner))
            parts.append(mm(jnp.concatenate(scores, axis=0), dstack, TN))
        dx_within = jnp.concatenate(parts, axis=1)
        dt_rows.append(jnp.zeros((BLOCK - heads, BLOCK), f32))
        ddt_within = jnp.concatenate(dt_rows, axis=0).T

        state_in = state_ref[0, lane]
        sgrad = state_grad[lane]
        in_high, in_low = split2(state_in)
        sg_high, sg_low = split2(sgrad)
        dcarry = dlow_f * carry_x
        dc_high, dc_low = split2(dcarry)
        di_high, di_low = split2(dinner)
        dc = mm(dc_high, in_high, NT) + mm(dc_high, in_low, NT) + mm(dc_low, in_high, NT)
        dc = dc + mm(di_high, b_low) + mm(di_low, b_low)
        weighted = (x_f * end_x).astype(bf16)
        db = mm(weighted, sg_high, NT) + mm(weighted, sg_low, NT)
        db = db + mm(di_high, c_low, TN) + mm(di_low, c_low, TN)
        dbc_ref[:N, rows] = db.T.astype(bf16)
        dbc_ref[N:, rows] = dc.T.astype(bf16)
        dweighted = mm(b_low, sg_high) + mm(b_low, sg_low)
        dx = dx_within + dweighted * end_x
        dcum = mm_left(dlow_f * (mixed - skip * x_f) - x_f * dx, spread, NT)
        dend = mm_left(dweighted * x_f, spread, NT)
        touch = jnp.broadcast_to(total(sgrad * state_in), (SUB, width))
        dlast = total(dend * to_last * dt) + jnp.exp(last) * mm_left(touch, spread, NT)[0:1]
        dlog = mm(triu, dcum, precision=highest) + dlast
        neg_a = head_ref[NEG_A : NEG_A + 1, :]
        ddt = ddt_within + dend * to_last + dlog * neg_a
        raw = zx_ref[rows, 2 * width : 2 * width + BLOCK] + head_ref[DT_BIAS : DT_BIAS + 1, :]
        draw = ddt * sigmoid(raw) * head_ref[HEAD_MASK : HEAD_MASK + 1, :]
        dzx_ref[rows, 2 * width :] = draw.astype(bf16)
        dhead_ref[0:1, :] += total(draw)
        dhead_ref[1:2, :] += total(dlog * neg_a * dt)
        state_grad[lane] = keep * (mm(c_low, dc_high, TN) + mm(c_low, dc_low, TN) + last_x * sgrad)

        dx = dx + skip * dmixed
        dconv = dx * chan_ref[MASK : MASK + 1, :] * (act * (1.0 + conv * (1.0 - act)))
        pad_d[lane, :BLOCK] = dconv
        pad_d[lane, BLOCK:] = next_conv[lane]
        next_conv[lane] = dconv[:SUB] * keep
        pad_x[lane, :SUB] = tail_ref[0, lane]
        pad_x[lane, SUB:] = zx_ref[rows, width : 2 * width]
        dpre = jnp.zeros((BLOCK, width), f32)
        for k in range(KCONV):
            dpre = dpre + pad_d[lane, KCONV - 1 - k : KCONV - 1 - k + BLOCK, :] * chan_ref[k : k + 1, :]
            dchan_ref[k : k + 1, :] += total(dconv * pad_x[lane, SUB - KCONV + 1 + k : SUB - KCONV + 1 + k + BLOCK, :])
        dchan_ref[BIAS : BIAS + 1, :] += total(dconv)
        dzx_ref[rows, width : 2 * width] = dpre.astype(bf16)


def entry_kernel(valid_ref, start_ref, x_ref, cot_ref, gain_ref, bc_ref, dt_ref, normed_ref, bgrad_ref, third_ref, starts_ref, *, peers):
    rows = x_ref.shape[0]
    lanes = rows // BLOCK
    x = x_ref[...].astype(f32)
    normed_ref[...] = (x * lax.rsqrt(jnp.mean(x * x, axis=-1, keepdims=True) + epsilon) * gain_ref[...]).astype(bf16)
    row = lax.broadcasted_iota(jnp.int32, (BLOCK, 1), 0)
    for lane in range(lanes):
        at = slice(lane * BLOCK, (lane + 1) * BLOCK)
        mask = (row < valid_ref[0, lane]).astype(f32)
        bgrad_ref[at, :] = (cot_ref[at, :].astype(f32) * mask).astype(bf16)
    bc, dt = bc_ref[...].astype(f32), dt_ref[...].astype(f32)
    share, heads = bc.shape[1] // peers, dt.shape[1] // peers
    rest = jnp.zeros((rows, BLOCK - share - heads), f32)
    for s in range(peers):
        tile = [dt[:, s * heads : (s + 1) * heads], bc[:, s * share : (s + 1) * share], rest]
        third_ref[s] = jnp.concatenate(tile, axis=1).astype(bf16)
    sub = lax.broadcasted_iota(jnp.int32, (SUB, BLOCK), 0)
    tile = jnp.zeros((SUB, BLOCK), f32)
    for lane in range(lanes):
        tile = jnp.where(sub == lane, start_ref[0, lane].astype(f32), tile)
    starts_ref[...] = tile


def entry(valid, starts, tokens, cotangent, gain, w_bc, w_dt, peers):
    smem, vmem = pl.BlockSpec(memory_space=pltpu.SMEM), pl.BlockSpec(memory_space=pltpu.VMEM)
    return pl.pallas_call(
        partial(entry_kernel, peers=peers),
        in_specs=[smem] * 2 + [vmem] * 5,
        out_specs=[vmem] * 4,
        out_shape=[
            jax.ShapeDtypeStruct(tokens.shape, bf16), jax.ShapeDtypeStruct(tokens.shape, bf16),
            jax.ShapeDtypeStruct((peers, w_bc.shape[0], BLOCK), bf16), jax.ShapeDtypeStruct((SUB, BLOCK), f32),
        ],
        compiler_params=pltpu.CompilerParams(vmem_limit_bytes=32 << 20),
        name="entry",
    )(valid, starts, tokens, cotangent, gain[None], w_bc, w_dt)


def run_backward(keep, zx, grad, chan, head, spread, conv, mix, bc, step_arr, state, tail, scale, lanes, heads):
    rows, width = grad.shape
    step = lanes * BLOCK
    blocks = rows // step
    by_block = lambda cols: pl.BlockSpec((step, cols), lambda c: (blocks - 1 - c, 0))
    whole = lambda a: pl.BlockSpec(a.shape, lambda c: (0,) * a.ndim)
    fixed = lambda shape: pl.BlockSpec(shape, lambda c: (0,) * len(shape))
    per_lane = lambda r, cols: pl.BlockSpec((1, lanes, r, cols), lambda c: (blocks - 1 - c, 0, 0, 0))
    return pl.pallas_call(
        partial(backward_kernel, lanes=lanes, heads=heads, blocks=blocks),
        grid=(blocks,),
        in_specs=[
            pl.BlockSpec(memory_space=pltpu.SMEM), by_block(2 * width + BLOCK), by_block(width),
            whole(chan), whole(head), whole(spread),
            by_block(width), by_block(width), by_block(2 * N), by_block(2 * BLOCK),
            per_lane(N, width), per_lane(SUB, width), by_block(SUB),
        ],
        out_specs=[
            by_block(2 * width + BLOCK), pl.BlockSpec((2 * N, step), lambda c: (0, blocks - 1 - c)),
            fixed((SUB, width)), fixed((SUB, BLOCK)),
        ],
        out_shape=[
            jax.ShapeDtypeStruct((rows, 2 * width + BLOCK), bf16),
            jax.ShapeDtypeStruct((2 * N, rows), bf16), jax.ShapeDtypeStruct((SUB, width), f32),
            jax.ShapeDtypeStruct((SUB, BLOCK), f32),
        ],
        scratch_shapes=[
            pltpu.VMEM((lanes, N, width), f32), pltpu.VMEM((lanes, SUB, width), f32),
            pltpu.VMEM((lanes, BLOCK + SUB, width), f32), pltpu.VMEM((lanes, BLOCK + SUB, width), f32),
        ],
        compiler_params=pltpu.CompilerParams(vmem_limit_bytes=48 << 20, dimension_semantics=("arbitrary",)),
        cost_estimate=pl.CostEstimate(flops=rows * width * 6144, bytes_accessed=rows * width * 40, transcendentals=rows * width * 6),
        name="mix_backward",
    )(keep, zx, grad, chan, head, spread, conv, mix, bc, step_arr, state, tail, scale)


MESH = pl.DeviceIdType.MESH


def greet(others):
    barrier = pltpu.get_barrier_semaphore()
    for other in others:
        pl.semaphore_signal(barrier, inc=1, device_id=other, device_id_type=MESH)
    pl.semaphore_wait(barrier, len(others))


def remote(src, dst, send, recv, device):
    return pltpu.make_async_remote_copy(
        src_ref=src, dst_ref=dst, send_sem=send, recv_sem=recv, device_id=device, device_id_type=MESH
    )


class Rows:
    def __init__(self, own_ref, all_ref, sems, peers):
        self.own, self.all, self.sems, self.peers = own_ref, all_ref, sems, peers
        self.width, self.place = lax.axis_index("width"), lax.axis_index("seq")
        self.chips, self.chip = peers // 2, self.place // 2

    def hop(self, ref, s, step, by):
        send, recv = self.sems[0 if by > 0 else 2], self.sems[1 if by > 0 else 3]
        device = (self.width, jnp.clip(self.place + 2 * by, 0, self.peers - 1))
        return remote(ref, self.all.at[s], send.at[step], recv.at[step], device)

    def over(self, ref, s, slot):
        device = (self.width, jnp.bitwise_xor(self.place, 1))
        return remote(ref, self.all.at[s], self.sems[4].at[slot], self.sems[5].at[slot], device)

    def inside(self, by):
        return self.chip + 1 < self.chips if by > 0 else self.chip > 0

    def reached(self, by, step):
        return self.chip >= step if by > 0 else self.chip + step < self.chips

    def source(self, by, step):
        return jnp.clip(self.place - 2 * by * step, 0, self.peers - 1)

    def keep(self):
        return pltpu.make_async_copy(self.own, self.all.at[self.place], self.sems[6])

    def start(self):
        self.keep().start()
        for by in (1, -1):
            @pl.when(self.inside(by))
            def _():
                self.hop(self.own, self.place, 0, by).start()
        self.over(self.own, self.place, 0).start()

    def pass_on(self, step):
        for by in (1, -1):
            @pl.when(self.reached(by, step))
            def _():
                s = self.source(by, step)
                ref = self.all.at[s]
                self.hop(ref, s, step - 1, by).wait_recv()

                @pl.when(self.inside(by))
                def _():
                    self.hop(ref, s, step, by).start()
                self.over(ref, s, 2 * step - (by > 0)).start()

    def arrived(self):
        self.keep().wait()
        self.over(self.own, self.place, 0).wait()
        for step in range(1, self.chips):
            for by in (1, -1):
                @pl.when(self.reached(by, step))
                def _():
                    s = self.source(by, step)
                    self.over(self.all.at[s], s, 2 * step - (by > 0)).wait()

    def sent(self):
        for step in range(self.chips):
            for by in (1, -1):
                @pl.when(self.inside(by) & self.reached(by, step))
                def _():
                    s = self.source(by, step)
                    self.hop(self.all.at[s], s, step, by).wait_send()


ROW_SEMS = 7


def row_sems(chips):
    dma = pltpu.SemaphoreType.DMA
    return [dma((chips,)), dma((chips,)), dma((chips,)), dma((chips,)), dma((2 * chips,)), dma((2 * chips,)), dma(())]


def front_kernel(
    zx_ref, third_ref, bc_ref, own_ref, grad_ref, start_ref, chan_ref, bc_par_ref, head_ref, spread_ref,
    w_ref, rows_ref, grads_ref, starts_ref, out_zx, out_conv, out_mix, out_bc, out_step, out_state, out_tail,
    w_v, rows_v, starts_v, zx_v, conv_v, mix_v, bc_v, step_v, state_v, tail_v,
    state, tail_x, tail_b, pad_x, pad_b,
    w_send, w_recv, st_send, st_recv, own_sem, wide_send, wide_recv, in_sem, out_sem, *sems,
    peers, widths, lanes, heads,
):
    width, place = lax.axis_index("width"), lax.axis_index("seq")
    chips = peers // 2
    chans = heads * HEAD_DIM
    quarter = zx_ref.shape[0] // widths
    ring = [lax.rem(place + by, peers) for by in range(1, peers)]
    cross = [jnp.bitwise_xor(width, m) for m in range(1, widths)]
    greet([(width, s) for s in ring] + [(w, place) for w in cross])
    mine = pl.ds(pl.multiple_of(width * quarter, quarter), quarter)
    rows = Rows(own_ref, rows_ref, sems[:ROW_SEMS], peers)
    grads = Rows(grad_ref, grads_ref, sems[ROW_SEMS:], peers)

    def columns(half, s):
        return pl.ds(pl.multiple_of(half * peers * chans + s * chans, 128), chans)

    wide = 2 * chans
    spots = [pl.ds(0, chans), pl.ds(chans, chans), pl.ds(wide, BLOCK), pl.ds(wide + BLOCK, 2 * N)]

    def parts(s):
        return [zx_ref.at[mine, columns(0, s)], zx_ref.at[mine, columns(1, s)], third_ref.at[s, mine], bc_ref.at[mine]]

    pushes = []
    for i, s in enumerate(ring):
        for k, (part, spot) in enumerate(zip(parts(s), spots)):
            pushes.append(remote(part, w_ref.at[place, width, :, spot], w_send.at[k, i], w_recv.at[k, i], (width, s)))
        pushes.append(remote(start_ref, starts_ref.at[place], st_send.at[i], st_recv.at[i], (width, s)))
    for push in pushes:
        push.start()
    keeps = [
        pltpu.make_async_copy(part, w_ref.at[place, width, :, spot], own_sem.at[k])
        for k, (part, spot) in enumerate(zip(parts(place), spots))
    ]
    keeps.append(pltpu.make_async_copy(start_ref, starts_ref.at[place], own_sem.at[4]))
    for keep in keeps:
        keep.start()
    rows.start()

    for push in pushes:
        push.wait_recv()
    for keep in keeps:
        keep.wait()
    shares = [
        remote(w_ref.at[:, width], w_ref.at[:, width], wide_send.at[m], wide_recv.at[m], (w, place)) for m, w in enumerate(cross)
    ]
    for share in shares:
        share.start()
    for step in range(1, chips - 1):
        rows.pass_on(step)
    grads.start()
    for share in shares:
        share.wait_recv()
    in_w = pltpu.make_async_copy(w_ref, w_v, own_sem.at[0])
    in_starts = pltpu.make_async_copy(starts_ref, starts_v, own_sem.at[1])
    in_w.start()
    in_starts.start()
    rows.pass_on(chips - 1)
    rows.arrived()
    loads = [pltpu.make_async_copy(rows_ref.at[c], rows_v.at[c], in_sem.at[c]) for c in range(peers)]
    for load in loads:
        load.start()
    for array in (state, tail_x, tail_b):
        array[...] = jnp.zeros_like(array)
    in_w.wait()
    in_starts.wait()

    outs = [
        (zx_v, out_zx), (conv_v, out_conv), (mix_v, out_mix), (bc_v, out_bc), (step_v, out_step), (state_v, out_state), (tail_v, out_tail)
    ]

    def out_copies(c):
        return [pltpu.make_async_copy(src.at[c], dst.at[c], out_sem.at[k, c]) for k, (src, dst) in enumerate(outs)]

    def compute(first, last):
        @pl.loop(first, last)
        def _(c):
            pltpu.make_async_copy(rows_ref.at[c], rows_v.at[c], in_sem.at[c]).wait()
            weights = w_v[...].reshape(w_v.shape[0] * w_v.shape[1] * w_v.shape[2], w_v.shape[3])
            zx_v[c] = mm(rows_v[c], weights)
            spread = spread_ref[...]
            for lane in range(lanes):
                forward_block(
                    1.0 - starts_v[c, lane : lane + 1, :], zx_v.at[c], chan_ref, bc_par_ref, head_ref, spread,
                    conv_v.at[c], mix_v.at[c], bc_v.at[c], step_v.at[c], state_v.at[c], tail_v.at[c],
                    state, tail_x, tail_b, pad_x, pad_b, lane=lane, heads=heads,
                )
            for copy in out_copies(c):
                copy.start()

    per = -(-peers // 2)
    for step in range(1, chips):
        first, last = min((step - 1) * per, peers), min(step * per, peers)
        if step == chips - 1:
            last = peers
        if first < last:
            compute(first, last)
        grads.pass_on(step)

    grads.arrived()
    for share in shares:
        share.wait_send()
    for push in pushes:
        push.wait_send()
    rows.sent()
    grads.sent()

    @pl.loop(0, peers)
    def _(c):
        for copy in out_copies(c):
            copy.wait()


def front(w_zx, third, w_bc, own_rows, own_grads, start_tile, chan, bc_par, head, spread, lanes, heads):
    peers, widths = lax.axis_size("seq"), lax.axis_size("width")
    own, model = own_rows.shape
    quarter = own // widths
    chans = heads * HEAD_DIM
    cols = 2 * chans + BLOCK + 2 * N
    dma = pltpu.SemaphoreType.DMA
    anywhere, vmem = pl.BlockSpec(memory_space=pl.ANY), pl.BlockSpec(memory_space=pltpu.VMEM)
    gathered = [
        ((peers, widths, quarter, cols), bf16), ((peers, own, model), bf16), ((peers, own, model), bf16),
        ((peers,) + start_tile.shape, f32),
    ]
    computed = [
        ((peers, own, cols), f32), ((peers, own, chans), f32), ((peers, own, chans), f32), ((peers, own, 2 * N), bf16),
        ((peers, own, 2 * BLOCK), f32), ((peers, lanes, N, chans), f32), ((peers, lanes, SUB, chans), f32),
    ]
    return pl.pallas_call(
        partial(front_kernel, peers=peers, widths=widths, lanes=lanes, heads=heads),
        in_specs=[anywhere] * 6 + [vmem] * 4,
        out_specs=[anywhere] * (len(gathered) + len(computed)),
        out_shape=[jax.ShapeDtypeStruct(*a) for a in gathered + computed],
        scratch_shapes=[
            *[pltpu.VMEM(*a) for a in (gathered[0], gathered[1], gathered[3], *computed)],
            pltpu.VMEM((lanes, N, chans), f32), pltpu.VMEM((lanes, SUB, chans), f32), pltpu.VMEM((lanes, SUB, 2 * N), f32),
            pltpu.VMEM((lanes, BLOCK + SUB, chans), f32), pltpu.VMEM((lanes, BLOCK + SUB, 2 * N), f32),
            dma((4, peers - 1)), dma((4, peers - 1)), dma((peers - 1,)), dma((peers - 1,)),
            dma((5,)), dma((widths - 1,)), dma((widths - 1,)), dma((peers,)), dma((len(computed), peers)),
            *row_sems(peers // 2), *row_sems(peers // 2),
        ],
        compiler_params=pltpu.CompilerParams(collective_id=1, has_side_effects=True, vmem_limit_bytes=60 << 20),
        name="front",
    )(w_zx, third, w_bc, own_rows, own_grads, start_tile, chan, bc_par, head, spread)


ROWS_AT_ONCE = 16


def add_into(dst, others, rows):
    @pl.loop(0, rows // ROWS_AT_ONCE)
    def _(i):
        at = pl.ds(pl.multiple_of(i * ROWS_AT_ONCE, ROWS_AT_ONCE), ROWS_AT_ONCE)
        value = dst[at].astype(f32)
        for other in others:
            value = value + other[at].astype(f32)
        dst[at] = value.astype(dst.dtype)


def scatter_kernel(
    part_ref, wide_ref, third_ref, x_ref, cot_ref, gain_ref, rows_ref, out_ref, out_third_ref,
    mine, from_core, up, down, own0, own1, own2, got0, got1, got2, piece0, piece1, piece2,
    local_sem, core_send, core_recv, up_send, up_recv, down_send, down_recv,
    own_sem, q_send, q_recv, p_send, p_recv, o_send, o_recv,
    *, peers, widths,
):
    width, place = lax.axis_index("width"), lax.axis_index("seq")
    chips = peers // 2
    chip, core = place // 2, lax.rem(place, 2)
    mate = (width, jnp.bitwise_xor(place, 1))
    ring = [lax.rem(place + by, peers) for by in range(1, peers)]
    cross = [jnp.bitwise_xor(width, m) for m in range(1, widths)]
    greet([(width, s) for s in ring] + [(w, place) for w in cross])
    half = wide_ref.shape[3] // 2
    sets = [
        (wide_ref, out_ref, pl.ds(0, half), own0, got0, piece0),
        (wide_ref, out_ref, pl.ds(half, half), own1, got1, piece1),
        (third_ref, out_third_ref, pl.ds(0, BLOCK), own2, got2, piece2),
    ]

    def remote(src, dst, send, recv, device):
        return pltpu.make_async_remote_copy(
            src_ref=src, dst_ref=dst, send_sem=send, recv_sem=recv, device_id=device, device_id_type=MESH
        )

    locals_ = [pltpu.make_async_copy(part_ref.at[2 * q + core], mine.at[q], local_sem.at[q]) for q in range(chips)]
    to_core = [
        remote(part_ref.at[2 * q + 1 - core], from_core.at[q], core_send.at[q], core_recv.at[q], mate) for q in range(chips)
    ]
    own_in, to_width = [], []
    for k, (src, dst, cols, own, got, piece) in enumerate(sets):
        own_in.append(pltpu.make_async_copy(src.at[:, width, :, cols], own, own_sem.at[0, k]))
        to_width.append([
            remote(src.at[:, w, :, cols], got.at[m], q_send.at[k, m], q_recv.at[k, m], (w, place)) for m, w in enumerate(cross)
        ])
    for copy in locals_ + to_core + own_in + to_width[0] + to_width[1] + to_width[2]:
        copy.start()
    rows = mine.shape[1]
    for q in range(chips):
        locals_[q].wait()
        to_core[q].wait_recv()
        add_into(mine.at[q], [from_core.at[q]], rows)

    def flow(by):
        return (up, up_send, up_recv) if by > 0 else (down, down_send, down_recv)

    def sends(by, step):
        far = chips - step
        return chip + far < chips if by > 0 else chip >= far

    def later(by):
        return chip > 0 if by > 0 else chip + 1 < chips

    def hop(src, by, step):
        buffer, send, recv = flow(by)
        return remote(
            src, buffer.at[step - 1], send.at[step - 1], recv.at[step - 1], (width, jnp.clip(place + 2 * by, 0, peers - 1))
        )

    def staged(by, step):
        return flow(by)[0].at[step - 2]

    def run_hops(step):
        for by in (1, -1):
            owner = jnp.clip(chip + by * (chips - step), 0, chips - 1)

            def direct():
                hop(mine.at[owner], by, step).start()

            def relayed():
                hop(staged(by, step), by, step - 1).wait_recv()
                add_into(staged(by, step), [mine.at[owner]], rows)
                hop(staged(by, step), by, step).start()

            if step == 1:
                pl.when(sends(by, step))(direct)
            else:
                pl.when(sends(by, step) & jnp.logical_not(later(by)))(direct)
                pl.when(sends(by, step) & later(by))(relayed)

    to_owner, to_all, kept = [None] * 3, [None] * 3, []

    def exchange(k):
        src, dst, cols, own, got, piece = sets[k]
        own_in[k].wait()
        for copy in to_width[k]:
            copy.wait_recv()
        for s in range(peers):
            add_into(own.at[s], [got.at[m, s] for m in range(widths - 1)], own.shape[1])
        to_owner[k] = [
            remote(own.at[s], piece.at[place], p_send.at[k, i], p_recv.at[k, i], (width, s)) for i, s in enumerate(ring)
        ]
        keep = pltpu.make_async_copy(own.at[place], piece.at[place], own_sem.at[1, k])
        for copy in to_owner[k] + [keep]:
            copy.start()
        kept.append(keep)

    def spread(k):
        src, dst, cols, own, got, piece = sets[k]
        for copy in to_owner[k]:
            copy.wait_recv()
        kept[k].wait()
        to_all[k] = [
            remote(piece, dst.at[:, width, :, cols], o_send.at[k, m], o_recv.at[k, m], (w, place)) for m, w in enumerate(cross)
        ]
        to_all[k].append(pltpu.make_async_copy(piece, dst.at[:, width, :, cols], own_sem.at[2, k]))
        for copy in to_all[k]:
            copy.start()

    run_hops(1)
    exchange(0)
    if chips > 2:
        run_hops(2)
    spread(0)
    exchange(1)
    exchange(2)
    for step in range(3, chips):
        run_hops(step)
    spread(1)
    spread(2)

    for by in (1, -1):
        @pl.when(later(by))
        def _():
            buffer = flow(by)[0].at[chips - 2]
            hop(buffer, by, chips - 1).wait_recv()
            add_into(mine.at[chip], [buffer], rows)

    gain = gain_ref[...]

    @pl.loop(0, rows // ROWS_AT_ONCE)
    def _(i):
        at = pl.ds(pl.multiple_of(i * ROWS_AT_ONCE, ROWS_AT_ONCE), ROWS_AT_ONCE)
        x = x_ref[at, :].astype(f32)
        rate = lax.rsqrt(jnp.mean(x * x, axis=-1, keepdims=True) + epsilon)
        unit = x * rate
        pulled = mine[chip, at].astype(f32) * gain
        inner = jnp.mean(pulled * unit, axis=-1, keepdims=True)
        rows_ref[at, :] = cot_ref[at, :].astype(f32) + rate * (pulled - unit * inner)

    for step in range(1, chips):
        for by in (1, -1):
            @pl.when(sends(by, step))
            def _():
                hop(mine.at[0], by, step).wait_send()
    for copy in to_core:
        copy.wait_send()
    for k in range(len(sets)):
        for copy in to_width[k] + to_owner[k]:
            copy.wait_send()
        for copy in to_all[k]:
            copy.wait()


def scattered_out(part, wide, third, x_rows, cotangent, gain):
    peers, widths = lax.axis_size("seq"), lax.axis_size("width")
    chips = peers // 2
    dma = pltpu.SemaphoreType.DMA
    anywhere = pl.BlockSpec(memory_space=pl.ANY)
    vmem = pl.BlockSpec(memory_space=pltpu.VMEM)
    block = part.shape[1:]
    half = wide.shape[3] // 2
    pieces = [(peers, wide.shape[2], cols) for cols in (half, half, third.shape[3])]
    return pl.pallas_call(
        partial(scatter_kernel, peers=peers, widths=widths),
        in_specs=[anywhere] * 3 + [vmem] * 3,
        out_specs=[vmem, anywhere, anywhere],
        out_shape=[
            jax.ShapeDtypeStruct(block, f32), jax.ShapeDtypeStruct(wide.shape, bf16), jax.ShapeDtypeStruct(third.shape, bf16)
        ],
        scratch_shapes=[
            pltpu.VMEM((chips,) + block, bf16), pltpu.VMEM((chips,) + block, bf16),
            pltpu.VMEM((chips - 1,) + block, bf16), pltpu.VMEM((chips - 1,) + block, bf16),
            *[pltpu.VMEM(piece, bf16) for piece in pieces],
            *[pltpu.VMEM((widths - 1,) + piece, bf16) for piece in pieces],
            *[pltpu.VMEM(piece, bf16) for piece in pieces],
            dma((chips,)), dma((chips,)), dma((chips,)),
            dma((chips - 1,)), dma((chips - 1,)), dma((chips - 1,)), dma((chips - 1,)),
            dma((3, 3)), dma((3, widths - 1)), dma((3, widths - 1)), dma((3, peers - 1)), dma((3, peers - 1)),
            dma((3, widths - 1)), dma((3, widths - 1)),
        ],
        compiler_params=pltpu.CompilerParams(collective_id=2, has_side_effects=True, vmem_limit_bytes=48 << 20),
        name="scatter_out",
    )(part, wide, third, x_rows, cotangent, gain)


def bc_kernel(got_ref, pre_ref, par_ref, keep_ref, ddt_ref, third_ref, dpar_ref, pre_t, *, at):
    chans, times = pre_t.shape
    for i in range(times // BLOCK):
        rows = slice(i * BLOCK, (i + 1) * BLOCK)
        pre_t[:, rows] = pre_ref[rows, :].T[at : at + chans]
    dbc = got_ref[0].astype(f32)
    for s in range(1, got_ref.shape[0]):
        dbc = dbc + got_ref[s].astype(f32)
    pre = pre_t[...]
    in_block = lax.rem(lax.broadcasted_iota(jnp.int32, (chans, times), 1), BLOCK)
    keep, keep_next = keep_ref[0:1, :], keep_ref[1:2, :]
    conv = jnp.broadcast_to(par_ref[:, BIAS : BIAS + 1], (chans, times))
    shifted = []
    for j in range(KCONV):
        moved = pre
        if j:
            moved = jnp.where(in_block >= j, pltpu.roll(pre, j, 1), keep * pltpu.roll(pre, BLOCK + j, 1))
        shifted.append(moved)
        conv = conv + moved * par_ref[:, KCONV - 1 - j : KCONV - j]
    act = sigmoid(conv)
    dconv = dbc * (act * (1.0 + conv * (1.0 - act)))
    dpre = dconv * par_ref[:, KCONV - 1 : KCONV]
    lane = lax.broadcasted_iota(jnp.int32, (chans, BLOCK), 1)
    dpar = jnp.where(lane == BIAS, jnp.sum(dconv, axis=1, keepdims=True), 0.0)
    for j in range(KCONV):
        dpar = dpar + jnp.where(lane == KCONV - 1 - j, jnp.sum(dconv * shifted[j], axis=1, keepdims=True), 0.0)
        if j:
            back = jnp.where(
                in_block < BLOCK - j, pltpu.roll(dconv, times - j, 1), keep_next * pltpu.roll(dconv, times - BLOCK - j, 1)
            )
            dpre = dpre + back * par_ref[:, KCONV - 1 - j : KCONV - j]
    dpar_ref[...] = dpar
    for i in range(times // BLOCK):
        tile = dpre[:, i * BLOCK : (i + 1) * BLOCK]
        below = jnp.zeros((BLOCK - at - chans, BLOCK), f32)
        tile = jnp.concatenate([jnp.zeros((at, BLOCK), f32), tile, below], axis=0).T
        rows = slice(i * BLOCK, (i + 1) * BLOCK)
        third_ref[rows, :] = (tile + ddt_ref[rows, :].astype(f32)).astype(bf16)


def bc_backward(got, zx, par, keep, dzx, at, chans):
    rows = dzx.shape[0]
    share = got.shape[1]
    third = pl.BlockSpec((rows, BLOCK), lambda i: (0, 2 * chans // BLOCK))
    whole = lambda a: pl.BlockSpec(a.shape, lambda i: (0,) * a.ndim)
    return pl.pallas_call(
        partial(bc_kernel, at=at),
        grid=(1,),
        in_specs=[whole(got), third, whole(par), whole(keep), third],
        out_specs=[pl.BlockSpec((rows, BLOCK), lambda i: (0, 0)), pl.BlockSpec((share, BLOCK), lambda i: (0, 0))],
        out_shape=[jax.ShapeDtypeStruct((rows, BLOCK), bf16), jax.ShapeDtypeStruct((share, BLOCK), f32)],
        scratch_shapes=[pltpu.VMEM((share, rows), f32)],
        compiler_params=pltpu.CompilerParams(vmem_limit_bytes=32 << 20),
        name="bc_backward",
    )(got, zx, par, keep, dzx)


def sum_kernel(own_ref, out_ref, got, send_sem, recv_sem, *, peers):
    place = lax.axis_index("seq")
    width = lax.axis_index("width")
    barrier = pltpu.get_barrier_semaphore()
    for by in range(1, peers):
        pl.semaphore_signal(
            barrier, inc=1, device_id=(width, lax.rem(place + by, peers)), device_id_type=pl.DeviceIdType.MESH
        )
    pl.semaphore_wait(barrier, peers - 1)
    copies = []
    for by in range(1, peers):
        copies.append(
            pltpu.make_async_remote_copy(
                src_ref=own_ref, dst_ref=got.at[by - 1], send_sem=send_sem.at[by - 1], recv_sem=recv_sem.at[by - 1],
                device_id=(width, lax.rem(place + by, peers)), device_id_type=pl.DeviceIdType.MESH,
            )
        )
        copies[-1].start()
    total = own_ref[...]
    for by in range(1, peers):
        copies[by - 1].wait()
        total = total + got[by - 1]
    out_ref[...] = total


def summed_small(value):
    peers = lax.axis_size("seq")
    return pl.pallas_call(
        partial(sum_kernel, peers=peers),
        out_shape=jax.ShapeDtypeStruct(value.shape, f32),
        in_specs=[pl.BlockSpec(memory_space=pltpu.VMEM)],
        out_specs=pl.BlockSpec(memory_space=pltpu.VMEM),
        scratch_shapes=[
            pltpu.VMEM((peers - 1,) + value.shape, f32),
            pltpu.SemaphoreType.DMA((peers - 1,)), pltpu.SemaphoreType.DMA((peers - 1,)),
        ],
        compiler_params=pltpu.CompilerParams(collective_id=0, has_side_effects=True),
        name="row_sums",
    )(value)


def laid_kernel(in_ref, third_ref, w_ref, bc_ref, dt_ref, gain_ref, out_ref, out_bc_ref, out_dt_ref, norm_ref, *, heads, share):
    peers, rows, wide = in_ref.shape[0], in_ref.shape[2], in_ref.shape[3]
    chans = wide // 2
    lane = jnp.zeros((rows, BLOCK), f32)
    for s in range(peers):
        for half in (0, 1):
            at = (half * peers + s) * chans
            value = in_ref[s, 0, :, half * chans : (half + 1) * chans].astype(f32)
            out_ref[:, at : at + chans] = value
            value = value * w_ref[:, at : at + chans].astype(f32)
            for j in range(chans // BLOCK):
                lane = lane + value[:, j * BLOCK : (j + 1) * BLOCK]
    third = [third_ref[s, 0].astype(f32) for s in range(peers)]
    bc = jnp.concatenate([t[:, heads : heads + share] for t in third], axis=1)
    dt = jnp.concatenate([t[:, :heads] for t in third], axis=1)
    out_bc_ref[...] = bc
    out_dt_ref[...] = dt
    total = jnp.sum(lane, axis=1, keepdims=True) + jnp.sum(bc * bc_ref[...].astype(f32), axis=1, keepdims=True)
    total = total + jnp.sum(dt * dt_ref[...].astype(f32), axis=1, keepdims=True)
    norm_ref[...] = total / gain_ref[...]


def laid_out(wide, third, w_zx, w_bc, w_dt, gain, heads):
    peers, widths, quarter, cols = wide.shape
    rows = widths * quarter
    steps = 2 * widths
    cut = rows // steps
    share = w_bc.shape[1] // peers
    by_rows = lambda a: pl.BlockSpec((cut, a.shape[1]), lambda i: (i, 0))
    by_piece = lambda a: pl.BlockSpec((peers, 1, cut, a.shape[3]), lambda i: (0, i // 2, i % 2, 0))
    shapes = [jax.ShapeDtypeStruct(a.shape, f32) for a in (w_zx, w_bc, w_dt, gain)]
    return pl.pallas_call(
        partial(laid_kernel, heads=heads, share=share),
        grid=(steps,),
        in_specs=[by_piece(wide), by_piece(third)] + [by_rows(a) for a in (w_zx, w_bc, w_dt, gain)],
        out_specs=[by_rows(a) for a in shapes],
        out_shape=shapes,
        compiler_params=pltpu.CompilerParams(vmem_limit_bytes=32 << 20),
        name="lay_out",
    )(wide, third, w_zx, w_bc, w_dt, gain)


def crossed(value, axis, mask):
    return lax.ppermute(value, axis, [(i, i ^ mask) for i in range(lax.axis_size(axis))])


def pick(value, index):
    return lax.dynamic_index_in_dim(value, index, 0, False)


def quarters_sent(value):
    widths, width = lax.axis_size("width"), lax.axis_index("width")
    value = value.reshape((widths, value.shape[0] // widths) + value.shape[1:])
    sent = [crossed(pick(value, jnp.bitwise_xor(width, m)), "width", m) for m in range(1, widths)]
    return [pick(value, width)] + sent


def quarters_back(total):
    widths = lax.axis_size("width")
    return [total] + [crossed(total, "width", m) for m in range(1, widths)]


def quarters_joined(pieces):
    width = lax.axis_index("width")
    stacked = jnp.stack(pieces)
    whole = jnp.stack([pick(stacked, jnp.bitwise_xor(width, j)) for j in range(len(pieces))])
    return whole.reshape((-1,) + whole.shape[2:]).astype(f32)


def packed_rows(rows, count):
    flat = jnp.stack(rows)
    return jnp.pad(flat, ((0, count - len(rows)), (0, 0)))


def heads_body(
    tokens, cotangent, starts, valid, norm_gain, w_zx, w_bc, w_dt, conv_w, conv_b, dt_bias, a_log, d_skip, gate_gain, w_out
):
    peers = lax.axis_size("seq")
    widths = lax.axis_size("width")
    place = lax.axis_index("seq")
    lanes = starts.shape[1]
    heads = H // peers
    chans = heads * HEAD_DIM
    own, model = tokens.shape
    rows = own * peers
    active = jnp.right_shift(jnp.int32(H), widths - 1 - lax.axis_index("width"))
    count = (active * HEAD_DIM).astype(f32)
    first = place * heads

    share = 2 * N // peers
    used = heads + share
    normed_own, bgrad_own, third_src, start_tile = entry(valid, starts, tokens, cotangent, norm_gain, w_bc, w_dt, peers)
    row_mask = (jnp.arange(BLOCK)[None, :] < valid[0][:, None]).astype(f32).reshape(-1, 1)
    taps_x = lax.dynamic_slice_in_dim(conv_w, first * HEAD_DIM, chans, 0).T
    of_chans = lambda a: lax.dynamic_slice_in_dim(a, first * HEAD_DIM, chans, 0)
    of_heads = lambda a: jnp.pad(lax.dynamic_slice_in_dim(a, first, heads, 0), (0, BLOCK - heads))
    head_on = (jnp.arange(BLOCK) < jnp.minimum(active - first, heads)).astype(f32)
    chan_on = (jnp.arange(chans) // HEAD_DIM < active - first).astype(f32)
    skip_x = jnp.repeat(lax.dynamic_slice_in_dim(d_skip, first, heads, 0), HEAD_DIM)
    chan = packed_rows([*taps_x, of_chans(conv_b), skip_x, of_chans(gate_gain), chan_on], SUB)
    bc_par = packed_rows([*conv_w[E:].T, conv_b[E:]], SUB)
    head = packed_rows([of_heads(dt_bias), of_heads(-jnp.exp(a_log)), head_on], SUB)
    spread = (jnp.arange(chans)[None, :] // HEAD_DIM == jnp.arange(BLOCK)[:, None]).astype(bf16)

    weights, normed, bgrad, starts_all, *computed = front(
        w_zx, third_src, w_bc, normed_own, bgrad_own, start_tile, chan, bc_par, head, spread, lanes, heads
    )
    weights = weights.reshape(model, -1)
    normed, bgrad = normed.reshape(rows, model), bgrad.reshape(rows, model)
    keep = 1.0 - starts_all[:, :lanes, 0]
    zx, conv, mix, bc, steps = [a.reshape(rows, a.shape[-1]) for a in computed[:5]]
    state, tail = computed[5:]
    mixed_grad, sums = run_grad(bgrad, w_out, zx, mix, chan, lanes)
    sums = summed_small(sums[:, :, :2, :].reshape(-1, BLOCK)).reshape(peers, lanes, 2, BLOCK)
    gate_rate = lax.rsqrt(sums[:, :, 0] / count + epsilon).reshape(rows, 1)
    gate_pull = gate_rate * gate_rate * gate_rate * sums[:, :, 1].reshape(rows, 1) / count
    scale = jnp.pad(jnp.concatenate([gate_rate, gate_pull], axis=1), ((0, 0), (0, SUB - 2)))
    mixed_low = lax.optimization_barrier(
        (mix * jax.nn.silu(zx[:, :chans]) * gate_rate * chan[GAIN]).astype(bf16)
    )
    branch = lax.psum_scatter(mm(mixed_low, w_out).astype(bf16), "seq", scatter_dimension=0, tiled=True).astype(f32)
    output = (tokens.astype(f32) + row_mask * branch).astype(bf16)
    out_part = mm(mixed_low, bgrad, TN).astype(bf16)
    scale, out_part = lax.optimization_barrier((scale, out_part))
    out_quarters = quarters_sent(out_part)

    dzx, dbc, dchan, dhead = run_backward(
        keep, zx, mixed_grad, chan, head, spread, conv, mix, bc, steps, state, tail, scale, lanes, heads
    )
    dzx, dbc, out_quarters = lax.optimization_barrier((dzx, dbc, out_quarters))
    out_pieces = quarters_back(sum(q.astype(f32) for q in out_quarters).astype(bf16))

    got = lax.all_to_all(dbc.reshape(peers, share, rows), "seq", 0, 0, tiled=True)
    of_share = lambda a: lax.dynamic_slice_in_dim(a, E + place * share, share, 0)
    share_par = jnp.pad(jnp.concatenate([of_share(conv_w), of_share(conv_b)[:, None]], axis=1), ((0, 0), (0, BLOCK - BIAS - 1)))
    over_time = lambda a: jnp.repeat(a.reshape(-1), BLOCK)
    keep_next = jnp.concatenate([keep[1:], jnp.zeros_like(keep[:1])], axis=0)
    third, dshare = bc_backward(
        got, zx, share_par, packed_rows([over_time(keep), over_time(keep_next)], SUB), dzx, heads, chans
    )

    at_heads = lambda a: lax.dynamic_update_slice_in_dim(jnp.zeros((H,), f32), a, first, 0)
    at_chans = lambda a: lax.dynamic_update_slice_in_dim(jnp.zeros((E,), f32), a, first * HEAD_DIM, 0)
    at_share = lambda a: lax.dynamic_update_slice_in_dim(jnp.zeros((2 * N,), f32), a, place * share, 0)
    skip = jnp.sum(dchan[SKIP].reshape(heads, HEAD_DIM), axis=1)
    small = [jnp.concatenate([at_chans(dchan[k]), at_share(dshare[:, k])]) for k in range(KCONV + 1)]
    small += [at_chans(dchan[GAIN]), at_heads(dhead[0, :heads]), at_heads(dhead[1, :heads]), at_heads(skip)]
    sizes = [a.shape[0] // peers for a in small]
    small = jnp.concatenate([a.reshape(peers, -1) for a in small], axis=1)
    per_row = -(-small.shape[1] // own)
    small = jnp.pad(small, ((0, 0), (0, own * per_row - small.shape[1]))).reshape(model, per_row)

    wide = mm(normed, dzx[:, : 2 * chans], TN).astype(bf16)
    wide, out_pieces = lax.optimization_barrier((wide, out_pieces))
    out_grad = quarters_joined(out_pieces)
    wide_third = jnp.concatenate(
        [mm(normed, third, TN)[:, :used], small, jnp.zeros((model, BLOCK - used - per_row), f32)], axis=1
    ).astype(bf16)
    part = mm(lax.dynamic_update_slice(dzx, third, (0, 2 * chans)), weights[:, : 2 * chans + BLOCK], NT).astype(bf16)
    by_owner = lambda a: a.reshape(peers, widths, own // widths, -1)
    part, output, out_grad = lax.optimization_barrier((part, output, out_grad))
    input_grad, wide, wide_third = scattered_out(
        part.reshape(peers, own, model), by_owner(wide), by_owner(wide_third), tokens, cotangent, norm_gain[None]
    )
    gain_rows = lax.dynamic_slice_in_dim(norm_gain, place * own, own, 0)[:, None]
    grad_zx, grad_bc, grad_dt, grad_norm = laid_out(wide, wide_third, w_zx, w_bc, w_dt, gain_rows, heads)
    grad_norm = grad_norm[:, 0]
    summed = jnp.sum(wide_third.reshape(peers, own, BLOCK)[:, :, used : used + per_row].astype(f32), axis=0).reshape(-1)
    pieces = [summed[sum(sizes[:i]) : sum(sizes[: i + 1])] for i in range(len(sizes))]
    grad_taps = jnp.stack(pieces[:KCONV], axis=1)
    grad_bias, grad_gain, grad_dtb, grad_alog, grad_skip = pieces[KCONV:]
    return (
        output, input_grad, grad_norm, grad_zx, grad_bc, grad_dt, grad_taps, grad_bias, grad_dtb, grad_alog, grad_skip,
        grad_gain, out_grad,
    )


def passed_along(array, axis, by):
    peers = lax.axis_size(axis)
    pairs = [(i, i + by) for i in range(peers) if 0 <= i + by < peers]
    return lax.ppermute(array, axis, pairs)


def carried_in(part, axis, combine, identity, reverse):
    count = lax.axis_size(axis)
    place = lax.axis_index(axis)
    at = count - 1 - place if reverse else place
    by = -1 if reverse else 1
    state = jax.tree.map(lambda a, e: jnp.zeros_like(a) + jnp.asarray(e, a.dtype), part, identity)

    def one(lap, state):
        sent = combine(state, part)
        got = jax.tree.map(lambda a: passed_along(a, axis, by), sent)
        return jax.tree.map(lambda old, new: jnp.where(at == lap + 1, new, old), state, got)

    return lax.fori_loop(0, count - 1, one, state)


def round_value(v):
    return lax.optimization_barrier(v.astype(jnp.bfloat16)).astype(jnp.float32)


def keep_round(v):
    return (round_value(v), None)


def pass_grad(kept, grad):
    return (grad,)


def same_value(v):
    return v


def keep_same(v):
    return (v, None)


def round_grad(kept, grad):
    return (round_value(grad),)


def low(v):
    wrapped = jax.custom_vjp(round_value)
    wrapped.defvjp(keep_round, pass_grad)
    return wrapped(v)


def low_back(v):
    wrapped = jax.custom_vjp(same_value)
    wrapped.defvjp(keep_same, round_grad)
    return wrapped(v)


def rms_front(x_rows, norm_gain):
    mean_square = jnp.mean(x_rows * x_rows, axis=-1, keepdims=True)
    return x_rows * lax.rsqrt(mean_square + epsilon) * norm_gain


def rim_of(zx_pre, bc_pre, chan_mask):
    return jnp.concatenate(
        [zx_pre[:, BLOCK - KCONV + 1 :, E:] * chan_mask, bc_pre[:, BLOCK - KCONV + 1 :, :]], axis=-1
    )


def piece_front(
    zx_pre,
    bc_pre,
    dt_raw,
    rim_rows,
    conv_w,
    conv_b,
    dt_bias,
    a_log,
    chan_mask,
    head_mask,
    keep_rows,
):
    z_gate = zx_pre[..., :E] * chan_mask
    pre_conv = jnp.concatenate([zx_pre[..., E:] * chan_mask, bc_pre], axis=-1)
    padded = jnp.concatenate([rim_rows * keep_rows[:, None, None], pre_conv], axis=1)
    conv_out = conv_b + padded[:, 0:BLOCK, :] * conv_w[:, 0]
    for offset in range(1, KCONV):
        conv_out = conv_out + padded[:, offset : offset + BLOCK, :] * conv_w[:, offset]
    active = jax.nn.silu(conv_out)
    x_conv = low(active[..., :E] * chan_mask)
    b_conv = low(active[..., E : E + N])
    c_conv = low(active[..., E + N :])
    dt_step = jax.nn.softplus(dt_raw + dt_bias) * head_mask
    log_step = -jnp.exp(a_log) * dt_step
    return (z_gate, x_conv, b_conv, c_conv, dt_step, log_step)


def block_state(x_conv, b_conv, dt_step, log_step):
    cumulative = jnp.cumsum(log_step, axis=1)
    to_end = jnp.exp(cumulative[:, -1:, :] - cumulative) * dt_step
    weighted = low(x_conv.reshape(x_conv.shape[0], BLOCK, H, HEAD_DIM) * to_end[..., None])
    state_sum = jnp.einsum("lqhp,lqn->lhpn", weighted, b_conv, precision=highest)
    return (state_sum, cumulative[:, -1, :])


def piece_mix(
    z_gate, x_conv, b_conv, c_conv, dt_step, log_step, state_in, d_skip, gate_gain, chan_count
):
    lane_count = x_conv.shape[0]
    cumulative = jnp.cumsum(log_step, axis=1)
    cum_heads = jnp.swapaxes(cumulative, 1, 2)
    causal = jnp.arange(BLOCK)[:, None] >= jnp.arange(BLOCK)[None, :]
    spread = cum_heads[:, :, :, None] - cum_heads[:, :, None, :]
    decays = jnp.where(causal, jnp.exp(jnp.where(causal, spread, 0.0)), 0.0)
    inner_cb = jnp.einsum("lqn,lsn->lqs", c_conv, b_conv, precision=highest)
    scores = low(inner_cb[:, None] * decays * jnp.swapaxes(dt_step, 1, 2)[:, :, None, :])
    x_heads = x_conv.reshape(lane_count, BLOCK, H, HEAD_DIM)
    within = jnp.einsum("lhqs,lshp->lqhp", scores, x_heads, precision=highest)
    carried = (
        jnp.einsum("lqn,lhpn->lqhp", c_conv, state_in, precision=highest)
        * jnp.exp(cumulative)[..., None]
    )
    mixed_sum = low_back(within + carried) + d_skip[:, None] * x_heads
    gated_rows = mixed_sum.reshape(lane_count, BLOCK, E) * jax.nn.silu(z_gate)
    mean_square = jnp.sum(gated_rows * gated_rows, axis=-1, keepdims=True) / chan_count
    return low(gated_rows * lax.rsqrt(mean_square + epsilon) * gate_gain)


def mix_lanes(lane_inputs, d_skip, gate_gain, chan_count):

    def one_lane(pieces):
        lane_gate, lane_xconv, lane_bconv, lane_cconv, lane_step, lane_decay, lane_state = pieces
        return piece_mix(
            lane_gate[None],
            lane_xconv[None],
            lane_bconv[None],
            lane_cconv[None],
            lane_step[None],
            lane_decay[None],
            lane_state[None],
            d_skip,
            gate_gain,
            chan_count,
        )[0]

    return lax.map(one_lane, lane_inputs)


def mix_back_lanes(lane_inputs, mixed_grad, d_skip, gate_gain, chan_count):

    def lane_mix(z_gate, x_conv, b_conv, c_conv, dt_step, log_step, state_in, skip_coef, gain_coef):
        return piece_mix(
            z_gate[None],
            x_conv[None],
            b_conv[None],
            c_conv[None],
            dt_step[None],
            log_step[None],
            state_in[None],
            skip_coef,
            gain_coef,
            chan_count,
        )[0]

    def one_lane(pieces):
        (
            lane_gate,
            lane_xconv,
            lane_bconv,
            lane_cconv,
            lane_step,
            lane_decay,
            lane_state,
            lane_grad,
        ) = pieces
        unused, pull_lane = jax.vjp(
            lane_mix,
            lane_gate,
            lane_xconv,
            lane_bconv,
            lane_cconv,
            lane_step,
            lane_decay,
            lane_state,
            d_skip,
            gate_gain,
        )
        return pull_lane(lane_grad)

    lane_grads = lax.map(one_lane, lane_inputs + (mixed_grad,))
    return (lane_grads[:7], jnp.sum(lane_grads[7], axis=0), jnp.sum(lane_grads[8], axis=0))


def chain_combine(earlier, latter):
    return (earlier[0] * latter[0], latter[0][:, :, None, None] * earlier[1] + latter[1])


def share_out(out_grad):
    return lax.psum_scatter(out_grad, "seq", scatter_dimension=0, tiled=True)


def contract_rows(left, right):
    return lax.dot_general(
        left, right, (((0,), (0,)), ((), ())), preferred_element_type=jnp.float32
    )


def contract_cols(left, right):
    return lax.dot_general(
        left, right, (((1,), (1,)), ((), ())), preferred_element_type=jnp.float32
    )


def rows_body(
    tokens,
    cotangent,
    starts,
    valid,
    norm_gain,
    w_zx,
    w_bc,
    w_dt,
    conv_w,
    conv_b,
    dt_bias,
    a_log,
    d_skip,
    gate_gain,
    w_out,
):
    lane_count = starts.shape[1]
    width_index = lax.axis_index("width")
    shift_bits = lax.axis_size("width") - 1 - width_index
    active_heads = jnp.right_shift(jnp.int32(H), shift_bits)
    chan_mask = (jnp.arange(E) // HEAD_DIM < active_heads).astype(jnp.float32)
    head_mask = (jnp.arange(H) < active_heads).astype(jnp.float32)
    chan_count = (active_heads * HEAD_DIM).astype(jnp.float32)
    keep_rows = 1.0 - starts[0].astype(jnp.float32)
    row_mask = (jnp.arange(BLOCK)[None, :] < valid[0][:, None]).astype(jnp.float32).reshape(-1, 1)
    x_rows = tokens.astype(jnp.float32)
    normed, norm_back = jax.vjp(rms_front, x_rows, norm_gain)
    normed_low = normed.astype(jnp.bfloat16)
    zx_full, bc_full, dt_full, out_full = (
        lax.all_gather(w_zx, "seq", axis=0, tiled=True),
        lax.all_gather(w_bc, "seq", axis=0, tiled=True),
        lax.all_gather(w_dt, "seq", axis=0, tiled=True),
        lax.all_gather(w_out, "seq", axis=0, tiled=True),
    )
    zx_pre = jnp.dot(normed_low, zx_full, preferred_element_type=jnp.float32).reshape(
        lane_count, BLOCK, 2 * E
    )
    bc_pre = jnp.dot(normed_low, bc_full, preferred_element_type=jnp.float32).reshape(
        lane_count, BLOCK, 2 * N
    )
    dt_raw = jnp.dot(normed_low, dt_full, preferred_element_type=jnp.float32).reshape(
        lane_count, BLOCK, H
    )
    rim_rows = passed_along(rim_of(zx_pre, bc_pre, chan_mask), "seq", 1)
    front_fn = partial(piece_front, chan_mask=chan_mask, head_mask=head_mask, keep_rows=keep_rows)
    front_out, front_back = jax.vjp(
        front_fn, zx_pre, bc_pre, dt_raw, rim_rows, conv_w, conv_b, dt_bias, a_log
    )
    z_gate, x_conv, b_conv, c_conv, dt_step, log_step = front_out
    (state_sum, log_total), state_back = jax.vjp(block_state, x_conv, b_conv, dt_step, log_step)
    carry_rate = jnp.exp(log_total) * keep_rows[:, None]
    identity = (jnp.ones_like(carry_rate), jnp.zeros_like(state_sum))
    prefix_pair = carried_in((carry_rate, state_sum), "seq", chain_combine, identity, False)
    state_in = prefix_pair[1] * keep_rows[:, None, None, None]
    lane_inputs = (z_gate, x_conv, b_conv, c_conv, dt_step, log_step, state_in)
    mixed_low = mix_lanes(lane_inputs, d_skip, gate_gain, chan_count)
    mixed_flat = mixed_low.reshape(-1, E).astype(jnp.bfloat16)
    branch = jnp.dot(mixed_flat, out_full, preferred_element_type=jnp.float32)
    output = (x_rows + row_mask * branch).astype(jnp.bfloat16)
    cot_rows = cotangent.astype(jnp.float32)
    branch_grad = (cot_rows * row_mask).astype(jnp.bfloat16)
    out_grad = contract_rows(mixed_flat, branch_grad)
    mixed_grad = contract_cols(branch_grad, out_full).reshape(lane_count, BLOCK, E)
    lane_grads, grad_skip, grad_gain = mix_back_lanes(
        lane_inputs, mixed_grad, d_skip, gate_gain, chan_count
    )
    grad_gate, grad_x, grad_b, grad_c, grad_dt, grad_log, grad_state = lane_grads
    later_pair = carried_in(
        (carry_rate, grad_state * keep_rows[:, None, None, None]),
        "seq",
        chain_combine,
        identity,
        True,
    )
    later_grad = later_pair[1]
    grad_total = jnp.exp(log_total) * jnp.sum(later_grad * state_in, axis=(2, 3))
    grad_x_more, grad_b_more, grad_dt_more, grad_log_more = state_back((later_grad, grad_total))
    grad_zx, grad_bc, grad_dtraw, grad_rim, grad_convw, grad_convb, grad_dtbias, grad_alog = (
        front_back(
            (
                grad_gate,
                grad_x + grad_x_more,
                grad_b + grad_b_more,
                grad_c,
                grad_dt + grad_dt_more,
                grad_log + grad_log_more,
            )
        )
    )
    rim_grad = passed_along(grad_rim.astype(jnp.bfloat16), "seq", -1).astype(grad_rim.dtype)
    grad_zx = grad_zx.at[:, BLOCK - KCONV + 1 :, E:].add(rim_grad[..., :E] * chan_mask)
    grad_bc = grad_bc.at[:, BLOCK - KCONV + 1 :, :].add(rim_grad[..., E:])
    zx_low = grad_zx.reshape(-1, 2 * E).astype(jnp.bfloat16)
    bc_low = grad_bc.reshape(-1, 2 * N).astype(jnp.bfloat16)
    dt_low = grad_dtraw.reshape(-1, H).astype(jnp.bfloat16)
    zx_weight_grad = contract_rows(normed_low, zx_low)
    bc_weight_grad = contract_rows(normed_low, bc_low)
    dt_weight_grad = contract_rows(normed_low, dt_low)
    normed_grad = (
        contract_cols(zx_low, zx_full)
        + contract_cols(bc_low, bc_full)
        + contract_cols(dt_low, dt_full)
    )
    grad_x_rows, grad_norm = norm_back(normed_grad)
    input_grad = cot_rows + grad_x_rows
    out_shard = share_out(out_grad)
    row_shards = (
        lax.psum_scatter(grad_norm, "seq", scatter_dimension=0, tiled=True),
        lax.psum_scatter(zx_weight_grad, "seq", scatter_dimension=0, tiled=True),
        lax.psum_scatter(bc_weight_grad, "seq", scatter_dimension=0, tiled=True),
        lax.psum_scatter(dt_weight_grad, "seq", scatter_dimension=0, tiled=True),
        lax.psum_scatter(grad_convw, "seq", scatter_dimension=0, tiled=True),
        lax.psum_scatter(grad_convb, "seq", scatter_dimension=0, tiled=True),
        lax.psum_scatter(grad_dtbias, "seq", scatter_dimension=0, tiled=True),
        lax.psum_scatter(grad_alog, "seq", scatter_dimension=0, tiled=True),
        lax.psum_scatter(grad_skip, "seq", scatter_dimension=0, tiled=True),
        lax.psum_scatter(grad_gain, "seq", scatter_dimension=0, tiled=True),
    )
    summed = lax.psum(
        (
            row_shards[0],
            row_shards[1],
            row_shards[2],
            row_shards[3],
            row_shards[4],
            row_shards[5],
            row_shards[6],
            row_shards[7],
            row_shards[8],
            row_shards[9],
            out_shard,
        ),
        "width",
    )
    return (
        output,
        input_grad,
        summed[0],
        summed[1],
        summed[2],
        summed[3],
        summed[4],
        summed[5],
        summed[6],
        summed[7],
        summed[8],
        summed[9],
        summed[10],
    )


def solution(mesh):
    in_specs = (
        P(("width", "seq"), None),
        P(("width", "seq"), None),
        P(("width", "seq"), None),
        P(("width", "seq"), None),
        P(),
        P("seq", None),
        P("seq", None),
        P("seq", None),
        P(),
        P(),
        P(),
        P(),
        P(),
        P(),
        P("seq", None),
    )
    out_specs = (
        P(("width", "seq"), None),
        P(("width", "seq"), None),
        P("seq"),
        P("seq", None),
        P("seq", None),
        P("seq", None),
        P("seq", None),
        P("seq"),
        P("seq"),
        P("seq"),
        P("seq"),
        P("seq"),
        P("seq", None),
    )
    body = heads_body if H % (2 * mesh.shape["seq"]) == 0 else rows_body
    return jax.shard_map(body, mesh=mesh, in_specs=in_specs, out_specs=out_specs, check_vma=False)
```

```python
from functools import partial

import jax
import jax.numpy as jnp
from jax import lax
from jax.experimental import pallas as pl
from jax.experimental.pallas import tpu as pltpu
from jax.sharding import PartitionSpec as P
import numpy as np

H = 64
HEAD_DIM = 64
N = 128
KCONV = 4
BLOCK = 128
E = 4096
SUB = 8

epsilon = 1e-05
highest = lax.Precision.HIGHEST
f32 = jnp.float32
bf16 = jnp.bfloat16

NN = ((1,), (0,))
NT = ((1,), (1,))
TN = ((0,), (0,))


def mm(left, right, dims=NN, precision=None):
    return lax.dot_general(left, right, (dims, ((), ())), precision=precision, preferred_element_type=f32)


def split2(value):
    high = value.astype(bf16)
    return high, (value - high.astype(f32)).astype(bf16)


def mm_right(left, right, dims=NN):
    high, low = split2(right)
    return mm(left, high, dims) + mm(left, low, dims)


def mm_left(left, right, dims=NN):
    high, low = split2(left)
    return mm(high, right, dims) + mm(low, right, dims)


def softplus(v):
    small = jnp.exp(-jnp.abs(v))
    log1p = jnp.where(small < 1e-4, small - 0.5 * small * small, jnp.log(1.0 + small))
    return jnp.maximum(v, 0.0) + log1p


def sigmoid(v):
    return 1.0 / (1.0 + jnp.exp(-v))


def grids():
    row = lax.broadcasted_iota(jnp.int32, (BLOCK, BLOCK), 0)
    col = lax.broadcasted_iota(jnp.int32, (BLOCK, BLOCK), 1)
    return row, col


def halves(pair, lane):
    zero = jnp.zeros_like(pair)
    return jnp.where(lane < HEAD_DIM, pair, zero), jnp.where(lane < HEAD_DIM, zero, pair)


def decay_of(cum, cum_t, head, causal):
    return jnp.exp(jnp.where(causal, cum[:, head : head + 1] - cum_t[head : head + 1, :], -1e30))


TAP, BIAS, SKIP, GAIN, MASK = 0, 4, 5, 6, 7
DT_BIAS, NEG_A, HEAD_MASK = 0, 1, 2


def forward_block(
    keep_row, zx_ref, chan_ref, bc_par_ref, head_ref, spread,
    conv_ref, mix_ref, bc_ref, step_ref, state_ref, tail_ref,
    state, tail_x, tail_b, pad_x, pad_b,
    *, lane, heads,
):
    width = heads * HEAD_DIM
    row, col = grids()
    causal = row >= col
    tril = causal.astype(f32)
    rows = pl.ds(lane * BLOCK, BLOCK)
    keep = jnp.concatenate([keep_row] * (width // BLOCK), axis=1)
    keep_b = jnp.concatenate([keep_row] * (2 * N // BLOCK), axis=1)

    pre = zx_ref[rows, width : 2 * width]
    before = tail_x[lane] * keep
    pad_x[lane, 0:SUB] = before
    pad_x[lane, SUB:] = pre
    tail_ref[lane] = before
    tail_x[lane] = pre[BLOCK - SUB :, :]
    conv = chan_ref[BIAS : BIAS + 1, :]
    for k in range(KCONV):
        conv = conv + pad_x[lane, SUB - KCONV + 1 + k : SUB - KCONV + 1 + k + BLOCK, :] * chan_ref[k : k + 1, :]
    conv_ref[rows, :] = conv
    x_low = (conv * sigmoid(conv) * chan_ref[MASK : MASK + 1, :]).astype(bf16)

    pre_b = zx_ref[rows, 2 * width + BLOCK :]
    pad_b[lane, 0:SUB] = tail_b[lane] * keep_b
    pad_b[lane, SUB:] = pre_b
    tail_b[lane] = pre_b[BLOCK - SUB :, :]
    conv_b = bc_par_ref[BIAS : BIAS + 1, :]
    for k in range(KCONV):
        conv_b = conv_b + pad_b[lane, SUB - KCONV + 1 + k : SUB - KCONV + 1 + k + BLOCK, :] * bc_par_ref[k : k + 1, :]
    bc_low = (conv_b * sigmoid(conv_b)).astype(bf16)
    bc_ref[rows, :] = bc_low
    b_low, c_low = bc_low[:, :N], bc_low[:, N:]

    raw = zx_ref[rows, 2 * width : 2 * width + BLOCK] + head_ref[DT_BIAS : DT_BIAS + 1, :]
    dt = softplus(raw) * head_ref[HEAD_MASK : HEAD_MASK + 1, :]
    cum = mm(tril, head_ref[NEG_A : NEG_A + 1, :] * dt, precision=highest)
    step_ref[rows, :BLOCK] = cum
    step_ref[rows, BLOCK:] = dt
    cum_t, dt_t = cum.T, dt.T
    last = cum[BLOCK - 1 :, :]
    carry_x = mm_left(jnp.exp(cum), spread)
    end_x = mm_left(jnp.exp(last - cum) * dt, spread)
    last_x = carry_x[BLOCK - 1 :, :]

    inner = mm(c_low, b_low, NT)
    parts = []
    for j in range(heads // 2):
        pair = x_low[:, 2 * HEAD_DIM * j : 2 * HEAD_DIM * (j + 1)]
        scores = [
            (inner * decay_of(cum, cum_t, h, causal) * dt_t[h : h + 1, :]).astype(bf16)
            for h in (2 * j, 2 * j + 1)
        ]
        parts.append(mm(jnp.concatenate(scores, axis=1), jnp.concatenate(halves(pair, col), axis=0)))
    within = jnp.concatenate(parts, axis=1)

    state_in = state[lane] * keep
    state_ref[lane] = state_in
    carried = mm_right(c_low, state_in) * carry_x
    x_f = x_low.astype(f32)
    mix_ref[rows, :] = within + carried + chan_ref[SKIP : SKIP + 1, :] * x_f
    weighted = (x_f * end_x).astype(bf16)
    state[lane] = last_x * state_in + mm(b_low, weighted, TN)


def backward_kernel(
    keep_ref, zx_ref, grad_ref, chan_ref, head_ref, spread_ref,
    conv_ref, mix_ref, bc_ref, step_ref, state_ref, tail_ref, scale_ref,
    dzx_ref, dbc_ref, dchan_ref, dhead_ref,
    state_grad, next_conv, pad_x, pad_d,
    *, lanes, heads, blocks,
):
    lap = pl.program_id(0)
    c = blocks - 1 - lap
    width = heads * HEAD_DIM
    row, col = grids()
    causal = row >= col
    triu = (col >= row).astype(f32)
    spread = spread_ref[...]

    @pl.when(lap == 0)
    def _():
        state_grad[...] = jnp.zeros_like(state_grad)
        next_conv[...] = jnp.zeros_like(next_conv)
        dchan_ref[...] = jnp.zeros_like(dchan_ref)
        dhead_ref[...] = jnp.zeros_like(dhead_ref)

    def total(value):
        return jnp.sum(value, axis=0, keepdims=True)

    for lane in range(lanes):
        rows = pl.ds(lane * BLOCK, BLOCK)
        keep = keep_ref[c, lane]
        z = zx_ref[rows, :width]
        conv = conv_ref[rows, :]
        mixed = mix_ref[rows, :]
        grad = grad_ref[rows, :]
        gain = chan_ref[GAIN : GAIN + 1, :]
        skip = chan_ref[SKIP : SKIP + 1, :]
        rate = scale_ref[rows, 0:1]
        pull = scale_ref[rows, 1:2]
        gate = sigmoid(z)
        silu = z * gate
        gated = mixed * silu
        dgated = grad * gain * rate - gated * pull
        dzx_ref[rows, :width] = (dgated * mixed * (gate * (1.0 + z * (1.0 - gate)))).astype(bf16)
        dmixed = dgated * silu
        act = sigmoid(conv)
        x_low = (conv * act * chan_ref[MASK : MASK + 1, :]).astype(bf16)
        x_f = x_low.astype(f32)
        dchan_ref[GAIN : GAIN + 1, :] += total(grad * gated * rate)
        dchan_ref[SKIP : SKIP + 1, :] += total(dmixed * x_f)
        dlow = dmixed.astype(bf16)
        dlow_f = dlow.astype(f32)

        b_low, c_low = bc_ref[rows, :N], bc_ref[rows, N:]
        cum, dt = step_ref[rows, :BLOCK], step_ref[rows, BLOCK:]
        cum_t, dt_t = cum.T, dt.T
        last = cum[BLOCK - 1 :, :]
        to_last = jnp.exp(last - cum)
        carry_x = mm_left(jnp.exp(cum), spread)
        end_x = mm_left(to_last * dt, spread)
        last_x = carry_x[BLOCK - 1 :, :]

        inner = mm(c_low, b_low, NT)
        dinner = jnp.zeros((BLOCK, BLOCK), f32)
        parts, dt_rows = [], []
        for j in range(heads // 2):
            lanes_j = slice(2 * HEAD_DIM * j, 2 * HEAD_DIM * (j + 1))
            pair, dpair = x_low[:, lanes_j], dlow[:, lanes_j]
            dstack = jnp.concatenate(halves(dpair, col), axis=0)
            dscores = mm(dstack, pair, NT)
            scores = []
            for i, h in enumerate((2 * j, 2 * j + 1)):
                decay = decay_of(cum, cum_t, h, causal)
                step = dt_t[h : h + 1, :]
                scores.append((inner * decay * step).astype(bf16))
                part = dscores[i * BLOCK : (i + 1) * BLOCK] * decay
                dinner = dinner + part * step
                dt_rows.append(total(part * inner))
            parts.append(mm(jnp.concatenate(scores, axis=0), dstack, TN))
        dx_within = jnp.concatenate(parts, axis=1)
        dt_rows.append(jnp.zeros((BLOCK - heads, BLOCK), f32))
        ddt_within = jnp.concatenate(dt_rows, axis=0).T

        state_in = state_ref[0, lane]
        sgrad = state_grad[lane]
        in_high, in_low = split2(state_in)
        sg_high, sg_low = split2(sgrad)
        dcarry = dlow_f * carry_x
        dc_high, dc_low = split2(dcarry)
        di_high, di_low = split2(dinner)
        dc = mm(dc_high, in_high, NT) + mm(dc_high, in_low, NT) + mm(dc_low, in_high, NT)
        dc = dc + mm(di_high, b_low) + mm(di_low, b_low)
        weighted = (x_f * end_x).astype(bf16)
        db = mm(weighted, sg_high, NT) + mm(weighted, sg_low, NT)
        db = db + mm(di_high, c_low, TN) + mm(di_low, c_low, TN)
        dbc_ref[:N, rows] = db.T.astype(bf16)
        dbc_ref[N:, rows] = dc.T.astype(bf16)
        dweighted = mm(b_low, sg_high) + mm(b_low, sg_low)
        dx = dx_within + dweighted * end_x
        dcum = mm_left(dlow_f * (mixed - skip * x_f) - x_f * dx, spread, NT)
        dend = mm_left(dweighted * x_f, spread, NT)
        touch = jnp.broadcast_to(total(sgrad * state_in), (SUB, width))
        dlast = total(dend * to_last * dt) + jnp.exp(last) * mm_left(touch, spread, NT)[0:1]
        dlog = mm(triu, dcum, precision=highest) + dlast
        neg_a = head_ref[NEG_A : NEG_A + 1, :]
        ddt = ddt_within + dend * to_last + dlog * neg_a
        raw = zx_ref[rows, 2 * width : 2 * width + BLOCK] + head_ref[DT_BIAS : DT_BIAS + 1, :]
        draw = ddt * sigmoid(raw) * head_ref[HEAD_MASK : HEAD_MASK + 1, :]
        dzx_ref[rows, 2 * width :] = draw.astype(bf16)
        dhead_ref[0:1, :] += total(draw)
        dhead_ref[1:2, :] += total(dlog * neg_a * dt)
        state_grad[lane] = keep * (mm(c_low, dc_high, TN) + mm(c_low, dc_low, TN) + last_x * sgrad)

        dx = dx + skip * dmixed
        dconv = dx * chan_ref[MASK : MASK + 1, :] * (act * (1.0 + conv * (1.0 - act)))
        pad_d[lane, :BLOCK] = dconv
        pad_d[lane, BLOCK:] = next_conv[lane]
        next_conv[lane] = dconv[:SUB] * keep
        pad_x[lane, :SUB] = tail_ref[0, lane]
        pad_x[lane, SUB:] = zx_ref[rows, width : 2 * width]
        dpre = jnp.zeros((BLOCK, width), f32)
        for k in range(KCONV):
            dpre = dpre + pad_d[lane, KCONV - 1 - k : KCONV - 1 - k + BLOCK, :] * chan_ref[k : k + 1, :]
            dchan_ref[k : k + 1, :] += total(dconv * pad_x[lane, SUB - KCONV + 1 + k : SUB - KCONV + 1 + k + BLOCK, :])
        dchan_ref[BIAS : BIAS + 1, :] += total(dconv)
        dzx_ref[rows, width : 2 * width] = dpre.astype(bf16)


def run_backward(keep, zx, grad, chan, head, spread, conv, mix, bc, step_arr, state, tail, scale, lanes, heads):
    rows, width = grad.shape
    step = lanes * BLOCK
    blocks = rows // step
    by_block = lambda cols: pl.BlockSpec((step, cols), lambda c: (blocks - 1 - c, 0))
    whole = lambda a: pl.BlockSpec(a.shape, lambda c: (0,) * a.ndim)
    fixed = lambda shape: pl.BlockSpec(shape, lambda c: (0,) * len(shape))
    per_lane = lambda r, cols: pl.BlockSpec((1, lanes, r, cols), lambda c: (blocks - 1 - c, 0, 0, 0))
    return pl.pallas_call(
        partial(backward_kernel, lanes=lanes, heads=heads, blocks=blocks),
        grid=(blocks,),
        in_specs=[
            pl.BlockSpec(memory_space=pltpu.SMEM), by_block(2 * width + BLOCK), by_block(width),
            whole(chan), whole(head), whole(spread),
            by_block(width), by_block(width), by_block(2 * N), by_block(2 * BLOCK),
            per_lane(N, width), per_lane(SUB, width), by_block(BLOCK),
        ],
        out_specs=[
            by_block(2 * width + BLOCK), pl.BlockSpec((2 * N, step), lambda c: (0, blocks - 1 - c)),
            fixed((SUB, width)), fixed((SUB, BLOCK)),
        ],
        out_shape=[
            jax.ShapeDtypeStruct((rows, 2 * width + BLOCK), bf16),
            jax.ShapeDtypeStruct((2 * N, rows), bf16), jax.ShapeDtypeStruct((SUB, width), f32),
            jax.ShapeDtypeStruct((SUB, BLOCK), f32),
        ],
        scratch_shapes=[
            pltpu.VMEM((lanes, N, width), f32), pltpu.VMEM((lanes, SUB, width), f32),
            pltpu.VMEM((lanes, BLOCK + SUB, width), f32), pltpu.VMEM((lanes, BLOCK + SUB, width), f32),
        ],
        compiler_params=pltpu.CompilerParams(vmem_limit_bytes=48 << 20, dimension_semantics=("arbitrary",)),
        cost_estimate=pl.CostEstimate(flops=rows * width * 6144, bytes_accessed=rows * width * 40, transcendentals=rows * width * 6),
        name="mix_backward",
    )(keep, zx, grad, chan, head, spread, conv, mix, bc, step_arr, state, tail, scale)


MESH = pl.DeviceIdType.MESH


def greet(others):
    for other in others:
        pl.semaphore_signal(pltpu.get_barrier_semaphore(), inc=1, device_id=other, device_id_type=MESH)


def met(others):
    pl.semaphore_wait(pltpu.get_barrier_semaphore(), len(others))


def remote(src, dst, send, recv, device):
    return pltpu.make_async_remote_copy(
        src_ref=src, dst_ref=dst, send_sem=send, recv_sem=recv, device_id=device, device_id_type=MESH
    )


class Rows:
    def __init__(self, own_ref, all_ref, sems, peers):
        self.own, self.all, self.sems, self.peers = own_ref, all_ref, sems, peers
        self.width, self.place = lax.axis_index("width"), lax.axis_index("seq")
        self.chips, self.chip = peers // 2, self.place // 2

    def hop(self, ref, s, step, by):
        send, recv = self.sems[0 if by > 0 else 2], self.sems[1 if by > 0 else 3]
        device = (self.width, jnp.clip(self.place + 2 * by, 0, self.peers - 1))
        return remote(ref, self.all.at[s], send.at[step], recv.at[step], device)

    def over(self, ref, s, slot):
        device = (self.width, jnp.bitwise_xor(self.place, 1))
        return remote(ref, self.all.at[s], self.sems[4].at[slot], self.sems[5].at[slot], device)

    def inside(self, by):
        return self.chip + 1 < self.chips if by > 0 else self.chip > 0

    def reached(self, by, step):
        return self.chip >= step if by > 0 else self.chip + step < self.chips

    def source(self, by, step):
        return jnp.clip(self.place - 2 * by * step, 0, self.peers - 1)

    def keep(self):
        return pltpu.make_async_copy(self.own, self.all.at[self.place], self.sems[6])

    def start(self):
        self.keep().start()
        for by in (1, -1):
            @pl.when(self.inside(by))
            def _():
                self.hop(self.own, self.place, 0, by).start()
        self.over(self.own, self.place, 0).start()

    def pass_on(self, step):
        for by in (1, -1):
            @pl.when(self.reached(by, step))
            def _():
                s = self.source(by, step)
                ref = self.all.at[s]
                self.hop(ref, s, step - 1, by).wait_recv()

                @pl.when(self.inside(by))
                def _():
                    self.hop(ref, s, step, by).start()
                self.over(ref, s, 2 * step - (by > 0)).start()

    def mate(self, by, step):
        if not step:
            return self.over(self.own, self.place, 0)
        s = self.source(by, step)
        return self.over(self.all.at[s], s, 2 * step - (by > 0))

    def arrived(self):
        self.keep().wait()
        self.mate(1, 0).wait_recv()
        for step in range(1, self.chips):
            for by in (1, -1):
                @pl.when(self.reached(by, step))
                def _():
                    self.mate(by, step).wait_recv()

    def sent(self):
        for step in range(self.chips):
            for by in (1, -1):
                @pl.when(self.inside(by) & self.reached(by, step))
                def _():
                    s = self.source(by, step)
                    self.hop(self.all.at[s], s, step, by).wait_send()
        self.mate(1, 0).wait_send()
        for step in range(1, self.chips):
            for by in (1, -1):
                @pl.when(self.reached(by, step))
                def _():
                    self.mate(by, step).wait_send()


ROW_SEMS = 7


def row_sems(chips):
    dma = pltpu.SemaphoreType.DMA
    return [dma((chips,)), dma((chips,)), dma((chips,)), dma((chips,)), dma((2 * chips,)), dma((2 * chips,)), dma(())]


def front_kernel(
    valid_ref, start_ref, x_ref, cot_ref, norm_gain_ref, bc_ref, dt_ref, taps_ref, bias_ref, dtb_ref, alog_ref, skip_ref,
    gain_ref, spread_ref, zx_ref, wout_ref,
    w_ref, rows_ref, grads_ref, starts_ref, chan_ref, head_ref,
    out_zx, out_mix, out_grad, out_scale, out_low, out_part, out_conv, out_bc, out_step, out_state, out_tail,
    w_v, rows_v, starts_v, wout_v, own_v, grad_v, third_v, start_v, bc_par,
    zx_v, mix_v, mgrad_v, scale_v, low_v, conv_v, bc_v, step_v, state_v, tail_v, sums, sums_got,
    state, tail_x, tail_b, pad_x, pad_b,
    w_send, w_recv, st_send, st_recv, own_sem, wide_send, wide_recv, in_sem, out_sem, slot_sem, sum_send, sum_recv, *sems,
    peers, widths, lanes, heads,
):
    width, place = lax.axis_index("width"), lax.axis_index("seq")
    chips = peers // 2
    chans = heads * HEAD_DIM
    quarter = zx_ref.shape[0] // widths
    ring = [lax.rem(place + by, peers) for by in range(1, peers)]
    cross = [jnp.bitwise_xor(width, m) for m in range(1, widths)]
    others = [(width, s) for s in ring] + [(w, place) for w in cross]
    greet(others)

    x = x_ref[...].astype(f32)
    own_v[...] = (x * lax.rsqrt(jnp.mean(x * x, axis=-1, keepdims=True) + epsilon) * norm_gain_ref[...]).astype(bf16)
    row = lax.broadcasted_iota(jnp.int32, (BLOCK, 1), 0)
    sub = lax.broadcasted_iota(jnp.int32, (SUB, BLOCK), 0)
    tile = jnp.zeros((SUB, BLOCK), f32)
    for lane in range(lanes):
        at = slice(lane * BLOCK, (lane + 1) * BLOCK)
        mask = (row < valid_ref[0, lane]).astype(f32)
        grad_v[at, :] = (cot_ref[at, :].astype(f32) * mask).astype(bf16)
        tile = jnp.where(sub == lane, start_ref[0, lane].astype(f32), tile)
    start_v[...] = tile
    bc, dt = bc_ref[...].astype(f32), dt_ref[...].astype(f32)
    share = bc.shape[1] // peers
    rest = jnp.zeros((bc.shape[0], BLOCK - share - heads), f32)
    for s in range(peers):
        columns = [dt[:, s * heads : (s + 1) * heads], bc[:, s * share : (s + 1) * share], rest]
        third_v[s] = jnp.concatenate(columns, axis=1).astype(bf16)
    met(others)

    mine = pl.ds(pl.multiple_of(width * quarter, quarter), quarter)
    rows = Rows(own_v, rows_ref, sems[:ROW_SEMS], peers)
    grads = Rows(grad_v, grads_ref, sems[ROW_SEMS:], peers)

    def columns_of(half, s):
        return pl.ds(pl.multiple_of(half * peers * chans + s * chans, 128), chans)

    wide = 2 * chans
    spots = [pl.ds(0, chans), pl.ds(chans, chans), pl.ds(wide, BLOCK), pl.ds(wide + BLOCK, 2 * N)]

    def parts(s):
        return [zx_ref.at[mine, columns_of(0, s)], zx_ref.at[mine, columns_of(1, s)], third_v.at[s, mine], bc_ref.at[mine]]

    pushes = []
    for i, s in enumerate(ring):
        for k, (part, spot) in enumerate(zip(parts(s), spots)):
            pushes.append(remote(part, w_ref.at[place, width, :, spot], w_send.at[k, i], w_recv.at[k, i], (width, s)))
        pushes.append(remote(start_v, starts_ref.at[place], st_send.at[i], st_recv.at[i], (width, s)))
    for push in pushes:
        push.start()
    keeps = [
        pltpu.make_async_copy(part, w_ref.at[place, width, :, spot], own_sem.at[k])
        for k, (part, spot) in enumerate(zip(parts(place), spots))
    ]
    keeps.append(pltpu.make_async_copy(start_v, starts_ref.at[place], own_sem.at[4]))
    for keep in keeps:
        keep.start()
    rows.start()

    active = jnp.right_shift(jnp.int32(H), widths - 1 - width)
    first = place * heads
    here = columns_of(0, place)
    spread = spread_ref[...]
    pick_row = lax.broadcasted_iota(jnp.int32, (H, BLOCK), 0)
    pick_lane = lax.broadcasted_iota(jnp.int32, (H, BLOCK), 1)
    chosen = ((pick_row == pick_lane + first) & (pick_lane < heads)).astype(f32)
    per_head = jnp.concatenate(
        [dtb_ref[...], -jnp.exp(alog_ref[...]), jnp.ones((1, H), f32), skip_ref[...], jnp.zeros((SUB - 4, H), f32)], axis=0
    )
    per_head = mm(per_head, chosen, precision=highest)
    head_lane = lax.broadcasted_iota(jnp.int32, (SUB, BLOCK), 1)
    head_ref[...] = jnp.where((sub == HEAD_MASK) & (head_lane + first >= active), 0.0, per_head)
    on_chans = mm(head_ref[...], spread.astype(f32), precision=highest)
    chan_ref[...] = jnp.concatenate(
        [taps_ref[:, here], bias_ref[:, here], on_chans[3:4], gain_ref[:, here], on_chans[HEAD_MASK : HEAD_MASK + 1]], axis=0
    )
    bc_par[...] = jnp.concatenate(
        [taps_ref[:, E:], bias_ref[:, E:], jnp.zeros((SUB - KCONV - 1, 2 * N), f32)], axis=0
    )

    for push in pushes:
        push.wait_recv()
    for keep in keeps:
        keep.wait()
    shares = [
        remote(w_ref.at[:, width], w_ref.at[:, width], wide_send.at[m], wide_recv.at[m], (w, place)) for m, w in enumerate(cross)
    ]
    for copy in shares:
        copy.start()
    for step in range(1, chips - 1):
        rows.pass_on(step)
    grads.start()
    for copy in shares:
        copy.wait_recv()
    in_w = pltpu.make_async_copy(w_ref, w_v, own_sem.at[0])
    in_starts = pltpu.make_async_copy(starts_ref, starts_v, own_sem.at[1])
    in_wout = pltpu.make_async_copy(wout_ref, wout_v, own_sem.at[2])
    for copy in (in_w, in_starts, in_wout):
        copy.start()
    rows.pass_on(chips - 1)
    rows.arrived()

    def load(src, s):
        return pltpu.make_async_copy(src.at[s], rows_v.at[s], in_sem.at[s])

    for c in range(peers):
        load(rows_ref, c).start()
    for array in (state, tail_x, tail_b):
        array[...] = jnp.zeros_like(array)
    for copy in (in_w, in_starts, in_wout):
        copy.wait()

    def out_copy(k, src, dst, c):
        return pltpu.make_async_copy(src.at[c], dst.at[c], out_sem.at[k, c])

    slots = [(conv_v, out_conv), (bc_v, out_bc), (step_v, out_step), (state_v, out_state), (tail_v, out_tail)]

    def slot_copies(c):
        slot = lax.rem(c, 2)
        return [pltpu.make_async_copy(src.at[slot], dst.at[c], slot_sem.at[k, slot]) for k, (src, dst) in enumerate(slots)]

    def compute(begin, end):
        @pl.loop(begin, end)
        def _(c):
            load(rows_ref, c).wait()

            @pl.when(c >= 2)
            def _():
                for copy in slot_copies(c - 2):
                    copy.wait()
            weights = w_v[...].reshape(w_v.shape[0] * w_v.shape[1] * w_v.shape[2], w_v.shape[3])
            zx_v[c] = mm(rows_v[c], weights)
            slot = lax.rem(c, 2)
            for lane in range(lanes):
                forward_block(
                    1.0 - starts_v[c, lane : lane + 1, :], zx_v.at[c], chan_ref, bc_par, head_ref, spread_ref[...],
                    conv_v.at[slot], mix_v.at[c], bc_v.at[slot], step_v.at[slot], state_v.at[slot], tail_v.at[slot],
                    state, tail_x, tail_b, pad_x, pad_b, lane=lane, heads=heads,
                )
            out_copy(0, zx_v, out_zx, c).start()
            out_copy(1, mix_v, out_mix, c).start()
            for copy in slot_copies(c):
                copy.start()

    def gated_of(c):
        z = zx_v[c, :, :chans]
        return mix_v[c] * (z * sigmoid(z))

    def mix_grad(s):
        load(grads_ref, s).wait()
        grad = mm(rows_v[s], wout_v[...], NT)
        mgrad_v[s] = grad
        out_copy(2, mgrad_v, out_grad, s).start()
        gated = gated_of(s)
        ones = jnp.ones((SUB, chans), bf16)
        square = mm_right(ones, gated * gated, NT)
        pulled = mm_right(ones, grad * chan_ref[GAIN : GAIN + 1, :] * gated, NT)
        for lane in range(lanes):
            at = slice(lane * BLOCK, (lane + 1) * BLOCK)
            sums[0, pl.ds(s * lanes + lane, 1), :] = square[:1, at]
            sums[1, pl.ds(s * lanes + lane, 1), :] = pulled[:1, at]

    per = -(-peers // 2)
    for step in range(1, chips):
        begin, end = min((step - 1) * per, peers), min(step * per, peers)
        if step == chips - 1:
            end = peers
        if begin < end:
            compute(begin, end)
        if step < chips - 1:
            grads.pass_on(step)

    def at_distance(step, act):
        if not step:
            act(place, None)
            act(jnp.bitwise_xor(place, 1), (1, 0))
        for by in (1, -1):
            if step:
                @pl.when(grads.reached(by, step))
                def _():
                    s = grads.source(by, step)
                    act(s, None)
                    act(jnp.bitwise_xor(s, 1), (by, step))

    def begin_load(s, mate):
        if mate is not None:
            grads.mate(*mate).wait_recv()
        load(grads_ref, s).start()

    grads.keep().wait()
    for step in range(chips - 1):
        at_distance(step, begin_load)
    for step in range(chips - 1):
        at_distance(step, lambda s, mate: mix_grad(s))
    grads.pass_on(chips - 1)
    at_distance(chips - 1, begin_load)
    at_distance(chips - 1, lambda s, mate: mix_grad(s))

    give = [remote(sums, sums_got.at[i], sum_send.at[i], sum_recv.at[i], (width, s)) for i, s in enumerate(ring)]
    for copy in give:
        copy.start()
    for copy in give:
        copy.wait_recv()
    total = sums[...]
    for i in range(peers - 1):
        total = total + sums_got[i]
    count = (active * HEAD_DIM).astype(f32)
    rate = lax.rsqrt(total[0] / count + epsilon)
    pull = rate * rate * rate * total[1] / count
    blank = jnp.zeros((BLOCK - 2 * lanes * peers, BLOCK), f32)
    by_time = jnp.concatenate([rate, pull, blank], axis=0).T
    lane_at = lax.broadcasted_iota(jnp.int32, (BLOCK, BLOCK), 1)
    for c in range(peers):
        for lane in range(lanes):
            i = c * lanes + lane
            j = lanes * peers + i
            scale_v[c, lane * BLOCK : (lane + 1) * BLOCK, :] = jnp.where(
                lane_at == 0, by_time[:, i : i + 1], jnp.where(lane_at == 1, by_time[:, j : j + 1], 0.0)
            )

    @pl.loop(0, peers)
    def _(c):
        low = (gated_of(c) * scale_v[c, :, 0:1] * chan_ref[GAIN : GAIN + 1, :]).astype(bf16)
        low_v[c] = low
        rows_v[c] = mm(low, wout_v[...]).astype(bf16)
        out_copy(3, scale_v, out_scale, c).start()
        out_copy(4, low_v, out_low, c).start()
        out_copy(5, rows_v, out_part, c).start()

    for copy in shares + pushes + give:
        copy.wait_send()
    rows.sent()
    grads.sent()
    for c in (peers - 2, peers - 1):
        for copy in slot_copies(c):
            copy.wait()

    @pl.loop(0, peers)
    def _(c):
        for k, (src, dst) in enumerate(
            [(zx_v, out_zx), (mix_v, out_mix), (mgrad_v, out_grad), (scale_v, out_scale), (low_v, out_low), (rows_v, out_part)]
        ):
            out_copy(k, src, dst, c).wait()


def front(valid, starts, tokens, cotangent, norm_gain, w_bc, w_dt, taps, bias, dt_bias, a_log, d_skip, gate_gain, spread, w_zx, w_out):
    peers, widths = lax.axis_size("seq"), lax.axis_size("width")
    own, model = tokens.shape
    lanes = starts.shape[1]
    quarter = own // widths
    chans = w_out.shape[0]
    heads = chans // HEAD_DIM
    cols = 2 * chans + BLOCK + 2 * N
    dma = pltpu.SemaphoreType.DMA
    anywhere, vmem = pl.BlockSpec(memory_space=pl.ANY), pl.BlockSpec(memory_space=pltpu.VMEM)
    smem = pl.BlockSpec(memory_space=pltpu.SMEM)
    w_all = ((peers, widths, quarter, cols), bf16)
    rows_all = ((peers, own, model), bf16)
    starts_all = ((peers, SUB, BLOCK), f32)
    per_chan, low = ((peers, own, chans), f32), ((peers, own, chans), bf16)
    whole = [((peers, own, cols), f32), per_chan, per_chan, ((peers, own, BLOCK), f32), low]
    streamed = [
        ((own, chans), f32), ((own, 2 * N), bf16), ((own, 2 * BLOCK), f32), ((lanes, N, chans), f32), ((lanes, SUB, chans), f32)
    ]
    outs = [w_all, rows_all, rows_all, starts_all, ((SUB, chans), f32), ((SUB, BLOCK), f32), *whole, rows_all]
    outs += [((peers,) + a[0], a[1]) for a in streamed]
    scratch = [w_all, rows_all, starts_all, ((chans, model), bf16), ((own, model), bf16), ((own, model), bf16)]
    scratch += [((peers, own, BLOCK), bf16), ((SUB, BLOCK), f32), ((SUB, 2 * N), f32), *whole]
    scratch += [((2,) + a[0], a[1]) for a in streamed]
    scratch += [((2, peers * lanes, BLOCK), f32), ((peers - 1, 2, peers * lanes, BLOCK), f32)]
    scratch += [((lanes, N, chans), f32), ((lanes, SUB, chans), f32), ((lanes, SUB, 2 * N), f32)]
    scratch += [((lanes, BLOCK + SUB, chans), f32), ((lanes, BLOCK + SUB, 2 * N), f32)]
    return pl.pallas_call(
        partial(front_kernel, peers=peers, widths=widths, lanes=lanes, heads=heads),
        in_specs=[smem] * 2 + [vmem] * 12 + [anywhere] * 2,
        out_specs=[anywhere] * 4 + [vmem] * 2 + [anywhere] * 11,
        out_shape=[jax.ShapeDtypeStruct(*a) for a in outs],
        scratch_shapes=[
            *[pltpu.VMEM(*a) for a in scratch],
            dma((4, peers - 1)), dma((4, peers - 1)), dma((peers - 1,)), dma((peers - 1,)),
            dma((5,)), dma((widths - 1,)), dma((widths - 1,)), dma((peers,)), dma((6, peers)), dma((5, 2)),
            dma((peers - 1,)), dma((peers - 1,)),
            *row_sems(peers // 2), *row_sems(peers // 2),
        ],
        compiler_params=pltpu.CompilerParams(collective_id=1, has_side_effects=True, vmem_limit_bytes=62 << 20),
        name="front",
    )(valid, starts, tokens, cotangent, norm_gain, w_bc, w_dt, taps, bias, dt_bias, a_log, d_skip, gate_gain, spread, w_zx, w_out)


ROWS_AT_ONCE = 16


def add_into(dst, others, rows):
    @pl.loop(0, rows // ROWS_AT_ONCE)
    def _(i):
        at = pl.ds(pl.multiple_of(i * ROWS_AT_ONCE, ROWS_AT_ONCE), ROWS_AT_ONCE)
        value = dst[at].astype(f32)
        for other in others:
            value = value + other[at].astype(f32)
        dst[at] = value.astype(dst.dtype)


def scatter_kernel(
    part_ref, wide_ref, third_ref, x_ref, cot_ref, gain_ref, rows_ref, out_ref, out_third_ref,
    mine, from_core, up, down, own0, own1, own2, got0, got1, got2, piece0, piece1, piece2,
    local_sem, core_send, core_recv, up_send, up_recv, down_send, down_recv,
    own_sem, q_send, q_recv, p_send, p_recv, o_send, o_recv,
    *, peers, widths,
):
    width, place = lax.axis_index("width"), lax.axis_index("seq")
    chips = peers // 2
    chip, core = place // 2, lax.rem(place, 2)
    mate = (width, jnp.bitwise_xor(place, 1))
    ring = [lax.rem(place + by, peers) for by in range(1, peers)]
    cross = [jnp.bitwise_xor(width, m) for m in range(1, widths)]
    others = [(width, s) for s in ring] + [(w, place) for w in cross]
    greet(others)
    met(others)
    half = wide_ref.shape[3] // 2
    sets = [
        (wide_ref, out_ref, pl.ds(0, half), own0, got0, piece0),
        (wide_ref, out_ref, pl.ds(half, half), own1, got1, piece1),
        (third_ref, out_third_ref, pl.ds(0, BLOCK), own2, got2, piece2),
    ]

    def remote(src, dst, send, recv, device):
        return pltpu.make_async_remote_copy(
            src_ref=src, dst_ref=dst, send_sem=send, recv_sem=recv, device_id=device, device_id_type=MESH
        )

    locals_ = [pltpu.make_async_copy(part_ref.at[2 * q + core], mine.at[q], local_sem.at[q]) for q in range(chips)]
    to_core = [
        remote(part_ref.at[2 * q + 1 - core], from_core.at[q], core_send.at[q], core_recv.at[q], mate) for q in range(chips)
    ]
    own_in, to_width = [], []
    for k, (src, dst, cols, own, got, piece) in enumerate(sets):
        own_in.append(pltpu.make_async_copy(src.at[:, width, :, cols], own, own_sem.at[0, k]))
        to_width.append([
            remote(src.at[:, w, :, cols], got.at[m], q_send.at[k, m], q_recv.at[k, m], (w, place)) for m, w in enumerate(cross)
        ])
    for copy in locals_ + to_core + own_in + to_width[0] + to_width[1] + to_width[2]:
        copy.start()
    rows = mine.shape[1]
    for q in range(chips):
        locals_[q].wait()
        to_core[q].wait_recv()
        add_into(mine.at[q], [from_core.at[q]], rows)

    def flow(by):
        return (up, up_send, up_recv) if by > 0 else (down, down_send, down_recv)

    def sends(by, step):
        far = chips - step
        return chip + far < chips if by > 0 else chip >= far

    def later(by):
        return chip > 0 if by > 0 else chip + 1 < chips

    def hop(src, by, step):
        buffer, send, recv = flow(by)
        return remote(
            src, buffer.at[step - 1], send.at[step - 1], recv.at[step - 1], (width, jnp.clip(place + 2 * by, 0, peers - 1))
        )

    def staged(by, step):
        return flow(by)[0].at[step - 2]

    def run_hops(step):
        for by in (1, -1):
            owner = jnp.clip(chip + by * (chips - step), 0, chips - 1)

            def direct():
                hop(mine.at[owner], by, step).start()

            def relayed():
                hop(staged(by, step), by, step - 1).wait_recv()
                add_into(staged(by, step), [mine.at[owner]], rows)
                hop(staged(by, step), by, step).start()

            if step == 1:
                pl.when(sends(by, step))(direct)
            else:
                pl.when(sends(by, step) & jnp.logical_not(later(by)))(direct)
                pl.when(sends(by, step) & later(by))(relayed)

    to_owner, to_all, kept = [None] * 3, [None] * 3, []

    def exchange(k):
        src, dst, cols, own, got, piece = sets[k]
        own_in[k].wait()
        for copy in to_width[k]:
            copy.wait_recv()
        for s in range(peers):
            add_into(own.at[s], [got.at[m, s] for m in range(widths - 1)], own.shape[1])
        to_owner[k] = [
            remote(own.at[s], piece.at[place], p_send.at[k, i], p_recv.at[k, i], (width, s)) for i, s in enumerate(ring)
        ]
        keep = pltpu.make_async_copy(own.at[place], piece.at[place], own_sem.at[1, k])
        for copy in to_owner[k] + [keep]:
            copy.start()
        kept.append(keep)

    def spread(k):
        src, dst, cols, own, got, piece = sets[k]
        for copy in to_owner[k]:
            copy.wait_recv()
        kept[k].wait()
        to_all[k] = [
            remote(piece, dst.at[:, width, :, cols], o_send.at[k, m], o_recv.at[k, m], (w, place)) for m, w in enumerate(cross)
        ]
        to_all[k].append(pltpu.make_async_copy(piece, dst.at[:, width, :, cols], own_sem.at[2, k]))
        for copy in to_all[k]:
            copy.start()

    run_hops(1)
    exchange(0)
    if chips > 2:
        run_hops(2)
    spread(0)
    exchange(1)
    exchange(2)
    for step in range(3, chips):
        run_hops(step)
    spread(1)
    spread(2)

    for by in (1, -1):
        @pl.when(later(by))
        def _():
            buffer = flow(by)[0].at[chips - 2]
            hop(buffer, by, chips - 1).wait_recv()
            add_into(mine.at[chip], [buffer], rows)

    gain = gain_ref[...]

    @pl.loop(0, rows // ROWS_AT_ONCE)
    def _(i):
        at = pl.ds(pl.multiple_of(i * ROWS_AT_ONCE, ROWS_AT_ONCE), ROWS_AT_ONCE)
        x = x_ref[at, :].astype(f32)
        rate = lax.rsqrt(jnp.mean(x * x, axis=-1, keepdims=True) + epsilon)
        unit = x * rate
        pulled = mine[chip, at].astype(f32) * gain
        inner = jnp.mean(pulled * unit, axis=-1, keepdims=True)
        rows_ref[at, :] = cot_ref[at, :].astype(f32) + rate * (pulled - unit * inner)

    for step in range(1, chips):
        for by in (1, -1):
            @pl.when(sends(by, step))
            def _():
                hop(mine.at[0], by, step).wait_send()
    for copy in to_core:
        copy.wait_send()
    for k in range(len(sets)):
        for copy in to_width[k] + to_owner[k]:
            copy.wait_send()
        for copy in to_all[k]:
            copy.wait()


def scattered_out(part, wide, third, x_rows, cotangent, gain):
    peers, widths = lax.axis_size("seq"), lax.axis_size("width")
    chips = peers // 2
    dma = pltpu.SemaphoreType.DMA
    anywhere = pl.BlockSpec(memory_space=pl.ANY)
    vmem = pl.BlockSpec(memory_space=pltpu.VMEM)
    block = part.shape[1:]
    half = wide.shape[3] // 2
    pieces = [(peers, wide.shape[2], cols) for cols in (half, half, third.shape[3])]
    return pl.pallas_call(
        partial(scatter_kernel, peers=peers, widths=widths),
        in_specs=[anywhere] * 3 + [vmem] * 3,
        out_specs=[vmem, anywhere, anywhere],
        out_shape=[
            jax.ShapeDtypeStruct(block, f32), jax.ShapeDtypeStruct(wide.shape, bf16), jax.ShapeDtypeStruct(third.shape, bf16)
        ],
        scratch_shapes=[
            pltpu.VMEM((chips,) + block, bf16), pltpu.VMEM((chips,) + block, bf16),
            pltpu.VMEM((chips - 1,) + block, bf16), pltpu.VMEM((chips - 1,) + block, bf16),
            *[pltpu.VMEM(piece, bf16) for piece in pieces],
            *[pltpu.VMEM((widths - 1,) + piece, bf16) for piece in pieces],
            *[pltpu.VMEM(piece, bf16) for piece in pieces],
            dma((chips,)), dma((chips,)), dma((chips,)),
            dma((chips - 1,)), dma((chips - 1,)), dma((chips - 1,)), dma((chips - 1,)),
            dma((3, 3)), dma((3, widths - 1)), dma((3, widths - 1)), dma((3, peers - 1)), dma((3, peers - 1)),
            dma((3, widths - 1)), dma((3, widths - 1)),
        ],
        compiler_params=pltpu.CompilerParams(collective_id=2, has_side_effects=True, vmem_limit_bytes=48 << 20),
        name="scatter_out",
    )(part, wide, third, x_rows, cotangent, gain)


def bc_kernel(got_ref, pre_ref, par_ref, keep_ref, ddt_ref, third_ref, dpar_ref, pre_t, *, at):
    chans, times = pre_t.shape
    for i in range(times // BLOCK):
        rows = slice(i * BLOCK, (i + 1) * BLOCK)
        pre_t[:, rows] = pre_ref[rows, :].T[at : at + chans]
    dbc = got_ref[0].astype(f32)
    for s in range(1, got_ref.shape[0]):
        dbc = dbc + got_ref[s].astype(f32)
    pre = pre_t[...]
    in_block = lax.rem(lax.broadcasted_iota(jnp.int32, (chans, times), 1), BLOCK)
    keep, keep_next = keep_ref[0:1, :], keep_ref[1:2, :]
    conv = jnp.broadcast_to(par_ref[:, BIAS : BIAS + 1], (chans, times))
    shifted = []
    for j in range(KCONV):
        moved = pre
        if j:
            moved = jnp.where(in_block >= j, pltpu.roll(pre, j, 1), keep * pltpu.roll(pre, BLOCK + j, 1))
        shifted.append(moved)
        conv = conv + moved * par_ref[:, KCONV - 1 - j : KCONV - j]
    act = sigmoid(conv)
    dconv = dbc * (act * (1.0 + conv * (1.0 - act)))
    dpre = dconv * par_ref[:, KCONV - 1 : KCONV]
    lane = lax.broadcasted_iota(jnp.int32, (chans, BLOCK), 1)
    dpar = jnp.where(lane == BIAS, jnp.sum(dconv, axis=1, keepdims=True), 0.0)
    for j in range(KCONV):
        dpar = dpar + jnp.where(lane == KCONV - 1 - j, jnp.sum(dconv * shifted[j], axis=1, keepdims=True), 0.0)
        if j:
            back = jnp.where(
                in_block < BLOCK - j, pltpu.roll(dconv, times - j, 1), keep_next * pltpu.roll(dconv, times - BLOCK - j, 1)
            )
            dpre = dpre + back * par_ref[:, KCONV - 1 - j : KCONV - j]
    dpar_ref[...] = dpar
    for i in range(times // BLOCK):
        tile = dpre[:, i * BLOCK : (i + 1) * BLOCK]
        below = jnp.zeros((BLOCK - at - chans, BLOCK), f32)
        tile = jnp.concatenate([jnp.zeros((at, BLOCK), f32), tile, below], axis=0).T
        rows = slice(i * BLOCK, (i + 1) * BLOCK)
        third_ref[rows, :] = (tile + ddt_ref[rows, :].astype(f32)).astype(bf16)


def bc_backward(got, zx, par, keep, dzx, at, chans):
    rows = dzx.shape[0]
    share = got.shape[1]
    third = pl.BlockSpec((rows, BLOCK), lambda i: (0, 2 * chans // BLOCK))
    whole = lambda a: pl.BlockSpec(a.shape, lambda i: (0,) * a.ndim)
    return pl.pallas_call(
        partial(bc_kernel, at=at),
        grid=(1,),
        in_specs=[whole(got), third, whole(par), whole(keep), third],
        out_specs=[pl.BlockSpec((rows, BLOCK), lambda i: (0, 0)), pl.BlockSpec((share, BLOCK), lambda i: (0, 0))],
        out_shape=[jax.ShapeDtypeStruct((rows, BLOCK), bf16), jax.ShapeDtypeStruct((share, BLOCK), f32)],
        scratch_shapes=[pltpu.VMEM((share, rows), f32)],
        compiler_params=pltpu.CompilerParams(vmem_limit_bytes=32 << 20),
        name="bc_backward",
    )(got, zx, par, keep, dzx)


def laid_kernel(in_ref, third_ref, w_ref, bc_ref, dt_ref, gain_ref, out_ref, out_bc_ref, out_dt_ref, norm_ref, *, heads, share):
    peers, rows, wide = in_ref.shape[0], in_ref.shape[2], in_ref.shape[3]
    chans = wide // 2
    lane = jnp.zeros((rows, BLOCK), f32)
    for s in range(peers):
        for half in (0, 1):
            at = (half * peers + s) * chans
            value = in_ref[s, 0, :, half * chans : (half + 1) * chans].astype(f32)
            out_ref[:, at : at + chans] = value
            value = value * w_ref[:, at : at + chans].astype(f32)
            for j in range(chans // BLOCK):
                lane = lane + value[:, j * BLOCK : (j + 1) * BLOCK]
    third = [third_ref[s, 0].astype(f32) for s in range(peers)]
    bc = jnp.concatenate([t[:, heads : heads + share] for t in third], axis=1)
    dt = jnp.concatenate([t[:, :heads] for t in third], axis=1)
    out_bc_ref[...] = bc
    out_dt_ref[...] = dt
    total = jnp.sum(lane, axis=1, keepdims=True) + jnp.sum(bc * bc_ref[...].astype(f32), axis=1, keepdims=True)
    total = total + jnp.sum(dt * dt_ref[...].astype(f32), axis=1, keepdims=True)
    norm_ref[...] = total / gain_ref[...]


def laid_out(wide, third, w_zx, w_bc, w_dt, gain, heads):
    peers, widths, quarter, cols = wide.shape
    rows = widths * quarter
    steps = 2 * widths
    cut = rows // steps
    share = w_bc.shape[1] // peers
    by_rows = lambda a: pl.BlockSpec((cut, a.shape[1]), lambda i: (i, 0))
    by_piece = lambda a: pl.BlockSpec((peers, 1, cut, a.shape[3]), lambda i: (0, i // 2, i % 2, 0))
    shapes = [jax.ShapeDtypeStruct(a.shape, f32) for a in (w_zx, w_bc, w_dt, gain)]
    return pl.pallas_call(
        partial(laid_kernel, heads=heads, share=share),
        grid=(steps,),
        in_specs=[by_piece(wide), by_piece(third)] + [by_rows(a) for a in (w_zx, w_bc, w_dt, gain)],
        out_specs=[by_rows(a) for a in shapes],
        out_shape=shapes,
        compiler_params=pltpu.CompilerParams(vmem_limit_bytes=32 << 20),
        name="lay_out",
    )(wide, third, w_zx, w_bc, w_dt, gain)


def crossed(value, axis, mask):
    return lax.ppermute(value, axis, [(i, i ^ mask) for i in range(lax.axis_size(axis))])


def pick(value, index):
    return lax.dynamic_index_in_dim(value, index, 0, False)


def quarters_sent(value):
    widths, width = lax.axis_size("width"), lax.axis_index("width")
    value = value.reshape((widths, value.shape[0] // widths) + value.shape[1:])
    sent = [crossed(pick(value, jnp.bitwise_xor(width, m)), "width", m) for m in range(1, widths)]
    return [pick(value, width)] + sent


def quarters_back(total):
    widths = lax.axis_size("width")
    return [total] + [crossed(total, "width", m) for m in range(1, widths)]


def quarters_joined(pieces):
    width = lax.axis_index("width")
    stacked = jnp.stack(pieces)
    whole = jnp.stack([pick(stacked, jnp.bitwise_xor(width, j)) for j in range(len(pieces))])
    return whole.reshape((-1,) + whole.shape[2:]).astype(f32)


def packed_rows(rows, count):
    flat = jnp.stack(rows)
    return jnp.pad(flat, ((0, count - len(rows)), (0, 0)))


def heads_body(
    tokens, cotangent, starts, valid, norm_gain, w_zx, w_bc, w_dt, conv_w, conv_b, dt_bias, a_log, d_skip, gate_gain, w_out
):
    peers = lax.axis_size("seq")
    widths = lax.axis_size("width")
    place = lax.axis_index("seq")
    lanes = starts.shape[1]
    heads = H // peers
    chans = heads * HEAD_DIM
    own, model = tokens.shape
    rows = own * peers
    first = place * heads
    share = 2 * N // peers
    used = heads + share
    row_mask = (jnp.arange(BLOCK)[None, :] < valid[0][:, None]).astype(f32).reshape(-1, 1)
    spread = jnp.asarray(np.arange(chans)[None, :] // HEAD_DIM == np.arange(BLOCK)[:, None], bf16)
    weights, normed, bgrad, starts_all, chan, head, *computed = front(
        valid, starts, tokens, cotangent, norm_gain[None], w_bc, w_dt, conv_w.T, conv_b[None], dt_bias[None], a_log[None],
        d_skip[None], gate_gain[None], spread, w_zx, w_out,
    )
    weights = weights.reshape(model, -1)
    normed, bgrad = normed.reshape(rows, model), bgrad.reshape(rows, model)
    keep = 1.0 - starts_all[:, :lanes, 0]
    zx, mix, mixed_grad, scale, mixed_low, part, conv, bc, steps = [a.reshape(rows, a.shape[-1]) for a in computed[:9]]
    state, tail = computed[9:]
    branch = lax.psum_scatter(part, "seq", scatter_dimension=0, tiled=True).astype(f32)
    output = (tokens.astype(f32) + row_mask * branch).astype(bf16)
    out_part = mm(mixed_low, bgrad, TN).astype(bf16)
    scale, out_part = lax.optimization_barrier((scale, out_part))
    out_quarters = quarters_sent(out_part)

    dzx, dbc, dchan, dhead = run_backward(
        keep, zx, mixed_grad, chan, head, spread, conv, mix, bc, steps, state, tail, scale, lanes, heads
    )
    dzx, dbc, out_quarters = lax.optimization_barrier((dzx, dbc, out_quarters))
    out_pieces = quarters_back(sum(q.astype(f32) for q in out_quarters).astype(bf16))

    got = lax.all_to_all(dbc.reshape(peers, share, rows), "seq", 0, 0, tiled=True)
    of_share = lambda a: lax.dynamic_slice_in_dim(a, E + place * share, share, 0)
    share_par = jnp.pad(jnp.concatenate([of_share(conv_w), of_share(conv_b)[:, None]], axis=1), ((0, 0), (0, BLOCK - BIAS - 1)))
    over_time = lambda a: jnp.repeat(a.reshape(-1), BLOCK)
    keep_next = jnp.concatenate([keep[1:], jnp.zeros_like(keep[:1])], axis=0)
    third, dshare = bc_backward(
        got, zx, share_par, packed_rows([over_time(keep), over_time(keep_next)], SUB), dzx, heads, chans
    )

    at_heads = lambda a: lax.dynamic_update_slice_in_dim(jnp.zeros((H,), f32), a, first, 0)
    at_chans = lambda a: lax.dynamic_update_slice_in_dim(jnp.zeros((E,), f32), a, first * HEAD_DIM, 0)
    at_share = lambda a: lax.dynamic_update_slice_in_dim(jnp.zeros((2 * N,), f32), a, place * share, 0)
    skip = jnp.sum(dchan[SKIP].reshape(heads, HEAD_DIM), axis=1)
    small = [jnp.concatenate([at_chans(dchan[k]), at_share(dshare[:, k])]) for k in range(KCONV + 1)]
    small += [at_chans(dchan[GAIN]), at_heads(dhead[0, :heads]), at_heads(dhead[1, :heads]), at_heads(skip)]
    sizes = [a.shape[0] // peers for a in small]
    small = jnp.concatenate([a.reshape(peers, -1) for a in small], axis=1)
    per_row = -(-small.shape[1] // own)
    small = jnp.pad(small, ((0, 0), (0, own * per_row - small.shape[1]))).reshape(model, per_row)

    wide = mm(normed, dzx[:, : 2 * chans], TN).astype(bf16)
    wide, out_pieces = lax.optimization_barrier((wide, out_pieces))
    out_grad = quarters_joined(out_pieces)
    wide_third = jnp.concatenate(
        [mm(normed, third, TN)[:, :used], small, jnp.zeros((model, BLOCK - used - per_row), f32)], axis=1
    ).astype(bf16)
    part = mm(lax.dynamic_update_slice(dzx, third, (0, 2 * chans)), weights[:, : 2 * chans + BLOCK], NT).astype(bf16)
    by_owner = lambda a: a.reshape(peers, widths, own // widths, -1)
    part, output, out_grad = lax.optimization_barrier((part, output, out_grad))
    input_grad, wide, wide_third = scattered_out(
        part.reshape(peers, own, model), by_owner(wide), by_owner(wide_third), tokens, cotangent, norm_gain[None]
    )
    gain_rows = lax.dynamic_slice_in_dim(norm_gain, place * own, own, 0)[:, None]
    grad_zx, grad_bc, grad_dt, grad_norm = laid_out(wide, wide_third, w_zx, w_bc, w_dt, gain_rows, heads)
    grad_norm = grad_norm[:, 0]
    summed = jnp.sum(wide_third.reshape(peers, own, BLOCK)[:, :, used : used + per_row].astype(f32), axis=0).reshape(-1)
    pieces = [summed[sum(sizes[:i]) : sum(sizes[: i + 1])] for i in range(len(sizes))]
    grad_taps = jnp.stack(pieces[:KCONV], axis=1)
    grad_bias, grad_gain, grad_dtb, grad_alog, grad_skip = pieces[KCONV:]
    return (
        output, input_grad, grad_norm, grad_zx, grad_bc, grad_dt, grad_taps, grad_bias, grad_dtb, grad_alog, grad_skip,
        grad_gain, out_grad,
    )


def passed_along(array, axis, by):
    peers = lax.axis_size(axis)
    pairs = [(i, i + by) for i in range(peers) if 0 <= i + by < peers]
    return lax.ppermute(array, axis, pairs)


def carried_in(part, axis, combine, identity, reverse):
    count = lax.axis_size(axis)
    place = lax.axis_index(axis)
    at = count - 1 - place if reverse else place
    by = -1 if reverse else 1
    state = jax.tree.map(lambda a, e: jnp.zeros_like(a) + jnp.asarray(e, a.dtype), part, identity)

    def one(lap, state):
        sent = combine(state, part)
        got = jax.tree.map(lambda a: passed_along(a, axis, by), sent)
        return jax.tree.map(lambda old, new: jnp.where(at == lap + 1, new, old), state, got)

    return lax.fori_loop(0, count - 1, one, state)


def round_value(v):
    return lax.optimization_barrier(v.astype(jnp.bfloat16)).astype(jnp.float32)


def keep_round(v):
    return (round_value(v), None)


def pass_grad(kept, grad):
    return (grad,)


def same_value(v):
    return v


def keep_same(v):
    return (v, None)


def round_grad(kept, grad):
    return (round_value(grad),)


def low(v):
    wrapped = jax.custom_vjp(round_value)
    wrapped.defvjp(keep_round, pass_grad)
    return wrapped(v)


def low_back(v):
    wrapped = jax.custom_vjp(same_value)
    wrapped.defvjp(keep_same, round_grad)
    return wrapped(v)


def rms_front(x_rows, norm_gain):
    mean_square = jnp.mean(x_rows * x_rows, axis=-1, keepdims=True)
    return x_rows * lax.rsqrt(mean_square + epsilon) * norm_gain


def rim_of(zx_pre, bc_pre, chan_mask):
    return jnp.concatenate(
        [zx_pre[:, BLOCK - KCONV + 1 :, E:] * chan_mask, bc_pre[:, BLOCK - KCONV + 1 :, :]], axis=-1
    )


def piece_front(
    zx_pre,
    bc_pre,
    dt_raw,
    rim_rows,
    conv_w,
    conv_b,
    dt_bias,
    a_log,
    chan_mask,
    head_mask,
    keep_rows,
):
    z_gate = zx_pre[..., :E] * chan_mask
    pre_conv = jnp.concatenate([zx_pre[..., E:] * chan_mask, bc_pre], axis=-1)
    padded = jnp.concatenate([rim_rows * keep_rows[:, None, None], pre_conv], axis=1)
    conv_out = conv_b + padded[:, 0:BLOCK, :] * conv_w[:, 0]
    for offset in range(1, KCONV):
        conv_out = conv_out + padded[:, offset : offset + BLOCK, :] * conv_w[:, offset]
    active = jax.nn.silu(conv_out)
    x_conv = low(active[..., :E] * chan_mask)
    b_conv = low(active[..., E : E + N])
    c_conv = low(active[..., E + N :])
    dt_step = jax.nn.softplus(dt_raw + dt_bias) * head_mask
    log_step = -jnp.exp(a_log) * dt_step
    return (z_gate, x_conv, b_conv, c_conv, dt_step, log_step)


def block_state(x_conv, b_conv, dt_step, log_step):
    cumulative = jnp.cumsum(log_step, axis=1)
    to_end = jnp.exp(cumulative[:, -1:, :] - cumulative) * dt_step
    weighted = low(x_conv.reshape(x_conv.shape[0], BLOCK, H, HEAD_DIM) * to_end[..., None])
    state_sum = jnp.einsum("lqhp,lqn->lhpn", weighted, b_conv, precision=highest)
    return (state_sum, cumulative[:, -1, :])


def piece_mix(
    z_gate, x_conv, b_conv, c_conv, dt_step, log_step, state_in, d_skip, gate_gain, chan_count
):
    lane_count = x_conv.shape[0]
    cumulative = jnp.cumsum(log_step, axis=1)
    cum_heads = jnp.swapaxes(cumulative, 1, 2)
    causal = jnp.arange(BLOCK)[:, None] >= jnp.arange(BLOCK)[None, :]
    spread = cum_heads[:, :, :, None] - cum_heads[:, :, None, :]
    decays = jnp.where(causal, jnp.exp(jnp.where(causal, spread, 0.0)), 0.0)
    inner_cb = jnp.einsum("lqn,lsn->lqs", c_conv, b_conv, precision=highest)
    scores = low(inner_cb[:, None] * decays * jnp.swapaxes(dt_step, 1, 2)[:, :, None, :])
    x_heads = x_conv.reshape(lane_count, BLOCK, H, HEAD_DIM)
    within = jnp.einsum("lhqs,lshp->lqhp", scores, x_heads, precision=highest)
    carried = (
        jnp.einsum("lqn,lhpn->lqhp", c_conv, state_in, precision=highest)
        * jnp.exp(cumulative)[..., None]
    )
    mixed_sum = low_back(within + carried) + d_skip[:, None] * x_heads
    gated_rows = mixed_sum.reshape(lane_count, BLOCK, E) * jax.nn.silu(z_gate)
    mean_square = jnp.sum(gated_rows * gated_rows, axis=-1, keepdims=True) / chan_count
    return low(gated_rows * lax.rsqrt(mean_square + epsilon) * gate_gain)


def mix_lanes(lane_inputs, d_skip, gate_gain, chan_count):

    def one_lane(pieces):
        lane_gate, lane_xconv, lane_bconv, lane_cconv, lane_step, lane_decay, lane_state = pieces
        return piece_mix(
            lane_gate[None],
            lane_xconv[None],
            lane_bconv[None],
            lane_cconv[None],
            lane_step[None],
            lane_decay[None],
            lane_state[None],
            d_skip,
            gate_gain,
            chan_count,
        )[0]

    return lax.map(one_lane, lane_inputs)


def mix_back_lanes(lane_inputs, mixed_grad, d_skip, gate_gain, chan_count):

    def lane_mix(z_gate, x_conv, b_conv, c_conv, dt_step, log_step, state_in, skip_coef, gain_coef):
        return piece_mix(
            z_gate[None],
            x_conv[None],
            b_conv[None],
            c_conv[None],
            dt_step[None],
            log_step[None],
            state_in[None],
            skip_coef,
            gain_coef,
            chan_count,
        )[0]

    def one_lane(pieces):
        (
            lane_gate,
            lane_xconv,
            lane_bconv,
            lane_cconv,
            lane_step,
            lane_decay,
            lane_state,
            lane_grad,
        ) = pieces
        unused, pull_lane = jax.vjp(
            lane_mix,
            lane_gate,
            lane_xconv,
            lane_bconv,
            lane_cconv,
            lane_step,
            lane_decay,
            lane_state,
            d_skip,
            gate_gain,
        )
        return pull_lane(lane_grad)

    lane_grads = lax.map(one_lane, lane_inputs + (mixed_grad,))
    return (lane_grads[:7], jnp.sum(lane_grads[7], axis=0), jnp.sum(lane_grads[8], axis=0))


def chain_combine(earlier, latter):
    return (earlier[0] * latter[0], latter[0][:, :, None, None] * earlier[1] + latter[1])


def share_out(out_grad):
    return lax.psum_scatter(out_grad, "seq", scatter_dimension=0, tiled=True)


def contract_rows(left, right):
    return lax.dot_general(
        left, right, (((0,), (0,)), ((), ())), preferred_element_type=jnp.float32
    )


def contract_cols(left, right):
    return lax.dot_general(
        left, right, (((1,), (1,)), ((), ())), preferred_element_type=jnp.float32
    )


def rows_body(
    tokens,
    cotangent,
    starts,
    valid,
    norm_gain,
    w_zx,
    w_bc,
    w_dt,
    conv_w,
    conv_b,
    dt_bias,
    a_log,
    d_skip,
    gate_gain,
    w_out,
):
    lane_count = starts.shape[1]
    width_index = lax.axis_index("width")
    shift_bits = lax.axis_size("width") - 1 - width_index
    active_heads = jnp.right_shift(jnp.int32(H), shift_bits)
    chan_mask = (jnp.arange(E) // HEAD_DIM < active_heads).astype(jnp.float32)
    head_mask = (jnp.arange(H) < active_heads).astype(jnp.float32)
    chan_count = (active_heads * HEAD_DIM).astype(jnp.float32)
    keep_rows = 1.0 - starts[0].astype(jnp.float32)
    row_mask = (jnp.arange(BLOCK)[None, :] < valid[0][:, None]).astype(jnp.float32).reshape(-1, 1)
    x_rows = tokens.astype(jnp.float32)
    normed, norm_back = jax.vjp(rms_front, x_rows, norm_gain)
    normed_low = normed.astype(jnp.bfloat16)
    zx_full, bc_full, dt_full, out_full = (
        lax.all_gather(w_zx, "seq", axis=0, tiled=True),
        lax.all_gather(w_bc, "seq", axis=0, tiled=True),
        lax.all_gather(w_dt, "seq", axis=0, tiled=True),
        lax.all_gather(w_out, "seq", axis=0, tiled=True),
    )
    zx_pre = jnp.dot(normed_low, zx_full, preferred_element_type=jnp.float32).reshape(
        lane_count, BLOCK, 2 * E
    )
    bc_pre = jnp.dot(normed_low, bc_full, preferred_element_type=jnp.float32).reshape(
        lane_count, BLOCK, 2 * N
    )
    dt_raw = jnp.dot(normed_low, dt_full, preferred_element_type=jnp.float32).reshape(
        lane_count, BLOCK, H
    )
    rim_rows = passed_along(rim_of(zx_pre, bc_pre, chan_mask), "seq", 1)
    front_fn = partial(piece_front, chan_mask=chan_mask, head_mask=head_mask, keep_rows=keep_rows)
    front_out, front_back = jax.vjp(
        front_fn, zx_pre, bc_pre, dt_raw, rim_rows, conv_w, conv_b, dt_bias, a_log
    )
    z_gate, x_conv, b_conv, c_conv, dt_step, log_step = front_out
    (state_sum, log_total), state_back = jax.vjp(block_state, x_conv, b_conv, dt_step, log_step)
    carry_rate = jnp.exp(log_total) * keep_rows[:, None]
    identity = (jnp.ones_like(carry_rate), jnp.zeros_like(state_sum))
    prefix_pair = carried_in((carry_rate, state_sum), "seq", chain_combine, identity, False)
    state_in = prefix_pair[1] * keep_rows[:, None, None, None]
    lane_inputs = (z_gate, x_conv, b_conv, c_conv, dt_step, log_step, state_in)
    mixed_low = mix_lanes(lane_inputs, d_skip, gate_gain, chan_count)
    mixed_flat = mixed_low.reshape(-1, E).astype(jnp.bfloat16)
    branch = jnp.dot(mixed_flat, out_full, preferred_element_type=jnp.float32)
    output = (x_rows + row_mask * branch).astype(jnp.bfloat16)
    cot_rows = cotangent.astype(jnp.float32)
    branch_grad = (cot_rows * row_mask).astype(jnp.bfloat16)
    out_grad = contract_rows(mixed_flat, branch_grad)
    mixed_grad = contract_cols(branch_grad, out_full).reshape(lane_count, BLOCK, E)
    lane_grads, grad_skip, grad_gain = mix_back_lanes(
        lane_inputs, mixed_grad, d_skip, gate_gain, chan_count
    )
    grad_gate, grad_x, grad_b, grad_c, grad_dt, grad_log, grad_state = lane_grads
    later_pair = carried_in(
        (carry_rate, grad_state * keep_rows[:, None, None, None]),
        "seq",
        chain_combine,
        identity,
        True,
    )
    later_grad = later_pair[1]
    grad_total = jnp.exp(log_total) * jnp.sum(later_grad * state_in, axis=(2, 3))
    grad_x_more, grad_b_more, grad_dt_more, grad_log_more = state_back((later_grad, grad_total))
    grad_zx, grad_bc, grad_dtraw, grad_rim, grad_convw, grad_convb, grad_dtbias, grad_alog = (
        front_back(
            (
                grad_gate,
                grad_x + grad_x_more,
                grad_b + grad_b_more,
                grad_c,
                grad_dt + grad_dt_more,
                grad_log + grad_log_more,
            )
        )
    )
    rim_grad = passed_along(grad_rim.astype(jnp.bfloat16), "seq", -1).astype(grad_rim.dtype)
    grad_zx = grad_zx.at[:, BLOCK - KCONV + 1 :, E:].add(rim_grad[..., :E] * chan_mask)
    grad_bc = grad_bc.at[:, BLOCK - KCONV + 1 :, :].add(rim_grad[..., E:])
    zx_low = grad_zx.reshape(-1, 2 * E).astype(jnp.bfloat16)
    bc_low = grad_bc.reshape(-1, 2 * N).astype(jnp.bfloat16)
    dt_low = grad_dtraw.reshape(-1, H).astype(jnp.bfloat16)
    zx_weight_grad = contract_rows(normed_low, zx_low)
    bc_weight_grad = contract_rows(normed_low, bc_low)
    dt_weight_grad = contract_rows(normed_low, dt_low)
    normed_grad = (
        contract_cols(zx_low, zx_full)
        + contract_cols(bc_low, bc_full)
        + contract_cols(dt_low, dt_full)
    )
    grad_x_rows, grad_norm = norm_back(normed_grad)
    input_grad = cot_rows + grad_x_rows
    out_shard = share_out(out_grad)
    row_shards = (
        lax.psum_scatter(grad_norm, "seq", scatter_dimension=0, tiled=True),
        lax.psum_scatter(zx_weight_grad, "seq", scatter_dimension=0, tiled=True),
        lax.psum_scatter(bc_weight_grad, "seq", scatter_dimension=0, tiled=True),
        lax.psum_scatter(dt_weight_grad, "seq", scatter_dimension=0, tiled=True),
        lax.psum_scatter(grad_convw, "seq", scatter_dimension=0, tiled=True),
        lax.psum_scatter(grad_convb, "seq", scatter_dimension=0, tiled=True),
        lax.psum_scatter(grad_dtbias, "seq", scatter_dimension=0, tiled=True),
        lax.psum_scatter(grad_alog, "seq", scatter_dimension=0, tiled=True),
        lax.psum_scatter(grad_skip, "seq", scatter_dimension=0, tiled=True),
        lax.psum_scatter(grad_gain, "seq", scatter_dimension=0, tiled=True),
    )
    summed = lax.psum(
        (
            row_shards[0],
            row_shards[1],
            row_shards[2],
            row_shards[3],
            row_shards[4],
            row_shards[5],
            row_shards[6],
            row_shards[7],
            row_shards[8],
            row_shards[9],
            out_shard,
        ),
        "width",
    )
    return (
        output,
        input_grad,
        summed[0],
        summed[1],
        summed[2],
        summed[3],
        summed[4],
        summed[5],
        summed[6],
        summed[7],
        summed[8],
        summed[9],
        summed[10],
    )


def solution(mesh):
    in_specs = (
        P(("width", "seq"), None),
        P(("width", "seq"), None),
        P(("width", "seq"), None),
        P(("width", "seq"), None),
        P(),
        P("seq", None),
        P("seq", None),
        P("seq", None),
        P(),
        P(),
        P(),
        P(),
        P(),
        P(),
        P("seq", None),
    )
    out_specs = (
        P(("width", "seq"), None),
        P(("width", "seq"), None),
        P("seq"),
        P("seq", None),
        P("seq", None),
        P("seq", None),
        P("seq", None),
        P("seq"),
        P("seq"),
        P("seq"),
        P("seq"),
        P("seq"),
        P("seq", None),
    )
    body = heads_body if H % (2 * mesh.shape["seq"]) == 0 else rows_body
    return jax.shard_map(body, mesh=mesh, in_specs=in_specs, out_specs=out_specs, check_vma=False)
```

```python
from functools import partial

import jax
import jax.numpy as jnp
from jax import lax
from jax.experimental import pallas as pl
from jax.experimental.pallas import tpu as pltpu
from jax.sharding import PartitionSpec as P
import numpy as np

H = 64
HEAD_DIM = 64
N = 128
KCONV = 4
BLOCK = 128
E = 4096
SUB = 8

epsilon = 1e-05
highest = lax.Precision.HIGHEST
f32 = jnp.float32
bf16 = jnp.bfloat16

NN = ((1,), (0,))
NT = ((1,), (1,))
TN = ((0,), (0,))


def mm(left, right, dims=NN, precision=None):
    return lax.dot_general(left, right, (dims, ((), ())), precision=precision, preferred_element_type=f32)


def split2(value):
    high = value.astype(bf16)
    return high, (value - high.astype(f32)).astype(bf16)


def mm_right(left, right, dims=NN):
    high, low = split2(right)
    return mm(left, high, dims) + mm(left, low, dims)


def mm_left(left, right, dims=NN):
    high, low = split2(left)
    return mm(high, right, dims) + mm(low, right, dims)


def softplus(v):
    small = jnp.exp(-jnp.abs(v))
    log1p = jnp.where(small < 1e-4, small - 0.5 * small * small, jnp.log(1.0 + small))
    return jnp.maximum(v, 0.0) + log1p


def sigmoid(v):
    return 1.0 / (1.0 + jnp.exp(-v))


def grids():
    row = lax.broadcasted_iota(jnp.int32, (BLOCK, BLOCK), 0)
    col = lax.broadcasted_iota(jnp.int32, (BLOCK, BLOCK), 1)
    return row, col


def halves(pair, lane):
    zero = jnp.zeros_like(pair)
    return jnp.where(lane < HEAD_DIM, pair, zero), jnp.where(lane < HEAD_DIM, zero, pair)


def decay_of(cum, cum_t, head, causal):
    return jnp.exp(jnp.where(causal, cum[:, head : head + 1] - cum_t[head : head + 1, :], -1e30))


TAP, BIAS, SKIP, GAIN, MASK = 0, 4, 5, 6, 7
DT_BIAS, NEG_A, HEAD_MASK = 0, 1, 2


def forward_block(
    keep_row, zx_ref, chan_ref, bc_par_ref, head_ref, spread,
    conv_ref, mix_ref, bc_ref, step_ref, state_ref, tail_ref,
    state, tail_x, tail_b, pad_x, pad_b,
    *, lane, heads,
):
    width = heads * HEAD_DIM
    row, col = grids()
    causal = row >= col
    tril = causal.astype(f32)
    rows = pl.ds(lane * BLOCK, BLOCK)
    keep = jnp.concatenate([keep_row] * (width // BLOCK), axis=1)
    keep_b = jnp.concatenate([keep_row] * (2 * N // BLOCK), axis=1)

    pre = zx_ref[rows, width : 2 * width]
    before = tail_x[lane] * keep
    pad_x[lane, 0:SUB] = before
    pad_x[lane, SUB:] = pre
    tail_ref[lane] = before
    tail_x[lane] = pre[BLOCK - SUB :, :]
    conv = chan_ref[BIAS : BIAS + 1, :]
    for k in range(KCONV):
        conv = conv + pad_x[lane, SUB - KCONV + 1 + k : SUB - KCONV + 1 + k + BLOCK, :] * chan_ref[k : k + 1, :]
    conv_ref[rows, :] = conv
    x_low = (conv * sigmoid(conv) * chan_ref[MASK : MASK + 1, :]).astype(bf16)

    pre_b = zx_ref[rows, 2 * width + BLOCK :]
    pad_b[lane, 0:SUB] = tail_b[lane] * keep_b
    pad_b[lane, SUB:] = pre_b
    tail_b[lane] = pre_b[BLOCK - SUB :, :]
    conv_b = bc_par_ref[BIAS : BIAS + 1, :]
    for k in range(KCONV):
        conv_b = conv_b + pad_b[lane, SUB - KCONV + 1 + k : SUB - KCONV + 1 + k + BLOCK, :] * bc_par_ref[k : k + 1, :]
    bc_low = (conv_b * sigmoid(conv_b)).astype(bf16)
    bc_ref[rows, :] = bc_low
    b_low, c_low = bc_low[:, :N], bc_low[:, N:]

    raw = zx_ref[rows, 2 * width : 2 * width + BLOCK] + head_ref[DT_BIAS : DT_BIAS + 1, :]
    dt = softplus(raw) * head_ref[HEAD_MASK : HEAD_MASK + 1, :]
    cum = mm(tril, head_ref[NEG_A : NEG_A + 1, :] * dt, precision=highest)
    step_ref[rows, :BLOCK] = cum
    step_ref[rows, BLOCK:] = dt
    cum_t, dt_t = cum.T, dt.T
    last = cum[BLOCK - 1 :, :]
    carry_x = mm_left(jnp.exp(cum), spread)
    end_x = mm_left(jnp.exp(last - cum) * dt, spread)
    last_x = carry_x[BLOCK - 1 :, :]

    inner = mm(c_low, b_low, NT)
    parts = []
    for j in range(heads // 2):
        pair = x_low[:, 2 * HEAD_DIM * j : 2 * HEAD_DIM * (j + 1)]
        scores = [
            (inner * decay_of(cum, cum_t, h, causal) * dt_t[h : h + 1, :]).astype(bf16)
            for h in (2 * j, 2 * j + 1)
        ]
        parts.append(mm(jnp.concatenate(scores, axis=1), jnp.concatenate(halves(pair, col), axis=0)))
    within = jnp.concatenate(parts, axis=1)

    state_in = state[lane] * keep
    state_ref[lane] = state_in
    carried = mm_right(c_low, state_in) * carry_x
    x_f = x_low.astype(f32)
    mix_ref[rows, :] = within + carried + chan_ref[SKIP : SKIP + 1, :] * x_f
    weighted = (x_f * end_x).astype(bf16)
    state[lane] = last_x * state_in + mm(b_low, weighted, TN)


def backward_kernel(
    keep_ref, zx_ref, grad_ref, chan_ref, head_ref, spread_ref,
    conv_ref, mix_ref, bc_ref, step_ref, state_ref, tail_ref, scale_ref,
    dzx_ref, dbc_ref, dchan_ref, dhead_ref,
    state_grad, next_conv, pad_x, pad_d,
    *, lanes, heads, blocks,
):
    lap = pl.program_id(0)
    c = blocks - 1 - lap
    width = heads * HEAD_DIM
    row, col = grids()
    causal = row >= col
    triu = (col >= row).astype(f32)
    spread = spread_ref[...]

    @pl.when(lap == 0)
    def _():
        state_grad[...] = jnp.zeros_like(state_grad)
        next_conv[...] = jnp.zeros_like(next_conv)
        dchan_ref[...] = jnp.zeros_like(dchan_ref)
        dhead_ref[...] = jnp.zeros_like(dhead_ref)

    def total(value):
        return jnp.sum(value, axis=0, keepdims=True)

    for lane in range(lanes):
        rows = pl.ds(lane * BLOCK, BLOCK)
        keep = keep_ref[c, lane]
        z = zx_ref[rows, :width]
        conv = conv_ref[rows, :]
        mixed = mix_ref[rows, :]
        grad = grad_ref[rows, :]
        gain = chan_ref[GAIN : GAIN + 1, :]
        skip = chan_ref[SKIP : SKIP + 1, :]
        rate = scale_ref[rows, 0:1]
        pull = scale_ref[rows, 1:2]
        gate = sigmoid(z)
        silu = z * gate
        gated = mixed * silu
        dgated = grad * gain * rate - gated * pull
        dzx_ref[rows, :width] = (dgated * mixed * (gate * (1.0 + z * (1.0 - gate)))).astype(bf16)
        dmixed = dgated * silu
        act = sigmoid(conv)
        x_low = (conv * act * chan_ref[MASK : MASK + 1, :]).astype(bf16)
        x_f = x_low.astype(f32)
        dchan_ref[GAIN : GAIN + 1, :] += total(grad * gated * rate)
        dchan_ref[SKIP : SKIP + 1, :] += total(dmixed * x_f)
        dlow = dmixed.astype(bf16)
        dlow_f = dlow.astype(f32)

        b_low, c_low = bc_ref[rows, :N], bc_ref[rows, N:]
        cum, dt = step_ref[rows, :BLOCK], step_ref[rows, BLOCK:]
        cum_t, dt_t = cum.T, dt.T
        last = cum[BLOCK - 1 :, :]
        to_last = jnp.exp(last - cum)
        carry_x = mm_left(jnp.exp(cum), spread)
        end_x = mm_left(to_last * dt, spread)
        last_x = carry_x[BLOCK - 1 :, :]

        inner = mm(c_low, b_low, NT)
        dinner = jnp.zeros((BLOCK, BLOCK), f32)
        parts, dt_rows = [], []
        for j in range(heads // 2):
            lanes_j = slice(2 * HEAD_DIM * j, 2 * HEAD_DIM * (j + 1))
            pair, dpair = x_low[:, lanes_j], dlow[:, lanes_j]
            dstack = jnp.concatenate(halves(dpair, col), axis=0)
            dscores = mm(dstack, pair, NT)
            scores = []
            for i, h in enumerate((2 * j, 2 * j + 1)):
                decay = decay_of(cum, cum_t, h, causal)
                step = dt_t[h : h + 1, :]
                scores.append((inner * decay * step).astype(bf16))
                part = dscores[i * BLOCK : (i + 1) * BLOCK] * decay
                dinner = dinner + part * step
                dt_rows.append(total(part * inner))
            parts.append(mm(jnp.concatenate(scores, axis=0), dstack, TN))
        dx_within = jnp.concatenate(parts, axis=1)
        dt_rows.append(jnp.zeros((BLOCK - heads, BLOCK), f32))
        ddt_within = jnp.concatenate(dt_rows, axis=0).T

        state_in = state_ref[0, lane]
        sgrad = state_grad[lane]
        in_high, in_low = split2(state_in)
        sg_high, sg_low = split2(sgrad)
        dcarry = dlow_f * carry_x
        dc_high, dc_low = split2(dcarry)
        di_high, di_low = split2(dinner)
        dc = mm(dc_high, in_high, NT) + mm(dc_high, in_low, NT) + mm(dc_low, in_high, NT)
        dc = dc + mm(di_high, b_low) + mm(di_low, b_low)
        weighted = (x_f * end_x).astype(bf16)
        db = mm(weighted, sg_high, NT) + mm(weighted, sg_low, NT)
        db = db + mm(di_high, c_low, TN) + mm(di_low, c_low, TN)
        dbc_ref[:N, rows] = db.T.astype(bf16)
        dbc_ref[N:, rows] = dc.T.astype(bf16)
        dweighted = mm(b_low, sg_high) + mm(b_low, sg_low)
        dx = dx_within + dweighted * end_x
        dcum = mm_left(dlow_f * (mixed - skip * x_f) - x_f * dx, spread, NT)
        dend = mm_left(dweighted * x_f, spread, NT)
        touch = jnp.broadcast_to(total(sgrad * state_in), (SUB, width))
        dlast = total(dend * to_last * dt) + jnp.exp(last) * mm_left(touch, spread, NT)[0:1]
        dlog = mm(triu, dcum, precision=highest) + dlast
        neg_a = head_ref[NEG_A : NEG_A + 1, :]
        ddt = ddt_within + dend * to_last + dlog * neg_a
        raw = zx_ref[rows, 2 * width : 2 * width + BLOCK] + head_ref[DT_BIAS : DT_BIAS + 1, :]
        draw = ddt * sigmoid(raw) * head_ref[HEAD_MASK : HEAD_MASK + 1, :]
        dzx_ref[rows, 2 * width :] = draw.astype(bf16)
        dhead_ref[0:1, :] += total(draw)
        dhead_ref[1:2, :] += total(dlog * neg_a * dt)
        state_grad[lane] = keep * (mm(c_low, dc_high, TN) + mm(c_low, dc_low, TN) + last_x * sgrad)

        dx = dx + skip * dmixed
        dconv = dx * chan_ref[MASK : MASK + 1, :] * (act * (1.0 + conv * (1.0 - act)))
        pad_d[lane, :BLOCK] = dconv
        pad_d[lane, BLOCK:] = next_conv[lane]
        next_conv[lane] = dconv[:SUB] * keep
        pad_x[lane, :SUB] = tail_ref[0, lane]
        pad_x[lane, SUB:] = zx_ref[rows, width : 2 * width]
        dpre = jnp.zeros((BLOCK, width), f32)
        for k in range(KCONV):
            dpre = dpre + pad_d[lane, KCONV - 1 - k : KCONV - 1 - k + BLOCK, :] * chan_ref[k : k + 1, :]
            dchan_ref[k : k + 1, :] += total(dconv * pad_x[lane, SUB - KCONV + 1 + k : SUB - KCONV + 1 + k + BLOCK, :])
        dchan_ref[BIAS : BIAS + 1, :] += total(dconv)
        dzx_ref[rows, width : 2 * width] = dpre.astype(bf16)


def run_backward(keep, zx, grad, chan, head, spread, conv, mix, bc, step_arr, state, tail, scale, lanes, heads):
    rows, width = grad.shape
    step = lanes * BLOCK
    blocks = rows // step
    by_block = lambda cols: pl.BlockSpec((step, cols), lambda c: (blocks - 1 - c, 0))
    whole = lambda a: pl.BlockSpec(a.shape, lambda c: (0,) * a.ndim)
    fixed = lambda shape: pl.BlockSpec(shape, lambda c: (0,) * len(shape))
    per_lane = lambda r, cols: pl.BlockSpec((1, lanes, r, cols), lambda c: (blocks - 1 - c, 0, 0, 0))
    return pl.pallas_call(
        partial(backward_kernel, lanes=lanes, heads=heads, blocks=blocks),
        grid=(blocks,),
        in_specs=[
            pl.BlockSpec(memory_space=pltpu.SMEM), by_block(2 * width + BLOCK), by_block(width),
            whole(chan), whole(head), whole(spread),
            by_block(width), by_block(width), by_block(2 * N), by_block(2 * BLOCK),
            per_lane(N, width), per_lane(SUB, width), by_block(BLOCK),
        ],
        out_specs=[
            by_block(2 * width + BLOCK), pl.BlockSpec((2 * N, step), lambda c: (0, blocks - 1 - c)),
            fixed((SUB, width)), fixed((SUB, BLOCK)),
        ],
        out_shape=[
            jax.ShapeDtypeStruct((rows, 2 * width + BLOCK), bf16),
            jax.ShapeDtypeStruct((2 * N, rows), bf16), jax.ShapeDtypeStruct((SUB, width), f32),
            jax.ShapeDtypeStruct((SUB, BLOCK), f32),
        ],
        scratch_shapes=[
            pltpu.VMEM((lanes, N, width), f32), pltpu.VMEM((lanes, SUB, width), f32),
            pltpu.VMEM((lanes, BLOCK + SUB, width), f32), pltpu.VMEM((lanes, BLOCK + SUB, width), f32),
        ],
        compiler_params=pltpu.CompilerParams(vmem_limit_bytes=48 << 20, dimension_semantics=("arbitrary",)),
        cost_estimate=pl.CostEstimate(flops=rows * width * 6144, bytes_accessed=rows * width * 40, transcendentals=rows * width * 6),
        name="mix_backward",
    )(keep, zx, grad, chan, head, spread, conv, mix, bc, step_arr, state, tail, scale)


MESH = pl.DeviceIdType.MESH


def greet(others):
    for other in others:
        pl.semaphore_signal(pltpu.get_barrier_semaphore(), inc=1, device_id=other, device_id_type=MESH)


def met(others):
    pl.semaphore_wait(pltpu.get_barrier_semaphore(), len(others))


def remote(src, dst, send, recv, device):
    return pltpu.make_async_remote_copy(
        src_ref=src, dst_ref=dst, send_sem=send, recv_sem=recv, device_id=device, device_id_type=MESH
    )


class Rows:
    def __init__(self, own_ref, all_ref, sems, peers):
        self.own, self.all, self.sems, self.peers = own_ref, all_ref, sems, peers
        self.width, self.place = lax.axis_index("width"), lax.axis_index("seq")
        self.chips, self.chip = peers // 2, self.place // 2

    def hop(self, ref, s, step, by):
        send, recv = self.sems[0 if by > 0 else 2], self.sems[1 if by > 0 else 3]
        device = (self.width, jnp.clip(self.place + 2 * by, 0, self.peers - 1))
        return remote(ref, self.all.at[s], send.at[step], recv.at[step], device)

    def over(self, ref, s, slot):
        device = (self.width, jnp.bitwise_xor(self.place, 1))
        return remote(ref, self.all.at[s], self.sems[4].at[slot], self.sems[5].at[slot], device)

    def inside(self, by):
        return self.chip + 1 < self.chips if by > 0 else self.chip > 0

    def reached(self, by, step):
        return self.chip >= step if by > 0 else self.chip + step < self.chips

    def source(self, by, step):
        return jnp.clip(self.place - 2 * by * step, 0, self.peers - 1)

    def keep(self):
        return pltpu.make_async_copy(self.own, self.all.at[self.place], self.sems[6])

    def start(self):
        self.keep().start()
        for by in (1, -1):
            @pl.when(self.inside(by))
            def _():
                self.hop(self.own, self.place, 0, by).start()
        self.over(self.own, self.place, 0).start()

    def pass_on(self, step):
        for by in (1, -1):
            @pl.when(self.reached(by, step))
            def _():
                s = self.source(by, step)
                ref = self.all.at[s]
                self.hop(ref, s, step - 1, by).wait_recv()

                @pl.when(self.inside(by))
                def _():
                    self.hop(ref, s, step, by).start()
                self.over(ref, s, 2 * step - (by > 0)).start()

    def mate(self, by, step):
        if not step:
            return self.over(self.own, self.place, 0)
        s = self.source(by, step)
        return self.over(self.all.at[s], s, 2 * step - (by > 0))

    def arrived(self):
        self.keep().wait()
        self.mate(1, 0).wait_recv()
        for step in range(1, self.chips):
            for by in (1, -1):
                @pl.when(self.reached(by, step))
                def _():
                    self.mate(by, step).wait_recv()

    def sent(self):
        for step in range(self.chips):
            for by in (1, -1):
                @pl.when(self.inside(by) & self.reached(by, step))
                def _():
                    s = self.source(by, step)
                    self.hop(self.all.at[s], s, step, by).wait_send()
        self.mate(1, 0).wait_send()
        for step in range(1, self.chips):
            for by in (1, -1):
                @pl.when(self.reached(by, step))
                def _():
                    self.mate(by, step).wait_send()


ROW_SEMS = 7


def row_sems(chips):
    dma = pltpu.SemaphoreType.DMA
    return [dma((chips,)), dma((chips,)), dma((chips,)), dma((chips,)), dma((2 * chips,)), dma((2 * chips,)), dma(())]


def front_kernel(
    valid_ref, start_ref, x_ref, cot_ref, norm_gain_ref, bc_ref, dt_ref, taps_ref, bias_ref, dtb_ref, alog_ref, skip_ref,
    gain_ref, spread_ref, zx_ref, wout_ref,
    w_ref, rows_ref, grads_ref, starts_ref, chan_ref, head_ref,
    out_zx, out_mix, out_grad, out_scale, out_low, out_part, out_conv, out_bc, out_step, out_state, out_tail,
    w_v, rows_v, starts_v, wout_v, own_v, grad_v, third_v, start_v, bc_par,
    zx_v, mix_v, mgrad_v, scale_v, low_v, conv_v, bc_v, step_v, state_v, tail_v, sums, sums_got,
    state, tail_x, tail_b, pad_x, pad_b,
    w_send, w_recv, st_send, st_recv, own_sem, wide_send, wide_recv, in_sem, out_sem, slot_sem, sum_send, sum_recv, *sems,
    peers, widths, lanes, heads,
):
    width, place = lax.axis_index("width"), lax.axis_index("seq")
    chips = peers // 2
    chans = heads * HEAD_DIM
    quarter = zx_ref.shape[0] // widths
    ring = [lax.rem(place + by, peers) for by in range(1, peers)]
    cross = [jnp.bitwise_xor(width, m) for m in range(1, widths)]
    others = [(width, s) for s in ring] + [(w, place) for w in cross]
    greet(others)

    x = x_ref[...].astype(f32)
    own_v[...] = (x * lax.rsqrt(jnp.mean(x * x, axis=-1, keepdims=True) + epsilon) * norm_gain_ref[...]).astype(bf16)
    row = lax.broadcasted_iota(jnp.int32, (BLOCK, 1), 0)
    sub = lax.broadcasted_iota(jnp.int32, (SUB, BLOCK), 0)
    tile = jnp.zeros((SUB, BLOCK), f32)
    for lane in range(lanes):
        at = slice(lane * BLOCK, (lane + 1) * BLOCK)
        mask = (row < valid_ref[0, lane]).astype(f32)
        grad_v[at, :] = (cot_ref[at, :].astype(f32) * mask).astype(bf16)
        tile = jnp.where(sub == lane, start_ref[0, lane].astype(f32), tile)
    start_v[...] = tile
    bc, dt = bc_ref[...].astype(f32), dt_ref[...].astype(f32)
    share = bc.shape[1] // peers
    rest = jnp.zeros((bc.shape[0], BLOCK - share - heads), f32)
    for s in range(peers):
        columns = [dt[:, s * heads : (s + 1) * heads], bc[:, s * share : (s + 1) * share], rest]
        third_v[s] = jnp.concatenate(columns, axis=1).astype(bf16)
    met(others)

    mine = pl.ds(pl.multiple_of(width * quarter, quarter), quarter)
    rows = Rows(own_v, rows_ref, sems[:ROW_SEMS], peers)
    grads = Rows(grad_v, grads_ref, sems[ROW_SEMS:], peers)

    def columns_of(half, s):
        return pl.ds(pl.multiple_of(half * peers * chans + s * chans, 128), chans)

    wide = 2 * chans
    spots = [pl.ds(0, chans), pl.ds(chans, chans), pl.ds(wide, BLOCK), pl.ds(wide + BLOCK, 2 * N)]

    def parts(s):
        return [zx_ref.at[mine, columns_of(0, s)], zx_ref.at[mine, columns_of(1, s)], third_v.at[s, mine], bc_ref.at[mine]]

    pushes = []
    for i, s in enumerate(ring):
        for k, (part, spot) in enumerate(zip(parts(s), spots)):
            pushes.append(remote(part, w_ref.at[place, width, :, spot], w_send.at[k, i], w_recv.at[k, i], (width, s)))
        pushes.append(remote(start_v, starts_ref.at[place], st_send.at[i], st_recv.at[i], (width, s)))
    for push in pushes:
        push.start()
    keeps = [
        pltpu.make_async_copy(part, w_ref.at[place, width, :, spot], own_sem.at[k])
        for k, (part, spot) in enumerate(zip(parts(place), spots))
    ]
    keeps.append(pltpu.make_async_copy(start_v, starts_ref.at[place], own_sem.at[4]))
    for keep in keeps:
        keep.start()
    rows.start()

    active = jnp.right_shift(jnp.int32(H), widths - 1 - width)
    first = place * heads
    here = columns_of(0, place)
    spread = spread_ref[...]
    pick_row = lax.broadcasted_iota(jnp.int32, (H, BLOCK), 0)
    pick_lane = lax.broadcasted_iota(jnp.int32, (H, BLOCK), 1)
    chosen = ((pick_row == pick_lane + first) & (pick_lane < heads)).astype(f32)
    per_head = jnp.concatenate(
        [dtb_ref[...], -jnp.exp(alog_ref[...]), jnp.ones((1, H), f32), skip_ref[...], jnp.zeros((SUB - 4, H), f32)], axis=0
    )
    per_head = mm(per_head, chosen, precision=highest)
    head_lane = lax.broadcasted_iota(jnp.int32, (SUB, BLOCK), 1)
    head_ref[...] = jnp.where((sub == HEAD_MASK) & (head_lane + first >= active), 0.0, per_head)
    on_chans = mm(head_ref[...], spread.astype(f32), precision=highest)
    chan_ref[...] = jnp.concatenate(
        [taps_ref[:, here], bias_ref[:, here], on_chans[3:4], gain_ref[:, here], on_chans[HEAD_MASK : HEAD_MASK + 1]], axis=0
    )
    bc_par[...] = jnp.concatenate(
        [taps_ref[:, E:], bias_ref[:, E:], jnp.zeros((SUB - KCONV - 1, 2 * N), f32)], axis=0
    )

    for push in pushes:
        push.wait_recv()
    for keep in keeps:
        keep.wait()
    shares = [
        remote(w_ref.at[:, width], w_ref.at[:, width], wide_send.at[m], wide_recv.at[m], (w, place)) for m, w in enumerate(cross)
    ]
    for copy in shares:
        copy.start()
    for step in range(1, chips - 1):
        rows.pass_on(step)
    grads.start()
    for copy in shares:
        copy.wait_recv()
    in_w = pltpu.make_async_copy(w_ref, w_v, own_sem.at[0])
    in_starts = pltpu.make_async_copy(starts_ref, starts_v, own_sem.at[1])
    in_wout = pltpu.make_async_copy(wout_ref, wout_v, own_sem.at[2])
    for copy in (in_w, in_starts, in_wout):
        copy.start()
    rows.pass_on(chips - 1)
    rows.arrived()

    def load(src, s):
        return pltpu.make_async_copy(src.at[s], rows_v.at[s], in_sem.at[s])

    for c in range(peers):
        load(rows_ref, c).start()
    for array in (state, tail_x, tail_b):
        array[...] = jnp.zeros_like(array)
    for copy in (in_w, in_starts, in_wout):
        copy.wait()

    def out_copy(k, src, dst, c):
        return pltpu.make_async_copy(src.at[c], dst.at[c], out_sem.at[k, c])

    slots = [(conv_v, out_conv), (bc_v, out_bc), (step_v, out_step), (state_v, out_state), (tail_v, out_tail)]

    def slot_copies(c):
        slot = lax.rem(c, 2)
        return [pltpu.make_async_copy(src.at[slot], dst.at[c], slot_sem.at[k, slot]) for k, (src, dst) in enumerate(slots)]

    def compute(begin, end):
        @pl.loop(begin, end)
        def _(c):
            load(rows_ref, c).wait()

            @pl.when(c >= 2)
            def _():
                for copy in slot_copies(c - 2):
                    copy.wait()
            weights = w_v[...].reshape(w_v.shape[0] * w_v.shape[1] * w_v.shape[2], w_v.shape[3])
            zx_v[c] = mm(rows_v[c], weights)
            slot = lax.rem(c, 2)
            for lane in range(lanes):
                forward_block(
                    1.0 - starts_v[c, lane : lane + 1, :], zx_v.at[c], chan_ref, bc_par, head_ref, spread_ref[...],
                    conv_v.at[slot], mix_v.at[c], bc_v.at[slot], step_v.at[slot], state_v.at[slot], tail_v.at[slot],
                    state, tail_x, tail_b, pad_x, pad_b, lane=lane, heads=heads,
                )
            out_copy(0, zx_v, out_zx, c).start()
            out_copy(1, mix_v, out_mix, c).start()
            for copy in slot_copies(c):
                copy.start()

    def gated_of(c):
        z = zx_v[c, :, :chans]
        return mix_v[c] * (z * sigmoid(z))

    def mix_grad(s):
        load(grads_ref, s).wait()
        grad = mm(rows_v[s], wout_v[...], NT)
        mgrad_v[s] = grad
        out_copy(2, mgrad_v, out_grad, s).start()
        gated = gated_of(s)
        ones = jnp.ones((SUB, chans), bf16)
        square = mm_right(ones, gated * gated, NT)
        pulled = mm_right(ones, grad * chan_ref[GAIN : GAIN + 1, :] * gated, NT)
        for lane in range(lanes):
            at = slice(lane * BLOCK, (lane + 1) * BLOCK)
            sums[0, pl.ds(s * lanes + lane, 1), :] = square[:1, at]
            sums[1, pl.ds(s * lanes + lane, 1), :] = pulled[:1, at]

    per = -(-peers // 2)
    for step in range(1, chips):
        begin, end = min((step - 1) * per, peers), min(step * per, peers)
        if step == chips - 1:
            end = peers
        if begin < end:
            compute(begin, end)
        if step < chips - 1:
            grads.pass_on(step)

    def at_distance(step, act):
        if not step:
            act(place, None)
            act(jnp.bitwise_xor(place, 1), (1, 0))
        for by in (1, -1):
            if step:
                @pl.when(grads.reached(by, step))
                def _():
                    s = grads.source(by, step)
                    act(s, None)
                    act(jnp.bitwise_xor(s, 1), (by, step))

    def begin_load(s, mate):
        if mate is not None:
            grads.mate(*mate).wait_recv()
        load(grads_ref, s).start()

    grads.keep().wait()
    for step in range(chips - 1):
        at_distance(step, begin_load)
    for step in range(chips - 1):
        at_distance(step, lambda s, mate: mix_grad(s))
    grads.pass_on(chips - 1)
    at_distance(chips - 1, begin_load)
    at_distance(chips - 1, lambda s, mate: mix_grad(s))

    give = [remote(sums, sums_got.at[i], sum_send.at[i], sum_recv.at[i], (width, s)) for i, s in enumerate(ring)]
    for copy in give:
        copy.start()
    for copy in give:
        copy.wait_recv()
    total = sums[...]
    for i in range(peers - 1):
        total = total + sums_got[i]
    count = (active * HEAD_DIM).astype(f32)
    rate = lax.rsqrt(total[0] / count + epsilon)
    pull = rate * rate * rate * total[1] / count
    blank = jnp.zeros((BLOCK - 2 * lanes * peers, BLOCK), f32)
    by_time = jnp.concatenate([rate, pull, blank], axis=0).T
    lane_at = lax.broadcasted_iota(jnp.int32, (BLOCK, BLOCK), 1)
    for c in range(peers):
        for lane in range(lanes):
            i = c * lanes + lane
            j = lanes * peers + i
            scale_v[c, lane * BLOCK : (lane + 1) * BLOCK, :] = jnp.where(
                lane_at == 0, by_time[:, i : i + 1], jnp.where(lane_at == 1, by_time[:, j : j + 1], 0.0)
            )

    @pl.loop(0, peers)
    def _(c):
        low = (gated_of(c) * scale_v[c, :, 0:1] * chan_ref[GAIN : GAIN + 1, :]).astype(bf16)
        low_v[c] = low
        rows_v[c] = mm(low, wout_v[...]).astype(bf16)
        out_copy(3, scale_v, out_scale, c).start()
        out_copy(4, low_v, out_low, c).start()
        out_copy(5, rows_v, out_part, c).start()

    for copy in shares + pushes + give:
        copy.wait_send()
    rows.sent()
    grads.sent()
    for c in (peers - 2, peers - 1):
        for copy in slot_copies(c):
            copy.wait()

    @pl.loop(0, peers)
    def _(c):
        for k, (src, dst) in enumerate(
            [(zx_v, out_zx), (mix_v, out_mix), (mgrad_v, out_grad), (scale_v, out_scale), (low_v, out_low), (rows_v, out_part)]
        ):
            out_copy(k, src, dst, c).wait()


def front(valid, starts, tokens, cotangent, norm_gain, w_bc, w_dt, taps, bias, dt_bias, a_log, d_skip, gate_gain, spread, w_zx, w_out):
    peers, widths = lax.axis_size("seq"), lax.axis_size("width")
    own, model = tokens.shape
    lanes = starts.shape[1]
    quarter = own // widths
    chans = w_out.shape[0]
    heads = chans // HEAD_DIM
    cols = 2 * chans + BLOCK + 2 * N
    dma = pltpu.SemaphoreType.DMA
    anywhere, vmem = pl.BlockSpec(memory_space=pl.ANY), pl.BlockSpec(memory_space=pltpu.VMEM)
    smem = pl.BlockSpec(memory_space=pltpu.SMEM)
    w_all = ((peers, widths, quarter, cols), bf16)
    rows_all = ((peers, own, model), bf16)
    starts_all = ((peers, SUB, BLOCK), f32)
    per_chan, low = ((peers, own, chans), f32), ((peers, own, chans), bf16)
    whole = [((peers, own, cols), f32), per_chan, per_chan, ((peers, own, BLOCK), f32), low]
    streamed = [
        ((own, chans), f32), ((own, 2 * N), bf16), ((own, 2 * BLOCK), f32), ((lanes, N, chans), f32), ((lanes, SUB, chans), f32)
    ]
    outs = [w_all, rows_all, rows_all, starts_all, ((SUB, chans), f32), ((SUB, BLOCK), f32), *whole, rows_all]
    outs += [((peers,) + a[0], a[1]) for a in streamed]
    scratch = [w_all, rows_all, starts_all, ((chans, model), bf16), ((own, model), bf16), ((own, model), bf16)]
    scratch += [((peers, own, BLOCK), bf16), ((SUB, BLOCK), f32), ((SUB, 2 * N), f32), *whole]
    scratch += [((2,) + a[0], a[1]) for a in streamed]
    scratch += [((2, peers * lanes, BLOCK), f32), ((peers - 1, 2, peers * lanes, BLOCK), f32)]
    scratch += [((lanes, N, chans), f32), ((lanes, SUB, chans), f32), ((lanes, SUB, 2 * N), f32)]
    scratch += [((lanes, BLOCK + SUB, chans), f32), ((lanes, BLOCK + SUB, 2 * N), f32)]
    return pl.pallas_call(
        partial(front_kernel, peers=peers, widths=widths, lanes=lanes, heads=heads),
        in_specs=[smem] * 2 + [vmem] * 12 + [anywhere] * 2,
        out_specs=[anywhere] * 4 + [vmem] * 2 + [anywhere] * 11,
        out_shape=[jax.ShapeDtypeStruct(*a) for a in outs],
        scratch_shapes=[
            *[pltpu.VMEM(*a) for a in scratch],
            dma((4, peers - 1)), dma((4, peers - 1)), dma((peers - 1,)), dma((peers - 1,)),
            dma((5,)), dma((widths - 1,)), dma((widths - 1,)), dma((peers,)), dma((6, peers)), dma((5, 2)),
            dma((peers - 1,)), dma((peers - 1,)),
            *row_sems(peers // 2), *row_sems(peers // 2),
        ],
        compiler_params=pltpu.CompilerParams(collective_id=1, has_side_effects=True, vmem_limit_bytes=62 << 20),
        name="front",
    )(valid, starts, tokens, cotangent, norm_gain, w_bc, w_dt, taps, bias, dt_bias, a_log, d_skip, gate_gain, spread, w_zx, w_out)


ROWS_AT_ONCE = 16


def add_into(dst, others, rows):
    @pl.loop(0, rows // ROWS_AT_ONCE)
    def _(i):
        at = pl.ds(pl.multiple_of(i * ROWS_AT_ONCE, ROWS_AT_ONCE), ROWS_AT_ONCE)
        value = dst[at].astype(f32)
        for other in others:
            value = value + other[at].astype(f32)
        dst[at] = value.astype(dst.dtype)


def bc_back(dbc, pre, par_ref, keep, keep_next):
    chans, times = pre.shape
    in_block = lax.rem(lax.broadcasted_iota(jnp.int32, (chans, times), 1), BLOCK)
    conv = jnp.broadcast_to(par_ref[:, BIAS : BIAS + 1], (chans, times))
    shifted = []
    for j in range(KCONV):
        moved = pre
        if j:
            moved = jnp.where(in_block >= j, pltpu.roll(pre, j, 1), keep * pltpu.roll(pre, BLOCK + j, 1))
        shifted.append(moved)
        conv = conv + moved * par_ref[:, KCONV - 1 - j : KCONV - j]
    act = sigmoid(conv)
    dconv = dbc * (act * (1.0 + conv * (1.0 - act)))
    dpre = dconv * par_ref[:, KCONV - 1 : KCONV]
    lane = lax.broadcasted_iota(jnp.int32, (chans, BLOCK), 1)
    dpar = jnp.where(lane == BIAS, jnp.sum(dconv, axis=1, keepdims=True), 0.0)
    for j in range(KCONV):
        dpar = dpar + jnp.where(lane == KCONV - 1 - j, jnp.sum(dconv * shifted[j], axis=1, keepdims=True), 0.0)
        if j:
            back = jnp.where(
                in_block < BLOCK - j, pltpu.roll(dconv, times - j, 1), keep_next * pltpu.roll(dconv, times - BLOCK - j, 1)
            )
            dpre = dpre + back * par_ref[:, KCONV - 1 - j : KCONV - j]
    return dpre, dpar


def scatter_kernel(
    got_ref, zx_ref, dzx_ref, w_ref, normed_ref, wide_ref, par_ref, keep_ref, small_ref, x_ref, cot_ref, gain_ref,
    rows_ref, out_ref, out_third_ref,
    got_v, pre_v, dz_v, w_v, normed_v, third_t, third_g,
    mine, to_mate, from_core, up, down, own0, own1, own2, got0, got1, got2, piece0, piece1, piece2,
    load_sem, core_send, core_recv, up_send, up_recv, down_send, down_recv,
    own_sem, q_send, q_recv, p_send, p_recv, o_send, o_recv,
    *, peers, widths, heads,
):
    width, place = lax.axis_index("width"), lax.axis_index("seq")
    chips = peers // 2
    chip, core = place // 2, lax.rem(place, 2)
    mate = (width, jnp.bitwise_xor(place, 1))
    ring = [lax.rem(place + by, peers) for by in range(1, peers)]
    cross = [jnp.bitwise_xor(width, m) for m in range(1, widths)]
    others = [(width, s) for s in ring] + [(w, place) for w in cross]
    greet(others)
    half = wide_ref.shape[3] // 2
    wide = 2 * half
    own = mine.shape[1]
    share, times = got_v.shape[1], got_v.shape[2]
    loads = [
        pltpu.make_async_copy(src, dst, load_sem.at[k])
        for k, (src, dst) in enumerate([
            (got_ref, got_v), (zx_ref.at[:, :, wide : wide + BLOCK], pre_v), (dzx_ref, dz_v), (w_ref, w_v), (normed_ref, normed_v)
        ])
    ]
    for load in loads:
        load.start()
    met(others)

    strip = third_g.shape[0] // widths
    lanes_of = lambda s: pl.ds(pl.multiple_of(s * own, BLOCK), own)
    strip_of = lambda w: pl.ds(pl.multiple_of(w * strip, 16), strip)
    sets = [
        (lambda w: wide_ref.at[:, w, :, 0:half], own0, got0, lambda s: own0.at[s], piece0, lambda w: out_ref.at[:, w, :, 0:half]),
        (lambda w: wide_ref.at[:, w, :, half:wide], own1, got1, lambda s: own1.at[s], piece1, lambda w: out_ref.at[:, w, :, half:wide]),
        (lambda w: third_g.at[strip_of(w)], own2, got2, lambda s: own2.at[:, lanes_of(s)], piece2, lambda w: out_third_ref.at[:, w]),
    ]
    own_in, to_width = [None] * 3, [None] * 3

    def begin(k):
        part, kept, arrived = sets[k][:3]
        own_in[k] = pltpu.make_async_copy(part(width), kept, own_sem.at[0, k])
        to_width[k] = [
            remote(part(w), arrived.at[m], q_send.at[k, m], q_recv.at[k, m], (w, place)) for m, w in enumerate(cross)
        ]
        for copy in [own_in[k]] + to_width[k]:
            copy.start()

    begin(0)
    begin(1)

    def flow(by):
        return (up, up_send, up_recv) if by > 0 else (down, down_send, down_recv)

    def sends(by, step):
        far = chips - step
        return chip + far < chips if by > 0 else chip >= far

    def later(by):
        return chip > 0 if by > 0 else chip + 1 < chips

    def hop(src, by, step):
        buffer, send, recv = flow(by)
        return remote(
            src, buffer.at[step - 1], send.at[step - 1], recv.at[step - 1], (width, jnp.clip(place + 2 * by, 0, peers - 1))
        )

    def staged(by, step):
        return flow(by)[0].at[step - 2]

    def run_hops(step):
        for by in (1, -1):
            owner = jnp.clip(chip + by * (chips - step), 0, chips - 1)

            def direct():
                hop(mine.at[owner], by, step).start()

            def relayed():
                hop(staged(by, step), by, step - 1).wait_recv()
                add_into(staged(by, step), [mine.at[owner]], own)
                hop(staged(by, step), by, step).start()

            if step == 1:
                pl.when(sends(by, step))(direct)
            else:
                pl.when(sends(by, step) & jnp.logical_not(later(by)))(direct)
                pl.when(sends(by, step) & later(by))(relayed)

    to_owner, to_all, kept_piece = [None] * 3, [None] * 3, [None] * 3

    def exchange(k):
        part, kept, arrived, piece_of, piece, out = sets[k]
        own_in[k].wait()
        for copy in to_width[k]:
            copy.wait_recv()
        if kept.ndim == 3:
            for s in range(peers):
                add_into(kept.at[s], [arrived.at[m, s] for m in range(widths - 1)], kept.shape[1])
        else:
            add_into(kept, [arrived.at[m] for m in range(widths - 1)], kept.shape[0])
        to_owner[k] = [
            remote(piece_of(s), piece.at[place], p_send.at[k, i], p_recv.at[k, i], (width, s)) for i, s in enumerate(ring)
        ]
        kept_piece[k] = pltpu.make_async_copy(piece_of(place), piece.at[place], own_sem.at[1, k])
        for copy in to_owner[k] + [kept_piece[k]]:
            copy.start()

    def spread(k):
        piece, out = sets[k][4:]
        for copy in to_owner[k]:
            copy.wait_recv()
        kept_piece[k].wait()
        to_all[k] = [remote(piece, out(width), o_send.at[k, m], o_recv.at[k, m], (w, place)) for m, w in enumerate(cross)]
        to_all[k].append(pltpu.make_async_copy(piece, out(width), own_sem.at[2, k]))
        for copy in to_all[k]:
            copy.start()

    for load in loads[:3]:
        load.wait()
    dbc = got_v[0].astype(f32)
    for s in range(1, peers):
        dbc = dbc + got_v[s].astype(f32)
    block_rows = pre_v.shape[1]
    spots = [(c, slice(l * BLOCK, (l + 1) * BLOCK)) for c in range(peers) for l in range(block_rows // BLOCK)]
    pre = jnp.concatenate([pre_v[c, at, :].T[heads : heads + share] for c, at in spots], axis=1)
    dpre, dpar = bc_back(dbc, pre, par_ref, keep_ref[0:1, :], keep_ref[1:2, :])
    for i, (c, at) in enumerate(spots):
        tile = jnp.concatenate(
            [
                dz_v[c, at, wide:].astype(f32).T[:heads], dpre[:, i * BLOCK : (i + 1) * BLOCK],
                jnp.zeros((BLOCK - heads - share, BLOCK), f32),
            ],
            axis=0,
        )
        third_t[:, i * BLOCK : (i + 1) * BLOCK] = tile.astype(bf16)
        dz_v[c, at, wide:] = tile.T.astype(bf16)
    loads[3].wait()

    def partial_rows(s):
        weights = w_v[...].reshape(w_v.shape[0] * w_v.shape[1] * w_v.shape[2], w_v.shape[3])
        return mm(dz_v[s], weights[:, : wide + BLOCK], NT).astype(bf16)

    def order(i):
        return jnp.where(chip < chips // 2, chips - 1 - i, i)

    def over(q):
        return remote(to_mate.at[q], from_core.at[q], core_send.at[q], core_recv.at[q], mate)

    def whole_sum(q):
        over(q).wait_recv()
        add_into(mine.at[q], [from_core.at[q]], own)

    for i in range(chips):
        q = order(i)
        to_mate[q] = partial_rows(2 * q + 1 - core)
        over(q).start()
        mine[q] = partial_rows(2 * q + core)
        if i:
            whole_sum(order(i - 1))
        if i == 1:
            run_hops(1)
    whole_sum(order(chips - 1))

    loads[4].wait()
    small_at = heads + share
    used = small_at + small_ref.shape[0]
    par_rows = jnp.concatenate([dpar, jnp.zeros((BLOCK - share, BLOCK), f32)], axis=0).T[:SUB]
    par_rows = jnp.concatenate([par_rows, jnp.zeros((SUB, own - BLOCK), f32)], axis=1)
    grads = mm(third_t[...], normed_v[...].reshape(times, normed_v.shape[2]))
    tail = [jnp.zeros((third_g.shape[0] - used - SUB, third_g.shape[1]), f32)] if third_g.shape[0] > used + SUB else []
    third_g[...] = jnp.concatenate(
        [grads[:small_at], small_ref[...], jnp.concatenate([par_rows] * peers, axis=1), *tail], axis=0
    ).astype(bf16)
    begin(2)

    exchange(0)
    if chips > 2:
        run_hops(2)
    spread(0)
    exchange(1)
    exchange(2)
    for step in range(3, chips):
        run_hops(step)
    spread(1)
    spread(2)

    for by in (1, -1):
        @pl.when(later(by))
        def _():
            buffer = flow(by)[0].at[chips - 2]
            hop(buffer, by, chips - 1).wait_recv()
            add_into(mine.at[chip], [buffer], own)

    gain = gain_ref[...]

    @pl.loop(0, own // ROWS_AT_ONCE)
    def _(i):
        at = pl.ds(pl.multiple_of(i * ROWS_AT_ONCE, ROWS_AT_ONCE), ROWS_AT_ONCE)
        x = x_ref[at, :].astype(f32)
        rate = lax.rsqrt(jnp.mean(x * x, axis=-1, keepdims=True) + epsilon)
        unit = x * rate
        pulled = mine[chip, at].astype(f32) * gain
        inner = jnp.mean(pulled * unit, axis=-1, keepdims=True)
        rows_ref[at, :] = cot_ref[at, :].astype(f32) + rate * (pulled - unit * inner)

    for step in range(1, chips):
        for by in (1, -1):
            @pl.when(sends(by, step))
            def _():
                hop(mine.at[0], by, step).wait_send()
    for q in range(chips):
        over(q).wait_send()
    for k in range(len(sets)):
        for copy in to_width[k] + to_owner[k]:
            copy.wait_send()
        for copy in to_all[k]:
            copy.wait()


def scattered_out(got, zx, dzx, weights, normed, wide, par, keep, small, x_rows, cotangent, gain, heads):
    peers, widths = lax.axis_size("seq"), lax.axis_size("width")
    chips = peers // 2
    dma = pltpu.SemaphoreType.DMA
    anywhere = pl.BlockSpec(memory_space=pl.ANY)
    vmem = pl.BlockSpec(memory_space=pltpu.VMEM)
    own, model = x_rows.shape
    half = wide.shape[3] // 2
    strips = -(-(heads + got.shape[1] + small.shape[0] + SUB) // (16 * widths)) * 16 * widths
    pieces = [(peers, wide.shape[2], half), (peers, wide.shape[2], half), (peers, strips // widths, own)]
    kept = pieces[:2] + [(strips // widths, model)]
    block = (own, model)
    zx, dzx, normed = [a.reshape(peers, own, a.shape[1]) for a in (zx, dzx, normed)]
    return pl.pallas_call(
        partial(scatter_kernel, peers=peers, widths=widths, heads=heads),
        in_specs=[anywhere] * 6 + [vmem] * 6,
        out_specs=[vmem, anywhere, anywhere],
        out_shape=[
            jax.ShapeDtypeStruct(block, f32), jax.ShapeDtypeStruct(wide.shape, bf16),
            jax.ShapeDtypeStruct((peers, widths, strips // widths, own), bf16),
        ],
        scratch_shapes=[
            pltpu.VMEM(got.shape, bf16), pltpu.VMEM((peers, own, BLOCK), f32), pltpu.VMEM(dzx.shape, bf16),
            pltpu.VMEM(weights.shape, bf16), pltpu.VMEM(normed.shape, bf16),
            pltpu.VMEM((BLOCK, peers * own), bf16), pltpu.VMEM((strips, model), bf16),
            *[pltpu.VMEM((chips,) + block, bf16)] * 3, *[pltpu.VMEM((chips - 1,) + block, bf16)] * 2,
            *[pltpu.VMEM(a, bf16) for a in kept],
            *[pltpu.VMEM((widths - 1,) + a, bf16) for a in kept],
            *[pltpu.VMEM(a, bf16) for a in pieces],
            dma((5,)), dma((chips,)), dma((chips,)),
            dma((chips - 1,)), dma((chips - 1,)), dma((chips - 1,)), dma((chips - 1,)),
            dma((3, 3)), dma((3, widths - 1)), dma((3, widths - 1)), dma((3, peers - 1)), dma((3, peers - 1)),
            dma((3, widths - 1)), dma((3, widths - 1)),
        ],
        compiler_params=pltpu.CompilerParams(collective_id=2, has_side_effects=True, vmem_limit_bytes=62 << 20),
        name="scatter_out",
    )(got, zx, dzx, weights, normed, wide, par, keep, small, x_rows, cotangent, gain)


def laid_kernel(in_ref, third_ref, w_ref, bc_ref, dt_ref, gain_ref, out_ref, out_bc_ref, out_dt_ref, norm_ref, rest, *, heads, share):
    peers, rows, wide = in_ref.shape[0], in_ref.shape[2], in_ref.shape[3]
    chans = wide // 2
    step = pl.program_id(0)

    @pl.when(step == 0)
    def _():
        third = [
            jnp.concatenate([third_ref[s, q].astype(f32) for q in range(third_ref.shape[1])], axis=0) for s in range(peers)
        ]
        dt = jnp.concatenate([t[:heads] for t in third], axis=0).T
        bc = jnp.concatenate([t[heads : heads + share] for t in third], axis=0).T
        out_bc_ref[...] = bc
        out_dt_ref[...] = dt
        total = jnp.sum(bc * bc_ref[...].astype(f32), axis=1, keepdims=True)
        rest[...] = total + jnp.sum(dt * dt_ref[...].astype(f32), axis=1, keepdims=True)

    lane = jnp.zeros((rows, BLOCK), f32)
    for s in range(peers):
        for half in (0, 1):
            at = (half * peers + s) * chans
            value = in_ref[s, 0, :, half * chans : (half + 1) * chans].astype(f32)
            out_ref[:, at : at + chans] = value
            value = value * w_ref[:, at : at + chans].astype(f32)
            for j in range(chans // BLOCK):
                lane = lane + value[:, j * BLOCK : (j + 1) * BLOCK]
    more = rest[pl.ds(pl.multiple_of(step * rows, SUB), rows), :]
    norm_ref[...] = (jnp.sum(lane, axis=1, keepdims=True) + more) / gain_ref[...]


def laid_out(wide, third, w_zx, w_bc, w_dt, gain, heads):
    peers, widths, quarter, cols = wide.shape
    rows = widths * quarter
    steps = 2 * widths
    cut = rows // steps
    share = w_bc.shape[1] // peers
    by_rows = lambda a: pl.BlockSpec((cut, a.shape[1]), lambda i: (i, 0))
    whole = lambda a: pl.BlockSpec(a.shape, lambda i: (0,) * len(a.shape))
    by_piece = pl.BlockSpec((peers, 1, cut, cols), lambda i: (0, i // 2, i % 2, 0))
    shapes = [jax.ShapeDtypeStruct(a.shape, f32) for a in (w_zx, w_bc, w_dt, gain)]
    return pl.pallas_call(
        partial(laid_kernel, heads=heads, share=share),
        grid=(steps,),
        in_specs=[by_piece, whole(third), by_rows(w_zx), whole(w_bc), whole(w_dt), by_rows(gain)],
        out_specs=[by_rows(w_zx), whole(w_bc), whole(w_dt), by_rows(gain)],
        out_shape=shapes,
        scratch_shapes=[pltpu.VMEM((rows, 1), f32)],
        compiler_params=pltpu.CompilerParams(vmem_limit_bytes=32 << 20),
        name="lay_out",
    )(wide, third, w_zx, w_bc, w_dt, gain)


def crossed(value, axis, mask):
    return lax.ppermute(value, axis, [(i, i ^ mask) for i in range(lax.axis_size(axis))])


def pick(value, index):
    return lax.dynamic_index_in_dim(value, index, 0, False)


def quarters_sent(value):
    widths, width = lax.axis_size("width"), lax.axis_index("width")
    value = value.reshape((widths, value.shape[0] // widths) + value.shape[1:])
    sent = [crossed(pick(value, jnp.bitwise_xor(width, m)), "width", m) for m in range(1, widths)]
    return [pick(value, width)] + sent


def quarters_back(total):
    widths = lax.axis_size("width")
    return [total] + [crossed(total, "width", m) for m in range(1, widths)]


def quarters_joined(pieces):
    width = lax.axis_index("width")
    stacked = jnp.stack(pieces)
    whole = jnp.stack([pick(stacked, jnp.bitwise_xor(width, j)) for j in range(len(pieces))])
    return whole.reshape((-1,) + whole.shape[2:]).astype(f32)


def packed_rows(rows, count):
    flat = jnp.stack(rows)
    return jnp.pad(flat, ((0, count - len(rows)), (0, 0)))


def heads_body(
    tokens, cotangent, starts, valid, norm_gain, w_zx, w_bc, w_dt, conv_w, conv_b, dt_bias, a_log, d_skip, gate_gain, w_out
):
    peers = lax.axis_size("seq")
    widths = lax.axis_size("width")
    place = lax.axis_index("seq")
    lanes = starts.shape[1]
    heads = H // peers
    chans = heads * HEAD_DIM
    own, model = tokens.shape
    rows = own * peers
    first = place * heads
    share = 2 * N // peers
    used = heads + share
    row_mask = (jnp.arange(BLOCK)[None, :] < valid[0][:, None]).astype(f32).reshape(-1, 1)
    spread = jnp.asarray(np.arange(chans)[None, :] // HEAD_DIM == np.arange(BLOCK)[:, None], bf16)
    weights, normed, bgrad, starts_all, chan, head, *computed = front(
        valid, starts, tokens, cotangent, norm_gain[None], w_bc, w_dt, conv_w.T, conv_b[None], dt_bias[None], a_log[None],
        d_skip[None], gate_gain[None], spread, w_zx, w_out,
    )
    normed, bgrad = normed.reshape(rows, model), bgrad.reshape(rows, model)
    keep = 1.0 - starts_all[:, :lanes, 0]
    zx, mix, mixed_grad, scale, mixed_low, part, conv, bc, steps = [a.reshape(rows, a.shape[-1]) for a in computed[:9]]
    state, tail = computed[9:]
    branch = lax.psum_scatter(part, "seq", scatter_dimension=0, tiled=True).astype(f32)
    output = (tokens.astype(f32) + row_mask * branch).astype(bf16)
    out_part = mm(mixed_low, bgrad, TN).astype(bf16)
    scale, out_part = lax.optimization_barrier((scale, out_part))
    out_quarters = quarters_sent(out_part)

    dzx, dbc, dchan, dhead = run_backward(
        keep, zx, mixed_grad, chan, head, spread, conv, mix, bc, steps, state, tail, scale, lanes, heads
    )
    dzx, dbc, out_quarters = lax.optimization_barrier((dzx, dbc, out_quarters))
    out_pieces = quarters_back(sum(q.astype(f32) for q in out_quarters).astype(bf16))

    got = lax.all_to_all(dbc.reshape(peers, share, rows), "seq", 0, 0, tiled=True)
    of_share = lambda a: lax.dynamic_slice_in_dim(a, E + place * share, share, 0)
    share_par = jnp.pad(jnp.concatenate([of_share(conv_w), of_share(conv_b)[:, None]], axis=1), ((0, 0), (0, BLOCK - BIAS - 1)))
    over_time = lambda a: jnp.repeat(a.reshape(-1), BLOCK)
    keep_next = jnp.concatenate([keep[1:], jnp.zeros_like(keep[:1])], axis=0)
    keep_rows = packed_rows([over_time(keep), over_time(keep_next)], SUB)

    at_heads = lambda a: lax.dynamic_update_slice_in_dim(jnp.zeros((H,), f32), a, first, 0)
    at_chans = lambda a: lax.dynamic_update_slice_in_dim(jnp.zeros((E,), f32), a, first * HEAD_DIM, 0)
    skip = jnp.sum(dchan[SKIP].reshape(heads, HEAD_DIM), axis=1)
    small = [jnp.pad(at_chans(dchan[k]), (0, 2 * N)) for k in range(KCONV + 1)]
    small += [at_chans(dchan[GAIN]), at_heads(dhead[0, :heads]), at_heads(dhead[1, :heads]), at_heads(skip)]
    sizes = [a.shape[0] // peers for a in small]
    small = jnp.concatenate([a.reshape(peers, -1) for a in small], axis=1)
    small_rows = -(-small.shape[1] // (own * SUB)) * SUB
    small = jnp.pad(small, ((0, 0), (0, own * small_rows - small.shape[1])))
    small = small.reshape(peers, small_rows, own).transpose(1, 0, 2).reshape(small_rows, model)

    wide = mm(normed, dzx[:, : 2 * chans], TN).astype(bf16)
    wide, out_pieces = lax.optimization_barrier((wide, out_pieces))
    out_grad = quarters_joined(out_pieces)
    got, output, out_grad = lax.optimization_barrier((got, output, out_grad))
    input_grad, wide, third = scattered_out(
        got, zx, dzx, weights, normed, wide.reshape(peers, widths, own // widths, -1), share_par, keep_rows, small,
        tokens, cotangent, norm_gain[None], heads,
    )
    gain_rows = lax.dynamic_slice_in_dim(norm_gain, place * own, own, 0)[:, None]
    grad_zx, grad_bc, grad_dt, grad_norm = laid_out(wide, third, w_zx, w_bc, w_dt, gain_rows, heads)
    grad_norm = grad_norm[:, 0]
    third = third.reshape(peers, -1, own)
    summed = jnp.sum(third[:, used : used + small_rows].astype(f32), axis=0).reshape(-1)
    pieces = [summed[sum(sizes[:i]) : sum(sizes[: i + 1])] for i in range(len(sizes))]
    of_bc = third[:, used + small_rows : used + small_rows + KCONV + 1, :share].astype(f32).transpose(1, 0, 2).reshape(KCONV + 1, 2 * N)
    own_chans = sizes[0]
    of_bc = lax.dynamic_slice_in_dim(jnp.pad(of_bc, ((0, 0), (E, 0))), place * own_chans, own_chans, 1)
    grad_taps = jnp.stack(pieces[:KCONV], axis=1) + of_bc[:KCONV].T
    grad_bias, grad_gain, grad_dtb, grad_alog, grad_skip = pieces[KCONV:]
    grad_bias = grad_bias + of_bc[KCONV]
    return (
        output, input_grad, grad_norm, grad_zx, grad_bc, grad_dt, grad_taps, grad_bias, grad_dtb, grad_alog, grad_skip,
        grad_gain, out_grad,
    )


def passed_along(array, axis, by):
    peers = lax.axis_size(axis)
    pairs = [(i, i + by) for i in range(peers) if 0 <= i + by < peers]
    return lax.ppermute(array, axis, pairs)


def carried_in(part, axis, combine, identity, reverse):
    count = lax.axis_size(axis)
    place = lax.axis_index(axis)
    at = count - 1 - place if reverse else place
    by = -1 if reverse else 1
    state = jax.tree.map(lambda a, e: jnp.zeros_like(a) + jnp.asarray(e, a.dtype), part, identity)

    def one(lap, state):
        sent = combine(state, part)
        got = jax.tree.map(lambda a: passed_along(a, axis, by), sent)
        return jax.tree.map(lambda old, new: jnp.where(at == lap + 1, new, old), state, got)

    return lax.fori_loop(0, count - 1, one, state)


def round_value(v):
    return lax.optimization_barrier(v.astype(jnp.bfloat16)).astype(jnp.float32)


def keep_round(v):
    return (round_value(v), None)


def pass_grad(kept, grad):
    return (grad,)


def same_value(v):
    return v


def keep_same(v):
    return (v, None)


def round_grad(kept, grad):
    return (round_value(grad),)


def low(v):
    wrapped = jax.custom_vjp(round_value)
    wrapped.defvjp(keep_round, pass_grad)
    return wrapped(v)


def low_back(v):
    wrapped = jax.custom_vjp(same_value)
    wrapped.defvjp(keep_same, round_grad)
    return wrapped(v)


def rms_front(x_rows, norm_gain):
    mean_square = jnp.mean(x_rows * x_rows, axis=-1, keepdims=True)
    return x_rows * lax.rsqrt(mean_square + epsilon) * norm_gain


def rim_of(zx_pre, bc_pre, chan_mask):
    return jnp.concatenate(
        [zx_pre[:, BLOCK - KCONV + 1 :, E:] * chan_mask, bc_pre[:, BLOCK - KCONV + 1 :, :]], axis=-1
    )


def piece_front(
    zx_pre,
    bc_pre,
    dt_raw,
    rim_rows,
    conv_w,
    conv_b,
    dt_bias,
    a_log,
    chan_mask,
    head_mask,
    keep_rows,
):
    z_gate = zx_pre[..., :E] * chan_mask
    pre_conv = jnp.concatenate([zx_pre[..., E:] * chan_mask, bc_pre], axis=-1)
    padded = jnp.concatenate([rim_rows * keep_rows[:, None, None], pre_conv], axis=1)
    conv_out = conv_b + padded[:, 0:BLOCK, :] * conv_w[:, 0]
    for offset in range(1, KCONV):
        conv_out = conv_out + padded[:, offset : offset + BLOCK, :] * conv_w[:, offset]
    active = jax.nn.silu(conv_out)
    x_conv = low(active[..., :E] * chan_mask)
    b_conv = low(active[..., E : E + N])
    c_conv = low(active[..., E + N :])
    dt_step = jax.nn.softplus(dt_raw + dt_bias) * head_mask
    log_step = -jnp.exp(a_log) * dt_step
    return (z_gate, x_conv, b_conv, c_conv, dt_step, log_step)


def block_state(x_conv, b_conv, dt_step, log_step):
    cumulative = jnp.cumsum(log_step, axis=1)
    to_end = jnp.exp(cumulative[:, -1:, :] - cumulative) * dt_step
    weighted = low(x_conv.reshape(x_conv.shape[0], BLOCK, H, HEAD_DIM) * to_end[..., None])
    state_sum = jnp.einsum("lqhp,lqn->lhpn", weighted, b_conv, precision=highest)
    return (state_sum, cumulative[:, -1, :])


def piece_mix(
    z_gate, x_conv, b_conv, c_conv, dt_step, log_step, state_in, d_skip, gate_gain, chan_count
):
    lane_count = x_conv.shape[0]
    cumulative = jnp.cumsum(log_step, axis=1)
    cum_heads = jnp.swapaxes(cumulative, 1, 2)
    causal = jnp.arange(BLOCK)[:, None] >= jnp.arange(BLOCK)[None, :]
    spread = cum_heads[:, :, :, None] - cum_heads[:, :, None, :]
    decays = jnp.where(causal, jnp.exp(jnp.where(causal, spread, 0.0)), 0.0)
    inner_cb = jnp.einsum("lqn,lsn->lqs", c_conv, b_conv, precision=highest)
    scores = low(inner_cb[:, None] * decays * jnp.swapaxes(dt_step, 1, 2)[:, :, None, :])
    x_heads = x_conv.reshape(lane_count, BLOCK, H, HEAD_DIM)
    within = jnp.einsum("lhqs,lshp->lqhp", scores, x_heads, precision=highest)
    carried = (
        jnp.einsum("lqn,lhpn->lqhp", c_conv, state_in, precision=highest)
        * jnp.exp(cumulative)[..., None]
    )
    mixed_sum = low_back(within + carried) + d_skip[:, None] * x_heads
    gated_rows = mixed_sum.reshape(lane_count, BLOCK, E) * jax.nn.silu(z_gate)
    mean_square = jnp.sum(gated_rows * gated_rows, axis=-1, keepdims=True) / chan_count
    return low(gated_rows * lax.rsqrt(mean_square + epsilon) * gate_gain)


def mix_lanes(lane_inputs, d_skip, gate_gain, chan_count):

    def one_lane(pieces):
        lane_gate, lane_xconv, lane_bconv, lane_cconv, lane_step, lane_decay, lane_state = pieces
        return piece_mix(
            lane_gate[None],
            lane_xconv[None],
            lane_bconv[None],
            lane_cconv[None],
            lane_step[None],
            lane_decay[None],
            lane_state[None],
            d_skip,
            gate_gain,
            chan_count,
        )[0]

    return lax.map(one_lane, lane_inputs)


def mix_back_lanes(lane_inputs, mixed_grad, d_skip, gate_gain, chan_count):

    def lane_mix(z_gate, x_conv, b_conv, c_conv, dt_step, log_step, state_in, skip_coef, gain_coef):
        return piece_mix(
            z_gate[None],
            x_conv[None],
            b_conv[None],
            c_conv[None],
            dt_step[None],
            log_step[None],
            state_in[None],
            skip_coef,
            gain_coef,
            chan_count,
        )[0]

    def one_lane(pieces):
        (
            lane_gate,
            lane_xconv,
            lane_bconv,
            lane_cconv,
            lane_step,
            lane_decay,
            lane_state,
            lane_grad,
        ) = pieces
        unused, pull_lane = jax.vjp(
            lane_mix,
            lane_gate,
            lane_xconv,
            lane_bconv,
            lane_cconv,
            lane_step,
            lane_decay,
            lane_state,
            d_skip,
            gate_gain,
        )
        return pull_lane(lane_grad)

    lane_grads = lax.map(one_lane, lane_inputs + (mixed_grad,))
    return (lane_grads[:7], jnp.sum(lane_grads[7], axis=0), jnp.sum(lane_grads[8], axis=0))


def chain_combine(earlier, latter):
    return (earlier[0] * latter[0], latter[0][:, :, None, None] * earlier[1] + latter[1])


def share_out(out_grad):
    return lax.psum_scatter(out_grad, "seq", scatter_dimension=0, tiled=True)


def contract_rows(left, right):
    return lax.dot_general(
        left, right, (((0,), (0,)), ((), ())), preferred_element_type=jnp.float32
    )


def contract_cols(left, right):
    return lax.dot_general(
        left, right, (((1,), (1,)), ((), ())), preferred_element_type=jnp.float32
    )


def rows_body(
    tokens,
    cotangent,
    starts,
    valid,
    norm_gain,
    w_zx,
    w_bc,
    w_dt,
    conv_w,
    conv_b,
    dt_bias,
    a_log,
    d_skip,
    gate_gain,
    w_out,
):
    lane_count = starts.shape[1]
    width_index = lax.axis_index("width")
    shift_bits = lax.axis_size("width") - 1 - width_index
    active_heads = jnp.right_shift(jnp.int32(H), shift_bits)
    chan_mask = (jnp.arange(E) // HEAD_DIM < active_heads).astype(jnp.float32)
    head_mask = (jnp.arange(H) < active_heads).astype(jnp.float32)
    chan_count = (active_heads * HEAD_DIM).astype(jnp.float32)
    keep_rows = 1.0 - starts[0].astype(jnp.float32)
    row_mask = (jnp.arange(BLOCK)[None, :] < valid[0][:, None]).astype(jnp.float32).reshape(-1, 1)
    x_rows = tokens.astype(jnp.float32)
    normed, norm_back = jax.vjp(rms_front, x_rows, norm_gain)
    normed_low = normed.astype(jnp.bfloat16)
    zx_full, bc_full, dt_full, out_full = (
        lax.all_gather(w_zx, "seq", axis=0, tiled=True),
        lax.all_gather(w_bc, "seq", axis=0, tiled=True),
        lax.all_gather(w_dt, "seq", axis=0, tiled=True),
        lax.all_gather(w_out, "seq", axis=0, tiled=True),
    )
    zx_pre = jnp.dot(normed_low, zx_full, preferred_element_type=jnp.float32).reshape(
        lane_count, BLOCK, 2 * E
    )
    bc_pre = jnp.dot(normed_low, bc_full, preferred_element_type=jnp.float32).reshape(
        lane_count, BLOCK, 2 * N
    )
    dt_raw = jnp.dot(normed_low, dt_full, preferred_element_type=jnp.float32).reshape(
        lane_count, BLOCK, H
    )
    rim_rows = passed_along(rim_of(zx_pre, bc_pre, chan_mask), "seq", 1)
    front_fn = partial(piece_front, chan_mask=chan_mask, head_mask=head_mask, keep_rows=keep_rows)
    front_out, front_back = jax.vjp(
        front_fn, zx_pre, bc_pre, dt_raw, rim_rows, conv_w, conv_b, dt_bias, a_log
    )
    z_gate, x_conv, b_conv, c_conv, dt_step, log_step = front_out
    (state_sum, log_total), state_back = jax.vjp(block_state, x_conv, b_conv, dt_step, log_step)
    carry_rate = jnp.exp(log_total) * keep_rows[:, None]
    identity = (jnp.ones_like(carry_rate), jnp.zeros_like(state_sum))
    prefix_pair = carried_in((carry_rate, state_sum), "seq", chain_combine, identity, False)
    state_in = prefix_pair[1] * keep_rows[:, None, None, None]
    lane_inputs = (z_gate, x_conv, b_conv, c_conv, dt_step, log_step, state_in)
    mixed_low = mix_lanes(lane_inputs, d_skip, gate_gain, chan_count)
    mixed_flat = mixed_low.reshape(-1, E).astype(jnp.bfloat16)
    branch = jnp.dot(mixed_flat, out_full, preferred_element_type=jnp.float32)
    output = (x_rows + row_mask * branch).astype(jnp.bfloat16)
    cot_rows = cotangent.astype(jnp.float32)
    branch_grad = (cot_rows * row_mask).astype(jnp.bfloat16)
    out_grad = contract_rows(mixed_flat, branch_grad)
    mixed_grad = contract_cols(branch_grad, out_full).reshape(lane_count, BLOCK, E)
    lane_grads, grad_skip, grad_gain = mix_back_lanes(
        lane_inputs, mixed_grad, d_skip, gate_gain, chan_count
    )
    grad_gate, grad_x, grad_b, grad_c, grad_dt, grad_log, grad_state = lane_grads
    later_pair = carried_in(
        (carry_rate, grad_state * keep_rows[:, None, None, None]),
        "seq",
        chain_combine,
        identity,
        True,
    )
    later_grad = later_pair[1]
    grad_total = jnp.exp(log_total) * jnp.sum(later_grad * state_in, axis=(2, 3))
    grad_x_more, grad_b_more, grad_dt_more, grad_log_more = state_back((later_grad, grad_total))
    grad_zx, grad_bc, grad_dtraw, grad_rim, grad_convw, grad_convb, grad_dtbias, grad_alog = (
        front_back(
            (
                grad_gate,
                grad_x + grad_x_more,
                grad_b + grad_b_more,
                grad_c,
                grad_dt + grad_dt_more,
                grad_log + grad_log_more,
            )
        )
    )
    rim_grad = passed_along(grad_rim.astype(jnp.bfloat16), "seq", -1).astype(grad_rim.dtype)
    grad_zx = grad_zx.at[:, BLOCK - KCONV + 1 :, E:].add(rim_grad[..., :E] * chan_mask)
    grad_bc = grad_bc.at[:, BLOCK - KCONV + 1 :, :].add(rim_grad[..., E:])
    zx_low = grad_zx.reshape(-1, 2 * E).astype(jnp.bfloat16)
    bc_low = grad_bc.reshape(-1, 2 * N).astype(jnp.bfloat16)
    dt_low = grad_dtraw.reshape(-1, H).astype(jnp.bfloat16)
    zx_weight_grad = contract_rows(normed_low, zx_low)
    bc_weight_grad = contract_rows(normed_low, bc_low)
    dt_weight_grad = contract_rows(normed_low, dt_low)
    normed_grad = (
        contract_cols(zx_low, zx_full)
        + contract_cols(bc_low, bc_full)
        + contract_cols(dt_low, dt_full)
    )
    grad_x_rows, grad_norm = norm_back(normed_grad)
    input_grad = cot_rows + grad_x_rows
    out_shard = share_out(out_grad)
    row_shards = (
        lax.psum_scatter(grad_norm, "seq", scatter_dimension=0, tiled=True),
        lax.psum_scatter(zx_weight_grad, "seq", scatter_dimension=0, tiled=True),
        lax.psum_scatter(bc_weight_grad, "seq", scatter_dimension=0, tiled=True),
        lax.psum_scatter(dt_weight_grad, "seq", scatter_dimension=0, tiled=True),
        lax.psum_scatter(grad_convw, "seq", scatter_dimension=0, tiled=True),
        lax.psum_scatter(grad_convb, "seq", scatter_dimension=0, tiled=True),
        lax.psum_scatter(grad_dtbias, "seq", scatter_dimension=0, tiled=True),
        lax.psum_scatter(grad_alog, "seq", scatter_dimension=0, tiled=True),
        lax.psum_scatter(grad_skip, "seq", scatter_dimension=0, tiled=True),
        lax.psum_scatter(grad_gain, "seq", scatter_dimension=0, tiled=True),
    )
    summed = lax.psum(
        (
            row_shards[0],
            row_shards[1],
            row_shards[2],
            row_shards[3],
            row_shards[4],
            row_shards[5],
            row_shards[6],
            row_shards[7],
            row_shards[8],
            row_shards[9],
            out_shard,
        ),
        "width",
    )
    return (
        output,
        input_grad,
        summed[0],
        summed[1],
        summed[2],
        summed[3],
        summed[4],
        summed[5],
        summed[6],
        summed[7],
        summed[8],
        summed[9],
        summed[10],
    )


def solution(mesh):
    in_specs = (
        P(("width", "seq"), None),
        P(("width", "seq"), None),
        P(("width", "seq"), None),
        P(("width", "seq"), None),
        P(),
        P("seq", None),
        P("seq", None),
        P("seq", None),
        P(),
        P(),
        P(),
        P(),
        P(),
        P(),
        P("seq", None),
    )
    out_specs = (
        P(("width", "seq"), None),
        P(("width", "seq"), None),
        P("seq"),
        P("seq", None),
        P("seq", None),
        P("seq", None),
        P("seq", None),
        P("seq"),
        P("seq"),
        P("seq"),
        P("seq"),
        P("seq"),
        P("seq", None),
    )
    body = heads_body if H % (2 * mesh.shape["seq"]) == 0 else rows_body
    return jax.shard_map(body, mesh=mesh, in_specs=in_specs, out_specs=out_specs, check_vma=False)
```

```python
from functools import partial

import jax
import jax.numpy as jnp
from jax import lax
from jax.experimental import pallas as pl
from jax.experimental.pallas import tpu as pltpu
from jax.sharding import PartitionSpec as P
import numpy as np

H = 64
HEAD_DIM = 64
N = 128
KCONV = 4
BLOCK = 128
E = 4096
SUB = 8

epsilon = 1e-05
highest = lax.Precision.HIGHEST
f32 = jnp.float32
bf16 = jnp.bfloat16

NN = ((1,), (0,))
NT = ((1,), (1,))
TN = ((0,), (0,))


def mm(left, right, dims=NN, precision=None):
    return lax.dot_general(left, right, (dims, ((), ())), precision=precision, preferred_element_type=f32)


def split2(value):
    high = value.astype(bf16)
    return high, (value - high.astype(f32)).astype(bf16)


def mm_right(left, right, dims=NN):
    high, low = split2(right)
    return mm(left, high, dims) + mm(left, low, dims)


def mm_left(left, right, dims=NN):
    high, low = split2(left)
    return mm(high, right, dims) + mm(low, right, dims)


def softplus(v):
    small = jnp.exp(-jnp.abs(v))
    log1p = jnp.where(small < 1e-4, small - 0.5 * small * small, jnp.log(1.0 + small))
    return jnp.maximum(v, 0.0) + log1p


def sigmoid(v):
    return 1.0 / (1.0 + jnp.exp(-v))


def grids():
    row = lax.broadcasted_iota(jnp.int32, (BLOCK, BLOCK), 0)
    col = lax.broadcasted_iota(jnp.int32, (BLOCK, BLOCK), 1)
    return row, col


def halves(pair, lane):
    zero = jnp.zeros_like(pair)
    return jnp.where(lane < HEAD_DIM, pair, zero), jnp.where(lane < HEAD_DIM, zero, pair)


def decay_of(cum, cum_t, head, causal):
    return jnp.exp(jnp.where(causal, cum[:, head : head + 1] - cum_t[head : head + 1, :], -1e30))


TAP, BIAS, SKIP, GAIN, MASK = 0, 4, 5, 6, 7
DT_BIAS, NEG_A, HEAD_MASK = 0, 1, 2


def forward_block(
    keep_row, zx_ref, chan_ref, bc_par_ref, head_ref, spread,
    conv_ref, mix_ref, bc_ref, step_ref, state_ref, tail_ref,
    state, tail_x, tail_b, pad_x, pad_b,
    *, lane, heads,
):
    width = heads * HEAD_DIM
    row, col = grids()
    causal = row >= col
    tril = causal.astype(f32)
    rows = pl.ds(lane * BLOCK, BLOCK)
    keep = jnp.concatenate([keep_row] * (width // BLOCK), axis=1)
    keep_b = jnp.concatenate([keep_row] * (2 * N // BLOCK), axis=1)

    pre = zx_ref[rows, width : 2 * width]
    before = tail_x[lane] * keep
    pad_x[lane, 0:SUB] = before
    pad_x[lane, SUB:] = pre
    tail_ref[lane] = before
    tail_x[lane] = pre[BLOCK - SUB :, :]
    conv = chan_ref[BIAS : BIAS + 1, :]
    for k in range(KCONV):
        conv = conv + pad_x[lane, SUB - KCONV + 1 + k : SUB - KCONV + 1 + k + BLOCK, :] * chan_ref[k : k + 1, :]
    conv_ref[rows, :] = conv
    x_low = (conv * sigmoid(conv) * chan_ref[MASK : MASK + 1, :]).astype(bf16)

    pre_b = zx_ref[rows, 2 * width + BLOCK :]
    pad_b[lane, 0:SUB] = tail_b[lane] * keep_b
    pad_b[lane, SUB:] = pre_b
    tail_b[lane] = pre_b[BLOCK - SUB :, :]
    conv_b = bc_par_ref[BIAS : BIAS + 1, :]
    for k in range(KCONV):
        conv_b = conv_b + pad_b[lane, SUB - KCONV + 1 + k : SUB - KCONV + 1 + k + BLOCK, :] * bc_par_ref[k : k + 1, :]
    bc_low = (conv_b * sigmoid(conv_b)).astype(bf16)
    bc_ref[rows, :] = bc_low
    b_low, c_low = bc_low[:, :N], bc_low[:, N:]

    raw = zx_ref[rows, 2 * width : 2 * width + BLOCK] + head_ref[DT_BIAS : DT_BIAS + 1, :]
    dt = softplus(raw) * head_ref[HEAD_MASK : HEAD_MASK + 1, :]
    cum = mm(tril, head_ref[NEG_A : NEG_A + 1, :] * dt, precision=highest)
    step_ref[rows, :BLOCK] = cum
    step_ref[rows, BLOCK:] = dt
    cum_t, dt_t = cum.T, dt.T
    last = cum[BLOCK - 1 :, :]
    carry_x = mm_left(jnp.exp(cum), spread)
    end_x = mm_left(jnp.exp(last - cum) * dt, spread)
    last_x = carry_x[BLOCK - 1 :, :]

    inner = mm(c_low, b_low, NT)
    parts = []
    for j in range(heads // 2):
        pair = x_low[:, 2 * HEAD_DIM * j : 2 * HEAD_DIM * (j + 1)]
        scores = [
            (inner * decay_of(cum, cum_t, h, causal) * dt_t[h : h + 1, :]).astype(bf16)
            for h in (2 * j, 2 * j + 1)
        ]
        parts.append(mm(jnp.concatenate(scores, axis=1), jnp.concatenate(halves(pair, col), axis=0)))
    within = jnp.concatenate(parts, axis=1)

    state_in = state[lane] * keep
    state_ref[lane] = state_in
    carried = mm_right(c_low, state_in) * carry_x
    x_f = x_low.astype(f32)
    mix_ref[rows, :] = within + carried + chan_ref[SKIP : SKIP + 1, :] * x_f
    weighted = (x_f * end_x).astype(bf16)
    state[lane] = last_x * state_in + mm(b_low, weighted, TN)


def backward_kernel(
    start_ref, zx_ref, grad_ref, chan_ref, head_ref, spread_ref,
    conv_ref, mix_ref, bc_ref, step_ref, state_ref, tail_ref, scale_ref,
    dzx_ref, dbc_ref, dchan_ref, dhead_ref,
    state_grad, next_conv, pad_x, pad_d,
    *, lanes, heads,
):
    lap = pl.program_id(0)
    width = heads * HEAD_DIM
    row, col = grids()
    causal = row >= col
    triu = (col >= row).astype(f32)
    spread = spread_ref[...]

    @pl.when(lap == 0)
    def _():
        state_grad[...] = jnp.zeros_like(state_grad)
        next_conv[...] = jnp.zeros_like(next_conv)
        dchan_ref[...] = jnp.zeros_like(dchan_ref)
        dhead_ref[...] = jnp.zeros_like(dhead_ref)

    def total(value):
        return jnp.sum(value, axis=0, keepdims=True)

    for lane in range(lanes):
        rows = pl.ds(lane * BLOCK, BLOCK)
        keep = 1.0 - jnp.concatenate([start_ref[0, lane : lane + 1, :]] * (width // BLOCK), axis=1)
        z = zx_ref[rows, :width]
        conv = conv_ref[rows, :]
        mixed = mix_ref[rows, :]
        grad = grad_ref[rows, :]
        gain = chan_ref[GAIN : GAIN + 1, :]
        skip = chan_ref[SKIP : SKIP + 1, :]
        rate = scale_ref[rows, 0:1]
        pull = scale_ref[rows, 1:2]
        gate = sigmoid(z)
        silu = z * gate
        gated = mixed * silu
        dgated = grad * gain * rate - gated * pull
        dzx_ref[rows, :width] = (dgated * mixed * (gate * (1.0 + z * (1.0 - gate)))).astype(bf16)
        dmixed = dgated * silu
        act = sigmoid(conv)
        x_low = (conv * act * chan_ref[MASK : MASK + 1, :]).astype(bf16)
        x_f = x_low.astype(f32)
        dchan_ref[GAIN : GAIN + 1, :] += total(grad * gated * rate)
        dchan_ref[SKIP : SKIP + 1, :] += total(dmixed * x_f)
        dlow = dmixed.astype(bf16)
        dlow_f = dlow.astype(f32)

        b_low, c_low = bc_ref[rows, :N], bc_ref[rows, N:]
        cum, dt = step_ref[rows, :BLOCK], step_ref[rows, BLOCK:]
        cum_t, dt_t = cum.T, dt.T
        last = cum[BLOCK - 1 :, :]
        to_last = jnp.exp(last - cum)
        carry_x = mm_left(jnp.exp(cum), spread)
        end_x = mm_left(to_last * dt, spread)
        last_x = carry_x[BLOCK - 1 :, :]

        inner = mm(c_low, b_low, NT)
        dinner = jnp.zeros((BLOCK, BLOCK), f32)
        parts, dt_rows = [], []
        for j in range(heads // 2):
            lanes_j = slice(2 * HEAD_DIM * j, 2 * HEAD_DIM * (j + 1))
            pair, dpair = x_low[:, lanes_j], dlow[:, lanes_j]
            dstack = jnp.concatenate(halves(dpair, col), axis=0)
            dscores = mm(dstack, pair, NT)
            scores = []
            for i, h in enumerate((2 * j, 2 * j + 1)):
                decay = decay_of(cum, cum_t, h, causal)
                step = dt_t[h : h + 1, :]
                scores.append((inner * decay * step).astype(bf16))
                part = dscores[i * BLOCK : (i + 1) * BLOCK] * decay
                dinner = dinner + part * step
                dt_rows.append(total(part * inner))
            parts.append(mm(jnp.concatenate(scores, axis=0), dstack, TN))
        dx_within = jnp.concatenate(parts, axis=1)
        dt_rows.append(jnp.zeros((BLOCK - heads, BLOCK), f32))
        ddt_within = jnp.concatenate(dt_rows, axis=0).T

        state_in = state_ref[0, lane]
        sgrad = state_grad[lane]
        in_high, in_low = split2(state_in)
        sg_high, sg_low = split2(sgrad)
        dcarry = dlow_f * carry_x
        dc_high, dc_low = split2(dcarry)
        di_high, di_low = split2(dinner)
        dc = mm(dc_high, in_high, NT) + mm(dc_high, in_low, NT) + mm(dc_low, in_high, NT)
        dc = dc + mm(di_high, b_low) + mm(di_low, b_low)
        weighted = (x_f * end_x).astype(bf16)
        db = mm(weighted, sg_high, NT) + mm(weighted, sg_low, NT)
        db = db + mm(di_high, c_low, TN) + mm(di_low, c_low, TN)
        dbc_ref[:N, rows] = db.T.astype(bf16)
        dbc_ref[N:, rows] = dc.T.astype(bf16)
        dweighted = mm(b_low, sg_high) + mm(b_low, sg_low)
        dx = dx_within + dweighted * end_x
        dcum = mm_left(dlow_f * (mixed - skip * x_f) - x_f * dx, spread, NT)
        dend = mm_left(dweighted * x_f, spread, NT)
        touch = jnp.broadcast_to(total(sgrad * state_in), (SUB, width))
        dlast = total(dend * to_last * dt) + jnp.exp(last) * mm_left(touch, spread, NT)[0:1]
        dlog = mm(triu, dcum, precision=highest) + dlast
        neg_a = head_ref[NEG_A : NEG_A + 1, :]
        ddt = ddt_within + dend * to_last + dlog * neg_a
        raw = zx_ref[rows, 2 * width : 2 * width + BLOCK] + head_ref[DT_BIAS : DT_BIAS + 1, :]
        draw = ddt * sigmoid(raw) * head_ref[HEAD_MASK : HEAD_MASK + 1, :]
        dzx_ref[rows, 2 * width :] = draw.astype(bf16)
        dhead_ref[0:1, :] += total(draw)
        dhead_ref[1:2, :] += total(dlog * neg_a * dt)
        state_grad[lane] = keep * (mm(c_low, dc_high, TN) + mm(c_low, dc_low, TN) + last_x * sgrad)

        dx = dx + skip * dmixed
        dconv = dx * chan_ref[MASK : MASK + 1, :] * (act * (1.0 + conv * (1.0 - act)))
        pad_d[lane, :BLOCK] = dconv
        pad_d[lane, BLOCK:] = next_conv[lane]
        next_conv[lane] = dconv[:SUB] * keep
        pad_x[lane, :SUB] = tail_ref[0, lane]
        pad_x[lane, SUB:] = zx_ref[rows, width : 2 * width]
        dpre = jnp.zeros((BLOCK, width), f32)
        for k in range(KCONV):
            dpre = dpre + pad_d[lane, KCONV - 1 - k : KCONV - 1 - k + BLOCK, :] * chan_ref[k : k + 1, :]
            dchan_ref[k : k + 1, :] += total(dconv * pad_x[lane, SUB - KCONV + 1 + k : SUB - KCONV + 1 + k + BLOCK, :])
        dchan_ref[BIAS : BIAS + 1, :] += total(dconv)
        dzx_ref[rows, width : 2 * width] = dpre.astype(bf16)


def run_backward(starts, zx, grad, chan, head, spread, conv, mix, bc, step_arr, state, tail, scale, lanes, heads):
    rows, width = grad.shape
    step = lanes * BLOCK
    blocks = rows // step
    by_block = lambda cols: pl.BlockSpec((step, cols), lambda c: (blocks - 1 - c, 0))
    whole = lambda a: pl.BlockSpec(a.shape, lambda c: (0,) * a.ndim)
    fixed = lambda shape: pl.BlockSpec(shape, lambda c: (0,) * len(shape))
    per_lane = lambda r, cols: pl.BlockSpec((1, lanes, r, cols), lambda c: (blocks - 1 - c, 0, 0, 0))
    return pl.pallas_call(
        partial(backward_kernel, lanes=lanes, heads=heads),
        grid=(blocks,),
        in_specs=[
            pl.BlockSpec((1, SUB, BLOCK), lambda c: (blocks - 1 - c, 0, 0)), by_block(2 * width + BLOCK), by_block(width),
            whole(chan), whole(head), whole(spread),
            by_block(width), by_block(width), by_block(2 * N), by_block(2 * BLOCK),
            per_lane(N, width), per_lane(SUB, width), by_block(BLOCK),
        ],
        out_specs=[
            by_block(2 * width + BLOCK), pl.BlockSpec((2 * N, step), lambda c: (0, blocks - 1 - c)),
            fixed((SUB, width)), fixed((SUB, BLOCK)),
        ],
        out_shape=[
            jax.ShapeDtypeStruct((rows, 2 * width + BLOCK), bf16),
            jax.ShapeDtypeStruct((2 * N, rows), bf16), jax.ShapeDtypeStruct((SUB, width), f32),
            jax.ShapeDtypeStruct((SUB, BLOCK), f32),
        ],
        scratch_shapes=[
            pltpu.VMEM((lanes, N, width), f32), pltpu.VMEM((lanes, SUB, width), f32),
            pltpu.VMEM((lanes, BLOCK + SUB, width), f32), pltpu.VMEM((lanes, BLOCK + SUB, width), f32),
        ],
        compiler_params=pltpu.CompilerParams(vmem_limit_bytes=48 << 20, dimension_semantics=("arbitrary",)),
        cost_estimate=pl.CostEstimate(flops=rows * width * 6144, bytes_accessed=rows * width * 40, transcendentals=rows * width * 6),
        name="mix_backward",
    )(starts, zx, grad, chan, head, spread, conv, mix, bc, step_arr, state, tail, scale)


MESH = pl.DeviceIdType.MESH


def greet(others):
    for other in others:
        pl.semaphore_signal(pltpu.get_barrier_semaphore(), inc=1, device_id=other, device_id_type=MESH)


def met(others):
    pl.semaphore_wait(pltpu.get_barrier_semaphore(), len(others))


def remote(src, dst, send, recv, device):
    return pltpu.make_async_remote_copy(
        src_ref=src, dst_ref=dst, send_sem=send, recv_sem=recv, device_id=device, device_id_type=MESH
    )


class Rows:
    def __init__(self, own_ref, all_ref, sems, peers):
        self.own, self.all, self.sems, self.peers = own_ref, all_ref, sems, peers
        self.width, self.place = lax.axis_index("width"), lax.axis_index("seq")
        self.chips, self.chip = peers // 2, self.place // 2

    def hop(self, ref, s, step, by):
        send, recv = self.sems[0 if by > 0 else 2], self.sems[1 if by > 0 else 3]
        device = (self.width, jnp.clip(self.place + 2 * by, 0, self.peers - 1))
        return remote(ref, self.all.at[s], send.at[step], recv.at[step], device)

    def over(self, ref, s, slot):
        device = (self.width, jnp.bitwise_xor(self.place, 1))
        return remote(ref, self.all.at[s], self.sems[4].at[slot], self.sems[5].at[slot], device)

    def inside(self, by):
        return self.chip + 1 < self.chips if by > 0 else self.chip > 0

    def reached(self, by, step):
        return self.chip >= step if by > 0 else self.chip + step < self.chips

    def source(self, by, step):
        return jnp.clip(self.place - 2 * by * step, 0, self.peers - 1)

    def keep(self):
        return pltpu.make_async_copy(self.own, self.all.at[self.place], self.sems[6])

    def start(self):
        self.keep().start()
        for by in (1, -1):
            @pl.when(self.inside(by))
            def _():
                self.hop(self.own, self.place, 0, by).start()
        self.over(self.own, self.place, 0).start()

    def pass_on(self, step):
        for by in (1, -1):
            @pl.when(self.reached(by, step))
            def _():
                s = self.source(by, step)
                ref = self.all.at[s]
                self.hop(ref, s, step - 1, by).wait_recv()

                @pl.when(self.inside(by))
                def _():
                    self.hop(ref, s, step, by).start()
                self.over(ref, s, 2 * step - (by > 0)).start()

    def mate(self, by, step):
        if not step:
            return self.over(self.own, self.place, 0)
        s = self.source(by, step)
        return self.over(self.all.at[s], s, 2 * step - (by > 0))

    def arrived(self):
        self.keep().wait()
        self.mate(1, 0).wait_recv()
        for step in range(1, self.chips):
            for by in (1, -1):
                @pl.when(self.reached(by, step))
                def _():
                    self.mate(by, step).wait_recv()

    def sent(self):
        for step in range(self.chips):
            for by in (1, -1):
                @pl.when(self.inside(by) & self.reached(by, step))
                def _():
                    s = self.source(by, step)
                    self.hop(self.all.at[s], s, step, by).wait_send()
        self.mate(1, 0).wait_send()
        for step in range(1, self.chips):
            for by in (1, -1):
                @pl.when(self.reached(by, step))
                def _():
                    self.mate(by, step).wait_send()


ROW_SEMS = 7


def row_sems(chips):
    dma = pltpu.SemaphoreType.DMA
    return [dma((chips,)), dma((chips,)), dma((chips,)), dma((chips,)), dma((2 * chips,)), dma((2 * chips,)), dma(())]


def front_kernel(
    valid_ref, start_ref, x_ref, cot_ref, norm_gain_ref, bc_ref, dt_ref, taps_ref, bias_ref, dtb_ref, alog_ref, skip_ref,
    gain_ref, spread_ref, zx_ref, wout_ref,
    w_ref, rows_ref, grads_ref, starts_ref, chan_ref, head_ref, bc_par,
    out_zx, out_mix, out_grad, out_scale, out_low, out_part, out_conv, out_bc, out_step, out_state, out_tail,
    w_v, rows_v, starts_v, wout_v, own_v, grad_v, third_v, start_v, part_got,
    zx_v, mix_v, mgrad_v, scale_v, low_v, conv_v, bc_v, step_v, state_v, tail_v, sums, sums_got,
    state, tail_x, tail_b, pad_x, pad_b,
    w_send, w_recv, st_send, st_recv, own_sem, wide_send, wide_recv, in_sem, out_sem, slot_sem, part_send, part_recv, part_sem, sum_send, sum_recv, *sems,
    peers, widths, lanes, heads,
):
    width, place = lax.axis_index("width"), lax.axis_index("seq")
    chips = peers // 2
    chans = heads * HEAD_DIM
    quarter = zx_ref.shape[0] // widths
    ring = [lax.rem(place + by, peers) for by in range(1, peers)]
    cross = [jnp.bitwise_xor(width, m) for m in range(1, widths)]
    others = [(width, s) for s in ring] + [(w, place) for w in cross]
    greet(others)

    x = x_ref[...].astype(f32)
    own_v[...] = (x * lax.rsqrt(jnp.mean(x * x, axis=-1, keepdims=True) + epsilon) * norm_gain_ref[...]).astype(bf16)
    row = lax.broadcasted_iota(jnp.int32, (BLOCK, 1), 0)
    sub = lax.broadcasted_iota(jnp.int32, (SUB, BLOCK), 0)
    tile = jnp.zeros((SUB, BLOCK), f32)
    for lane in range(lanes):
        at = slice(lane * BLOCK, (lane + 1) * BLOCK)
        mask = (row < valid_ref[0, lane]).astype(f32)
        grad_v[at, :] = (cot_ref[at, :].astype(f32) * mask).astype(bf16)
        tile = jnp.where(sub == lane, start_ref[0, lane].astype(f32), tile)
    start_v[...] = tile
    bc, dt = bc_ref[...].astype(f32), dt_ref[...].astype(f32)
    share = bc.shape[1] // peers
    rest = jnp.zeros((bc.shape[0], BLOCK - share - heads), f32)
    for s in range(peers):
        columns = [dt[:, s * heads : (s + 1) * heads], bc[:, s * share : (s + 1) * share], rest]
        third_v[s] = jnp.concatenate(columns, axis=1).astype(bf16)
    met(others)

    mine = pl.ds(pl.multiple_of(width * quarter, quarter), quarter)
    rows = Rows(own_v, rows_ref, sems[:ROW_SEMS], peers)
    grads = Rows(grad_v, grads_ref, sems[ROW_SEMS:], peers)

    def columns_of(half, s):
        return pl.ds(pl.multiple_of(half * peers * chans + s * chans, 128), chans)

    wide = 2 * chans
    spots = [pl.ds(0, chans), pl.ds(chans, chans), pl.ds(wide, BLOCK), pl.ds(wide + BLOCK, 2 * N)]

    def parts(s):
        return [zx_ref.at[mine, columns_of(0, s)], zx_ref.at[mine, columns_of(1, s)], third_v.at[s, mine], bc_ref.at[mine]]

    pushes = []
    for i, s in enumerate(ring):
        for k, (part, spot) in enumerate(zip(parts(s), spots)):
            pushes.append(remote(part, w_ref.at[place, width, :, spot], w_send.at[k, i], w_recv.at[k, i], (width, s)))
        pushes.append(remote(start_v, starts_ref.at[place], st_send.at[i], st_recv.at[i], (width, s)))
    for push in pushes:
        push.start()
    keeps = [
        pltpu.make_async_copy(part, w_ref.at[place, width, :, spot], own_sem.at[k])
        for k, (part, spot) in enumerate(zip(parts(place), spots))
    ]
    keeps.append(pltpu.make_async_copy(start_v, starts_ref.at[place], own_sem.at[4]))
    for keep in keeps:
        keep.start()
    rows.start()

    active = jnp.right_shift(jnp.int32(H), widths - 1 - width)
    first = place * heads
    here = columns_of(0, place)
    spread = spread_ref[...]
    pick_row = lax.broadcasted_iota(jnp.int32, (H, BLOCK), 0)
    pick_lane = lax.broadcasted_iota(jnp.int32, (H, BLOCK), 1)
    chosen = ((pick_row == pick_lane + first) & (pick_lane < heads)).astype(f32)
    per_head = jnp.concatenate(
        [dtb_ref[...], -jnp.exp(alog_ref[...]), jnp.ones((1, H), f32), skip_ref[...], jnp.zeros((SUB - 4, H), f32)], axis=0
    )
    per_head = mm(per_head, chosen, precision=highest)
    head_lane = lax.broadcasted_iota(jnp.int32, (SUB, BLOCK), 1)
    head_ref[...] = jnp.where((sub == HEAD_MASK) & (head_lane + first >= active), 0.0, per_head)
    on_chans = mm(head_ref[...], spread.astype(f32), precision=highest)
    chan_ref[...] = jnp.concatenate(
        [taps_ref[:, here], bias_ref[:, here], on_chans[3:4], gain_ref[:, here], on_chans[HEAD_MASK : HEAD_MASK + 1]], axis=0
    )
    bc_par[...] = jnp.concatenate(
        [taps_ref[:, E:], bias_ref[:, E:], jnp.zeros((SUB - KCONV - 1, 2 * N), f32)], axis=0
    )

    for push in pushes:
        push.wait_recv()
    for keep in keeps:
        keep.wait()
    shares = [
        remote(w_ref.at[:, width], w_ref.at[:, width], wide_send.at[m], wide_recv.at[m], (w, place)) for m, w in enumerate(cross)
    ]
    for copy in shares:
        copy.start()
    for step in range(1, chips - 1):
        rows.pass_on(step)
    grads.start()
    for copy in shares:
        copy.wait_recv()
    in_w = pltpu.make_async_copy(w_ref, w_v, own_sem.at[0])
    in_starts = pltpu.make_async_copy(starts_ref, starts_v, own_sem.at[1])
    in_wout = pltpu.make_async_copy(wout_ref, wout_v, own_sem.at[2])
    for copy in (in_w, in_starts, in_wout):
        copy.start()
    rows.pass_on(chips - 1)
    rows.arrived()

    def load(src, s):
        return pltpu.make_async_copy(src.at[s], rows_v.at[s], in_sem.at[s])

    for c in range(peers):
        load(rows_ref, c).start()
    for array in (state, tail_x, tail_b):
        array[...] = jnp.zeros_like(array)
    for copy in (in_w, in_starts, in_wout):
        copy.wait()

    def out_copy(k, src, dst, c):
        return pltpu.make_async_copy(src.at[c], dst.at[c], out_sem.at[k, c])

    slots = [(conv_v, out_conv), (bc_v, out_bc), (step_v, out_step), (state_v, out_state), (tail_v, out_tail)]

    def slot_copies(c):
        slot = lax.rem(c, 2)
        return [pltpu.make_async_copy(src.at[slot], dst.at[c], slot_sem.at[k, slot]) for k, (src, dst) in enumerate(slots)]

    def compute(begin, end):
        @pl.loop(begin, end)
        def _(c):
            load(rows_ref, c).wait()

            @pl.when(c >= 2)
            def _():
                for copy in slot_copies(c - 2):
                    copy.wait()
            weights = w_v[...].reshape(w_v.shape[0] * w_v.shape[1] * w_v.shape[2], w_v.shape[3])
            zx_v[c] = mm(rows_v[c], weights)
            slot = lax.rem(c, 2)
            for lane in range(lanes):
                forward_block(
                    1.0 - starts_v[c, lane : lane + 1, :], zx_v.at[c], chan_ref, bc_par, head_ref, spread_ref[...],
                    conv_v.at[slot], mix_v.at[c], bc_v.at[slot], step_v.at[slot], state_v.at[slot], tail_v.at[slot],
                    state, tail_x, tail_b, pad_x, pad_b, lane=lane, heads=heads,
                )
            out_copy(0, zx_v, out_zx, c).start()
            out_copy(1, mix_v, out_mix, c).start()
            for copy in slot_copies(c):
                copy.start()

    def gated_of(c):
        z = zx_v[c, :, :chans]
        return mix_v[c] * (z * sigmoid(z))

    def mix_grad(s):
        load(grads_ref, s).wait()
        grad = mm(rows_v[s], wout_v[...], NT)
        mgrad_v[s] = grad
        out_copy(2, mgrad_v, out_grad, s).start()
        gated = gated_of(s)
        ones = jnp.ones((SUB, chans), bf16)
        square = mm_right(ones, gated * gated, NT)
        pulled = mm_right(ones, grad * chan_ref[GAIN : GAIN + 1, :] * gated, NT)
        for lane in range(lanes):
            at = slice(lane * BLOCK, (lane + 1) * BLOCK)
            sums[0, pl.ds(s * lanes + lane, 1), :] = square[:1, at]
            sums[1, pl.ds(s * lanes + lane, 1), :] = pulled[:1, at]

    per = -(-peers // 2)
    for step in range(1, chips):
        begin, end = min((step - 1) * per, peers), min(step * per, peers)
        if step == chips - 1:
            end = peers
        if begin < end:
            compute(begin, end)
        if step < chips - 1:
            grads.pass_on(step)

    def at_distance(step, act):
        if not step:
            act(place, None)
            act(jnp.bitwise_xor(place, 1), (1, 0))
        for by in (1, -1):
            if step:
                @pl.when(grads.reached(by, step))
                def _():
                    s = grads.source(by, step)
                    act(s, None)
                    act(jnp.bitwise_xor(s, 1), (by, step))

    def begin_load(s, mate):
        if mate is not None:
            grads.mate(*mate).wait_recv()
        load(grads_ref, s).start()

    grads.keep().wait()
    for step in range(chips - 1):
        at_distance(step, begin_load)
    for step in range(chips - 1):
        at_distance(step, lambda s, mate: mix_grad(s))
    grads.pass_on(chips - 1)
    at_distance(chips - 1, begin_load)
    at_distance(chips - 1, lambda s, mate: mix_grad(s))

    give = [remote(sums, sums_got.at[i], sum_send.at[i], sum_recv.at[i], (width, s)) for i, s in enumerate(ring)]
    for copy in give:
        copy.start()
    for copy in give:
        copy.wait_recv()
    total = sums[...]
    for i in range(peers - 1):
        total = total + sums_got[i]
    count = (active * HEAD_DIM).astype(f32)
    rate = lax.rsqrt(total[0] / count + epsilon)
    pull = rate * rate * rate * total[1] / count
    blank = jnp.zeros((BLOCK - 2 * lanes * peers, BLOCK), f32)
    by_time = jnp.concatenate([rate, pull, blank], axis=0).T
    lane_at = lax.broadcasted_iota(jnp.int32, (BLOCK, BLOCK), 1)
    for c in range(peers):
        for lane in range(lanes):
            i = c * lanes + lane
            j = lanes * peers + i
            scale_v[c, lane * BLOCK : (lane + 1) * BLOCK, :] = jnp.where(
                lane_at == 0, by_time[:, i : i + 1], jnp.where(lane_at == 1, by_time[:, j : j + 1], 0.0)
            )

    core = lax.rem(place, 2)

    def part_over(q):
        return remote(
            rows_v.at[2 * q + 1 - core], part_got.at[q], part_send.at[q], part_recv.at[q], (width, jnp.bitwise_xor(place, 1))
        )

    def part_out(q):
        return pltpu.make_async_copy(rows_v.at[2 * q + core], out_part.at[q], part_sem.at[q])

    def part_sum(q):
        part_over(q).wait_recv()
        add_into(rows_v.at[2 * q + core], [part_got.at[q]], rows_v.shape[1])
        part_out(q).start()

    @pl.loop(0, chips)
    def _(q):
        for c in (2 * q + 1 - core, 2 * q + core):
            low = (gated_of(c) * scale_v[c, :, 0:1] * chan_ref[GAIN : GAIN + 1, :]).astype(bf16)
            low_v[c] = low
            rows_v[c] = mm(low, wout_v[...]).astype(bf16)
            out_copy(3, scale_v, out_scale, c).start()
            out_copy(4, low_v, out_low, c).start()
        part_over(q).start()

        @pl.when(q > 0)
        def _():
            part_sum(q - 1)

    part_sum(chips - 1)

    for copy in shares + pushes + give:
        copy.wait_send()
    rows.sent()
    grads.sent()
    for c in (peers - 2, peers - 1):
        for copy in slot_copies(c):
            copy.wait()

    @pl.loop(0, peers)
    def _(c):
        for k, (src, dst) in enumerate(
            [(zx_v, out_zx), (mix_v, out_mix), (mgrad_v, out_grad), (scale_v, out_scale), (low_v, out_low)]
        ):
            out_copy(k, src, dst, c).wait()

    for q in range(chips):
        part_over(q).wait_send()
        part_out(q).wait()


def front(valid, starts, tokens, cotangent, norm_gain, w_bc, w_dt, taps, bias, dt_bias, a_log, d_skip, gate_gain, spread, w_zx, w_out):
    peers, widths = lax.axis_size("seq"), lax.axis_size("width")
    own, model = tokens.shape
    lanes = starts.shape[1]
    quarter = own // widths
    chans = w_out.shape[0]
    heads = chans // HEAD_DIM
    cols = 2 * chans + BLOCK + 2 * N
    dma = pltpu.SemaphoreType.DMA
    anywhere, vmem = pl.BlockSpec(memory_space=pl.ANY), pl.BlockSpec(memory_space=pltpu.VMEM)
    smem = pl.BlockSpec(memory_space=pltpu.SMEM)
    w_all = ((peers, widths, quarter, cols), bf16)
    rows_all = ((peers, own, model), bf16)
    part_all = ((peers // 2, own, model), bf16)
    starts_all = ((peers, SUB, BLOCK), f32)
    per_chan, low = ((peers, own, chans), f32), ((peers, own, chans), bf16)
    whole = [((peers, own, cols), f32), per_chan, per_chan, ((peers, own, BLOCK), f32), low]
    streamed = [
        ((own, chans), f32), ((own, 2 * N), bf16), ((own, 2 * BLOCK), f32), ((lanes, N, chans), f32), ((lanes, SUB, chans), f32)
    ]
    outs = [w_all, rows_all, rows_all, starts_all, ((SUB, chans), f32), ((SUB, BLOCK), f32), ((SUB, 2 * N), f32), *whole, part_all]
    outs += [((peers,) + a[0], a[1]) for a in streamed]
    scratch = [w_all, rows_all, starts_all, ((chans, model), bf16), ((own, model), bf16), ((own, model), bf16)]
    scratch += [((peers, own, BLOCK), bf16), ((SUB, BLOCK), f32), part_all, *whole]
    scratch += [((2,) + a[0], a[1]) for a in streamed]
    scratch += [((2, peers * lanes, BLOCK), f32), ((peers - 1, 2, peers * lanes, BLOCK), f32)]
    scratch += [((lanes, N, chans), f32), ((lanes, SUB, chans), f32), ((lanes, SUB, 2 * N), f32)]
    scratch += [((lanes, BLOCK + SUB, chans), f32), ((lanes, BLOCK + SUB, 2 * N), f32)]
    return pl.pallas_call(
        partial(front_kernel, peers=peers, widths=widths, lanes=lanes, heads=heads),
        in_specs=[smem] * 2 + [vmem] * 12 + [anywhere] * 2,
        out_specs=[anywhere] * 4 + [vmem] * 3 + [anywhere] * 11,
        out_shape=[jax.ShapeDtypeStruct(*a) for a in outs],
        scratch_shapes=[
            *[pltpu.VMEM(*a) for a in scratch],
            dma((4, peers - 1)), dma((4, peers - 1)), dma((peers - 1,)), dma((peers - 1,)),
            dma((5,)), dma((widths - 1,)), dma((widths - 1,)), dma((peers,)), dma((5, peers)), dma((5, 2)),
            dma((peers // 2,)), dma((peers // 2,)), dma((peers // 2,)), dma((peers - 1,)), dma((peers - 1,)),
            *row_sems(peers // 2), *row_sems(peers // 2),
        ],
        compiler_params=pltpu.CompilerParams(collective_id=1, has_side_effects=True, vmem_limit_bytes=62 << 20),
        name="front",
    )(valid, starts, tokens, cotangent, norm_gain, w_bc, w_dt, taps, bias, dt_bias, a_log, d_skip, gate_gain, spread, w_zx, w_out)


ROWS_AT_ONCE = 16


def add_into(dst, others, rows):
    @pl.loop(0, rows // ROWS_AT_ONCE)
    def _(i):
        at = pl.ds(pl.multiple_of(i * ROWS_AT_ONCE, ROWS_AT_ONCE), ROWS_AT_ONCE)
        value = dst[at].astype(f32)
        for other in others:
            value = value + other[at].astype(f32)
        dst[at] = value.astype(dst.dtype)


def bc_back(dbc, pre, par_ref, keep, keep_next):
    chans, times = pre.shape
    in_block = lax.rem(lax.broadcasted_iota(jnp.int32, (chans, times), 1), BLOCK)
    conv = jnp.broadcast_to(par_ref[:, BIAS : BIAS + 1], (chans, times))
    shifted = []
    for j in range(KCONV):
        moved = pre
        if j:
            moved = jnp.where(in_block >= j, pltpu.roll(pre, j, 1), keep * pltpu.roll(pre, BLOCK + j, 1))
        shifted.append(moved)
        conv = conv + moved * par_ref[:, KCONV - 1 - j : KCONV - j]
    act = sigmoid(conv)
    dconv = dbc * (act * (1.0 + conv * (1.0 - act)))
    dpre = dconv * par_ref[:, KCONV - 1 : KCONV]
    lane = lax.broadcasted_iota(jnp.int32, (chans, BLOCK), 1)
    dpar = jnp.where(lane == BIAS, jnp.sum(dconv, axis=1, keepdims=True), 0.0)
    for j in range(KCONV):
        dpar = dpar + jnp.where(lane == KCONV - 1 - j, jnp.sum(dconv * shifted[j], axis=1, keepdims=True), 0.0)
        if j:
            back = jnp.where(
                in_block < BLOCK - j, pltpu.roll(dconv, times - j, 1), keep_next * pltpu.roll(dconv, times - BLOCK - j, 1)
            )
            dpre = dpre + back * par_ref[:, KCONV - 1 - j : KCONV - j]
    return dpre, dpar


def scatter_kernel(
    got_ref, zx_ref, dzx_ref, w_ref, normed_ref, wide_ref, par_ref, start_ref, small_ref,
    rows_ref, out_ref, out_third_ref,
    got_v, pre_v, dz_v, w_v, normed_v, third_t, third_g, par_t,
    mine, to_mate, from_core, up, down, own0, own1, own2, got0, got1, got2, piece0, piece1, piece2,
    load_sem, core_send, core_recv, up_send, up_recv, down_send, down_recv,
    own_sem, q_send, q_recv, p_send, p_recv, o_send, o_recv,
    *, peers, widths, heads,
):
    width, place = lax.axis_index("width"), lax.axis_index("seq")
    chips = peers // 2
    chip, core = place // 2, lax.rem(place, 2)
    mate = (width, jnp.bitwise_xor(place, 1))
    ring = [lax.rem(place + by, peers) for by in range(1, peers)]
    cross = [jnp.bitwise_xor(width, m) for m in range(1, widths)]
    others = [(width, s) for s in ring] + [(w, place) for w in cross]
    greet(others)
    half = wide_ref.shape[3] // 2
    wide = 2 * half
    own = mine.shape[1]
    share, times = got_v.shape[1], got_v.shape[2]
    loads = [
        pltpu.make_async_copy(src, dst, load_sem.at[k])
        for k, (src, dst) in enumerate([
            (got_ref, got_v), (zx_ref.at[:, :, wide : wide + BLOCK], pre_v), (dzx_ref, dz_v), (w_ref, w_v), (normed_ref, normed_v)
        ])
    ]
    for load in loads:
        load.start()
    met(others)

    strip = third_g.shape[0] // widths
    lanes_of = lambda s: pl.ds(pl.multiple_of(s * own, BLOCK), own)
    strip_of = lambda w: pl.ds(pl.multiple_of(w * strip, 16), strip)
    sets = [
        (lambda w: wide_ref.at[:, w, :, 0:half], own0, got0, lambda s: own0.at[s], piece0, lambda w: out_ref.at[:, w, :, 0:half]),
        (lambda w: wide_ref.at[:, w, :, half:wide], own1, got1, lambda s: own1.at[s], piece1, lambda w: out_ref.at[:, w, :, half:wide]),
        (lambda w: third_g.at[strip_of(w)], own2, got2, lambda s: own2.at[:, lanes_of(s)], piece2, lambda w: out_third_ref.at[:, w]),
    ]
    own_in, to_width = [None] * 3, [None] * 3

    def begin(k):
        part, kept, arrived = sets[k][:3]
        own_in[k] = pltpu.make_async_copy(part(width), kept, own_sem.at[0, k])
        to_width[k] = [
            remote(part(w), arrived.at[m], q_send.at[k, m], q_recv.at[k, m], (w, place)) for m, w in enumerate(cross)
        ]
        for copy in [own_in[k]] + to_width[k]:
            copy.start()

    begin(0)
    begin(1)

    def flow(by):
        return (up, up_send, up_recv) if by > 0 else (down, down_send, down_recv)

    def sends(by, step):
        far = chips - step
        return chip + far < chips if by > 0 else chip >= far

    def later(by):
        return chip > 0 if by > 0 else chip + 1 < chips

    def hop(src, by, step):
        buffer, send, recv = flow(by)
        return remote(
            src, buffer.at[step - 1], send.at[step - 1], recv.at[step - 1], (width, jnp.clip(place + 2 * by, 0, peers - 1))
        )

    def staged(by, step):
        return flow(by)[0].at[step - 2]

    def run_hops(step):
        for by in (1, -1):
            owner = jnp.clip(chip + by * (chips - step), 0, chips - 1)

            def direct():
                hop(mine.at[owner], by, step).start()

            def relayed():
                hop(staged(by, step), by, step - 1).wait_recv()
                add_into(staged(by, step), [mine.at[owner]], own)
                hop(staged(by, step), by, step).start()

            if step == 1:
                pl.when(sends(by, step))(direct)
            else:
                pl.when(sends(by, step) & jnp.logical_not(later(by)))(direct)
                pl.when(sends(by, step) & later(by))(relayed)

    to_owner, to_all, kept_piece = [None] * 3, [None] * 3, [None] * 3

    def exchange(k):
        part, kept, arrived, piece_of, piece, out = sets[k]
        own_in[k].wait()
        for copy in to_width[k]:
            copy.wait_recv()
        if kept.ndim == 3:
            for s in range(peers):
                add_into(kept.at[s], [arrived.at[m, s] for m in range(widths - 1)], kept.shape[1])
        else:
            add_into(kept, [arrived.at[m] for m in range(widths - 1)], kept.shape[0])
        to_owner[k] = [
            remote(piece_of(s), piece.at[place], p_send.at[k, i], p_recv.at[k, i], (width, s)) for i, s in enumerate(ring)
        ]
        kept_piece[k] = pltpu.make_async_copy(piece_of(place), piece.at[place], own_sem.at[1, k])
        for copy in to_owner[k] + [kept_piece[k]]:
            copy.start()

    def spread(k):
        piece, out = sets[k][4:]
        for copy in to_owner[k]:
            copy.wait_recv()
        kept_piece[k].wait()
        to_all[k] = [remote(piece, out(width), o_send.at[k, m], o_recv.at[k, m], (w, place)) for m, w in enumerate(cross)]
        to_all[k].append(pltpu.make_async_copy(piece, out(width), own_sem.at[2, k]))
        for copy in to_all[k]:
            copy.start()

    for load in loads[:3]:
        load.wait()
    dbc = got_v[0].astype(f32)
    for s in range(1, peers):
        dbc = dbc + got_v[s].astype(f32)
    block_rows = pre_v.shape[1]
    spots = [(c, slice(l * BLOCK, (l + 1) * BLOCK)) for c in range(peers) for l in range(block_rows // BLOCK)]
    pre = jnp.concatenate([pre_v[c, at, :].T[heads : heads + share] for c, at in spots], axis=1)
    par = jnp.concatenate([par_ref[...], jnp.zeros((BLOCK - SUB, 2 * N), f32)], axis=0)
    for i in range(2 * N // BLOCK):
        par_t[i * BLOCK : (i + 1) * BLOCK, :] = par[:, i * BLOCK : (i + 1) * BLOCK].T
    keep = [1.0 - start_ref[c, l : l + 1, :] for c in range(peers) for l in range(block_rows // BLOCK)]
    keep_next = keep[block_rows // BLOCK :] + [jnp.zeros((1, BLOCK), f32)] * (block_rows // BLOCK)
    own_par = par_t.at[pl.ds(pl.multiple_of(place * share, SUB), share)]
    dpre, dpar = bc_back(dbc, pre, own_par, jnp.concatenate(keep, axis=1), jnp.concatenate(keep_next, axis=1))
    for i, (c, at) in enumerate(spots):
        tile = jnp.concatenate(
            [
                dz_v[c, at, wide:].astype(f32).T[:heads], dpre[:, i * BLOCK : (i + 1) * BLOCK],
                jnp.zeros((BLOCK - heads - share, BLOCK), f32),
            ],
            axis=0,
        )
        third_t[:, i * BLOCK : (i + 1) * BLOCK] = tile.astype(bf16)
        dz_v[c, at, wide:] = tile.T.astype(bf16)
    loads[3].wait()

    def partial_rows(s):
        weights = w_v[...].reshape(w_v.shape[0] * w_v.shape[1] * w_v.shape[2], w_v.shape[3])
        return mm(dz_v[s], weights[:, : wide + BLOCK], NT).astype(bf16)

    def order(i):
        return jnp.where(chip < chips // 2, chips - 1 - i, i)

    def over(q):
        return remote(to_mate.at[q], from_core.at[q], core_send.at[q], core_recv.at[q], mate)

    def whole_sum(q):
        over(q).wait_recv()
        add_into(mine.at[q], [from_core.at[q]], own)

    for i in range(chips):
        q = order(i)
        to_mate[q] = partial_rows(2 * q + 1 - core)
        over(q).start()
        mine[q] = partial_rows(2 * q + core)
        if i > 1:
            whole_sum(order(i - 1))
        if not i:
            whole_sum(q)
            run_hops(1)
    whole_sum(order(chips - 1))

    loads[4].wait()
    small_at = heads + share
    used = small_at + small_ref.shape[0]
    par_rows = jnp.concatenate([dpar, jnp.zeros((BLOCK - share, BLOCK), f32)], axis=0).T[:SUB]
    par_rows = jnp.concatenate([par_rows, jnp.zeros((SUB, own - BLOCK), f32)], axis=1)
    grads = mm(third_t[...], normed_v[...].reshape(times, normed_v.shape[2]))
    tail = [jnp.zeros((third_g.shape[0] - used - SUB, third_g.shape[1]), f32)] if third_g.shape[0] > used + SUB else []
    third_g[...] = jnp.concatenate(
        [grads[:small_at], small_ref[...], jnp.concatenate([par_rows] * peers, axis=1), *tail], axis=0
    ).astype(bf16)
    begin(2)

    exchange(0)
    if chips > 2:
        run_hops(2)
    spread(0)
    exchange(1)
    exchange(2)
    for step in range(3, chips):
        run_hops(step)
    spread(1)
    spread(2)

    for by in (1, -1):
        @pl.when(later(by))
        def _():
            buffer = flow(by)[0].at[chips - 2]
            hop(buffer, by, chips - 1).wait_recv()
            add_into(mine.at[chip], [buffer], own)

    rows_ref[...] = mine[chip]

    for step in range(1, chips):
        for by in (1, -1):
            @pl.when(sends(by, step))
            def _():
                hop(mine.at[0], by, step).wait_send()
    for q in range(chips):
        over(q).wait_send()
    for k in range(len(sets)):
        for copy in to_width[k] + to_owner[k]:
            copy.wait_send()
        for copy in to_all[k]:
            copy.wait()


def scattered_out(got, zx, dzx, weights, normed, wide, par, starts, small, heads):
    peers, widths = lax.axis_size("seq"), lax.axis_size("width")
    chips = peers // 2
    dma = pltpu.SemaphoreType.DMA
    anywhere = pl.BlockSpec(memory_space=pl.ANY)
    vmem = pl.BlockSpec(memory_space=pltpu.VMEM)
    own, model = normed.shape[0] // peers, normed.shape[1]
    half = wide.shape[3] // 2
    strips = -(-(heads + got.shape[1] + small.shape[0] + SUB) // (16 * widths)) * 16 * widths
    pieces = [(peers, wide.shape[2], half), (peers, wide.shape[2], half), (peers, strips // widths, own)]
    kept = pieces[:2] + [(strips // widths, model)]
    block = (own, model)
    zx, dzx, normed = [a.reshape(peers, own, a.shape[1]) for a in (zx, dzx, normed)]
    return pl.pallas_call(
        partial(scatter_kernel, peers=peers, widths=widths, heads=heads),
        in_specs=[anywhere] * 6 + [vmem] * 3,
        out_specs=[vmem, anywhere, anywhere],
        out_shape=[
            jax.ShapeDtypeStruct(block, bf16), jax.ShapeDtypeStruct(wide.shape, bf16),
            jax.ShapeDtypeStruct((peers, widths, strips // widths, own), bf16),
        ],
        scratch_shapes=[
            pltpu.VMEM(got.shape, bf16), pltpu.VMEM((peers, own, BLOCK), f32), pltpu.VMEM(dzx.shape, bf16),
            pltpu.VMEM(weights.shape, bf16), pltpu.VMEM(normed.shape, bf16),
            pltpu.VMEM((BLOCK, peers * own), bf16), pltpu.VMEM((strips, model), bf16), pltpu.VMEM((2 * N, BLOCK), f32),
            *[pltpu.VMEM((chips,) + block, bf16)] * 3, *[pltpu.VMEM((chips - 1,) + block, bf16)] * 2,
            *[pltpu.VMEM(a, bf16) for a in kept],
            *[pltpu.VMEM((widths - 1,) + a, bf16) for a in kept],
            *[pltpu.VMEM(a, bf16) for a in pieces],
            dma((5,)), dma((chips,)), dma((chips,)),
            dma((chips - 1,)), dma((chips - 1,)), dma((chips - 1,)), dma((chips - 1,)),
            dma((3, 3)), dma((3, widths - 1)), dma((3, widths - 1)), dma((3, peers - 1)), dma((3, peers - 1)),
            dma((3, widths - 1)), dma((3, widths - 1)),
        ],
        compiler_params=pltpu.CompilerParams(collective_id=2, has_side_effects=True, vmem_limit_bytes=62 << 20),
        name="scatter_out",
    )(got, zx, dzx, weights, normed, wide, par, starts, small)


def laid_kernel(
    in_ref, third_ref, w_ref, bc_ref, dt_ref, gain_ref, rows_ref, x_ref, cot_ref, norm_gain_ref,
    out_ref, out_bc_ref, out_dt_ref, norm_ref, out_rows_ref, rest,
    *, heads, share,
):
    peers, rows, wide = in_ref.shape[0], in_ref.shape[2], in_ref.shape[3]
    chans = wide // 2
    step = pl.program_id(0)

    @pl.when(step == 0)
    def _():
        third = [
            jnp.concatenate([third_ref[s, q].astype(f32) for q in range(third_ref.shape[1])], axis=0) for s in range(peers)
        ]
        dt = jnp.concatenate([t[:heads] for t in third], axis=0).T
        bc = jnp.concatenate([t[heads : heads + share] for t in third], axis=0).T
        out_bc_ref[...] = bc
        out_dt_ref[...] = dt
        total = jnp.sum(bc * bc_ref[...].astype(f32), axis=1, keepdims=True)
        rest[...] = total + jnp.sum(dt * dt_ref[...].astype(f32), axis=1, keepdims=True)

    lane = jnp.zeros((rows, BLOCK), f32)
    for s in range(peers):
        for half in (0, 1):
            at = (half * peers + s) * chans
            value = in_ref[s, 0, :, half * chans : (half + 1) * chans].astype(f32)
            out_ref[:, at : at + chans] = value
            value = value * w_ref[:, at : at + chans].astype(f32)
            for j in range(chans // BLOCK):
                lane = lane + value[:, j * BLOCK : (j + 1) * BLOCK]
    x = x_ref[...].astype(f32)
    rate = lax.rsqrt(jnp.mean(x * x, axis=-1, keepdims=True) + epsilon)
    unit = x * rate
    pulled = rows_ref[...].astype(f32) * norm_gain_ref[...]
    inner = jnp.mean(pulled * unit, axis=-1, keepdims=True)
    out_rows_ref[...] = cot_ref[...].astype(f32) + rate * (pulled - unit * inner)
    more = rest[pl.ds(pl.multiple_of(step * rows, SUB), rows), :]
    norm_ref[...] = (jnp.sum(lane, axis=1, keepdims=True) + more) / gain_ref[...]


def laid_out(wide, third, w_zx, w_bc, w_dt, gain, normed_grad, x_rows, cotangent, norm_gain, heads):
    peers, widths, quarter, cols = wide.shape
    rows = widths * quarter
    cut = quarter
    share = w_bc.shape[1] // peers
    by_rows = lambda a: pl.BlockSpec((cut, a.shape[1]), lambda i: (i, 0))
    whole = lambda a: pl.BlockSpec(a.shape, lambda i: (0,) * len(a.shape))
    by_piece = pl.BlockSpec((peers, 1, cut, cols), lambda i: (0, i, 0, 0))
    shapes = [jax.ShapeDtypeStruct(a.shape, f32) for a in (w_zx, w_bc, w_dt, gain, x_rows)]
    return pl.pallas_call(
        partial(laid_kernel, heads=heads, share=share),
        grid=(widths,),
        in_specs=[
            by_piece, whole(third), by_rows(w_zx), whole(w_bc), whole(w_dt), by_rows(gain),
            by_rows(normed_grad), by_rows(x_rows), by_rows(cotangent), whole(norm_gain),
        ],
        out_specs=[by_rows(w_zx), whole(w_bc), whole(w_dt), by_rows(gain), by_rows(x_rows)],
        out_shape=shapes,
        scratch_shapes=[pltpu.VMEM((rows, 1), f32)],
        compiler_params=pltpu.CompilerParams(vmem_limit_bytes=62 << 20),
        name="lay_out",
    )(wide, third, w_zx, w_bc, w_dt, gain, normed_grad, x_rows, cotangent, norm_gain)


def crossed(value, axis, mask):
    return lax.ppermute(value, axis, [(i, i ^ mask) for i in range(lax.axis_size(axis))])


def pick(value, index):
    return lax.dynamic_index_in_dim(value, index, 0, False)


def quarters_sent(value):
    widths, width = lax.axis_size("width"), lax.axis_index("width")
    value = value.reshape((widths, value.shape[0] // widths) + value.shape[1:])
    sent = [crossed(pick(value, jnp.bitwise_xor(width, m)), "width", m) for m in range(1, widths)]
    return [pick(value, width)] + sent


def quarters_back(total):
    widths = lax.axis_size("width")
    return [total] + [crossed(total, "width", m) for m in range(1, widths)]


def quarters_joined(pieces):
    width = lax.axis_index("width")
    stacked = jnp.stack(pieces)
    whole = jnp.stack([pick(stacked, jnp.bitwise_xor(width, j)) for j in range(len(pieces))])
    return whole.reshape((-1,) + whole.shape[2:]).astype(f32)


def heads_body(
    tokens, cotangent, starts, valid, norm_gain, w_zx, w_bc, w_dt, conv_w, conv_b, dt_bias, a_log, d_skip, gate_gain, w_out
):
    peers = lax.axis_size("seq")
    widths = lax.axis_size("width")
    place = lax.axis_index("seq")
    lanes = starts.shape[1]
    heads = H // peers
    chans = heads * HEAD_DIM
    own, model = tokens.shape
    rows = own * peers
    first = place * heads
    share = 2 * N // peers
    used = heads + share
    row_mask = (jnp.arange(BLOCK)[None, :] < valid[0][:, None]).astype(f32).reshape(-1, 1)
    spread = jnp.asarray(np.arange(chans)[None, :] // HEAD_DIM == np.arange(BLOCK)[:, None], bf16)
    weights, normed, bgrad, starts_all, chan, head, bc_par, *computed = front(
        valid, starts, tokens, cotangent, norm_gain[None], w_bc, w_dt, conv_w.T, conv_b[None], dt_bias[None], a_log[None],
        d_skip[None], gate_gain[None], spread, w_zx, w_out,
    )
    normed, bgrad = normed.reshape(rows, model), bgrad.reshape(rows, model)
    zx, mix, mixed_grad, scale, mixed_low = [a.reshape(rows, a.shape[-1]) for a in computed[:5]]
    part = computed[5].reshape(rows // 2, model)
    conv, bc, steps = [a.reshape(rows, a.shape[-1]) for a in computed[6:9]]
    state, tail = computed[9:]
    like_cores = [list(range(core, peers, 2)) for core in range(2)]
    branch = lax.psum_scatter(part, "seq", scatter_dimension=0, axis_index_groups=like_cores, tiled=True).astype(f32)
    output = (tokens.astype(f32) + row_mask * branch).astype(bf16)
    out_part = mm(mixed_low, bgrad, TN).astype(bf16)
    scale, out_part = lax.optimization_barrier((scale, out_part))
    out_quarters = quarters_sent(out_part)

    dzx, dbc, dchan, dhead = run_backward(
        starts_all, zx, mixed_grad, chan, head, spread, conv, mix, bc, steps, state, tail, scale, lanes, heads
    )
    dzx, dbc, out_quarters = lax.optimization_barrier((dzx, dbc, out_quarters))
    out_pieces = quarters_back(sum(q.astype(f32) for q in out_quarters).astype(bf16))

    got = lax.all_to_all(dbc.reshape(peers, share, rows), "seq", 0, 0, tiled=True)

    at_heads = lambda a: lax.dynamic_update_slice_in_dim(jnp.zeros((H,), f32), a, first, 0)
    at_chans = lambda a: lax.dynamic_update_slice_in_dim(jnp.zeros((E,), f32), a, first * HEAD_DIM, 0)
    skip = jnp.sum(dchan[SKIP].reshape(heads, HEAD_DIM), axis=1)
    small = [jnp.pad(at_chans(dchan[k]), (0, 2 * N)) for k in range(KCONV + 1)]
    small += [at_chans(dchan[GAIN]), at_heads(dhead[0, :heads]), at_heads(dhead[1, :heads]), at_heads(skip)]
    sizes = [a.shape[0] // peers for a in small]
    small = jnp.concatenate([a.reshape(peers, -1) for a in small], axis=1)
    small_rows = -(-small.shape[1] // (own * SUB)) * SUB
    small = jnp.pad(small, ((0, 0), (0, own * small_rows - small.shape[1])))
    small = small.reshape(peers, small_rows, own).transpose(1, 0, 2).reshape(small_rows, model)

    wide = mm(normed, dzx[:, : 2 * chans], TN).astype(bf16)
    wide, out_pieces = lax.optimization_barrier((wide, out_pieces))
    out_grad = quarters_joined(out_pieces)
    got, output, out_grad = lax.optimization_barrier((got, output, out_grad))
    normed_grad, wide, third = scattered_out(
        got, zx, dzx, weights, normed, wide.reshape(peers, widths, own // widths, -1), bc_par, starts_all, small, heads,
    )
    gain_rows = lax.dynamic_slice_in_dim(norm_gain, place * own, own, 0)[:, None]
    grad_zx, grad_bc, grad_dt, grad_norm, input_grad = laid_out(
        wide, third, w_zx, w_bc, w_dt, gain_rows, normed_grad, tokens, cotangent, norm_gain[None], heads
    )
    grad_norm = grad_norm[:, 0]
    third = third.reshape(peers, -1, own)
    summed = jnp.sum(third[:, used : used + small_rows].astype(f32), axis=0).reshape(-1)
    pieces = [summed[sum(sizes[:i]) : sum(sizes[: i + 1])] for i in range(len(sizes))]
    of_bc = third[:, used + small_rows : used + small_rows + KCONV + 1, :share].astype(f32).transpose(1, 0, 2).reshape(KCONV + 1, 2 * N)
    own_chans = sizes[0]
    of_bc = lax.dynamic_slice_in_dim(jnp.pad(of_bc, ((0, 0), (E, 0))), place * own_chans, own_chans, 1)
    grad_taps = jnp.stack(pieces[:KCONV], axis=1) + of_bc[:KCONV].T
    grad_bias, grad_gain, grad_dtb, grad_alog, grad_skip = pieces[KCONV:]
    grad_bias = grad_bias + of_bc[KCONV]
    return (
        output, input_grad, grad_norm, grad_zx, grad_bc, grad_dt, grad_taps, grad_bias, grad_dtb, grad_alog, grad_skip,
        grad_gain, out_grad,
    )


def passed_along(array, axis, by):
    peers = lax.axis_size(axis)
    pairs = [(i, i + by) for i in range(peers) if 0 <= i + by < peers]
    return lax.ppermute(array, axis, pairs)


def carried_in(part, axis, combine, identity, reverse):
    count = lax.axis_size(axis)
    place = lax.axis_index(axis)
    at = count - 1 - place if reverse else place
    by = -1 if reverse else 1
    state = jax.tree.map(lambda a, e: jnp.zeros_like(a) + jnp.asarray(e, a.dtype), part, identity)

    def one(lap, state):
        sent = combine(state, part)
        got = jax.tree.map(lambda a: passed_along(a, axis, by), sent)
        return jax.tree.map(lambda old, new: jnp.where(at == lap + 1, new, old), state, got)

    return lax.fori_loop(0, count - 1, one, state)


def round_value(v):
    return lax.optimization_barrier(v.astype(jnp.bfloat16)).astype(jnp.float32)


def keep_round(v):
    return (round_value(v), None)


def pass_grad(kept, grad):
    return (grad,)


def same_value(v):
    return v


def keep_same(v):
    return (v, None)


def round_grad(kept, grad):
    return (round_value(grad),)


def low(v):
    wrapped = jax.custom_vjp(round_value)
    wrapped.defvjp(keep_round, pass_grad)
    return wrapped(v)


def low_back(v):
    wrapped = jax.custom_vjp(same_value)
    wrapped.defvjp(keep_same, round_grad)
    return wrapped(v)


def rms_front(x_rows, norm_gain):
    mean_square = jnp.mean(x_rows * x_rows, axis=-1, keepdims=True)
    return x_rows * lax.rsqrt(mean_square + epsilon) * norm_gain


def rim_of(zx_pre, bc_pre, chan_mask):
    return jnp.concatenate(
        [zx_pre[:, BLOCK - KCONV + 1 :, E:] * chan_mask, bc_pre[:, BLOCK - KCONV + 1 :, :]], axis=-1
    )


def piece_front(
    zx_pre,
    bc_pre,
    dt_raw,
    rim_rows,
    conv_w,
    conv_b,
    dt_bias,
    a_log,
    chan_mask,
    head_mask,
    keep_rows,
):
    z_gate = zx_pre[..., :E] * chan_mask
    pre_conv = jnp.concatenate([zx_pre[..., E:] * chan_mask, bc_pre], axis=-1)
    padded = jnp.concatenate([rim_rows * keep_rows[:, None, None], pre_conv], axis=1)
    conv_out = conv_b + padded[:, 0:BLOCK, :] * conv_w[:, 0]
    for offset in range(1, KCONV):
        conv_out = conv_out + padded[:, offset : offset + BLOCK, :] * conv_w[:, offset]
    active = jax.nn.silu(conv_out)
    x_conv = low(active[..., :E] * chan_mask)
    b_conv = low(active[..., E : E + N])
    c_conv = low(active[..., E + N :])
    dt_step = jax.nn.softplus(dt_raw + dt_bias) * head_mask
    log_step = -jnp.exp(a_log) * dt_step
    return (z_gate, x_conv, b_conv, c_conv, dt_step, log_step)


def block_state(x_conv, b_conv, dt_step, log_step):
    cumulative = jnp.cumsum(log_step, axis=1)
    to_end = jnp.exp(cumulative[:, -1:, :] - cumulative) * dt_step
    weighted = low(x_conv.reshape(x_conv.shape[0], BLOCK, H, HEAD_DIM) * to_end[..., None])
    state_sum = jnp.einsum("lqhp,lqn->lhpn", weighted, b_conv, precision=highest)
    return (state_sum, cumulative[:, -1, :])


def piece_mix(
    z_gate, x_conv, b_conv, c_conv, dt_step, log_step, state_in, d_skip, gate_gain, chan_count
):
    lane_count = x_conv.shape[0]
    cumulative = jnp.cumsum(log_step, axis=1)
    cum_heads = jnp.swapaxes(cumulative, 1, 2)
    causal = jnp.arange(BLOCK)[:, None] >= jnp.arange(BLOCK)[None, :]
    spread = cum_heads[:, :, :, None] - cum_heads[:, :, None, :]
    decays = jnp.where(causal, jnp.exp(jnp.where(causal, spread, 0.0)), 0.0)
    inner_cb = jnp.einsum("lqn,lsn->lqs", c_conv, b_conv, precision=highest)
    scores = low(inner_cb[:, None] * decays * jnp.swapaxes(dt_step, 1, 2)[:, :, None, :])
    x_heads = x_conv.reshape(lane_count, BLOCK, H, HEAD_DIM)
    within = jnp.einsum("lhqs,lshp->lqhp", scores, x_heads, precision=highest)
    carried = (
        jnp.einsum("lqn,lhpn->lqhp", c_conv, state_in, precision=highest)
        * jnp.exp(cumulative)[..., None]
    )
    mixed_sum = low_back(within + carried) + d_skip[:, None] * x_heads
    gated_rows = mixed_sum.reshape(lane_count, BLOCK, E) * jax.nn.silu(z_gate)
    mean_square = jnp.sum(gated_rows * gated_rows, axis=-1, keepdims=True) / chan_count
    return low(gated_rows * lax.rsqrt(mean_square + epsilon) * gate_gain)


def mix_lanes(lane_inputs, d_skip, gate_gain, chan_count):

    def one_lane(pieces):
        lane_gate, lane_xconv, lane_bconv, lane_cconv, lane_step, lane_decay, lane_state = pieces
        return piece_mix(
            lane_gate[None],
            lane_xconv[None],
            lane_bconv[None],
            lane_cconv[None],
            lane_step[None],
            lane_decay[None],
            lane_state[None],
            d_skip,
            gate_gain,
            chan_count,
        )[0]

    return lax.map(one_lane, lane_inputs)


def mix_back_lanes(lane_inputs, mixed_grad, d_skip, gate_gain, chan_count):

    def lane_mix(z_gate, x_conv, b_conv, c_conv, dt_step, log_step, state_in, skip_coef, gain_coef):
        return piece_mix(
            z_gate[None],
            x_conv[None],
            b_conv[None],
            c_conv[None],
            dt_step[None],
            log_step[None],
            state_in[None],
            skip_coef,
            gain_coef,
            chan_count,
        )[0]

    def one_lane(pieces):
        (
            lane_gate,
            lane_xconv,
            lane_bconv,
            lane_cconv,
            lane_step,
            lane_decay,
            lane_state,
            lane_grad,
        ) = pieces
        unused, pull_lane = jax.vjp(
            lane_mix,
            lane_gate,
            lane_xconv,
            lane_bconv,
            lane_cconv,
            lane_step,
            lane_decay,
            lane_state,
            d_skip,
            gate_gain,
        )
        return pull_lane(lane_grad)

    lane_grads = lax.map(one_lane, lane_inputs + (mixed_grad,))
    return (lane_grads[:7], jnp.sum(lane_grads[7], axis=0), jnp.sum(lane_grads[8], axis=0))


def chain_combine(earlier, latter):
    return (earlier[0] * latter[0], latter[0][:, :, None, None] * earlier[1] + latter[1])


def share_out(out_grad):
    return lax.psum_scatter(out_grad, "seq", scatter_dimension=0, tiled=True)


def contract_rows(left, right):
    return lax.dot_general(
        left, right, (((0,), (0,)), ((), ())), preferred_element_type=jnp.float32
    )


def contract_cols(left, right):
    return lax.dot_general(
        left, right, (((1,), (1,)), ((), ())), preferred_element_type=jnp.float32
    )


def rows_body(
    tokens,
    cotangent,
    starts,
    valid,
    norm_gain,
    w_zx,
    w_bc,
    w_dt,
    conv_w,
    conv_b,
    dt_bias,
    a_log,
    d_skip,
    gate_gain,
    w_out,
):
    lane_count = starts.shape[1]
    width_index = lax.axis_index("width")
    shift_bits = lax.axis_size("width") - 1 - width_index
    active_heads = jnp.right_shift(jnp.int32(H), shift_bits)
    chan_mask = (jnp.arange(E) // HEAD_DIM < active_heads).astype(jnp.float32)
    head_mask = (jnp.arange(H) < active_heads).astype(jnp.float32)
    chan_count = (active_heads * HEAD_DIM).astype(jnp.float32)
    keep_rows = 1.0 - starts[0].astype(jnp.float32)
    row_mask = (jnp.arange(BLOCK)[None, :] < valid[0][:, None]).astype(jnp.float32).reshape(-1, 1)
    x_rows = tokens.astype(jnp.float32)
    normed, norm_back = jax.vjp(rms_front, x_rows, norm_gain)
    normed_low = normed.astype(jnp.bfloat16)
    zx_full, bc_full, dt_full, out_full = (
        lax.all_gather(w_zx, "seq", axis=0, tiled=True),
        lax.all_gather(w_bc, "seq", axis=0, tiled=True),
        lax.all_gather(w_dt, "seq", axis=0, tiled=True),
        lax.all_gather(w_out, "seq", axis=0, tiled=True),
    )
    zx_pre = jnp.dot(normed_low, zx_full, preferred_element_type=jnp.float32).reshape(
        lane_count, BLOCK, 2 * E
    )
    bc_pre = jnp.dot(normed_low, bc_full, preferred_element_type=jnp.float32).reshape(
        lane_count, BLOCK, 2 * N
    )
    dt_raw = jnp.dot(normed_low, dt_full, preferred_element_type=jnp.float32).reshape(
        lane_count, BLOCK, H
    )
    rim_rows = passed_along(rim_of(zx_pre, bc_pre, chan_mask), "seq", 1)
    front_fn = partial(piece_front, chan_mask=chan_mask, head_mask=head_mask, keep_rows=keep_rows)
    front_out, front_back = jax.vjp(
        front_fn, zx_pre, bc_pre, dt_raw, rim_rows, conv_w, conv_b, dt_bias, a_log
    )
    z_gate, x_conv, b_conv, c_conv, dt_step, log_step = front_out
    (state_sum, log_total), state_back = jax.vjp(block_state, x_conv, b_conv, dt_step, log_step)
    carry_rate = jnp.exp(log_total) * keep_rows[:, None]
    identity = (jnp.ones_like(carry_rate), jnp.zeros_like(state_sum))
    prefix_pair = carried_in((carry_rate, state_sum), "seq", chain_combine, identity, False)
    state_in = prefix_pair[1] * keep_rows[:, None, None, None]
    lane_inputs = (z_gate, x_conv, b_conv, c_conv, dt_step, log_step, state_in)
    mixed_low = mix_lanes(lane_inputs, d_skip, gate_gain, chan_count)
    mixed_flat = mixed_low.reshape(-1, E).astype(jnp.bfloat16)
    branch = jnp.dot(mixed_flat, out_full, preferred_element_type=jnp.float32)
    output = (x_rows + row_mask * branch).astype(jnp.bfloat16)
    cot_rows = cotangent.astype(jnp.float32)
    branch_grad = (cot_rows * row_mask).astype(jnp.bfloat16)
    out_grad = contract_rows(mixed_flat, branch_grad)
    mixed_grad = contract_cols(branch_grad, out_full).reshape(lane_count, BLOCK, E)
    lane_grads, grad_skip, grad_gain = mix_back_lanes(
        lane_inputs, mixed_grad, d_skip, gate_gain, chan_count
    )
    grad_gate, grad_x, grad_b, grad_c, grad_dt, grad_log, grad_state = lane_grads
    later_pair = carried_in(
        (carry_rate, grad_state * keep_rows[:, None, None, None]),
        "seq",
        chain_combine,
        identity,
        True,
    )
    later_grad = later_pair[1]
    grad_total = jnp.exp(log_total) * jnp.sum(later_grad * state_in, axis=(2, 3))
    grad_x_more, grad_b_more, grad_dt_more, grad_log_more = state_back((later_grad, grad_total))
    grad_zx, grad_bc, grad_dtraw, grad_rim, grad_convw, grad_convb, grad_dtbias, grad_alog = (
        front_back(
            (
                grad_gate,
                grad_x + grad_x_more,
                grad_b + grad_b_more,
                grad_c,
                grad_dt + grad_dt_more,
                grad_log + grad_log_more,
            )
        )
    )
    rim_grad = passed_along(grad_rim.astype(jnp.bfloat16), "seq", -1).astype(grad_rim.dtype)
    grad_zx = grad_zx.at[:, BLOCK - KCONV + 1 :, E:].add(rim_grad[..., :E] * chan_mask)
    grad_bc = grad_bc.at[:, BLOCK - KCONV + 1 :, :].add(rim_grad[..., E:])
    zx_low = grad_zx.reshape(-1, 2 * E).astype(jnp.bfloat16)
    bc_low = grad_bc.reshape(-1, 2 * N).astype(jnp.bfloat16)
    dt_low = grad_dtraw.reshape(-1, H).astype(jnp.bfloat16)
    zx_weight_grad = contract_rows(normed_low, zx_low)
    bc_weight_grad = contract_rows(normed_low, bc_low)
    dt_weight_grad = contract_rows(normed_low, dt_low)
    normed_grad = (
        contract_cols(zx_low, zx_full)
        + contract_cols(bc_low, bc_full)
        + contract_cols(dt_low, dt_full)
    )
    grad_x_rows, grad_norm = norm_back(normed_grad)
    input_grad = cot_rows + grad_x_rows
    out_shard = share_out(out_grad)
    row_shards = (
        lax.psum_scatter(grad_norm, "seq", scatter_dimension=0, tiled=True),
        lax.psum_scatter(zx_weight_grad, "seq", scatter_dimension=0, tiled=True),
        lax.psum_scatter(bc_weight_grad, "seq", scatter_dimension=0, tiled=True),
        lax.psum_scatter(dt_weight_grad, "seq", scatter_dimension=0, tiled=True),
        lax.psum_scatter(grad_convw, "seq", scatter_dimension=0, tiled=True),
        lax.psum_scatter(grad_convb, "seq", scatter_dimension=0, tiled=True),
        lax.psum_scatter(grad_dtbias, "seq", scatter_dimension=0, tiled=True),
        lax.psum_scatter(grad_alog, "seq", scatter_dimension=0, tiled=True),
        lax.psum_scatter(grad_skip, "seq", scatter_dimension=0, tiled=True),
        lax.psum_scatter(grad_gain, "seq", scatter_dimension=0, tiled=True),
    )
    summed = lax.psum(
        (
            row_shards[0],
            row_shards[1],
            row_shards[2],
            row_shards[3],
            row_shards[4],
            row_shards[5],
            row_shards[6],
            row_shards[7],
            row_shards[8],
            row_shards[9],
            out_shard,
        ),
        "width",
    )
    return (
        output,
        input_grad,
        summed[0],
        summed[1],
        summed[2],
        summed[3],
        summed[4],
        summed[5],
        summed[6],
        summed[7],
        summed[8],
        summed[9],
        summed[10],
    )


def solution(mesh):
    in_specs = (
        P(("width", "seq"), None),
        P(("width", "seq"), None),
        P(("width", "seq"), None),
        P(("width", "seq"), None),
        P(),
        P("seq", None),
        P("seq", None),
        P("seq", None),
        P(),
        P(),
        P(),
        P(),
        P(),
        P(),
        P("seq", None),
    )
    out_specs = (
        P(("width", "seq"), None),
        P(("width", "seq"), None),
        P("seq"),
        P("seq", None),
        P("seq", None),
        P("seq", None),
        P("seq", None),
        P("seq"),
        P("seq"),
        P("seq"),
        P("seq"),
        P("seq"),
        P("seq", None),
    )
    body = heads_body if H % (2 * mesh.shape["seq"]) == 0 else rows_body
    return jax.shard_map(body, mesh=mesh, in_specs=in_specs, out_specs=out_specs, check_vma=False)
```

```python
from functools import partial

import jax
import jax.numpy as jnp
from jax import lax
from jax.experimental import pallas as pl
from jax.experimental.pallas import tpu as pltpu
from jax.sharding import PartitionSpec as P
import numpy as np

H = 64
HEAD_DIM = 64
N = 128
KCONV = 4
BLOCK = 128
E = 4096
SUB = 8

epsilon = 1e-05
highest = lax.Precision.HIGHEST
f32 = jnp.float32
bf16 = jnp.bfloat16

NN = ((1,), (0,))
NT = ((1,), (1,))
TN = ((0,), (0,))


def mm(left, right, dims=NN, precision=None):
    return lax.dot_general(left, right, (dims, ((), ())), precision=precision, preferred_element_type=f32)


def split2(value):
    high = value.astype(bf16)
    return high, (value - high.astype(f32)).astype(bf16)


def mm_right(left, right, dims=NN):
    high, low = split2(right)
    return mm(left, high, dims) + mm(left, low, dims)


def mm_left(left, right, dims=NN):
    high, low = split2(left)
    return mm(high, right, dims) + mm(low, right, dims)


def softplus(v):
    small = jnp.exp(-jnp.abs(v))
    log1p = jnp.where(small < 1e-4, small - 0.5 * small * small, jnp.log(1.0 + small))
    return jnp.maximum(v, 0.0) + log1p


def sigmoid(v):
    return 1.0 / (1.0 + jnp.exp(-v))


def grids():
    row = lax.broadcasted_iota(jnp.int32, (BLOCK, BLOCK), 0)
    col = lax.broadcasted_iota(jnp.int32, (BLOCK, BLOCK), 1)
    return row, col


def halves(pair, lane):
    zero = jnp.zeros_like(pair)
    return jnp.where(lane < HEAD_DIM, pair, zero), jnp.where(lane < HEAD_DIM, zero, pair)


def decay_of(cum, cum_t, head, causal):
    return jnp.exp(jnp.where(causal, cum[:, head : head + 1] - cum_t[head : head + 1, :], -1e30))


TAP, BIAS, SKIP, GAIN, MASK = 0, 4, 5, 6, 7
DT_BIAS, NEG_A, HEAD_MASK = 0, 1, 2


def forward_block(
    keep_row, zx_ref, chan_ref, bc_par_ref, head_ref, spread,
    conv_ref, mix_ref, bc_ref, step_ref, state_ref, tail_ref,
    state, tail_x, tail_b, pad_x, pad_b,
    *, lane, heads,
):
    width = heads * HEAD_DIM
    row, col = grids()
    causal = row >= col
    tril = causal.astype(f32)
    rows = pl.ds(lane * BLOCK, BLOCK)
    keep = jnp.concatenate([keep_row] * (width // BLOCK), axis=1)
    keep_b = jnp.concatenate([keep_row] * (2 * N // BLOCK), axis=1)

    pre = zx_ref[rows, width : 2 * width]
    before = tail_x[lane] * keep
    pad_x[lane, 0:SUB] = before
    pad_x[lane, SUB:] = pre
    tail_ref[lane] = before
    tail_x[lane] = pre[BLOCK - SUB :, :]
    conv = chan_ref[BIAS : BIAS + 1, :]
    for k in range(KCONV):
        conv = conv + pad_x[lane, SUB - KCONV + 1 + k : SUB - KCONV + 1 + k + BLOCK, :] * chan_ref[k : k + 1, :]
    conv_ref[rows, :] = conv
    x_low = (conv * sigmoid(conv) * chan_ref[MASK : MASK + 1, :]).astype(bf16)

    pre_b = zx_ref[rows, 2 * width + BLOCK :]
    pad_b[lane, 0:SUB] = tail_b[lane] * keep_b
    pad_b[lane, SUB:] = pre_b
    tail_b[lane] = pre_b[BLOCK - SUB :, :]
    conv_b = bc_par_ref[BIAS : BIAS + 1, :]
    for k in range(KCONV):
        conv_b = conv_b + pad_b[lane, SUB - KCONV + 1 + k : SUB - KCONV + 1 + k + BLOCK, :] * bc_par_ref[k : k + 1, :]
    bc_low = (conv_b * sigmoid(conv_b)).astype(bf16)
    bc_ref[rows, :] = bc_low
    b_low, c_low = bc_low[:, :N], bc_low[:, N:]

    raw = zx_ref[rows, 2 * width : 2 * width + BLOCK] + head_ref[DT_BIAS : DT_BIAS + 1, :]
    dt = softplus(raw) * head_ref[HEAD_MASK : HEAD_MASK + 1, :]
    cum = mm(tril, head_ref[NEG_A : NEG_A + 1, :] * dt, precision=highest)
    step_ref[rows, :BLOCK] = cum
    step_ref[rows, BLOCK:] = dt
    cum_t, dt_t = cum.T, dt.T
    last = cum[BLOCK - 1 :, :]
    carry_x = mm_left(jnp.exp(cum), spread)
    end_x = mm_left(jnp.exp(last - cum) * dt, spread)
    last_x = carry_x[BLOCK - 1 :, :]

    inner = mm(c_low, b_low, NT)
    parts = []
    for j in range(heads // 2):
        pair = x_low[:, 2 * HEAD_DIM * j : 2 * HEAD_DIM * (j + 1)]
        scores = [
            (inner * decay_of(cum, cum_t, h, causal) * dt_t[h : h + 1, :]).astype(bf16)
            for h in (2 * j, 2 * j + 1)
        ]
        parts.append(mm(jnp.concatenate(scores, axis=1), jnp.concatenate(halves(pair, col), axis=0)))
    within = jnp.concatenate(parts, axis=1)

    state_in = state[lane] * keep
    state_ref[lane] = state_in
    carried = mm_right(c_low, state_in) * carry_x
    x_f = x_low.astype(f32)
    mix_ref[rows, :] = within + carried + chan_ref[SKIP : SKIP + 1, :] * x_f
    weighted = (x_f * end_x).astype(bf16)
    state[lane] = last_x * state_in + mm(b_low, weighted, TN)


def backward_kernel(
    start_ref, zx_ref, grad_ref, chan_ref, head_ref, spread_ref,
    conv_ref, mix_ref, bc_ref, step_ref, state_ref, tail_ref, scale_ref,
    dzx_ref, dbc_ref, dchan_ref, dhead_ref,
    state_grad, next_conv, pad_x, pad_d,
    *, lanes, heads,
):
    lap = pl.program_id(0)
    width = heads * HEAD_DIM
    row, col = grids()
    causal = row >= col
    triu = (col >= row).astype(f32)
    spread = spread_ref[...]

    @pl.when(lap == 0)
    def _():
        state_grad[...] = jnp.zeros_like(state_grad)
        next_conv[...] = jnp.zeros_like(next_conv)
        dchan_ref[...] = jnp.zeros_like(dchan_ref)
        dhead_ref[...] = jnp.zeros_like(dhead_ref)

    def total(value):
        return jnp.sum(value, axis=0, keepdims=True)

    for lane in range(lanes):
        rows = pl.ds(lane * BLOCK, BLOCK)
        keep = 1.0 - jnp.concatenate([start_ref[0, lane : lane + 1, :]] * (width // BLOCK), axis=1)
        z = zx_ref[rows, :width]
        conv = conv_ref[rows, :]
        mixed = mix_ref[rows, :]
        grad = grad_ref[rows, :]
        gain = chan_ref[GAIN : GAIN + 1, :]
        skip = chan_ref[SKIP : SKIP + 1, :]
        rate = scale_ref[rows, 0:1]
        pull = scale_ref[rows, 1:2]
        gate = sigmoid(z)
        silu = z * gate
        gated = mixed * silu
        dgated = grad * gain * rate - gated * pull
        dzx_ref[rows, :width] = (dgated * mixed * (gate * (1.0 + z * (1.0 - gate)))).astype(bf16)
        dmixed = dgated * silu
        act = sigmoid(conv)
        x_low = (conv * act * chan_ref[MASK : MASK + 1, :]).astype(bf16)
        x_f = x_low.astype(f32)
        dchan_ref[GAIN : GAIN + 1, :] += total(grad * gated * rate)
        dchan_ref[SKIP : SKIP + 1, :] += total(dmixed * x_f)
        dlow = dmixed.astype(bf16)
        dlow_f = dlow.astype(f32)

        b_low, c_low = bc_ref[rows, :N], bc_ref[rows, N:]
        cum, dt = step_ref[rows, :BLOCK], step_ref[rows, BLOCK:]
        cum_t, dt_t = cum.T, dt.T
        last = cum[BLOCK - 1 :, :]
        to_last = jnp.exp(last - cum)
        carry_x = mm_left(jnp.exp(cum), spread)
        end_x = mm_left(to_last * dt, spread)
        last_x = carry_x[BLOCK - 1 :, :]

        inner = mm(c_low, b_low, NT)
        dinner = jnp.zeros((BLOCK, BLOCK), f32)
        parts, dt_rows = [], []
        for j in range(heads // 2):
            lanes_j = slice(2 * HEAD_DIM * j, 2 * HEAD_DIM * (j + 1))
            pair, dpair = x_low[:, lanes_j], dlow[:, lanes_j]
            dstack = jnp.concatenate(halves(dpair, col), axis=0)
            dscores = mm(dstack, pair, NT)
            scores = []
            for i, h in enumerate((2 * j, 2 * j + 1)):
                decay = decay_of(cum, cum_t, h, causal)
                step = dt_t[h : h + 1, :]
                scores.append((inner * decay * step).astype(bf16))
                part = dscores[i * BLOCK : (i + 1) * BLOCK] * decay
                dinner = dinner + part * step
                dt_rows.append(total(part * inner))
            parts.append(mm(jnp.concatenate(scores, axis=0), dstack, TN))
        dx_within = jnp.concatenate(parts, axis=1)
        dt_rows.append(jnp.zeros((BLOCK - heads, BLOCK), f32))
        ddt_within = jnp.concatenate(dt_rows, axis=0).T

        state_in = state_ref[0, lane]
        sgrad = state_grad[lane]
        in_high, in_low = split2(state_in)
        sg_high, sg_low = split2(sgrad)
        dcarry = dlow_f * carry_x
        dc_high, dc_low = split2(dcarry)
        di_high, di_low = split2(dinner)
        dc = mm(dc_high, in_high, NT) + mm(dc_high, in_low, NT) + mm(dc_low, in_high, NT)
        dc = dc + mm(di_high, b_low) + mm(di_low, b_low)
        weighted = (x_f * end_x).astype(bf16)
        db = mm(weighted, sg_high, NT) + mm(weighted, sg_low, NT)
        db = db + mm(di_high, c_low, TN) + mm(di_low, c_low, TN)
        dbc_ref[:N, rows] = db.T.astype(bf16)
        dbc_ref[N:, rows] = dc.T.astype(bf16)
        dweighted = mm(b_low, sg_high) + mm(b_low, sg_low)
        dx = dx_within + dweighted * end_x
        dcum = mm_left(dlow_f * (mixed - skip * x_f) - x_f * dx, spread, NT)
        dend = mm_left(dweighted * x_f, spread, NT)
        touch = jnp.broadcast_to(total(sgrad * state_in), (SUB, width))
        dlast = total(dend * to_last * dt) + jnp.exp(last) * mm_left(touch, spread, NT)[0:1]
        dlog = mm(triu, dcum, precision=highest) + dlast
        neg_a = head_ref[NEG_A : NEG_A + 1, :]
        ddt = ddt_within + dend * to_last + dlog * neg_a
        raw = zx_ref[rows, 2 * width : 2 * width + BLOCK] + head_ref[DT_BIAS : DT_BIAS + 1, :]
        draw = ddt * sigmoid(raw) * head_ref[HEAD_MASK : HEAD_MASK + 1, :]
        dzx_ref[rows, 2 * width :] = draw.astype(bf16)
        dhead_ref[0:1, :] += total(draw)
        dhead_ref[1:2, :] += total(dlog * neg_a * dt)
        state_grad[lane] = keep * (mm(c_low, dc_high, TN) + mm(c_low, dc_low, TN) + last_x * sgrad)

        dx = dx + skip * dmixed
        dconv = dx * chan_ref[MASK : MASK + 1, :] * (act * (1.0 + conv * (1.0 - act)))
        pad_d[lane, :BLOCK] = dconv
        pad_d[lane, BLOCK:] = next_conv[lane]
        next_conv[lane] = dconv[:SUB] * keep
        pad_x[lane, :SUB] = tail_ref[0, lane]
        pad_x[lane, SUB:] = zx_ref[rows, width : 2 * width]
        dpre = jnp.zeros((BLOCK, width), f32)
        for k in range(KCONV):
            dpre = dpre + pad_d[lane, KCONV - 1 - k : KCONV - 1 - k + BLOCK, :] * chan_ref[k : k + 1, :]
            dchan_ref[k : k + 1, :] += total(dconv * pad_x[lane, SUB - KCONV + 1 + k : SUB - KCONV + 1 + k + BLOCK, :])
        dchan_ref[BIAS : BIAS + 1, :] += total(dconv)
        dzx_ref[rows, width : 2 * width] = dpre.astype(bf16)


def run_backward(starts, zx, grad, chan, head, spread, conv, mix, bc, step_arr, state, tail, scale, lanes, heads):
    rows, width = grad.shape
    step = lanes * BLOCK
    blocks = rows // step
    by_block = lambda cols: pl.BlockSpec((step, cols), lambda c: (blocks - 1 - c, 0))
    whole = lambda a: pl.BlockSpec(a.shape, lambda c: (0,) * a.ndim)
    fixed = lambda shape: pl.BlockSpec(shape, lambda c: (0,) * len(shape))
    per_lane = lambda r, cols: pl.BlockSpec((1, lanes, r, cols), lambda c: (blocks - 1 - c, 0, 0, 0))
    return pl.pallas_call(
        partial(backward_kernel, lanes=lanes, heads=heads),
        grid=(blocks,),
        in_specs=[
            pl.BlockSpec((1, SUB, BLOCK), lambda c: (blocks - 1 - c, 0, 0)), by_block(2 * width + BLOCK), by_block(width),
            whole(chan), whole(head), whole(spread),
            by_block(width), by_block(width), by_block(2 * N), by_block(2 * BLOCK),
            per_lane(N, width), per_lane(SUB, width), by_block(BLOCK),
        ],
        out_specs=[
            by_block(2 * width + BLOCK), pl.BlockSpec((2 * N, step), lambda c: (0, blocks - 1 - c)),
            fixed((SUB, width)), fixed((SUB, BLOCK)),
        ],
        out_shape=[
            jax.ShapeDtypeStruct((rows, 2 * width + BLOCK), bf16),
            jax.ShapeDtypeStruct((2 * N, rows), bf16), jax.ShapeDtypeStruct((SUB, width), f32),
            jax.ShapeDtypeStruct((SUB, BLOCK), f32),
        ],
        scratch_shapes=[
            pltpu.VMEM((lanes, N, width), f32), pltpu.VMEM((lanes, SUB, width), f32),
            pltpu.VMEM((lanes, BLOCK + SUB, width), f32), pltpu.VMEM((lanes, BLOCK + SUB, width), f32),
        ],
        compiler_params=pltpu.CompilerParams(vmem_limit_bytes=48 << 20, dimension_semantics=("arbitrary",)),
        cost_estimate=pl.CostEstimate(flops=rows * width * 6144, bytes_accessed=rows * width * 40, transcendentals=rows * width * 6),
        name="mix_backward",
    )(starts, zx, grad, chan, head, spread, conv, mix, bc, step_arr, state, tail, scale)


MESH = pl.DeviceIdType.MESH


def greet(others):
    for other in others:
        pl.semaphore_signal(pltpu.get_barrier_semaphore(), inc=1, device_id=other, device_id_type=MESH)


def met(others):
    pl.semaphore_wait(pltpu.get_barrier_semaphore(), len(others))


def remote(src, dst, send, recv, device):
    return pltpu.make_async_remote_copy(
        src_ref=src, dst_ref=dst, send_sem=send, recv_sem=recv, device_id=device, device_id_type=MESH
    )


PARTS = 2


def part_of(ref, i):
    rows = ref.shape[0] // PARTS
    return ref.at[pl.ds(i * rows, rows)]


class Rows:
    def __init__(self, own_ref, all_ref, sems, peers):
        self.own, self.all, self.sems, self.peers = own_ref, all_ref, sems, peers
        self.width, self.place = lax.axis_index("width"), lax.axis_index("seq")
        self.chips, self.chip = peers // 2, self.place // 2

    def hop(self, ref, s, step, by, i):
        send, recv = self.sems[0 if by > 0 else 2], self.sems[1 if by > 0 else 3]
        device = (self.width, jnp.clip(self.place + 2 * by, 0, self.peers - 1))
        return remote(part_of(ref, i), part_of(self.all.at[s], i), send.at[step, i], recv.at[step, i], device)

    def over(self, ref, s, slot, i):
        device = (self.width, jnp.bitwise_xor(self.place, 1))
        send, recv = self.sems[4].at[slot, i], self.sems[5].at[slot, i]
        return remote(part_of(ref, i), part_of(self.all.at[s], i), send, recv, device)

    def inside(self, by):
        return self.chip + 1 < self.chips if by > 0 else self.chip > 0

    def reached(self, by, step):
        return self.chip >= step if by > 0 else self.chip + step < self.chips

    def source(self, by, step):
        return jnp.clip(self.place - 2 * by * step, 0, self.peers - 1)

    def keep(self):
        return pltpu.make_async_copy(self.own, self.all.at[self.place], self.sems[6])

    def start(self):
        for i in range(PARTS):
            for by in (1, -1):
                @pl.when(self.inside(by))
                def _():
                    self.hop(self.own, self.place, 0, by, i).start()
        self.keep().start()
        for copy in self.mate(1, 0):
            copy.start()

    def pass_on(self, step):
        for i in range(PARTS):
            for by in (1, -1):
                @pl.when(self.reached(by, step))
                def _():
                    s = self.source(by, step)
                    ref = self.all.at[s]
                    self.hop(ref, s, step - 1, by, i).wait_recv()

                    @pl.when(self.inside(by))
                    def _():
                        self.hop(ref, s, step, by, i).start()
                    self.over(ref, s, 2 * step - (by > 0), i).start()

    def mate(self, by, step):
        if not step:
            return [self.over(self.own, self.place, 0, i) for i in range(PARTS)]
        s = self.source(by, step)
        return [self.over(self.all.at[s], s, 2 * step - (by > 0), i) for i in range(PARTS)]

    def arrived(self):
        self.keep().wait()
        for copy in self.mate(1, 0):
            copy.wait_recv()
        for step in range(1, self.chips):
            for by in (1, -1):
                @pl.when(self.reached(by, step))
                def _():
                    for copy in self.mate(by, step):
                        copy.wait_recv()

    def sent(self):
        for step in range(self.chips):
            for by in (1, -1):
                @pl.when(self.inside(by) & self.reached(by, step))
                def _():
                    s = self.source(by, step)
                    for i in range(PARTS):
                        self.hop(self.all.at[s], s, step, by, i).wait_send()
        for copy in self.mate(1, 0):
            copy.wait_send()
        for step in range(1, self.chips):
            for by in (1, -1):
                @pl.when(self.reached(by, step))
                def _():
                    for copy in self.mate(by, step):
                        copy.wait_send()


ROW_SEMS = 7


def row_sems(chips):
    dma = pltpu.SemaphoreType.DMA
    return [dma((chips, PARTS))] * 4 + [dma((2 * chips, PARTS))] * 2 + [dma(())]


def front_kernel(
    valid_ref, start_ref, x_ref, cot_ref, norm_gain_ref, bc_ref, dt_ref, taps_ref, bias_ref, dtb_ref, alog_ref, skip_ref,
    gain_ref, spread_ref, zx_ref, wout_ref,
    w_ref, rows_ref, grads_ref, starts_ref, chan_ref, head_ref, bc_par,
    out_zx, out_mix, out_grad, out_scale, out_wout, out_up, out_down, out_mine, out_conv, out_bc, out_step, out_state, out_tail,
    w_v, rows_v, starts_v, wout_v, own_v, grad_v, third_v, start_v, part_got,
    z_v, mix_v, scale_v, low_v, zx_v, mgrad_v, conv_v, bc_v, step_v, state_v, tail_v, bgrad_v, up, down, wout_grad, sums, sums_got,
    state, tail_x, tail_b, pad_x, pad_b,
    w_send, w_recv, st_send, st_recv, own_sem, wide_send, wide_recv, in_sem, out_sem, slot_sem, grad_sem, part_send, part_recv, branch_sem,
    up_send, up_recv, down_send, down_recv, sum_send, sum_recv, *sems,
    peers, widths, lanes, heads,
):
    width, place = lax.axis_index("width"), lax.axis_index("seq")
    chips = peers // 2
    chans = heads * HEAD_DIM
    quarter = zx_ref.shape[0] // widths
    ring = [lax.rem(place + by, peers) for by in range(1, peers)]
    cross = [jnp.bitwise_xor(width, m) for m in range(1, widths)]
    others = [(width, s) for s in ring] + [(w, place) for w in cross]
    greet(others)

    x = x_ref[...].astype(f32)
    own_v[...] = (x * lax.rsqrt(jnp.mean(x * x, axis=-1, keepdims=True) + epsilon) * norm_gain_ref[...]).astype(bf16)
    row = lax.broadcasted_iota(jnp.int32, (BLOCK, 1), 0)
    sub = lax.broadcasted_iota(jnp.int32, (SUB, BLOCK), 0)
    tile = jnp.zeros((SUB, BLOCK), f32)
    for lane in range(lanes):
        at = slice(lane * BLOCK, (lane + 1) * BLOCK)
        mask = (row < valid_ref[0, lane]).astype(f32)
        grad_v[at, :] = (cot_ref[at, :].astype(f32) * mask).astype(bf16)
        tile = jnp.where(sub == lane, start_ref[0, lane].astype(f32), tile)
    start_v[...] = tile
    bc, dt = bc_ref[...].astype(f32), dt_ref[...].astype(f32)
    share = bc.shape[1] // peers
    rest = jnp.zeros((bc.shape[0], BLOCK - share - heads), f32)
    for s in range(peers):
        columns = [dt[:, s * heads : (s + 1) * heads], bc[:, s * share : (s + 1) * share], rest]
        third_v[s] = jnp.concatenate(columns, axis=1).astype(bf16)
    met(others)

    mine = pl.ds(pl.multiple_of(width * quarter, quarter), quarter)
    rows = Rows(own_v, rows_ref, sems[:ROW_SEMS], peers)
    grads = Rows(grad_v, grads_ref, sems[ROW_SEMS:], peers)

    def columns_of(half, s):
        return pl.ds(pl.multiple_of(half * peers * chans + s * chans, 128), chans)

    wide = 2 * chans
    spots = [pl.ds(0, chans), pl.ds(chans, chans), pl.ds(wide, BLOCK), pl.ds(wide + BLOCK, 2 * N)]

    def parts(s):
        return [zx_ref.at[mine, columns_of(0, s)], zx_ref.at[mine, columns_of(1, s)], third_v.at[s, mine], bc_ref.at[mine]]

    pushes = []
    for i, s in enumerate(ring):
        for k, (part, spot) in enumerate(zip(parts(s), spots)):
            pushes.append(remote(part, w_ref.at[place, width, :, spot], w_send.at[k, i], w_recv.at[k, i], (width, s)))
        pushes.append(remote(start_v, starts_ref.at[place], st_send.at[i], st_recv.at[i], (width, s)))
    for push in pushes:
        push.start()
    keeps = [
        pltpu.make_async_copy(part, w_ref.at[place, width, :, spot], own_sem.at[k])
        for k, (part, spot) in enumerate(zip(parts(place), spots))
    ]
    keeps.append(pltpu.make_async_copy(start_v, starts_ref.at[place], own_sem.at[4]))
    for keep in keeps:
        keep.start()
    rows.start()

    active = jnp.right_shift(jnp.int32(H), widths - 1 - width)
    first = place * heads
    here = columns_of(0, place)
    spread = spread_ref[...]
    pick_row = lax.broadcasted_iota(jnp.int32, (H, BLOCK), 0)
    pick_lane = lax.broadcasted_iota(jnp.int32, (H, BLOCK), 1)
    chosen = ((pick_row == pick_lane + first) & (pick_lane < heads)).astype(f32)
    per_head = jnp.concatenate(
        [dtb_ref[...], -jnp.exp(alog_ref[...]), jnp.ones((1, H), f32), skip_ref[...], jnp.zeros((SUB - 4, H), f32)], axis=0
    )
    per_head = mm(per_head, chosen, precision=highest)
    head_lane = lax.broadcasted_iota(jnp.int32, (SUB, BLOCK), 1)
    head_ref[...] = jnp.where((sub == HEAD_MASK) & (head_lane + first >= active), 0.0, per_head)
    on_chans = mm(head_ref[...], spread.astype(f32), precision=highest)
    chan_ref[...] = jnp.concatenate(
        [taps_ref[:, here], bias_ref[:, here], on_chans[3:4], gain_ref[:, here], on_chans[HEAD_MASK : HEAD_MASK + 1]], axis=0
    )
    bc_par[...] = jnp.concatenate(
        [taps_ref[:, E:], bias_ref[:, E:], jnp.zeros((SUB - KCONV - 1, 2 * N), f32)], axis=0
    )

    for push in pushes:
        push.wait_recv()
    for keep in keeps:
        keep.wait()
    shares = [
        remote(w_ref.at[:, width], w_ref.at[:, width], wide_send.at[m], wide_recv.at[m], (w, place)) for m, w in enumerate(cross)
    ]
    for copy in shares:
        copy.start()
    for step in range(1, chips - 1):
        rows.pass_on(step)
    grads.start()
    for copy in shares:
        copy.wait_recv()
    in_w = pltpu.make_async_copy(w_ref, w_v, own_sem.at[0])
    in_starts = pltpu.make_async_copy(starts_ref, starts_v, own_sem.at[1])
    in_wout = pltpu.make_async_copy(wout_ref, wout_v, own_sem.at[2])
    for copy in (in_w, in_starts, in_wout):
        copy.start()
    rows.pass_on(chips - 1)
    rows.arrived()

    def load(src, s):
        return pltpu.make_async_copy(src.at[s], rows_v.at[s], in_sem.at[s])

    for c in range(peers):
        load(rows_ref, c).start()
    for array in (state, tail_x, tail_b):
        array[...] = jnp.zeros_like(array)
    for copy in (in_w, in_starts, in_wout):
        copy.wait()

    def out_copy(k, src, dst, c):
        return pltpu.make_async_copy(src.at[c], dst.at[c], out_sem.at[k, c])

    slots = [
        (zx_v, out_zx), (conv_v, out_conv), (bc_v, out_bc), (step_v, out_step), (state_v, out_state), (tail_v, out_tail)
    ]

    def slot_copies(c):
        slot = lax.rem(c, 2)
        return [pltpu.make_async_copy(src.at[slot], dst.at[c], slot_sem.at[k, slot]) for k, (src, dst) in enumerate(slots)]

    def compute(begin, end):
        @pl.loop(begin, end)
        def _(c):
            load(rows_ref, c).wait()

            @pl.when(c >= 2)
            def _():
                for copy in slot_copies(c - 2):
                    copy.wait()
            weights = w_v[...].reshape(w_v.shape[0] * w_v.shape[1] * w_v.shape[2], w_v.shape[3])
            slot = lax.rem(c, 2)
            zx = mm(rows_v[c], weights)
            zx_v[slot] = zx
            z_v[c] = zx[:, :chans]
            for lane in range(lanes):
                forward_block(
                    1.0 - starts_v[c, lane : lane + 1, :], zx_v.at[slot], chan_ref, bc_par, head_ref, spread_ref[...],
                    conv_v.at[slot], mix_v.at[c], bc_v.at[slot], step_v.at[slot], state_v.at[slot], tail_v.at[slot],
                    state, tail_x, tail_b, pad_x, pad_b, lane=lane, heads=heads,
                )
            out_copy(0, mix_v, out_mix, c).start()
            for copy in slot_copies(c):
                copy.start()
            gated = gated_of(c)
            square = mm_right(jnp.ones((SUB, chans), bf16), gated * gated, NT)
            for lane in range(lanes):
                sums[0, pl.ds(c * lanes + lane, 1), :] = square[:1, lane * BLOCK : (lane + 1) * BLOCK]

    def gated_of(c):
        z = z_v[c]
        return mix_v[c] * (z * sigmoid(z))

    core = lax.rem(place, 2)

    def give(k):
        copies = [
            remote(sums.at[k], sums_got.at[k, i], sum_send.at[k, i], sum_recv.at[k, i], (width, s)) for i, s in enumerate(ring)
        ]
        for copy in copies:
            copy.start()
        return copies

    def whole(k, copies):
        total = sums[k]
        for i, copy in enumerate(copies):
            copy.wait_recv()
            total = total + sums_got[k, i]
        return total

    def by_time(value):
        return jnp.concatenate([value, jnp.zeros((BLOCK - lanes * peers, BLOCK), f32)], axis=0).T

    def load_grad(s, slot):
        return pltpu.make_async_copy(grads_ref.at[s], bgrad_v.at[slot], in_sem.at[slot])

    def grad_out(s, slot):
        return pltpu.make_async_copy(mgrad_v.at[slot], out_grad.at[s], grad_sem.at[slot])

    def mix_grads(q, first):
        for slot in range(2):
            load_grad(2 * q + slot, slot).start()
        for slot in range(2):
            s = 2 * q + slot
            load_grad(s, slot).wait()
            if not first:
                grad_out(s, slot).wait()
            grad = mm(bgrad_v[slot], wout_v[...], NT)
            mgrad_v[slot] = grad
            grad_out(s, slot).start()
            pulled = mm_right(jnp.ones((SUB, chans), bf16), grad * chan_ref[GAIN : GAIN + 1, :] * gated_of(s), NT)
            for lane in range(lanes):
                sums[1, pl.ds(s * lanes + lane, 1), :] = pulled[:1, lane * BLOCK : (lane + 1) * BLOCK]
        rows_q = low_v[pl.ds(2 * q, 2)].reshape(2 * low_v.shape[1], chans)
        both = bgrad_v[...].reshape(2 * bgrad_v.shape[1], bgrad_v.shape[2])
        part = mm(rows_q, both, TN)
        wout_grad[...] = part if first else wout_grad[...] + part

    def mine(q):
        return rows_v.at[2 * q + core]

    def part_over(q):
        return remote(
            rows_v.at[2 * q + 1 - core], part_got.at[q], part_send.at[q], part_recv.at[q], (width, jnp.bitwise_xor(place, 1))
        )

    def part_sum(q):
        part_over(q).wait_recv()
        add_into(mine(q), [part_got.at[q]], rows_v.shape[1])

    def sends(by, step):
        far = chips - step
        return unit_chip + far < chips if by > 0 else unit_chip >= far

    def later(by):
        return unit_chip > 0 if by > 0 else unit_chip + 1 < chips

    unit_chip = place // 2

    def branch_hop(src, by, step, i):
        buffer, send, recv = (up, up_send, up_recv) if by > 0 else (down, down_send, down_recv)
        return remote(
            part_of(src, i), part_of(buffer.at[step - 1], i), send.at[step - 1, i], recv.at[step - 1, i],
            (width, jnp.clip(place + 2 * by, 0, peers - 1)),
        )

    def branch_stage(by, step):
        return (up if by > 0 else down).at[step - 2]

    def branch_hops(step):
        for i in range(PARTS):
            for by in (1, -1):
                owner = jnp.clip(unit_chip + by * (chips - step), 0, chips - 1)
                last = step == chips - 1

                def direct():
                    branch_hop(mine(owner), by, step, i).start()

                def relayed():
                    stage = branch_stage(by, step)
                    branch_hop(stage, by, step - 1, i).wait_recv()
                    add_into(part_of(stage, i), [part_of(mine(owner), i)], rows_v.shape[1] // PARTS)
                    if not last:
                        branch_hop(stage, by, step, i).start()

                if step == 1:
                    pl.when(sends(by, step))(direct)
                    continue
                if not last:
                    pl.when(sends(by, step) & jnp.logical_not(later(by)))(direct)
                pl.when(sends(by, step) & later(by))(relayed)

    def branch_out(k, src):
        return pltpu.make_async_copy(src, (out_mine, out_up, out_down)[k], branch_sem.at[k])

    def branch_outs(act):
        act(branch_out(0, mine(unit_chip)))
        for k, by in ((1, 1), (2, -1)):
            owner = jnp.clip(unit_chip + by, 0, chips - 1)

            @pl.when(later(by))
            def _():
                act(branch_out(k, branch_stage(by, chips - 1)))

            @pl.when(jnp.logical_not(later(by)))
            def _():
                act(branch_out(k, mine(owner)))

    compute(0, peers)
    squares = give(0)
    grads.pass_on(1)

    def mates_here(step):
        if not step:
            for copy in grads.mate(1, 0):
                copy.wait_recv()
        for by in (1, -1):
            if step:
                @pl.when(grads.reached(by, step))
                def _():
                    for copy in grads.mate(by, step):
                        copy.wait_recv()

    def at_distance(step):
        for by in (1, -1):
            @pl.when(grads.reached(by, step))
            def _():
                mix_grads(grads.source(by, step) // 2, False)

    @pl.loop(0, chips)
    def _(i):
        q = jnp.where(unit_chip < chips // 2, chips - 1 - i, i)
        for c in (2 * q + 1 - core, 2 * q + core):
            low = (gated_of(c) * chan_ref[GAIN : GAIN + 1, :]).astype(bf16)
            rows_v[c] = mm(low, wout_v[...]).astype(bf16)
        part_over(q).start()

    for q in range(chips):
        part_sum(q)
    branch_hops(1)
    count = (active * HEAD_DIM).astype(f32)
    rate = lax.rsqrt(whole(0, squares) / count + epsilon)
    rate_t = by_time(rate)
    lane_at = lax.broadcasted_iota(jnp.int32, (BLOCK, BLOCK), 1)
    spots_of = [(c, slice(lane * BLOCK, (lane + 1) * BLOCK)) for c in range(peers) for lane in range(lanes)]
    for i, (c, at) in enumerate(spots_of):
        scale_v[c, at, :] = jnp.where(lane_at == 0, rate_t[:, i : i + 1], 0.0)

    @pl.loop(0, peers)
    def _(c):
        low_v[c] = (gated_of(c) * scale_v[c, :, 0:1] * chan_ref[GAIN : GAIN + 1, :]).astype(bf16)

    grads.pass_on(2)
    grads.keep().wait()
    mates_here(0)
    mix_grads(unit_chip, True)
    mates_here(1)
    at_distance(1)
    for step in range(2, chips - 1):
        branch_hops(step)
        mates_here(step)
        at_distance(step)
    grads.pass_on(chips - 1)
    mates_here(chips - 1)
    at_distance(chips - 1)
    crosses = give(1)
    bgrad_v[...] = wout_grad[...].astype(bf16).reshape(bgrad_v.shape)
    wout_out = pltpu.make_async_copy(bgrad_v, out_wout, own_sem.at[3])
    wout_out.start()
    branch_hops(chips - 1)
    branch_outs(lambda copy: copy.start())
    pull_t = by_time(rate * rate * rate * whole(1, crosses) / count)
    for i, (c, at) in enumerate(spots_of):
        scale_v[c, at, :] = jnp.where(lane_at == 1, pull_t[:, i : i + 1], scale_v[c, at, :])
    for c in range(peers):
        out_copy(1, scale_v, out_scale, c).start()

    for copy in shares + pushes + squares + crosses:
        copy.wait_send()
    rows.sent()
    grads.sent()
    for c in (peers - 2, peers - 1):
        for copy in slot_copies(c):
            copy.wait()

    @pl.loop(0, peers)
    def _(c):
        for k, (src, dst) in enumerate([(mix_v, out_mix), (scale_v, out_scale)]):
            out_copy(k, src, dst, c).wait()

    for q in range(chips):
        part_over(q).wait_send()
    for step in range(1, chips - 1):
        for by in (1, -1):
            @pl.when(sends(by, step))
            def _():
                for i in range(PARTS):
                    branch_hop(mine(0), by, step, i).wait_send()
    for slot in range(2):
        grad_out(slot, slot).wait()
    wout_out.wait()
    branch_outs(lambda copy: copy.wait())


def front(valid, starts, tokens, cotangent, norm_gain, w_bc, w_dt, taps, bias, dt_bias, a_log, d_skip, gate_gain, spread, w_zx, w_out):
    peers, widths = lax.axis_size("seq"), lax.axis_size("width")
    own, model = tokens.shape
    lanes = starts.shape[1]
    quarter = own // widths
    chans = w_out.shape[0]
    heads = chans // HEAD_DIM
    cols = 2 * chans + BLOCK + 2 * N
    dma = pltpu.SemaphoreType.DMA
    anywhere, vmem = pl.BlockSpec(memory_space=pl.ANY), pl.BlockSpec(memory_space=pltpu.VMEM)
    smem = pl.BlockSpec(memory_space=pltpu.SMEM)
    w_all = ((peers, widths, quarter, cols), bf16)
    rows_all = ((peers, own, model), bf16)
    part_all = ((peers // 2, own, model), bf16)
    starts_all = ((peers, SUB, BLOCK), f32)
    per_chan, low = ((peers, own, chans), f32), ((peers, own, chans), bf16)
    block = ((own, model), bf16)
    streamed = [
        ((own, cols), f32), ((own, chans), f32), ((own, chans), f32), ((own, 2 * N), bf16), ((own, 2 * BLOCK), f32),
        ((lanes, N, chans), f32), ((lanes, SUB, chans), f32),
    ]
    scale = ((peers, own, BLOCK), f32)
    of = lambda count, a: ((count,) + a[0], a[1])
    outs = [w_all, rows_all, rows_all, starts_all, ((SUB, chans), f32), ((SUB, BLOCK), f32), ((SUB, 2 * N), f32)]
    outs += [of(peers, streamed[0]), per_chan, per_chan, scale, of(chans // own, block), block, block, block]
    outs += [of(peers, a) for a in streamed[2:]]
    scratch = [w_all, rows_all, starts_all, ((chans, model), bf16), ((own, model), bf16), ((own, model), bf16)]
    scratch += [((peers, own, BLOCK), bf16), ((SUB, BLOCK), f32), part_all, per_chan, per_chan, scale, low]
    scratch += [of(2, a) for a in streamed]
    scratch += [of(2, block)] * 3 + [((chans, model), f32)]
    scratch += [((2, peers * lanes, BLOCK), f32), ((2, peers - 1, peers * lanes, BLOCK), f32)]
    scratch += [((lanes, N, chans), f32), ((lanes, SUB, chans), f32), ((lanes, SUB, 2 * N), f32)]
    scratch += [((lanes, BLOCK + SUB, chans), f32), ((lanes, BLOCK + SUB, 2 * N), f32)]
    return pl.pallas_call(
        partial(front_kernel, peers=peers, widths=widths, lanes=lanes, heads=heads),
        in_specs=[smem] * 2 + [vmem] * 12 + [anywhere] * 2,
        out_specs=[anywhere] * 4 + [vmem] * 3 + [anywhere] * 13,
        out_shape=[jax.ShapeDtypeStruct(*a) for a in outs],
        scratch_shapes=[
            *[pltpu.VMEM(*a) for a in scratch],
            dma((4, peers - 1)), dma((4, peers - 1)), dma((peers - 1,)), dma((peers - 1,)),
            dma((5,)), dma((widths - 1,)), dma((widths - 1,)), dma((peers,)), dma((2, peers)), dma((6, 2)), dma((2,)),
            dma((peers // 2,)), dma((peers // 2,)), dma((3,)), *[dma((2, PARTS))] * 4,
            dma((2, peers - 1)), dma((2, peers - 1)),
            *row_sems(peers // 2), *row_sems(peers // 2),
        ],
        compiler_params=pltpu.CompilerParams(collective_id=1, has_side_effects=True, vmem_limit_bytes=62 << 20),
        name="front",
    )(valid, starts, tokens, cotangent, norm_gain, w_bc, w_dt, taps, bias, dt_bias, a_log, d_skip, gate_gain, spread, w_zx, w_out)


ROWS_AT_ONCE = 16


def add_into(dst, others, rows):
    @pl.loop(0, rows // ROWS_AT_ONCE)
    def _(i):
        at = pl.ds(pl.multiple_of(i * ROWS_AT_ONCE, ROWS_AT_ONCE), ROWS_AT_ONCE)
        value = dst[at].astype(f32)
        for other in others:
            value = value + other[at].astype(f32)
        dst[at] = value.astype(dst.dtype)


def bc_back(dbc, pre, par_ref, keep, keep_next):
    chans, times = pre.shape
    in_block = lax.rem(lax.broadcasted_iota(jnp.int32, (chans, times), 1), BLOCK)
    conv = jnp.broadcast_to(par_ref[:, BIAS : BIAS + 1], (chans, times))
    shifted = []
    for j in range(KCONV):
        moved = pre
        if j:
            moved = jnp.where(in_block >= j, pltpu.roll(pre, j, 1), keep * pltpu.roll(pre, BLOCK + j, 1))
        shifted.append(moved)
        conv = conv + moved * par_ref[:, KCONV - 1 - j : KCONV - j]
    act = sigmoid(conv)
    dconv = dbc * (act * (1.0 + conv * (1.0 - act)))
    dpre = dconv * par_ref[:, KCONV - 1 : KCONV]
    lane = lax.broadcasted_iota(jnp.int32, (chans, BLOCK), 1)
    dpar = jnp.where(lane == BIAS, jnp.sum(dconv, axis=1, keepdims=True), 0.0)
    for j in range(KCONV):
        dpar = dpar + jnp.where(lane == KCONV - 1 - j, jnp.sum(dconv * shifted[j], axis=1, keepdims=True), 0.0)
        if j:
            back = jnp.where(
                in_block < BLOCK - j, pltpu.roll(dconv, times - j, 1), keep_next * pltpu.roll(dconv, times - BLOCK - j, 1)
            )
            dpre = dpre + back * par_ref[:, KCONV - 1 - j : KCONV - j]
    return dpre, dpar


def scatter_kernel(
    got_ref, zx_ref, dzx_ref, w_ref, normed_ref, wide_ref, par_ref, start_ref, small_ref,
    rows_ref, out_ref, out_third_ref,
    got_v, pre_v, dz_v, w_v, normed_v, third_t, third_g, par_t,
    mine, to_mate, from_core, up, down, own0, own1, own2, got0, got1, got2, piece0, piece1, piece2,
    load_sem, core_send, core_recv, up_send, up_recv, down_send, down_recv,
    own_sem, q_send, q_recv, p_send, p_recv, o_send, o_recv,
    *, peers, widths, heads,
):
    width, place = lax.axis_index("width"), lax.axis_index("seq")
    chips = peers // 2
    chip, core = place // 2, lax.rem(place, 2)
    mate = (width, jnp.bitwise_xor(place, 1))
    ring = [lax.rem(place + by, peers) for by in range(1, peers)]
    cross = [jnp.bitwise_xor(width, m) for m in range(1, widths)]
    others = [(width, s) for s in ring] + [(w, place) for w in cross]
    greet(others)
    half = wide_ref.shape[3] // 2
    wide = 2 * half
    own = mine.shape[1]
    share, times = got_v.shape[1], got_v.shape[2]
    loads = [
        pltpu.make_async_copy(src, dst, load_sem.at[k])
        for k, (src, dst) in enumerate([
            (got_ref, got_v), (zx_ref.at[:, :, wide : wide + BLOCK], pre_v), (dzx_ref, dz_v), (w_ref, w_v), (normed_ref, normed_v)
        ])
    ]
    for load in loads:
        load.start()
    met(others)

    strip = third_g.shape[0] // widths
    lanes_of = lambda s: pl.ds(pl.multiple_of(s * own, BLOCK), own)
    strip_of = lambda w: pl.ds(pl.multiple_of(w * strip, 16), strip)
    sets = [
        (lambda w: wide_ref.at[:, w, :, 0:half], own0, got0, lambda s: own0.at[s], piece0, lambda w: out_ref.at[:, w, :, 0:half]),
        (lambda w: wide_ref.at[:, w, :, half:wide], own1, got1, lambda s: own1.at[s], piece1, lambda w: out_ref.at[:, w, :, half:wide]),
        (lambda w: third_g.at[strip_of(w)], own2, got2, lambda s: own2.at[:, lanes_of(s)], piece2, lambda w: out_third_ref.at[:, w]),
    ]
    own_in, to_width = [None] * 3, [None] * 3

    def begin(k):
        part, kept, arrived = sets[k][:3]
        own_in[k] = pltpu.make_async_copy(part(width), kept, own_sem.at[0, k])
        to_width[k] = [
            remote(part(w), arrived.at[m], q_send.at[k, m], q_recv.at[k, m], (w, place)) for m, w in enumerate(cross)
        ]
        for copy in [own_in[k]] + to_width[k]:
            copy.start()

    begin(0)
    begin(1)

    def flow(by):
        return (up, up_send, up_recv) if by > 0 else (down, down_send, down_recv)

    def sends(by, step):
        far = chips - step
        return chip + far < chips if by > 0 else chip >= far

    def later(by):
        return chip > 0 if by > 0 else chip + 1 < chips

    def hop(src, by, step, i):
        buffer, send, recv = flow(by)
        return remote(
            part_of(src, i), part_of(buffer.at[step - 1], i), send.at[step - 1, i], recv.at[step - 1, i],
            (width, jnp.clip(place + 2 * by, 0, peers - 1)),
        )

    def staged(by, step):
        return flow(by)[0].at[step - 2]

    def run_hops(step):
        for i in range(PARTS):
            for by in (1, -1):
                owner = jnp.clip(chip + by * (chips - step), 0, chips - 1)

                def direct():
                    hop(mine.at[owner], by, step, i).start()

                def relayed():
                    stage = staged(by, step)
                    hop(stage, by, step - 1, i).wait_recv()
                    add_into(part_of(stage, i), [part_of(mine.at[owner], i)], own // PARTS)
                    hop(stage, by, step, i).start()

                if step == 1:
                    pl.when(sends(by, step))(direct)
                else:
                    pl.when(sends(by, step) & jnp.logical_not(later(by)))(direct)
                    pl.when(sends(by, step) & later(by))(relayed)

    to_owner, to_all, kept_piece = [None] * 3, [None] * 3, [None] * 3

    def exchange(k):
        part, kept, arrived, piece_of, piece, out = sets[k]
        own_in[k].wait()
        for copy in to_width[k]:
            copy.wait_recv()
        if kept.ndim == 3:
            for s in range(peers):
                add_into(kept.at[s], [arrived.at[m, s] for m in range(widths - 1)], kept.shape[1])
        else:
            add_into(kept, [arrived.at[m] for m in range(widths - 1)], kept.shape[0])
        to_owner[k] = [
            remote(piece_of(s), piece.at[place], p_send.at[k, i], p_recv.at[k, i], (width, s)) for i, s in enumerate(ring)
        ]
        kept_piece[k] = pltpu.make_async_copy(piece_of(place), piece.at[place], own_sem.at[1, k])
        for copy in to_owner[k] + [kept_piece[k]]:
            copy.start()

    def spread(k):
        piece, out = sets[k][4:]
        for copy in to_owner[k]:
            copy.wait_recv()
        kept_piece[k].wait()
        to_all[k] = [remote(piece, out(width), o_send.at[k, m], o_recv.at[k, m], (w, place)) for m, w in enumerate(cross)]
        to_all[k].append(pltpu.make_async_copy(piece, out(width), own_sem.at[2, k]))
        for copy in to_all[k]:
            copy.start()

    for load in loads[:3]:
        load.wait()
    dbc = got_v[0].astype(f32)
    for s in range(1, peers):
        dbc = dbc + got_v[s].astype(f32)
    block_rows = pre_v.shape[1]
    spots = [(c, slice(l * BLOCK, (l + 1) * BLOCK)) for c in range(peers) for l in range(block_rows // BLOCK)]
    pre = jnp.concatenate([pre_v[c, at, :].T[heads : heads + share] for c, at in spots], axis=1)
    par = jnp.concatenate([par_ref[...], jnp.zeros((BLOCK - SUB, 2 * N), f32)], axis=0)
    for i in range(2 * N // BLOCK):
        par_t[i * BLOCK : (i + 1) * BLOCK, :] = par[:, i * BLOCK : (i + 1) * BLOCK].T
    keep = [1.0 - start_ref[c, l : l + 1, :] for c in range(peers) for l in range(block_rows // BLOCK)]
    keep_next = keep[block_rows // BLOCK :] + [jnp.zeros((1, BLOCK), f32)] * (block_rows // BLOCK)
    own_par = par_t.at[pl.ds(pl.multiple_of(place * share, SUB), share)]
    dpre, dpar = bc_back(dbc, pre, own_par, jnp.concatenate(keep, axis=1), jnp.concatenate(keep_next, axis=1))
    for i, (c, at) in enumerate(spots):
        tile = jnp.concatenate(
            [
                dz_v[c, at, wide:].astype(f32).T[:heads], dpre[:, i * BLOCK : (i + 1) * BLOCK],
                jnp.zeros((BLOCK - heads - share, BLOCK), f32),
            ],
            axis=0,
        )
        third_t[:, i * BLOCK : (i + 1) * BLOCK] = tile.astype(bf16)
        dz_v[c, at, wide:] = tile.T.astype(bf16)
    loads[3].wait()

    def partial_rows(s):
        weights = w_v[...].reshape(w_v.shape[0] * w_v.shape[1] * w_v.shape[2], w_v.shape[3])
        return mm(dz_v[s], weights[:, : wide + BLOCK], NT).astype(bf16)

    def order(i):
        return jnp.where(chip < chips // 2, chips - 1 - i, i)

    def over(q):
        return remote(to_mate.at[q], from_core.at[q], core_send.at[q], core_recv.at[q], mate)

    def whole_sum(q):
        over(q).wait_recv()
        add_into(mine.at[q], [from_core.at[q]], own)

    for i in range(chips):
        q = order(i)
        to_mate[q] = partial_rows(2 * q + 1 - core)
        over(q).start()
        mine[q] = partial_rows(2 * q + core)
        if i > 1:
            whole_sum(order(i - 1))
        if not i:
            whole_sum(q)
            run_hops(1)
    whole_sum(order(chips - 1))

    loads[4].wait()
    small_at = heads + share
    used = small_at + small_ref.shape[0]
    par_rows = jnp.concatenate([dpar, jnp.zeros((BLOCK - share, BLOCK), f32)], axis=0).T[:SUB]
    par_rows = jnp.concatenate([par_rows, jnp.zeros((SUB, own - BLOCK), f32)], axis=1)
    grads = mm(third_t[...], normed_v[...].reshape(times, normed_v.shape[2]))
    tail = [jnp.zeros((third_g.shape[0] - used - SUB, third_g.shape[1]), f32)] if third_g.shape[0] > used + SUB else []
    third_g[...] = jnp.concatenate(
        [grads[:small_at], small_ref[...], jnp.concatenate([par_rows] * peers, axis=1), *tail], axis=0
    ).astype(bf16)
    begin(2)

    exchange(0)
    if chips > 2:
        run_hops(2)
    spread(0)
    exchange(1)
    exchange(2)
    for step in range(3, chips):
        run_hops(step)
    spread(1)
    spread(2)

    for by in (1, -1):
        @pl.when(later(by))
        def _():
            buffer = flow(by)[0].at[chips - 2]
            for i in range(PARTS):
                hop(buffer, by, chips - 1, i).wait_recv()
                add_into(part_of(mine.at[chip], i), [part_of(buffer, i)], own // PARTS)

    rows_ref[...] = mine[chip]

    for step in range(1, chips):
        for by in (1, -1):
            @pl.when(sends(by, step))
            def _():
                for i in range(PARTS):
                    hop(mine.at[0], by, step, i).wait_send()
    for q in range(chips):
        over(q).wait_send()
    for k in range(len(sets)):
        for copy in to_width[k] + to_owner[k]:
            copy.wait_send()
        for copy in to_all[k]:
            copy.wait()


def scattered_out(got, zx, dzx, weights, normed, wide, par, starts, small, heads):
    peers, widths = lax.axis_size("seq"), lax.axis_size("width")
    chips = peers // 2
    dma = pltpu.SemaphoreType.DMA
    anywhere = pl.BlockSpec(memory_space=pl.ANY)
    vmem = pl.BlockSpec(memory_space=pltpu.VMEM)
    own, model = normed.shape[0] // peers, normed.shape[1]
    half = wide.shape[3] // 2
    strips = -(-(heads + got.shape[1] + small.shape[0] + SUB) // (16 * widths)) * 16 * widths
    pieces = [(peers, wide.shape[2], half), (peers, wide.shape[2], half), (peers, strips // widths, own)]
    kept = pieces[:2] + [(strips // widths, model)]
    block = (own, model)
    zx, dzx, normed = [a.reshape(peers, own, a.shape[1]) for a in (zx, dzx, normed)]
    return pl.pallas_call(
        partial(scatter_kernel, peers=peers, widths=widths, heads=heads),
        in_specs=[anywhere] * 6 + [vmem] * 3,
        out_specs=[vmem, anywhere, anywhere],
        out_shape=[
            jax.ShapeDtypeStruct(block, bf16), jax.ShapeDtypeStruct(wide.shape, bf16),
            jax.ShapeDtypeStruct((peers, widths, strips // widths, own), bf16),
        ],
        scratch_shapes=[
            pltpu.VMEM(got.shape, bf16), pltpu.VMEM((peers, own, BLOCK), f32), pltpu.VMEM(dzx.shape, bf16),
            pltpu.VMEM(weights.shape, bf16), pltpu.VMEM(normed.shape, bf16),
            pltpu.VMEM((BLOCK, peers * own), bf16), pltpu.VMEM((strips, model), bf16), pltpu.VMEM((2 * N, BLOCK), f32),
            *[pltpu.VMEM((chips,) + block, bf16)] * 3, *[pltpu.VMEM((chips - 1,) + block, bf16)] * 2,
            *[pltpu.VMEM(a, bf16) for a in kept],
            *[pltpu.VMEM((widths - 1,) + a, bf16) for a in kept],
            *[pltpu.VMEM(a, bf16) for a in pieces],
            dma((5,)), dma((chips,)), dma((chips,)),
            *[dma((chips - 1, PARTS))] * 4,
            dma((3, 3)), dma((3, widths - 1)), dma((3, widths - 1)), dma((3, peers - 1)), dma((3, peers - 1)),
            dma((3, widths - 1)), dma((3, widths - 1)),
        ],
        compiler_params=pltpu.CompilerParams(collective_id=2, has_side_effects=True, vmem_limit_bytes=62 << 20),
        name="scatter_out",
    )(got, zx, dzx, weights, normed, wide, par, starts, small)


def laid_kernel(
    in_ref, third_ref, w_ref, bc_ref, dt_ref, gain_ref, rows_ref, x_ref, cot_ref, norm_gain_ref,
    out_ref, out_bc_ref, out_dt_ref, norm_ref, out_rows_ref, rest,
    *, heads, share,
):
    peers, rows, wide = in_ref.shape[0], in_ref.shape[2], in_ref.shape[3]
    chans = wide // 2
    step = pl.program_id(0)

    @pl.when(step == 0)
    def _():
        third = [
            jnp.concatenate([third_ref[s, q].astype(f32) for q in range(third_ref.shape[1])], axis=0) for s in range(peers)
        ]
        dt = jnp.concatenate([t[:heads] for t in third], axis=0).T
        bc = jnp.concatenate([t[heads : heads + share] for t in third], axis=0).T
        out_bc_ref[...] = bc
        out_dt_ref[...] = dt
        total = jnp.sum(bc * bc_ref[...].astype(f32), axis=1, keepdims=True)
        rest[...] = total + jnp.sum(dt * dt_ref[...].astype(f32), axis=1, keepdims=True)

    lane = jnp.zeros((rows, BLOCK), f32)
    for s in range(peers):
        for half in (0, 1):
            at = (half * peers + s) * chans
            value = in_ref[s, 0, :, half * chans : (half + 1) * chans].astype(f32)
            out_ref[:, at : at + chans] = value
            value = value * w_ref[:, at : at + chans].astype(f32)
            for j in range(chans // BLOCK):
                lane = lane + value[:, j * BLOCK : (j + 1) * BLOCK]
    x = x_ref[...].astype(f32)
    rate = lax.rsqrt(jnp.mean(x * x, axis=-1, keepdims=True) + epsilon)
    unit = x * rate
    pulled = rows_ref[...].astype(f32) * norm_gain_ref[...]
    inner = jnp.mean(pulled * unit, axis=-1, keepdims=True)
    out_rows_ref[...] = cot_ref[...].astype(f32) + rate * (pulled - unit * inner)
    more = rest[pl.ds(pl.multiple_of(step * rows, SUB), rows), :]
    norm_ref[...] = (jnp.sum(lane, axis=1, keepdims=True) + more) / gain_ref[...]


def laid_out(wide, third, w_zx, w_bc, w_dt, gain, normed_grad, x_rows, cotangent, norm_gain, heads):
    peers, widths, quarter, cols = wide.shape
    rows = widths * quarter
    cut = quarter
    share = w_bc.shape[1] // peers
    by_rows = lambda a: pl.BlockSpec((cut, a.shape[1]), lambda i: (i, 0))
    whole = lambda a: pl.BlockSpec(a.shape, lambda i: (0,) * len(a.shape))
    by_piece = pl.BlockSpec((peers, 1, cut, cols), lambda i: (0, i, 0, 0))
    shapes = [jax.ShapeDtypeStruct(a.shape, f32) for a in (w_zx, w_bc, w_dt, gain, x_rows)]
    return pl.pallas_call(
        partial(laid_kernel, heads=heads, share=share),
        grid=(widths,),
        in_specs=[
            by_piece, whole(third), by_rows(w_zx), whole(w_bc), whole(w_dt), by_rows(gain),
            by_rows(normed_grad), by_rows(x_rows), by_rows(cotangent), whole(norm_gain),
        ],
        out_specs=[by_rows(w_zx), whole(w_bc), whole(w_dt), by_rows(gain), by_rows(x_rows)],
        out_shape=shapes,
        scratch_shapes=[pltpu.VMEM((rows, 1), f32)],
        compiler_params=pltpu.CompilerParams(vmem_limit_bytes=62 << 20),
        name="lay_out",
    )(wide, third, w_zx, w_bc, w_dt, gain, normed_grad, x_rows, cotangent, norm_gain)


def crossed(value, axis, mask):
    return lax.ppermute(value, axis, [(i, i ^ mask) for i in range(lax.axis_size(axis))])


def pick(value, index):
    return lax.dynamic_index_in_dim(value, index, 0, False)


def quarters_sent(value):
    widths, width = lax.axis_size("width"), lax.axis_index("width")
    value = value.reshape((widths, value.shape[0] // widths) + value.shape[1:])
    sent = [crossed(pick(value, jnp.bitwise_xor(width, m)), "width", m) for m in range(1, widths)]
    return [pick(value, width)] + sent


def quarters_back(total):
    widths = lax.axis_size("width")
    return [total] + [crossed(total, "width", m) for m in range(1, widths)]


def quarters_joined(pieces):
    width = lax.axis_index("width")
    stacked = jnp.stack(pieces)
    whole = jnp.stack([pick(stacked, jnp.bitwise_xor(width, j)) for j in range(len(pieces))])
    return whole.reshape((-1,) + whole.shape[2:]).astype(f32)


def heads_body(
    tokens, cotangent, starts, valid, norm_gain, w_zx, w_bc, w_dt, conv_w, conv_b, dt_bias, a_log, d_skip, gate_gain, w_out
):
    peers = lax.axis_size("seq")
    widths = lax.axis_size("width")
    place = lax.axis_index("seq")
    lanes = starts.shape[1]
    heads = H // peers
    chans = heads * HEAD_DIM
    own, model = tokens.shape
    rows = own * peers
    first = place * heads
    share = 2 * N // peers
    used = heads + share
    row_mask = (jnp.arange(BLOCK)[None, :] < valid[0][:, None]).astype(f32).reshape(-1, 1)
    spread = jnp.asarray(np.arange(chans)[None, :] // HEAD_DIM == np.arange(BLOCK)[:, None], bf16)
    weights, normed, bgrad, starts_all, chan, head, bc_par, *computed = front(
        valid, starts, tokens, cotangent, norm_gain[None], w_bc, w_dt, conv_w.T, conv_b[None], dt_bias[None], a_log[None],
        d_skip[None], gate_gain[None], spread, w_zx, w_out,
    )
    normed, bgrad = normed.reshape(rows, model), bgrad.reshape(rows, model)
    zx, mix, mixed_grad, scale = [a.reshape(rows, a.shape[-1]) for a in computed[:4]]
    out_part, up, down, branch = computed[4:8]
    conv, bc, steps = [a.reshape(rows, a.shape[-1]) for a in computed[8:11]]
    state, tail = computed[11:]
    above = lax.ppermute(up, "seq", [(i, i + 2) for i in range(peers - 2)])
    below = lax.ppermute(down, "seq", [(i + 2, i) for i in range(peers - 2)])
    out_quarters = quarters_sent(out_part.reshape(chans, model))
    dzx, dbc, dchan, dhead = run_backward(
        starts_all, zx, mixed_grad, chan, head, spread, conv, mix, bc, steps, state, tail, scale, lanes, heads
    )
    dzx, dbc, out_quarters = lax.optimization_barrier((dzx, dbc, out_quarters))
    out_pieces = quarters_back(sum(q.astype(f32) for q in out_quarters).astype(bf16))

    got = lax.all_to_all(dbc.reshape(peers, share, rows), "seq", 0, 0, tiled=True)

    at_heads = lambda a: lax.dynamic_update_slice_in_dim(jnp.zeros((H,), f32), a, first, 0)
    at_chans = lambda a: lax.dynamic_update_slice_in_dim(jnp.zeros((E,), f32), a, first * HEAD_DIM, 0)
    skip = jnp.sum(dchan[SKIP].reshape(heads, HEAD_DIM), axis=1)
    small = [jnp.pad(at_chans(dchan[k]), (0, 2 * N)) for k in range(KCONV + 1)]
    small += [at_chans(dchan[GAIN]), at_heads(dhead[0, :heads]), at_heads(dhead[1, :heads]), at_heads(skip)]
    sizes = [a.shape[0] // peers for a in small]
    small = jnp.concatenate([a.reshape(peers, -1) for a in small], axis=1)
    small_rows = -(-small.shape[1] // (own * SUB)) * SUB
    small = jnp.pad(small, ((0, 0), (0, own * small_rows - small.shape[1])))
    small = small.reshape(peers, small_rows, own).transpose(1, 0, 2).reshape(small_rows, model)

    wide = mm(normed, dzx[:, : 2 * chans], TN).astype(bf16)
    wide, out_pieces = lax.optimization_barrier((wide, out_pieces))
    out_grad = quarters_joined(out_pieces)
    branch = branch.astype(f32) + above.astype(f32) + below.astype(f32)
    own_rate = lax.dynamic_slice(scale, (place * own, 0), (own, 1))
    output = (tokens.astype(f32) + row_mask * own_rate * branch).astype(bf16)
    got, output, out_grad = lax.optimization_barrier((got, output, out_grad))
    normed_grad, wide, third = scattered_out(
        got, zx, dzx, weights, normed, wide.reshape(peers, widths, own // widths, -1), bc_par, starts_all, small, heads,
    )
    gain_rows = lax.dynamic_slice_in_dim(norm_gain, place * own, own, 0)[:, None]
    grad_zx, grad_bc, grad_dt, grad_norm, input_grad = laid_out(
        wide, third, w_zx, w_bc, w_dt, gain_rows, normed_grad, tokens, cotangent, norm_gain[None], heads
    )
    grad_norm = grad_norm[:, 0]
    third = third.reshape(peers, -1, own)
    summed = jnp.sum(third[:, used : used + small_rows].astype(f32), axis=0).reshape(-1)
    pieces = [summed[sum(sizes[:i]) : sum(sizes[: i + 1])] for i in range(len(sizes))]
    of_bc = third[:, used + small_rows : used + small_rows + KCONV + 1, :share].astype(f32).transpose(1, 0, 2).reshape(KCONV + 1, 2 * N)
    own_chans = sizes[0]
    of_bc = lax.dynamic_slice_in_dim(jnp.pad(of_bc, ((0, 0), (E, 0))), place * own_chans, own_chans, 1)
    grad_taps = jnp.stack(pieces[:KCONV], axis=1) + of_bc[:KCONV].T
    grad_bias, grad_gain, grad_dtb, grad_alog, grad_skip = pieces[KCONV:]
    grad_bias = grad_bias + of_bc[KCONV]
    return (
        output, input_grad, grad_norm, grad_zx, grad_bc, grad_dt, grad_taps, grad_bias, grad_dtb, grad_alog, grad_skip,
        grad_gain, out_grad,
    )


def passed_along(array, axis, by):
    peers = lax.axis_size(axis)
    pairs = [(i, i + by) for i in range(peers) if 0 <= i + by < peers]
    return lax.ppermute(array, axis, pairs)


def carried_in(part, axis, combine, identity, reverse):
    count = lax.axis_size(axis)
    place = lax.axis_index(axis)
    at = count - 1 - place if reverse else place
    by = -1 if reverse else 1
    state = jax.tree.map(lambda a, e: jnp.zeros_like(a) + jnp.asarray(e, a.dtype), part, identity)

    def one(lap, state):
        sent = combine(state, part)
        got = jax.tree.map(lambda a: passed_along(a, axis, by), sent)
        return jax.tree.map(lambda old, new: jnp.where(at == lap + 1, new, old), state, got)

    return lax.fori_loop(0, count - 1, one, state)


def round_value(v):
    return lax.optimization_barrier(v.astype(jnp.bfloat16)).astype(jnp.float32)


def keep_round(v):
    return (round_value(v), None)


def pass_grad(kept, grad):
    return (grad,)


def same_value(v):
    return v


def keep_same(v):
    return (v, None)


def round_grad(kept, grad):
    return (round_value(grad),)


def low(v):
    wrapped = jax.custom_vjp(round_value)
    wrapped.defvjp(keep_round, pass_grad)
    return wrapped(v)


def low_back(v):
    wrapped = jax.custom_vjp(same_value)
    wrapped.defvjp(keep_same, round_grad)
    return wrapped(v)


def rms_front(x_rows, norm_gain):
    mean_square = jnp.mean(x_rows * x_rows, axis=-1, keepdims=True)
    return x_rows * lax.rsqrt(mean_square + epsilon) * norm_gain


def rim_of(zx_pre, bc_pre, chan_mask):
    return jnp.concatenate(
        [zx_pre[:, BLOCK - KCONV + 1 :, E:] * chan_mask, bc_pre[:, BLOCK - KCONV + 1 :, :]], axis=-1
    )


def piece_front(
    zx_pre,
    bc_pre,
    dt_raw,
    rim_rows,
    conv_w,
    conv_b,
    dt_bias,
    a_log,
    chan_mask,
    head_mask,
    keep_rows,
):
    z_gate = zx_pre[..., :E] * chan_mask
    pre_conv = jnp.concatenate([zx_pre[..., E:] * chan_mask, bc_pre], axis=-1)
    padded = jnp.concatenate([rim_rows * keep_rows[:, None, None], pre_conv], axis=1)
    conv_out = conv_b + padded[:, 0:BLOCK, :] * conv_w[:, 0]
    for offset in range(1, KCONV):
        conv_out = conv_out + padded[:, offset : offset + BLOCK, :] * conv_w[:, offset]
    active = jax.nn.silu(conv_out)
    x_conv = low(active[..., :E] * chan_mask)
    b_conv = low(active[..., E : E + N])
    c_conv = low(active[..., E + N :])
    dt_step = jax.nn.softplus(dt_raw + dt_bias) * head_mask
    log_step = -jnp.exp(a_log) * dt_step
    return (z_gate, x_conv, b_conv, c_conv, dt_step, log_step)


def block_state(x_conv, b_conv, dt_step, log_step):
    cumulative = jnp.cumsum(log_step, axis=1)
    to_end = jnp.exp(cumulative[:, -1:, :] - cumulative) * dt_step
    weighted = low(x_conv.reshape(x_conv.shape[0], BLOCK, H, HEAD_DIM) * to_end[..., None])
    state_sum = jnp.einsum("lqhp,lqn->lhpn", weighted, b_conv, precision=highest)
    return (state_sum, cumulative[:, -1, :])


def piece_mix(
    z_gate, x_conv, b_conv, c_conv, dt_step, log_step, state_in, d_skip, gate_gain, chan_count
):
    lane_count = x_conv.shape[0]
    cumulative = jnp.cumsum(log_step, axis=1)
    cum_heads = jnp.swapaxes(cumulative, 1, 2)
    causal = jnp.arange(BLOCK)[:, None] >= jnp.arange(BLOCK)[None, :]
    spread = cum_heads[:, :, :, None] - cum_heads[:, :, None, :]
    decays = jnp.where(causal, jnp.exp(jnp.where(causal, spread, 0.0)), 0.0)
    inner_cb = jnp.einsum("lqn,lsn->lqs", c_conv, b_conv, precision=highest)
    scores = low(inner_cb[:, None] * decays * jnp.swapaxes(dt_step, 1, 2)[:, :, None, :])
    x_heads = x_conv.reshape(lane_count, BLOCK, H, HEAD_DIM)
    within = jnp.einsum("lhqs,lshp->lqhp", scores, x_heads, precision=highest)
    carried = (
        jnp.einsum("lqn,lhpn->lqhp", c_conv, state_in, precision=highest)
        * jnp.exp(cumulative)[..., None]
    )
    mixed_sum = low_back(within + carried) + d_skip[:, None] * x_heads
    gated_rows = mixed_sum.reshape(lane_count, BLOCK, E) * jax.nn.silu(z_gate)
    mean_square = jnp.sum(gated_rows * gated_rows, axis=-1, keepdims=True) / chan_count
    return low(gated_rows * lax.rsqrt(mean_square + epsilon) * gate_gain)


def mix_lanes(lane_inputs, d_skip, gate_gain, chan_count):

    def one_lane(pieces):
        lane_gate, lane_xconv, lane_bconv, lane_cconv, lane_step, lane_decay, lane_state = pieces
        return piece_mix(
            lane_gate[None],
            lane_xconv[None],
            lane_bconv[None],
            lane_cconv[None],
            lane_step[None],
            lane_decay[None],
            lane_state[None],
            d_skip,
            gate_gain,
            chan_count,
        )[0]

    return lax.map(one_lane, lane_inputs)


def mix_back_lanes(lane_inputs, mixed_grad, d_skip, gate_gain, chan_count):

    def lane_mix(z_gate, x_conv, b_conv, c_conv, dt_step, log_step, state_in, skip_coef, gain_coef):
        return piece_mix(
            z_gate[None],
            x_conv[None],
            b_conv[None],
            c_conv[None],
            dt_step[None],
            log_step[None],
            state_in[None],
            skip_coef,
            gain_coef,
            chan_count,
        )[0]

    def one_lane(pieces):
        (
            lane_gate,
            lane_xconv,
            lane_bconv,
            lane_cconv,
            lane_step,
            lane_decay,
            lane_state,
            lane_grad,
        ) = pieces
        unused, pull_lane = jax.vjp(
            lane_mix,
            lane_gate,
            lane_xconv,
            lane_bconv,
            lane_cconv,
            lane_step,
            lane_decay,
            lane_state,
            d_skip,
            gate_gain,
        )
        return pull_lane(lane_grad)

    lane_grads = lax.map(one_lane, lane_inputs + (mixed_grad,))
    return (lane_grads[:7], jnp.sum(lane_grads[7], axis=0), jnp.sum(lane_grads[8], axis=0))


def chain_combine(earlier, latter):
    return (earlier[0] * latter[0], latter[0][:, :, None, None] * earlier[1] + latter[1])


def share_out(out_grad):
    return lax.psum_scatter(out_grad, "seq", scatter_dimension=0, tiled=True)


def contract_rows(left, right):
    return lax.dot_general(
        left, right, (((0,), (0,)), ((), ())), preferred_element_type=jnp.float32
    )


def contract_cols(left, right):
    return lax.dot_general(
        left, right, (((1,), (1,)), ((), ())), preferred_element_type=jnp.float32
    )


def rows_body(
    tokens,
    cotangent,
    starts,
    valid,
    norm_gain,
    w_zx,
    w_bc,
    w_dt,
    conv_w,
    conv_b,
    dt_bias,
    a_log,
    d_skip,
    gate_gain,
    w_out,
):
    lane_count = starts.shape[1]
    width_index = lax.axis_index("width")
    shift_bits = lax.axis_size("width") - 1 - width_index
    active_heads = jnp.right_shift(jnp.int32(H), shift_bits)
    chan_mask = (jnp.arange(E) // HEAD_DIM < active_heads).astype(jnp.float32)
    head_mask = (jnp.arange(H) < active_heads).astype(jnp.float32)
    chan_count = (active_heads * HEAD_DIM).astype(jnp.float32)
    keep_rows = 1.0 - starts[0].astype(jnp.float32)
    row_mask = (jnp.arange(BLOCK)[None, :] < valid[0][:, None]).astype(jnp.float32).reshape(-1, 1)
    x_rows = tokens.astype(jnp.float32)
    normed, norm_back = jax.vjp(rms_front, x_rows, norm_gain)
    normed_low = normed.astype(jnp.bfloat16)
    zx_full, bc_full, dt_full, out_full = (
        lax.all_gather(w_zx, "seq", axis=0, tiled=True),
        lax.all_gather(w_bc, "seq", axis=0, tiled=True),
        lax.all_gather(w_dt, "seq", axis=0, tiled=True),
        lax.all_gather(w_out, "seq", axis=0, tiled=True),
    )
    zx_pre = jnp.dot(normed_low, zx_full, preferred_element_type=jnp.float32).reshape(
        lane_count, BLOCK, 2 * E
    )
    bc_pre = jnp.dot(normed_low, bc_full, preferred_element_type=jnp.float32).reshape(
        lane_count, BLOCK, 2 * N
    )
    dt_raw = jnp.dot(normed_low, dt_full, preferred_element_type=jnp.float32).reshape(
        lane_count, BLOCK, H
    )
    rim_rows = passed_along(rim_of(zx_pre, bc_pre, chan_mask), "seq", 1)
    front_fn = partial(piece_front, chan_mask=chan_mask, head_mask=head_mask, keep_rows=keep_rows)
    front_out, front_back = jax.vjp(
        front_fn, zx_pre, bc_pre, dt_raw, rim_rows, conv_w, conv_b, dt_bias, a_log
    )
    z_gate, x_conv, b_conv, c_conv, dt_step, log_step = front_out
    (state_sum, log_total), state_back = jax.vjp(block_state, x_conv, b_conv, dt_step, log_step)
    carry_rate = jnp.exp(log_total) * keep_rows[:, None]
    identity = (jnp.ones_like(carry_rate), jnp.zeros_like(state_sum))
    prefix_pair = carried_in((carry_rate, state_sum), "seq", chain_combine, identity, False)
    state_in = prefix_pair[1] * keep_rows[:, None, None, None]
    lane_inputs = (z_gate, x_conv, b_conv, c_conv, dt_step, log_step, state_in)
    mixed_low = mix_lanes(lane_inputs, d_skip, gate_gain, chan_count)
    mixed_flat = mixed_low.reshape(-1, E).astype(jnp.bfloat16)
    branch = jnp.dot(mixed_flat, out_full, preferred_element_type=jnp.float32)
    output = (x_rows + row_mask * branch).astype(jnp.bfloat16)
    cot_rows = cotangent.astype(jnp.float32)
    branch_grad = (cot_rows * row_mask).astype(jnp.bfloat16)
    out_grad = contract_rows(mixed_flat, branch_grad)
    mixed_grad = contract_cols(branch_grad, out_full).reshape(lane_count, BLOCK, E)
    lane_grads, grad_skip, grad_gain = mix_back_lanes(
        lane_inputs, mixed_grad, d_skip, gate_gain, chan_count
    )
    grad_gate, grad_x, grad_b, grad_c, grad_dt, grad_log, grad_state = lane_grads
    later_pair = carried_in(
        (carry_rate, grad_state * keep_rows[:, None, None, None]),
        "seq",
        chain_combine,
        identity,
        True,
    )
    later_grad = later_pair[1]
    grad_total = jnp.exp(log_total) * jnp.sum(later_grad * state_in, axis=(2, 3))
    grad_x_more, grad_b_more, grad_dt_more, grad_log_more = state_back((later_grad, grad_total))
    grad_zx, grad_bc, grad_dtraw, grad_rim, grad_convw, grad_convb, grad_dtbias, grad_alog = (
        front_back(
            (
                grad_gate,
                grad_x + grad_x_more,
                grad_b + grad_b_more,
                grad_c,
                grad_dt + grad_dt_more,
                grad_log + grad_log_more,
            )
        )
    )
    rim_grad = passed_along(grad_rim.astype(jnp.bfloat16), "seq", -1).astype(grad_rim.dtype)
    grad_zx = grad_zx.at[:, BLOCK - KCONV + 1 :, E:].add(rim_grad[..., :E] * chan_mask)
    grad_bc = grad_bc.at[:, BLOCK - KCONV + 1 :, :].add(rim_grad[..., E:])
    zx_low = grad_zx.reshape(-1, 2 * E).astype(jnp.bfloat16)
    bc_low = grad_bc.reshape(-1, 2 * N).astype(jnp.bfloat16)
    dt_low = grad_dtraw.reshape(-1, H).astype(jnp.bfloat16)
    zx_weight_grad = contract_rows(normed_low, zx_low)
    bc_weight_grad = contract_rows(normed_low, bc_low)
    dt_weight_grad = contract_rows(normed_low, dt_low)
    normed_grad = (
        contract_cols(zx_low, zx_full)
        + contract_cols(bc_low, bc_full)
        + contract_cols(dt_low, dt_full)
    )
    grad_x_rows, grad_norm = norm_back(normed_grad)
    input_grad = cot_rows + grad_x_rows
    out_shard = share_out(out_grad)
    row_shards = (
        lax.psum_scatter(grad_norm, "seq", scatter_dimension=0, tiled=True),
        lax.psum_scatter(zx_weight_grad, "seq", scatter_dimension=0, tiled=True),
        lax.psum_scatter(bc_weight_grad, "seq", scatter_dimension=0, tiled=True),
        lax.psum_scatter(dt_weight_grad, "seq", scatter_dimension=0, tiled=True),
        lax.psum_scatter(grad_convw, "seq", scatter_dimension=0, tiled=True),
        lax.psum_scatter(grad_convb, "seq", scatter_dimension=0, tiled=True),
        lax.psum_scatter(grad_dtbias, "seq", scatter_dimension=0, tiled=True),
        lax.psum_scatter(grad_alog, "seq", scatter_dimension=0, tiled=True),
        lax.psum_scatter(grad_skip, "seq", scatter_dimension=0, tiled=True),
        lax.psum_scatter(grad_gain, "seq", scatter_dimension=0, tiled=True),
    )
    summed = lax.psum(
        (
            row_shards[0],
            row_shards[1],
            row_shards[2],
            row_shards[3],
            row_shards[4],
            row_shards[5],
            row_shards[6],
            row_shards[7],
            row_shards[8],
            row_shards[9],
            out_shard,
        ),
        "width",
    )
    return (
        output,
        input_grad,
        summed[0],
        summed[1],
        summed[2],
        summed[3],
        summed[4],
        summed[5],
        summed[6],
        summed[7],
        summed[8],
        summed[9],
        summed[10],
    )


def solution(mesh):
    in_specs = (
        P(("width", "seq"), None),
        P(("width", "seq"), None),
        P(("width", "seq"), None),
        P(("width", "seq"), None),
        P(),
        P("seq", None),
        P("seq", None),
        P("seq", None),
        P(),
        P(),
        P(),
        P(),
        P(),
        P(),
        P("seq", None),
    )
    out_specs = (
        P(("width", "seq"), None),
        P(("width", "seq"), None),
        P("seq"),
        P("seq", None),
        P("seq", None),
        P("seq", None),
        P("seq", None),
        P("seq"),
        P("seq"),
        P("seq"),
        P("seq"),
        P("seq"),
        P("seq", None),
    )
    body = heads_body if H % (2 * mesh.shape["seq"]) == 0 else rows_body
    return jax.shard_map(body, mesh=mesh, in_specs=in_specs, out_specs=out_specs, check_vma=False)
```

```python
from functools import partial

import jax
import jax.numpy as jnp
from jax import lax
from jax.experimental import pallas as pl
from jax.experimental.pallas import tpu as pltpu
from jax.sharding import PartitionSpec as P
import numpy as np

H = 64
HEAD_DIM = 64
N = 128
KCONV = 4
BLOCK = 128
E = 4096
SUB = 8

epsilon = 1e-05
highest = lax.Precision.HIGHEST
f32 = jnp.float32
bf16 = jnp.bfloat16

NN = ((1,), (0,))
NT = ((1,), (1,))
TN = ((0,), (0,))


def mm(left, right, dims=NN, precision=None):
    return lax.dot_general(left, right, (dims, ((), ())), precision=precision, preferred_element_type=f32)


def split2(value):
    high = value.astype(bf16)
    return high, (value - high.astype(f32)).astype(bf16)


def mm_right(left, right, dims=NN):
    high, low = split2(right)
    return mm(left, high, dims) + mm(left, low, dims)


def mm_left(left, right, dims=NN):
    high, low = split2(left)
    return mm(high, right, dims) + mm(low, right, dims)


def softplus(v):
    small = jnp.exp(-jnp.abs(v))
    log1p = jnp.where(small < 1e-4, small - 0.5 * small * small, jnp.log(1.0 + small))
    return jnp.maximum(v, 0.0) + log1p


def sigmoid(v):
    return 1.0 / (1.0 + jnp.exp(-v))


def grids():
    row = lax.broadcasted_iota(jnp.int32, (BLOCK, BLOCK), 0)
    col = lax.broadcasted_iota(jnp.int32, (BLOCK, BLOCK), 1)
    return row, col


def halves(pair, lane):
    zero = jnp.zeros_like(pair)
    return jnp.where(lane < HEAD_DIM, pair, zero), jnp.where(lane < HEAD_DIM, zero, pair)


def decay_of(cum, cum_t, head, causal):
    return jnp.exp(jnp.where(causal, cum[:, head : head + 1] - cum_t[head : head + 1, :], -1e30))


TAP, BIAS, SKIP, GAIN, MASK = 0, 4, 5, 6, 7
DT_BIAS, NEG_A, HEAD_MASK = 0, 1, 2


def forward_block(
    keep_row, zx_ref, chan_ref, bc_par_ref, head_ref, spread,
    conv_ref, mix_ref, bc_ref, step_ref, state_ref, tail_ref,
    state, tail_x, tail_b, pad_x, pad_b,
    *, lane, heads,
):
    width = heads * HEAD_DIM
    row, col = grids()
    causal = row >= col
    tril = causal.astype(f32)
    rows = pl.ds(lane * BLOCK, BLOCK)
    keep = jnp.concatenate([keep_row] * (width // BLOCK), axis=1)
    keep_b = jnp.concatenate([keep_row] * (2 * N // BLOCK), axis=1)

    pre = zx_ref[rows, width : 2 * width]
    before = tail_x[lane] * keep
    pad_x[lane, 0:SUB] = before
    pad_x[lane, SUB:] = pre
    tail_ref[lane] = before
    tail_x[lane] = pre[BLOCK - SUB :, :]
    conv = chan_ref[BIAS : BIAS + 1, :]
    for k in range(KCONV):
        conv = conv + pad_x[lane, SUB - KCONV + 1 + k : SUB - KCONV + 1 + k + BLOCK, :] * chan_ref[k : k + 1, :]
    conv_ref[rows, :] = conv
    x_low = (conv * sigmoid(conv) * chan_ref[MASK : MASK + 1, :]).astype(bf16)

    pre_b = zx_ref[rows, 2 * width + BLOCK :]
    pad_b[lane, 0:SUB] = tail_b[lane] * keep_b
    pad_b[lane, SUB:] = pre_b
    tail_b[lane] = pre_b[BLOCK - SUB :, :]
    conv_b = bc_par_ref[BIAS : BIAS + 1, :]
    for k in range(KCONV):
        conv_b = conv_b + pad_b[lane, SUB - KCONV + 1 + k : SUB - KCONV + 1 + k + BLOCK, :] * bc_par_ref[k : k + 1, :]
    bc_low = (conv_b * sigmoid(conv_b)).astype(bf16)
    bc_ref[rows, :] = bc_low
    b_low, c_low = bc_low[:, :N], bc_low[:, N:]

    raw = zx_ref[rows, 2 * width : 2 * width + BLOCK] + head_ref[DT_BIAS : DT_BIAS + 1, :]
    dt = softplus(raw) * head_ref[HEAD_MASK : HEAD_MASK + 1, :]
    cum = mm(tril, head_ref[NEG_A : NEG_A + 1, :] * dt, precision=highest)
    step_ref[rows, :BLOCK] = cum
    step_ref[rows, BLOCK:] = dt
    cum_t, dt_t = cum.T, dt.T
    last = cum[BLOCK - 1 :, :]
    carry_x = mm_left(jnp.exp(cum), spread)
    end_x = mm_left(jnp.exp(last - cum) * dt, spread)
    last_x = carry_x[BLOCK - 1 :, :]

    inner = mm(c_low, b_low, NT)
    parts = []
    for j in range(heads // 2):
        pair = x_low[:, 2 * HEAD_DIM * j : 2 * HEAD_DIM * (j + 1)]
        scores = [
            (inner * decay_of(cum, cum_t, h, causal) * dt_t[h : h + 1, :]).astype(bf16)
            for h in (2 * j, 2 * j + 1)
        ]
        parts.append(mm(jnp.concatenate(scores, axis=1), jnp.concatenate(halves(pair, col), axis=0)))
    within = jnp.concatenate(parts, axis=1)

    state_in = state[lane] * keep
    state_ref[lane] = state_in
    carried = mm_right(c_low, state_in) * carry_x
    x_f = x_low.astype(f32)
    mix_ref[rows, :] = within + carried + chan_ref[SKIP : SKIP + 1, :] * x_f
    weighted = (x_f * end_x).astype(bf16)
    state[lane] = last_x * state_in + mm(b_low, weighted, TN)


def backward_kernel(
    start_ref, zx_ref, grad_ref, chan_ref, head_ref, spread_ref,
    conv_ref, mix_ref, bc_ref, step_ref, state_ref, tail_ref, scale_ref,
    dzx_ref, dbc_ref, dchan_ref, dhead_ref,
    state_grad, next_conv, pad_x, pad_d,
    *, lanes, heads,
):
    lap = pl.program_id(0)
    width = heads * HEAD_DIM
    row, col = grids()
    causal = row >= col
    triu = (col >= row).astype(f32)
    spread = spread_ref[...]

    @pl.when(lap == 0)
    def _():
        state_grad[...] = jnp.zeros_like(state_grad)
        next_conv[...] = jnp.zeros_like(next_conv)
        dchan_ref[...] = jnp.zeros_like(dchan_ref)
        dhead_ref[...] = jnp.zeros_like(dhead_ref)

    def total(value):
        return jnp.sum(value, axis=0, keepdims=True)

    for lane in range(lanes):
        rows = pl.ds(lane * BLOCK, BLOCK)
        keep = 1.0 - jnp.concatenate([start_ref[0, lane : lane + 1, :]] * (width // BLOCK), axis=1)
        z = zx_ref[rows, :width]
        conv = conv_ref[rows, :]
        mixed = mix_ref[rows, :]
        grad = grad_ref[rows, :]
        gain = chan_ref[GAIN : GAIN + 1, :]
        skip = chan_ref[SKIP : SKIP + 1, :]
        rate = scale_ref[rows, 0:1]
        pull = scale_ref[rows, 1:2]
        gate = sigmoid(z)
        silu = z * gate
        gated = mixed * silu
        dgated = grad * gain * rate - gated * pull
        dzx_ref[rows, :width] = (dgated * mixed * (gate * (1.0 + z * (1.0 - gate)))).astype(bf16)
        dmixed = dgated * silu
        act = sigmoid(conv)
        x_low = (conv * act * chan_ref[MASK : MASK + 1, :]).astype(bf16)
        x_f = x_low.astype(f32)
        dchan_ref[GAIN : GAIN + 1, :] += total(grad * gated * rate)
        dchan_ref[SKIP : SKIP + 1, :] += total(dmixed * x_f)
        dlow = dmixed.astype(bf16)
        dlow_f = dlow.astype(f32)

        b_low, c_low = bc_ref[rows, :N], bc_ref[rows, N:]
        cum, dt = step_ref[rows, :BLOCK], step_ref[rows, BLOCK:]
        cum_t, dt_t = cum.T, dt.T
        last = cum[BLOCK - 1 :, :]
        to_last = jnp.exp(last - cum)
        carry_x = mm_left(jnp.exp(cum), spread)
        end_x = mm_left(to_last * dt, spread)
        last_x = carry_x[BLOCK - 1 :, :]

        inner = mm(c_low, b_low, NT)
        dinner = jnp.zeros((BLOCK, BLOCK), f32)
        parts, dt_rows = [], []
        for j in range(heads // 2):
            lanes_j = slice(2 * HEAD_DIM * j, 2 * HEAD_DIM * (j + 1))
            pair, dpair = x_low[:, lanes_j], dlow[:, lanes_j]
            dstack = jnp.concatenate(halves(dpair, col), axis=0)
            dscores = mm(dstack, pair, NT)
            scores = []
            for i, h in enumerate((2 * j, 2 * j + 1)):
                decay = decay_of(cum, cum_t, h, causal)
                step = dt_t[h : h + 1, :]
                scores.append((inner * decay * step).astype(bf16))
                part = dscores[i * BLOCK : (i + 1) * BLOCK] * decay
                dinner = dinner + part * step
                dt_rows.append(total(part * inner))
            parts.append(mm(jnp.concatenate(scores, axis=0), dstack, TN))
        dx_within = jnp.concatenate(parts, axis=1)
        dt_rows.append(jnp.zeros((BLOCK - heads, BLOCK), f32))
        ddt_within = jnp.concatenate(dt_rows, axis=0).T

        state_in = state_ref[0, lane]
        sgrad = state_grad[lane]
        in_high, in_low = split2(state_in)
        sg_high, sg_low = split2(sgrad)
        dcarry = dlow_f * carry_x
        dc_high, dc_low = split2(dcarry)
        di_high, di_low = split2(dinner)
        dc = mm(dc_high, in_high, NT) + mm(dc_high, in_low, NT) + mm(dc_low, in_high, NT)
        dc = dc + mm(di_high, b_low) + mm(di_low, b_low)
        weighted = (x_f * end_x).astype(bf16)
        db = mm(weighted, sg_high, NT) + mm(weighted, sg_low, NT)
        db = db + mm(di_high, c_low, TN) + mm(di_low, c_low, TN)
        dbc_ref[:N, rows] = db.T.astype(bf16)
        dbc_ref[N:, rows] = dc.T.astype(bf16)
        dweighted = mm(b_low, sg_high) + mm(b_low, sg_low)
        dx = dx_within + dweighted * end_x
        dcum = mm_left(dlow_f * (mixed - skip * x_f) - x_f * dx, spread, NT)
        dend = mm_left(dweighted * x_f, spread, NT)
        touch = jnp.broadcast_to(total(sgrad * state_in), (SUB, width))
        dlast = total(dend * to_last * dt) + jnp.exp(last) * mm_left(touch, spread, NT)[0:1]
        dlog = mm(triu, dcum, precision=highest) + dlast
        neg_a = head_ref[NEG_A : NEG_A + 1, :]
        ddt = ddt_within + dend * to_last + dlog * neg_a
        raw = zx_ref[rows, 2 * width : 2 * width + BLOCK] + head_ref[DT_BIAS : DT_BIAS + 1, :]
        draw = ddt * sigmoid(raw) * head_ref[HEAD_MASK : HEAD_MASK + 1, :]
        dzx_ref[rows, 2 * width :] = draw.astype(bf16)
        dhead_ref[0:1, :] += total(draw)
        dhead_ref[1:2, :] += total(dlog * neg_a * dt)
        state_grad[lane] = keep * (mm(c_low, dc_high, TN) + mm(c_low, dc_low, TN) + last_x * sgrad)

        dx = dx + skip * dmixed
        dconv = dx * chan_ref[MASK : MASK + 1, :] * (act * (1.0 + conv * (1.0 - act)))
        pad_d[lane, :BLOCK] = dconv
        pad_d[lane, BLOCK:] = next_conv[lane]
        next_conv[lane] = dconv[:SUB] * keep
        pad_x[lane, :SUB] = tail_ref[0, lane]
        pad_x[lane, SUB:] = zx_ref[rows, width : 2 * width]
        dpre = jnp.zeros((BLOCK, width), f32)
        for k in range(KCONV):
            dpre = dpre + pad_d[lane, KCONV - 1 - k : KCONV - 1 - k + BLOCK, :] * chan_ref[k : k + 1, :]
            dchan_ref[k : k + 1, :] += total(dconv * pad_x[lane, SUB - KCONV + 1 + k : SUB - KCONV + 1 + k + BLOCK, :])
        dchan_ref[BIAS : BIAS + 1, :] += total(dconv)
        dzx_ref[rows, width : 2 * width] = dpre.astype(bf16)


def run_backward(starts, zx, grad, chan, head, spread, conv, mix, bc, step_arr, state, tail, scale, lanes, heads):
    rows, width = grad.shape
    step = lanes * BLOCK
    blocks = rows // step
    by_block = lambda cols: pl.BlockSpec((step, cols), lambda c: (blocks - 1 - c, 0))
    whole = lambda a: pl.BlockSpec(a.shape, lambda c: (0,) * a.ndim)
    fixed = lambda shape: pl.BlockSpec(shape, lambda c: (0,) * len(shape))
    per_lane = lambda r, cols: pl.BlockSpec((1, lanes, r, cols), lambda c: (blocks - 1 - c, 0, 0, 0))
    return pl.pallas_call(
        partial(backward_kernel, lanes=lanes, heads=heads),
        grid=(blocks,),
        in_specs=[
            pl.BlockSpec((1, SUB, BLOCK), lambda c: (blocks - 1 - c, 0, 0)), by_block(2 * width + BLOCK), by_block(width),
            whole(chan), whole(head), whole(spread),
            by_block(width), by_block(width), by_block(2 * N), by_block(2 * BLOCK),
            per_lane(N, width), per_lane(SUB, width), by_block(BLOCK),
        ],
        out_specs=[
            by_block(2 * width + BLOCK), pl.BlockSpec((2 * N, step), lambda c: (0, blocks - 1 - c)),
            fixed((SUB, width)), fixed((SUB, BLOCK)),
        ],
        out_shape=[
            jax.ShapeDtypeStruct((rows, 2 * width + BLOCK), bf16),
            jax.ShapeDtypeStruct((2 * N, rows), bf16), jax.ShapeDtypeStruct((SUB, width), f32),
            jax.ShapeDtypeStruct((SUB, BLOCK), f32),
        ],
        scratch_shapes=[
            pltpu.VMEM((lanes, N, width), f32), pltpu.VMEM((lanes, SUB, width), f32),
            pltpu.VMEM((lanes, BLOCK + SUB, width), f32), pltpu.VMEM((lanes, BLOCK + SUB, width), f32),
        ],
        compiler_params=pltpu.CompilerParams(vmem_limit_bytes=62 << 20, dimension_semantics=("arbitrary",)),
        cost_estimate=pl.CostEstimate(flops=rows * width * 6144, bytes_accessed=rows * width * 40, transcendentals=rows * width * 6),
        name="mix_backward",
    )(starts, zx, grad, chan, head, spread, conv, mix, bc, step_arr, state, tail, scale)


MESH = pl.DeviceIdType.MESH


def greet(others):
    for other in others:
        pl.semaphore_signal(pltpu.get_barrier_semaphore(), inc=1, device_id=other, device_id_type=MESH)


def met(others):
    pl.semaphore_wait(pltpu.get_barrier_semaphore(), len(others))


def remote(src, dst, send, recv, device):
    return pltpu.make_async_remote_copy(
        src_ref=src, dst_ref=dst, send_sem=send, recv_sem=recv, device_id=device, device_id_type=MESH
    )


PARTS = 2


def part_of(ref, i):
    rows = ref.shape[0] // PARTS
    return ref.at[pl.ds(i * rows, rows)]


class Rows:
    def __init__(self, own_ref, all_ref, sems, peers):
        self.own, self.all, self.sems, self.peers = own_ref, all_ref, sems, peers
        self.width, self.place = lax.axis_index("width"), lax.axis_index("seq")
        self.chips, self.chip = peers // 2, self.place // 2

    def hop(self, ref, s, step, by, i):
        send, recv = self.sems[0 if by > 0 else 2], self.sems[1 if by > 0 else 3]
        device = (self.width, jnp.clip(self.place + 2 * by, 0, self.peers - 1))
        return remote(part_of(ref, i), part_of(self.all.at[s], i), send.at[step, i], recv.at[step, i], device)

    def over(self, ref, s, slot, i):
        device = (self.width, jnp.bitwise_xor(self.place, 1))
        send, recv = self.sems[4].at[slot, i], self.sems[5].at[slot, i]
        return remote(part_of(ref, i), part_of(self.all.at[s], i), send, recv, device)

    def inside(self, by):
        return self.chip + 1 < self.chips if by > 0 else self.chip > 0

    def reached(self, by, step):
        return self.chip >= step if by > 0 else self.chip + step < self.chips

    def source(self, by, step):
        return jnp.clip(self.place - 2 * by * step, 0, self.peers - 1)

    def keep(self):
        return pltpu.make_async_copy(self.own, self.all.at[self.place], self.sems[6])

    def start(self):
        for i in range(PARTS):
            for by in (1, -1):
                @pl.when(self.inside(by))
                def _():
                    self.hop(self.own, self.place, 0, by, i).start()
        self.keep().start()
        for copy in self.mate(1, 0):
            copy.start()

    def pass_on(self, step):
        for i in range(PARTS):
            for by in (1, -1):
                @pl.when(self.reached(by, step))
                def _():
                    s = self.source(by, step)
                    ref = self.all.at[s]
                    self.hop(ref, s, step - 1, by, i).wait_recv()

                    @pl.when(self.inside(by))
                    def _():
                        self.hop(ref, s, step, by, i).start()
                    self.over(ref, s, 2 * step - (by > 0), i).start()

    def mate(self, by, step):
        if not step:
            return [self.over(self.own, self.place, 0, i) for i in range(PARTS)]
        s = self.source(by, step)
        return [self.over(self.all.at[s], s, 2 * step - (by > 0), i) for i in range(PARTS)]

    def arrived(self):
        self.keep().wait()
        for copy in self.mate(1, 0):
            copy.wait_recv()
        for step in range(1, self.chips):
            for by in (1, -1):
                @pl.when(self.reached(by, step))
                def _():
                    for copy in self.mate(by, step):
                        copy.wait_recv()

    def sent(self):
        for step in range(self.chips):
            for by in (1, -1):
                @pl.when(self.inside(by) & self.reached(by, step))
                def _():
                    s = self.source(by, step)
                    for i in range(PARTS):
                        self.hop(self.all.at[s], s, step, by, i).wait_send()
        for copy in self.mate(1, 0):
            copy.wait_send()
        for step in range(1, self.chips):
            for by in (1, -1):
                @pl.when(self.reached(by, step))
                def _():
                    for copy in self.mate(by, step):
                        copy.wait_send()


ROW_SEMS = 7


def row_sems(chips):
    dma = pltpu.SemaphoreType.DMA
    return [dma((chips, PARTS))] * 4 + [dma((2 * chips, PARTS))] * 2 + [dma(())]


def front_kernel(
    valid_ref, start_ref, x_ref, cot_ref, norm_gain_ref, bc_ref, dt_ref, taps_ref, bias_ref, dtb_ref, alog_ref, skip_ref,
    gain_ref, spread_ref, zx_ref, wout_ref,
    w_ref, rows_ref, grads_ref, starts_ref, chan_ref, head_ref, bc_par,
    out_zx, out_mix, out_grad, out_scale, out_q0, out_q1, out_q2, out_q3, out_up, out_down, out_mine, out_conv, out_bc, out_step, out_state, out_tail,
    w_v, rows_v, starts_v, wout_v, own_v, grad_v, third_v, start_v, part_got,
    z_v, mix_v, scale_v, low_v, zx_v, mgrad_v, conv_v, bc_v, step_v, state_v, tail_v, bgrad_v, up, down, wout_grad, sums, sums_got,
    state, tail_x, tail_b, pad_x, pad_b,
    w_send, w_recv, st_send, st_recv, own_sem, wide_send, wide_recv, in_sem, out_sem, slot_sem, grad_sem, part_send, part_recv, branch_sem,
    up_send, up_recv, down_send, down_recv, sum_send, sum_recv, *sems,
    peers, widths, lanes, heads,
):
    width, place = lax.axis_index("width"), lax.axis_index("seq")
    chips = peers // 2
    chans = heads * HEAD_DIM
    quarter = zx_ref.shape[0] // widths
    ring = [lax.rem(place + by, peers) for by in range(1, peers)]
    cross = [jnp.bitwise_xor(width, m) for m in range(1, widths)]
    others = [(width, s) for s in ring] + [(w, place) for w in cross]
    greet(others)

    x = x_ref[...].astype(f32)
    own_v[...] = (x * lax.rsqrt(jnp.mean(x * x, axis=-1, keepdims=True) + epsilon) * norm_gain_ref[...]).astype(bf16)
    row = lax.broadcasted_iota(jnp.int32, (BLOCK, 1), 0)
    sub = lax.broadcasted_iota(jnp.int32, (SUB, BLOCK), 0)
    tile = jnp.zeros((SUB, BLOCK), f32)
    for lane in range(lanes):
        at = slice(lane * BLOCK, (lane + 1) * BLOCK)
        mask = (row < valid_ref[0, lane]).astype(f32)
        grad_v[at, :] = (cot_ref[at, :].astype(f32) * mask).astype(bf16)
        tile = jnp.where(sub == lane, start_ref[0, lane].astype(f32), tile)
    start_v[...] = tile
    bc, dt = bc_ref[...].astype(f32), dt_ref[...].astype(f32).T
    share = bc.shape[1] // peers
    rest = jnp.zeros((bc.shape[0], BLOCK - share - heads), f32)
    for s in range(peers):
        columns = [dt[:, s * heads : (s + 1) * heads], bc[:, s * share : (s + 1) * share], rest]
        third_v[s] = jnp.concatenate(columns, axis=1).astype(bf16)
    met(others)

    mine = pl.ds(pl.multiple_of(width * quarter, quarter), quarter)
    rows = Rows(own_v, rows_ref, sems[:ROW_SEMS], peers)
    grads = Rows(grad_v, grads_ref, sems[ROW_SEMS:], peers)

    def columns_of(half, s):
        return pl.ds(pl.multiple_of(half * peers * chans + s * chans, 128), chans)

    wide = 2 * chans
    spots = [pl.ds(0, chans), pl.ds(chans, chans), pl.ds(wide, BLOCK), pl.ds(wide + BLOCK, 2 * N)]

    def parts(s):
        return [zx_ref.at[mine, columns_of(0, s)], zx_ref.at[mine, columns_of(1, s)], third_v.at[s, mine], bc_ref.at[mine]]

    pushes = []
    for i, s in enumerate(ring):
        for k, (part, spot) in enumerate(zip(parts(s), spots)):
            pushes.append(remote(part, w_ref.at[place, width, :, spot], w_send.at[k, i], w_recv.at[k, i], (width, s)))
        pushes.append(remote(start_v, starts_ref.at[place], st_send.at[i], st_recv.at[i], (width, s)))
    for push in pushes:
        push.start()
    keeps = [
        pltpu.make_async_copy(part, w_ref.at[place, width, :, spot], own_sem.at[k])
        for k, (part, spot) in enumerate(zip(parts(place), spots))
    ]
    keeps.append(pltpu.make_async_copy(start_v, starts_ref.at[place], own_sem.at[4]))
    for keep in keeps:
        keep.start()
    rows.start()

    active = jnp.right_shift(jnp.int32(H), widths - 1 - width)
    first = place * heads
    here = columns_of(0, place)
    spread = spread_ref[...]
    pick_row = lax.broadcasted_iota(jnp.int32, (H, BLOCK), 0)
    pick_lane = lax.broadcasted_iota(jnp.int32, (H, BLOCK), 1)
    chosen = ((pick_row == pick_lane + first) & (pick_lane < heads)).astype(f32)
    per_head = jnp.concatenate(
        [dtb_ref[...], -jnp.exp(alog_ref[...]), jnp.ones((1, H), f32), skip_ref[...], jnp.zeros((SUB - 4, H), f32)], axis=0
    )
    per_head = mm(per_head, chosen, precision=highest)
    head_lane = lax.broadcasted_iota(jnp.int32, (SUB, BLOCK), 1)
    head_ref[...] = jnp.where((sub == HEAD_MASK) & (head_lane + first >= active), 0.0, per_head)
    on_chans = mm(head_ref[...], spread.astype(f32), precision=highest)
    chan_ref[...] = jnp.concatenate(
        [taps_ref[:, here], bias_ref[:, here], on_chans[3:4], gain_ref[:, here], on_chans[HEAD_MASK : HEAD_MASK + 1]], axis=0
    )
    bc_par[...] = jnp.concatenate(
        [taps_ref[:, E:], bias_ref[:, E:], jnp.zeros((SUB - KCONV - 1, 2 * N), f32)], axis=0
    )

    for push in pushes:
        push.wait_recv()
    for keep in keeps:
        keep.wait()
    shares = [
        remote(w_ref.at[:, width], w_ref.at[:, width], wide_send.at[m], wide_recv.at[m], (w, place)) for m, w in enumerate(cross)
    ]
    for copy in shares:
        copy.start()
    for step in range(1, chips - 1):
        rows.pass_on(step)
    grads.start()
    for copy in shares:
        copy.wait_recv()
    in_w = pltpu.make_async_copy(w_ref, w_v, own_sem.at[0])
    in_starts = pltpu.make_async_copy(starts_ref, starts_v, own_sem.at[1])
    in_wout = pltpu.make_async_copy(wout_ref, wout_v, own_sem.at[2])
    for copy in (in_w, in_starts, in_wout):
        copy.start()
    rows.pass_on(chips - 1)
    rows.arrived()

    def load(src, s):
        return pltpu.make_async_copy(src.at[s], rows_v.at[s], in_sem.at[s])

    for c in range(peers):
        load(rows_ref, c).start()
    for array in (state, tail_x, tail_b):
        array[...] = jnp.zeros_like(array)
    for copy in (in_w, in_starts, in_wout):
        copy.wait()

    def out_copy(k, src, dst, c):
        return pltpu.make_async_copy(src.at[c], dst.at[c], out_sem.at[k, c])

    slots = [
        (zx_v, out_zx), (conv_v, out_conv), (bc_v, out_bc), (step_v, out_step), (state_v, out_state), (tail_v, out_tail)
    ]

    def slot_copies(c):
        slot = lax.rem(c, 2)
        return [pltpu.make_async_copy(src.at[slot], dst.at[c], slot_sem.at[k, slot]) for k, (src, dst) in enumerate(slots)]

    def compute(begin, end):
        @pl.loop(begin, end)
        def _(c):
            load(rows_ref, c).wait()

            @pl.when(c >= 2)
            def _():
                for copy in slot_copies(c - 2):
                    copy.wait()
            weights = w_v[...].reshape(w_v.shape[0] * w_v.shape[1] * w_v.shape[2], w_v.shape[3])
            slot = lax.rem(c, 2)
            zx = mm(rows_v[c], weights)
            zx_v[slot] = zx
            z_v[c] = zx[:, :chans]
            for lane in range(lanes):
                forward_block(
                    1.0 - starts_v[c, lane : lane + 1, :], zx_v.at[slot], chan_ref, bc_par, head_ref, spread_ref[...],
                    conv_v.at[slot], mix_v.at[c], bc_v.at[slot], step_v.at[slot], state_v.at[slot], tail_v.at[slot],
                    state, tail_x, tail_b, pad_x, pad_b, lane=lane, heads=heads,
                )
            out_copy(0, mix_v, out_mix, c).start()
            for copy in slot_copies(c):
                copy.start()
            gated = gated_of(c)
            square = mm_right(jnp.ones((SUB, chans), bf16), gated * gated, NT)
            for lane in range(lanes):
                sums[0, pl.ds(c * lanes + lane, 1), :] = square[:1, lane * BLOCK : (lane + 1) * BLOCK]

    def gated_of(c):
        z = z_v[c]
        return mix_v[c] * (z * sigmoid(z))

    core = lax.rem(place, 2)

    def give(k):
        copies = [
            remote(sums.at[k], sums_got.at[k, i], sum_send.at[k, i], sum_recv.at[k, i], (width, s)) for i, s in enumerate(ring)
        ]
        for copy in copies:
            copy.start()
        return copies

    def whole(k, copies):
        total = sums[k]
        for i, copy in enumerate(copies):
            copy.wait_recv()
            total = total + sums_got[k, i]
        return total

    def by_time(value):
        return jnp.concatenate([value, jnp.zeros((BLOCK - lanes * peers, BLOCK), f32)], axis=0).T

    def load_grad(s, slot):
        return pltpu.make_async_copy(grads_ref.at[s], bgrad_v.at[slot], in_sem.at[slot])

    def grad_out(s, slot):
        return pltpu.make_async_copy(mgrad_v.at[slot], out_grad.at[s], grad_sem.at[slot])

    def mix_grads(q, first):
        for slot in range(2):
            load_grad(2 * q + slot, slot).start()
        for slot in range(2):
            s = 2 * q + slot
            load_grad(s, slot).wait()
            if not first:
                grad_out(s, slot).wait()
            grad = mm(bgrad_v[slot], wout_v[...], NT)
            mgrad_v[slot] = grad
            grad_out(s, slot).start()
            pulled = mm_right(jnp.ones((SUB, chans), bf16), grad * chan_ref[GAIN : GAIN + 1, :] * gated_of(s), NT)
            for lane in range(lanes):
                sums[1, pl.ds(s * lanes + lane, 1), :] = pulled[:1, lane * BLOCK : (lane + 1) * BLOCK]
        rows_q = low_v[pl.ds(2 * q, 2)].reshape(2 * low_v.shape[1], chans)
        both = bgrad_v[...].reshape(2 * bgrad_v.shape[1], bgrad_v.shape[2])
        part = mm(rows_q, both, TN)
        wout_grad[...] = part if first else wout_grad[...] + part

    def mine(q):
        return rows_v.at[2 * q + core]

    def part_over(q):
        return remote(
            rows_v.at[2 * q + 1 - core], part_got.at[q], part_send.at[q], part_recv.at[q], (width, jnp.bitwise_xor(place, 1))
        )

    def part_sum(q):
        part_over(q).wait_recv()
        add_into(mine(q), [part_got.at[q]], rows_v.shape[1])

    def sends(by, step):
        far = chips - step
        return unit_chip + far < chips if by > 0 else unit_chip >= far

    def later(by):
        return unit_chip > 0 if by > 0 else unit_chip + 1 < chips

    unit_chip = place // 2

    def branch_hop(src, by, step, i):
        buffer, send, recv = (up, up_send, up_recv) if by > 0 else (down, down_send, down_recv)
        return remote(
            part_of(src, i), part_of(buffer.at[step - 1], i), send.at[step - 1, i], recv.at[step - 1, i],
            (width, jnp.clip(place + 2 * by, 0, peers - 1)),
        )

    def branch_stage(by, step):
        return (up if by > 0 else down).at[step - 2]

    def branch_hops(step):
        for i in range(PARTS):
            for by in (1, -1):
                owner = jnp.clip(unit_chip + by * (chips - step), 0, chips - 1)
                last = step == chips - 1

                def direct():
                    branch_hop(mine(owner), by, step, i).start()

                def relayed():
                    stage = branch_stage(by, step)
                    branch_hop(stage, by, step - 1, i).wait_recv()
                    add_into(part_of(stage, i), [part_of(mine(owner), i)], rows_v.shape[1] // PARTS)
                    if not last:
                        branch_hop(stage, by, step, i).start()

                if step == 1:
                    pl.when(sends(by, step))(direct)
                    continue
                if not last:
                    pl.when(sends(by, step) & jnp.logical_not(later(by)))(direct)
                pl.when(sends(by, step) & later(by))(relayed)

    def branch_out(k, src):
        return pltpu.make_async_copy(src, (out_mine, out_up, out_down)[k], branch_sem.at[k])

    def branch_outs(act):
        act(branch_out(0, mine(unit_chip)))
        for k, by in ((1, 1), (2, -1)):
            owner = jnp.clip(unit_chip + by, 0, chips - 1)

            @pl.when(later(by))
            def _():
                act(branch_out(k, branch_stage(by, chips - 1)))

            @pl.when(jnp.logical_not(later(by)))
            def _():
                act(branch_out(k, mine(owner)))

    compute(0, peers)
    squares = give(0)
    grads.pass_on(1)

    def mates_here(step):
        if not step:
            for copy in grads.mate(1, 0):
                copy.wait_recv()
        for by in (1, -1):
            if step:
                @pl.when(grads.reached(by, step))
                def _():
                    for copy in grads.mate(by, step):
                        copy.wait_recv()

    def at_distance(step):
        for by in (1, -1):
            @pl.when(grads.reached(by, step))
            def _():
                mix_grads(grads.source(by, step) // 2, False)

    @pl.loop(0, chips)
    def _(i):
        q = jnp.where(unit_chip < chips // 2, chips - 1 - i, i)
        for c in (2 * q + 1 - core, 2 * q + core):
            low = (gated_of(c) * chan_ref[GAIN : GAIN + 1, :]).astype(bf16)
            rows_v[c] = mm(low, wout_v[...]).astype(bf16)
        part_over(q).start()

    for q in range(chips):
        part_sum(q)
    branch_hops(1)
    count = (active * HEAD_DIM).astype(f32)
    rate = lax.rsqrt(whole(0, squares) / count + epsilon)
    rate_t = by_time(rate)
    lane_at = lax.broadcasted_iota(jnp.int32, (BLOCK, BLOCK), 1)
    spots_of = [(c, slice(lane * BLOCK, (lane + 1) * BLOCK)) for c in range(peers) for lane in range(lanes)]
    for i, (c, at) in enumerate(spots_of):
        scale_v[c, at, :] = jnp.where(lane_at == 0, rate_t[:, i : i + 1], 0.0)

    @pl.loop(0, peers)
    def _(c):
        low_v[c] = (gated_of(c) * scale_v[c, :, 0:1] * chan_ref[GAIN : GAIN + 1, :]).astype(bf16)

    grads.pass_on(2)
    grads.keep().wait()
    mates_here(0)
    mix_grads(unit_chip, True)
    mates_here(1)
    at_distance(1)
    for step in range(2, chips - 1):
        branch_hops(step)
        mates_here(step)
        at_distance(step)
    grads.pass_on(chips - 1)
    mates_here(chips - 1)
    at_distance(chips - 1)
    crosses = give(1)
    bgrad_v[...] = wout_grad[...].astype(bf16).reshape(bgrad_v.shape)
    wout_rows = chans // widths
    per_block = bgrad_v.shape[1] // wout_rows

    def wout_quarter(m):
        j = jnp.bitwise_xor(width, m)
        rows_j = pl.ds(pl.multiple_of(lax.rem(j, per_block) * wout_rows, 16), wout_rows)
        return bgrad_v.at[j // per_block, rows_j]

    wout_out = [
        pltpu.make_async_copy(wout_quarter(m), dst, own_sem.at[m]) for m, dst in enumerate((out_q0, out_q1, out_q2, out_q3))
    ]
    for copy in wout_out:
        copy.start()
    branch_hops(chips - 1)
    branch_outs(lambda copy: copy.start())
    pull_t = by_time(rate * rate * rate * whole(1, crosses) / count)
    for i, (c, at) in enumerate(spots_of):
        scale_v[c, at, :] = jnp.where(lane_at == 1, pull_t[:, i : i + 1], scale_v[c, at, :])
    for c in range(peers):
        out_copy(1, scale_v, out_scale, c).start()

    for copy in shares + pushes + squares + crosses:
        copy.wait_send()
    rows.sent()
    grads.sent()
    for c in (peers - 2, peers - 1):
        for copy in slot_copies(c):
            copy.wait()

    @pl.loop(0, peers)
    def _(c):
        for k, (src, dst) in enumerate([(mix_v, out_mix), (scale_v, out_scale)]):
            out_copy(k, src, dst, c).wait()

    for q in range(chips):
        part_over(q).wait_send()
    for step in range(1, chips - 1):
        for by in (1, -1):
            @pl.when(sends(by, step))
            def _():
                for i in range(PARTS):
                    branch_hop(mine(0), by, step, i).wait_send()
    for slot in range(2):
        grad_out(slot, slot).wait()
    for copy in wout_out:
        copy.wait()
    branch_outs(lambda copy: copy.wait())


def front(valid, starts, tokens, cotangent, norm_gain, w_bc, w_dt, taps, bias, dt_bias, a_log, d_skip, gate_gain, spread, w_zx, w_out):
    peers, widths = lax.axis_size("seq"), lax.axis_size("width")
    own, model = tokens.shape
    lanes = starts.shape[1]
    quarter = own // widths
    chans = w_out.shape[0]
    heads = chans // HEAD_DIM
    cols = 2 * chans + BLOCK + 2 * N
    dma = pltpu.SemaphoreType.DMA
    anywhere, vmem = pl.BlockSpec(memory_space=pl.ANY), pl.BlockSpec(memory_space=pltpu.VMEM)
    smem = pl.BlockSpec(memory_space=pltpu.SMEM)
    w_all = ((peers, widths, quarter, cols), bf16)
    rows_all = ((peers, own, model), bf16)
    part_all = ((peers // 2, own, model), bf16)
    starts_all = ((peers, SUB, BLOCK), f32)
    per_chan, low = ((peers, own, chans), f32), ((peers, own, chans), bf16)
    block = ((own, model), bf16)
    streamed = [
        ((own, cols), f32), ((own, chans), f32), ((own, chans), f32), ((own, 2 * N), bf16), ((own, 2 * BLOCK), f32),
        ((lanes, N, chans), f32), ((lanes, SUB, chans), f32),
    ]
    scale = ((peers, own, BLOCK), f32)
    of = lambda count, a: ((count,) + a[0], a[1])
    outs = [w_all, rows_all, rows_all, starts_all, ((SUB, chans), f32), ((SUB, BLOCK), f32), ((SUB, 2 * N), f32)]
    outs += [of(peers, streamed[0]), per_chan, per_chan, scale, *[((chans // widths, model), bf16)] * 4, block, block, block]
    outs += [of(peers, a) for a in streamed[2:]]
    scratch = [w_all, rows_all, starts_all, ((chans, model), bf16), ((own, model), bf16), ((own, model), bf16)]
    scratch += [((peers, own, BLOCK), bf16), ((SUB, BLOCK), f32), part_all, per_chan, per_chan, scale, low]
    scratch += [of(2, a) for a in streamed]
    scratch += [of(2, block)] * 3 + [((chans, model), f32)]
    scratch += [((2, peers * lanes, BLOCK), f32), ((2, peers - 1, peers * lanes, BLOCK), f32)]
    scratch += [((lanes, N, chans), f32), ((lanes, SUB, chans), f32), ((lanes, SUB, 2 * N), f32)]
    scratch += [((lanes, BLOCK + SUB, chans), f32), ((lanes, BLOCK + SUB, 2 * N), f32)]
    return pl.pallas_call(
        partial(front_kernel, peers=peers, widths=widths, lanes=lanes, heads=heads),
        in_specs=[smem] * 2 + [vmem] * 12 + [anywhere] * 2,
        out_specs=[anywhere] * 4 + [vmem] * 3 + [anywhere] * 16,
        out_shape=[jax.ShapeDtypeStruct(*a) for a in outs],
        scratch_shapes=[
            *[pltpu.VMEM(*a) for a in scratch],
            dma((4, peers - 1)), dma((4, peers - 1)), dma((peers - 1,)), dma((peers - 1,)),
            dma((5,)), dma((widths - 1,)), dma((widths - 1,)), dma((peers,)), dma((2, peers)), dma((6, 2)), dma((2,)),
            dma((peers // 2,)), dma((peers // 2,)), dma((3,)), *[dma((2, PARTS))] * 4,
            dma((2, peers - 1)), dma((2, peers - 1)),
            *row_sems(peers // 2), *row_sems(peers // 2),
        ],
        compiler_params=pltpu.CompilerParams(collective_id=1, has_side_effects=True, vmem_limit_bytes=62 << 20),
        name="front",
    )(valid, starts, tokens, cotangent, norm_gain, w_bc, w_dt, taps, bias, dt_bias, a_log, d_skip, gate_gain, spread, w_zx, w_out)


ROWS_AT_ONCE = 16


def add_into(dst, others, rows):
    @pl.loop(0, rows // ROWS_AT_ONCE)
    def _(i):
        at = pl.ds(pl.multiple_of(i * ROWS_AT_ONCE, ROWS_AT_ONCE), ROWS_AT_ONCE)
        value = dst[at].astype(f32)
        for other in others:
            value = value + other[at].astype(f32)
        dst[at] = value.astype(dst.dtype)


def bc_back(dbc, pre, par_ref, keep, keep_next):
    chans, times = pre.shape
    in_block = lax.rem(lax.broadcasted_iota(jnp.int32, (chans, times), 1), BLOCK)
    conv = jnp.broadcast_to(par_ref[:, BIAS : BIAS + 1], (chans, times))
    shifted = []
    for j in range(KCONV):
        moved = pre
        if j:
            moved = jnp.where(in_block >= j, pltpu.roll(pre, j, 1), keep * pltpu.roll(pre, BLOCK + j, 1))
        shifted.append(moved)
        conv = conv + moved * par_ref[:, KCONV - 1 - j : KCONV - j]
    act = sigmoid(conv)
    dconv = dbc * (act * (1.0 + conv * (1.0 - act)))
    dpre = dconv * par_ref[:, KCONV - 1 : KCONV]
    lane = lax.broadcasted_iota(jnp.int32, (chans, BLOCK), 1)
    dpar = jnp.where(lane == BIAS, jnp.sum(dconv, axis=1, keepdims=True), 0.0)
    for j in range(KCONV):
        dpar = dpar + jnp.where(lane == KCONV - 1 - j, jnp.sum(dconv * shifted[j], axis=1, keepdims=True), 0.0)
        if j:
            back = jnp.where(
                in_block < BLOCK - j, pltpu.roll(dconv, times - j, 1), keep_next * pltpu.roll(dconv, times - BLOCK - j, 1)
            )
            dpre = dpre + back * par_ref[:, KCONV - 1 - j : KCONV - j]
    return dpre, dpar


def scatter_kernel(
    valid_ref, got_ref, zx_ref, dzx_ref, w_ref, normed_ref, wide_ref, scale_ref, par_ref, start_ref, dchan_ref, dhead_ref,
    x_ref, branch_ref, above_ref, below_ref,
    output_ref, rows_ref, out_ref, out_third_ref,
    got_v, pre_v, dz_v, w_v, normed_v, third_t, third_g, par_t, rate_v,
    mine, to_mate, from_core, up, down, own0, own1, own2, got0, got1, got2, piece0, piece1, piece2,
    load_sem, core_send, core_recv, up_send, up_recv, down_send, down_recv,
    own_sem, q_send, q_recv, p_send, p_recv, o_send, o_recv,
    *, peers, widths, heads,
):
    width, place = lax.axis_index("width"), lax.axis_index("seq")
    chips = peers // 2
    chip, core = place // 2, lax.rem(place, 2)
    mate = (width, jnp.bitwise_xor(place, 1))
    ring = [lax.rem(place + by, peers) for by in range(1, peers)]
    cross = [jnp.bitwise_xor(width, m) for m in range(1, widths)]
    others = [(width, s) for s in ring] + [(w, place) for w in cross]
    greet(others)
    half = wide_ref.shape[3] // 2
    wide = 2 * half
    own = mine.shape[1]
    share, times = got_v.shape[1], got_v.shape[2]
    loads = [
        pltpu.make_async_copy(src, dst, load_sem.at[k])
        for k, (src, dst) in enumerate([
            (got_ref, got_v), (zx_ref.at[:, :, wide : wide + BLOCK], pre_v), (dzx_ref, dz_v), (w_ref, w_v), (normed_ref, normed_v),
            (scale_ref.at[place], rate_v),
        ])
    ]
    for load in loads:
        load.start()
    met(others)

    strip = third_g.shape[0] // widths
    lanes_of = lambda s: pl.ds(pl.multiple_of(s * own, BLOCK), own)
    strip_of = lambda w: pl.ds(pl.multiple_of(w * strip, 16), strip)
    sets = [
        (lambda w: wide_ref.at[:, w, :, 0:half], own0, got0, lambda s: own0.at[s], piece0, lambda w: out_ref.at[:, w, :, 0:half]),
        (lambda w: wide_ref.at[:, w, :, half:wide], own1, got1, lambda s: own1.at[s], piece1, lambda w: out_ref.at[:, w, :, half:wide]),
        (lambda w: third_g.at[strip_of(w)], own2, got2, lambda s: own2.at[:, lanes_of(s)], piece2, lambda w: out_third_ref.at[:, w]),
    ]
    own_in, to_width = [None] * 3, [None] * 3

    def begin(k):
        part, kept, arrived = sets[k][:3]
        own_in[k] = pltpu.make_async_copy(part(width), kept, own_sem.at[0, k])
        to_width[k] = [
            remote(part(w), arrived.at[m], q_send.at[k, m], q_recv.at[k, m], (w, place)) for m, w in enumerate(cross)
        ]
        for copy in [own_in[k]] + to_width[k]:
            copy.start()

    begin(0)
    begin(1)

    def flow(by):
        return (up, up_send, up_recv) if by > 0 else (down, down_send, down_recv)

    def sends(by, step):
        far = chips - step
        return chip + far < chips if by > 0 else chip >= far

    def later(by):
        return chip > 0 if by > 0 else chip + 1 < chips

    def hop(src, by, step, i):
        buffer, send, recv = flow(by)
        return remote(
            part_of(src, i), part_of(buffer.at[step - 1], i), send.at[step - 1, i], recv.at[step - 1, i],
            (width, jnp.clip(place + 2 * by, 0, peers - 1)),
        )

    def staged(by, step):
        return flow(by)[0].at[step - 2]

    def run_hops(step):
        for i in range(PARTS):
            for by in (1, -1):
                owner = jnp.clip(chip + by * (chips - step), 0, chips - 1)

                def direct():
                    hop(mine.at[owner], by, step, i).start()

                def relayed():
                    stage = staged(by, step)
                    hop(stage, by, step - 1, i).wait_recv()
                    add_into(part_of(stage, i), [part_of(mine.at[owner], i)], own // PARTS)
                    hop(stage, by, step, i).start()

                if step == 1:
                    pl.when(sends(by, step))(direct)
                else:
                    pl.when(sends(by, step) & jnp.logical_not(later(by)))(direct)
                    pl.when(sends(by, step) & later(by))(relayed)

    to_owner, to_all, kept_piece = [None] * 3, [None] * 3, [None] * 3

    def exchange(k):
        part, kept, arrived, piece_of, piece, out = sets[k]
        own_in[k].wait()
        for copy in to_width[k]:
            copy.wait_recv()
        if kept.ndim == 3:
            for s in range(peers):
                add_into(kept.at[s], [arrived.at[m, s] for m in range(widths - 1)], kept.shape[1])
        else:
            add_into(kept, [arrived.at[m] for m in range(widths - 1)], kept.shape[0])
        to_owner[k] = [
            remote(piece_of(s), piece.at[place], p_send.at[k, i], p_recv.at[k, i], (width, s)) for i, s in enumerate(ring)
        ]
        kept_piece[k] = pltpu.make_async_copy(piece_of(place), piece.at[place], own_sem.at[1, k])
        for copy in to_owner[k] + [kept_piece[k]]:
            copy.start()

    def spread(k):
        piece, out = sets[k][4:]
        for copy in to_owner[k]:
            copy.wait_recv()
        kept_piece[k].wait()
        to_all[k] = [remote(piece, out(width), o_send.at[k, m], o_recv.at[k, m], (w, place)) for m, w in enumerate(cross)]
        to_all[k].append(pltpu.make_async_copy(piece, out(width), own_sem.at[2, k]))
        for copy in to_all[k]:
            copy.start()

    for load in loads[:3]:
        load.wait()
    dbc = got_v[0].astype(f32)
    for s in range(1, peers):
        dbc = dbc + got_v[s].astype(f32)
    block_rows = pre_v.shape[1]
    spots = [(c, slice(l * BLOCK, (l + 1) * BLOCK)) for c in range(peers) for l in range(block_rows // BLOCK)]
    pre = jnp.concatenate([pre_v[c, at, :].T[heads : heads + share] for c, at in spots], axis=1)
    par = jnp.concatenate([par_ref[...], jnp.zeros((BLOCK - SUB, 2 * N), f32)], axis=0)
    for i in range(2 * N // BLOCK):
        par_t[i * BLOCK : (i + 1) * BLOCK, :] = par[:, i * BLOCK : (i + 1) * BLOCK].T
    keep = [1.0 - start_ref[c, l : l + 1, :] for c in range(peers) for l in range(block_rows // BLOCK)]
    keep_next = keep[block_rows // BLOCK :] + [jnp.zeros((1, BLOCK), f32)] * (block_rows // BLOCK)
    own_par = par_t.at[pl.ds(pl.multiple_of(place * share, SUB), share)]
    dpre, dpar = bc_back(dbc, pre, own_par, jnp.concatenate(keep, axis=1), jnp.concatenate(keep_next, axis=1))
    for i, (c, at) in enumerate(spots):
        tile = jnp.concatenate(
            [
                dz_v[c, at, wide:].astype(f32).T[:heads], dpre[:, i * BLOCK : (i + 1) * BLOCK],
                jnp.zeros((BLOCK - heads - share, BLOCK), f32),
            ],
            axis=0,
        )
        third_t[:, i * BLOCK : (i + 1) * BLOCK] = tile.astype(bf16)
        dz_v[c, at, wide:] = tile.T.astype(bf16)
    loads[3].wait()

    def partial_rows(s):
        weights = w_v[...].reshape(w_v.shape[0] * w_v.shape[1] * w_v.shape[2], w_v.shape[3])
        return mm(dz_v[s], weights[:, : wide + BLOCK], NT).astype(bf16)

    def order(i):
        return jnp.where(chip < chips // 2, chips - 1 - i, i)

    def over(q):
        return remote(to_mate.at[q], from_core.at[q], core_send.at[q], core_recv.at[q], mate)

    def whole_sum(q):
        over(q).wait_recv()
        add_into(mine.at[q], [from_core.at[q]], own)

    for i in range(chips):
        q = order(i)
        to_mate[q] = partial_rows(2 * q + 1 - core)
        over(q).start()
        mine[q] = partial_rows(2 * q + core)
        if i > 1:
            whole_sum(order(i - 1))
        if not i:
            whole_sum(q)
            run_hops(1)
    whole_sum(order(chips - 1))

    loads[4].wait()
    small_at = heads + share
    chans = dchan_ref.shape[1]
    more_rows = jnp.concatenate([dhead_ref[0:1], dhead_ref[1:2], jnp.zeros((1, chans - 2 * BLOCK), f32)], axis=1)
    small = jnp.concatenate([dchan_ref[: SUB - 1], more_rows], axis=0)
    small = jnp.concatenate([small[:, i : i + own] for i in range(0, chans, own)], axis=0)
    used = small_at + small.shape[0]
    par_rows = jnp.concatenate([dpar, jnp.zeros((BLOCK - share, BLOCK), f32)], axis=0).T[:SUB]
    par_rows = jnp.concatenate([par_rows, jnp.zeros((SUB, own - BLOCK), f32)], axis=1)
    grads = mm(third_t[...], normed_v[...].reshape(times, normed_v.shape[2]))
    tail = [jnp.zeros((third_g.shape[0] - used - SUB, third_g.shape[1]), f32)] if third_g.shape[0] > used + SUB else []
    third_g[...] = jnp.concatenate(
        [grads[:small_at], jnp.concatenate([small] * peers, axis=1), jnp.concatenate([par_rows] * peers, axis=1), *tail], axis=0
    ).astype(bf16)
    begin(2)

    exchange(0)
    if chips > 2:
        run_hops(2)
    spread(0)
    exchange(1)
    exchange(2)
    for step in range(3, chips):
        run_hops(step)
    spread(1)
    spread(2)

    for by in (1, -1):
        @pl.when(later(by))
        def _():
            buffer = flow(by)[0].at[chips - 2]
            for i in range(PARTS):
                hop(buffer, by, chips - 1, i).wait_recv()
                add_into(part_of(mine.at[chip], i), [part_of(buffer, i)], own // PARTS)

    rows_ref[...] = mine[chip]
    loads[5].wait()
    for lane in range(block_rows // BLOCK):
        @pl.loop(0, BLOCK // ROWS_AT_ONCE)
        def _(i):
            at = pl.ds(pl.multiple_of(lane * BLOCK + i * ROWS_AT_ONCE, ROWS_AT_ONCE), ROWS_AT_ONCE)
            row = lax.broadcasted_iota(jnp.int32, (ROWS_AT_ONCE, 1), 0) + i * ROWS_AT_ONCE
            mask = (row < valid_ref[0, lane]).astype(f32)
            branch = branch_ref[at, :].astype(f32) + above_ref[at, :].astype(f32) + below_ref[at, :].astype(f32)
            output_ref[at, :] = (x_ref[at, :].astype(f32) + mask * rate_v[at, 0:1] * branch).astype(bf16)

    for step in range(1, chips):
        for by in (1, -1):
            @pl.when(sends(by, step))
            def _():
                for i in range(PARTS):
                    hop(mine.at[0], by, step, i).wait_send()
    for q in range(chips):
        over(q).wait_send()
    for k in range(len(sets)):
        for copy in to_width[k] + to_owner[k]:
            copy.wait_send()
        for copy in to_all[k]:
            copy.wait()


def scattered_out(
    valid, got, zx, dzx, weights, normed, wide, scale, par, starts, dchan, dhead, x_rows, branch, above, below, heads
):
    peers, widths = lax.axis_size("seq"), lax.axis_size("width")
    chips = peers // 2
    dma = pltpu.SemaphoreType.DMA
    anywhere = pl.BlockSpec(memory_space=pl.ANY)
    vmem = pl.BlockSpec(memory_space=pltpu.VMEM)
    own, model = normed.shape[0] // peers, normed.shape[1]
    half = wide.shape[3] // 2
    small_rows = SUB * dchan.shape[1] // own
    strips = -(-(heads + got.shape[1] + small_rows + SUB) // (16 * widths)) * 16 * widths
    pieces = [(peers, wide.shape[2], half), (peers, wide.shape[2], half), (peers, strips // widths, own)]
    kept = pieces[:2] + [(strips // widths, model)]
    block = (own, model)
    zx, dzx, normed, scale = [a.reshape(peers, own, a.shape[1]) for a in (zx, dzx, normed, scale)]
    return pl.pallas_call(
        partial(scatter_kernel, peers=peers, widths=widths, heads=heads),
        in_specs=[pl.BlockSpec(memory_space=pltpu.SMEM)] + [anywhere] * 7 + [vmem] * 8,
        out_specs=[vmem, vmem, anywhere, anywhere],
        out_shape=[
            jax.ShapeDtypeStruct(block, bf16), jax.ShapeDtypeStruct(block, bf16), jax.ShapeDtypeStruct(wide.shape, bf16),
            jax.ShapeDtypeStruct((peers, widths, strips // widths, own), bf16),
        ],
        scratch_shapes=[
            pltpu.VMEM(got.shape, bf16), pltpu.VMEM((peers, own, BLOCK), f32), pltpu.VMEM(dzx.shape, bf16),
            pltpu.VMEM(weights.shape, bf16), pltpu.VMEM(normed.shape, bf16),
            pltpu.VMEM((BLOCK, peers * own), bf16), pltpu.VMEM((strips, model), bf16), pltpu.VMEM((2 * N, BLOCK), f32),
            pltpu.VMEM((own, BLOCK), f32),
            *[pltpu.VMEM((chips,) + block, bf16)] * 3, *[pltpu.VMEM((chips - 1,) + block, bf16)] * 2,
            *[pltpu.VMEM(a, bf16) for a in kept],
            *[pltpu.VMEM((widths - 1,) + a, bf16) for a in kept],
            *[pltpu.VMEM(a, bf16) for a in pieces],
            dma((6,)), dma((chips,)), dma((chips,)),
            *[dma((chips - 1, PARTS))] * 4,
            dma((3, 3)), dma((3, widths - 1)), dma((3, widths - 1)), dma((3, peers - 1)), dma((3, peers - 1)),
            dma((3, widths - 1)), dma((3, widths - 1)),
        ],
        compiler_params=pltpu.CompilerParams(collective_id=2, has_side_effects=True, vmem_limit_bytes=62 << 20),
        name="scatter_out",
    )(valid, got, zx, dzx, weights, normed, wide, scale, par, starts, dchan, dhead, x_rows, branch, above, below)


def laid_kernel(
    in_ref, third_ref, w_ref, bc_ref, dt_ref, rows_ref, x_ref, cot_ref, norm_gain_ref,
    out_ref, out_bc_ref, out_dt_ref, norm_ref, out_rows_ref, sums,
    *, heads, share,
):
    peers, rows, wide = in_ref.shape[0], in_ref.shape[2], in_ref.shape[3]
    chans = wide // 2
    step = pl.program_id(0)

    @pl.when(step == 0)
    def _():
        third = [
            jnp.concatenate([third_ref[s, q].astype(f32) for q in range(third_ref.shape[1])], axis=0) for s in range(peers)
        ]
        dt = jnp.concatenate([t[:heads] for t in third], axis=0)
        bc = jnp.concatenate([t[heads : heads + share] for t in third], axis=0)
        out_dt_ref[...] = dt
        out_bc_ref[...] = bc.T
        norm_ref[...] = jnp.sum(dt * dt_ref[...].astype(f32), axis=0, keepdims=True)
        norm_ref[...] += jnp.sum(bc * bc_ref[...].astype(f32).T, axis=0, keepdims=True)

    lane = jnp.zeros((rows, BLOCK), f32)
    for s in range(peers):
        for half in (0, 1):
            at = (half * peers + s) * chans
            value = in_ref[s, 0, :, half * chans : (half + 1) * chans].astype(f32)
            out_ref[:, at : at + chans] = value
            value = value * w_ref[:, at : at + chans].astype(f32)
            for j in range(chans // BLOCK):
                lane = lane + value[:, j * BLOCK : (j + 1) * BLOCK]
    x = x_ref[...].astype(f32)
    rate = lax.rsqrt(jnp.mean(x * x, axis=-1, keepdims=True) + epsilon)
    unit = x * rate
    pulled = rows_ref[...].astype(f32) * norm_gain_ref[...]
    inner = jnp.mean(pulled * unit, axis=-1, keepdims=True)
    out_rows_ref[...] = cot_ref[...].astype(f32) + rate * (pulled - unit * inner)
    sums[pl.ds(pl.multiple_of(step * rows, SUB), rows), :] = lane

    @pl.when(step == pl.num_programs(0) - 1)
    def _():
        own = sums.shape[0]
        gain = norm_gain_ref[:, pl.ds(pl.multiple_of(lax.axis_index("seq") * own, BLOCK), own)]
        by_row = [jnp.sum(sums[i : i + BLOCK, :].T, axis=0, keepdims=True) for i in range(0, own, BLOCK)]
        norm_ref[...] = (norm_ref[...] + jnp.concatenate(by_row, axis=1)) / gain


def laid_out(wide, third, w_zx, w_bc, w_dt, normed_grad, x_rows, cotangent, norm_gain, heads):
    peers, widths, quarter, cols = wide.shape
    rows = widths * quarter
    cut = quarter
    share = w_bc.shape[1] // peers
    by_rows = lambda a: pl.BlockSpec((cut, a.shape[1]), lambda i: (i, 0))
    whole = lambda a: pl.BlockSpec(a.shape, lambda i: (0,) * len(a.shape))
    by_piece = pl.BlockSpec((peers, 1, cut, cols), lambda i: (0, i, 0, 0))
    norm = jax.ShapeDtypeStruct((1, rows), f32)
    shapes = [jax.ShapeDtypeStruct(a.shape, f32) for a in (w_zx, w_bc, w_dt, norm, x_rows)]
    return pl.pallas_call(
        partial(laid_kernel, heads=heads, share=share),
        grid=(widths,),
        in_specs=[
            by_piece, whole(third), by_rows(w_zx), whole(w_bc), whole(w_dt),
            by_rows(normed_grad), by_rows(x_rows), by_rows(cotangent), whole(norm_gain),
        ],
        out_specs=[by_rows(w_zx), whole(w_bc), whole(w_dt), whole(norm), by_rows(x_rows)],
        out_shape=shapes,
        scratch_shapes=[pltpu.VMEM((rows, BLOCK), f32)],
        compiler_params=pltpu.CompilerParams(vmem_limit_bytes=62 << 20),
        name="lay_out",
    )(wide, third, w_zx, w_bc, w_dt, normed_grad, x_rows, cotangent, norm_gain)


def crossed(value, axis, mask):
    return lax.ppermute(value, axis, [(i, i ^ mask) for i in range(lax.axis_size(axis))])


def pick(value, index):
    return lax.dynamic_index_in_dim(value, index, 0, False)


def quarters_back(total):
    widths = lax.axis_size("width")
    return [total] + [crossed(total, "width", m) for m in range(1, widths)]


def quarters_joined(pieces):
    width = lax.axis_index("width")
    stacked = jnp.stack(pieces)
    whole = jnp.stack([pick(stacked, jnp.bitwise_xor(width, j)) for j in range(len(pieces))])
    return whole.reshape((-1,) + whole.shape[2:]).astype(f32)


def heads_body(
    tokens, cotangent, starts, valid, norm_gain, w_zx, w_bc, w_dt, conv_w, conv_b, dt_bias, a_log, d_skip, gate_gain, w_out
):
    peers = lax.axis_size("seq")
    widths = lax.axis_size("width")
    place = lax.axis_index("seq")
    lanes = starts.shape[1]
    heads = H // peers
    chans = heads * HEAD_DIM
    own, model = tokens.shape
    rows = own * peers
    first = place * heads
    share = 2 * N // peers
    used = heads + share
    spread = jnp.asarray(np.arange(chans)[None, :] // HEAD_DIM == np.arange(BLOCK)[:, None], bf16)
    weights, normed, bgrad, starts_all, chan, head, bc_par, *computed = front(
        valid, starts, tokens, cotangent, norm_gain[None], w_bc, w_dt.T, conv_w.T, conv_b[None], dt_bias[None], a_log[None],
        d_skip[None], gate_gain[None], spread, w_zx, w_out,
    )
    normed, bgrad = normed.reshape(rows, model), bgrad.reshape(rows, model)
    zx, mix, mixed_grad, scale = [a.reshape(rows, a.shape[-1]) for a in computed[:4]]
    out_parts = computed[4:8]
    up, down, branch = computed[8:11]
    conv, bc, steps = [a.reshape(rows, a.shape[-1]) for a in computed[11:14]]
    state, tail = computed[14:]
    above = lax.ppermute(up, "seq", [(i, i + 2) for i in range(peers - 2)])
    below = lax.ppermute(down, "seq", [(i + 2, i) for i in range(peers - 2)])
    out_quarters = [out_parts[0]] + [crossed(out_parts[m], "width", m) for m in range(1, widths)]
    dzx, dbc, dchan, dhead = run_backward(
        starts_all, zx, mixed_grad, chan, head, spread, conv, mix, bc, steps, state, tail, scale, lanes, heads
    )
    dzx, dbc, out_quarters = lax.optimization_barrier((dzx, dbc, out_quarters))
    out_pieces = quarters_back(sum(q.astype(f32) for q in out_quarters).astype(bf16))

    got = lax.all_to_all(dbc.reshape(peers, share, rows), "seq", 0, 0, tiled=True)

    wide = mm(normed, dzx[:, : 2 * chans], TN).astype(bf16)
    wide, out_pieces = lax.optimization_barrier((wide, out_pieces))
    out_grad = quarters_joined(out_pieces)
    got, out_grad = lax.optimization_barrier((got, out_grad))
    output, normed_grad, wide, third = scattered_out(
        valid, got, zx, dzx, weights, normed, wide.reshape(peers, widths, own // widths, -1), scale, bc_par, starts_all, dchan,
        dhead, tokens, branch, above, below, heads,
    )
    grad_zx, grad_bc, grad_dt, grad_norm, input_grad = laid_out(
        wide, third, w_zx, w_bc, w_dt.T, normed_grad, tokens, cotangent, norm_gain[None], heads
    )
    grad_dt = grad_dt.T
    grad_norm = grad_norm[0]
    third = third.reshape(peers, -1, own).astype(f32)
    small_rows = SUB * chans // own
    small = third[:, used : used + small_rows].reshape(peers, chans // own, SUB, own).transpose(2, 0, 1, 3).reshape(SUB, peers, chans)
    of_bc = third[:, used + small_rows : used + small_rows + KCONV + 1, :share].transpose(1, 0, 2).reshape(KCONV + 1, 2 * N)
    of_conv = jnp.concatenate([small[: KCONV + 1].reshape(KCONV + 1, E), of_bc], axis=1)
    mine = lambda a, axis: lax.dynamic_slice_in_dim(a, place * (a.shape[axis] // peers), a.shape[axis] // peers, axis)
    of_conv = mine(of_conv, 1)
    grad_taps, grad_bias = of_conv[:KCONV].T, of_conv[BIAS]
    kept = pick(small.transpose(1, 0, 2), place)
    grad_gain, grad_skip = kept[GAIN], jnp.sum(kept[SKIP].reshape(heads, HEAD_DIM), axis=1)
    grad_dtb, grad_alog = kept[SUB - 1, :heads], kept[SUB - 1, BLOCK : BLOCK + heads]
    return (
        output, input_grad, grad_norm, grad_zx, grad_bc, grad_dt, grad_taps, grad_bias, grad_dtb, grad_alog, grad_skip,
        grad_gain, out_grad,
    )


def passed_along(array, axis, by):
    peers = lax.axis_size(axis)
    pairs = [(i, i + by) for i in range(peers) if 0 <= i + by < peers]
    return lax.ppermute(array, axis, pairs)


def carried_in(part, axis, combine, identity, reverse):
    count = lax.axis_size(axis)
    place = lax.axis_index(axis)
    at = count - 1 - place if reverse else place
    by = -1 if reverse else 1
    state = jax.tree.map(lambda a, e: jnp.zeros_like(a) + jnp.asarray(e, a.dtype), part, identity)

    def one(lap, state):
        sent = combine(state, part)
        got = jax.tree.map(lambda a: passed_along(a, axis, by), sent)
        return jax.tree.map(lambda old, new: jnp.where(at == lap + 1, new, old), state, got)

    return lax.fori_loop(0, count - 1, one, state)


def round_value(v):
    return lax.optimization_barrier(v.astype(jnp.bfloat16)).astype(jnp.float32)


def keep_round(v):
    return (round_value(v), None)


def pass_grad(kept, grad):
    return (grad,)


def same_value(v):
    return v


def keep_same(v):
    return (v, None)


def round_grad(kept, grad):
    return (round_value(grad),)


def low(v):
    wrapped = jax.custom_vjp(round_value)
    wrapped.defvjp(keep_round, pass_grad)
    return wrapped(v)


def low_back(v):
    wrapped = jax.custom_vjp(same_value)
    wrapped.defvjp(keep_same, round_grad)
    return wrapped(v)


def rms_front(x_rows, norm_gain):
    mean_square = jnp.mean(x_rows * x_rows, axis=-1, keepdims=True)
    return x_rows * lax.rsqrt(mean_square + epsilon) * norm_gain


def rim_of(zx_pre, bc_pre, chan_mask):
    return jnp.concatenate(
        [zx_pre[:, BLOCK - KCONV + 1 :, E:] * chan_mask, bc_pre[:, BLOCK - KCONV + 1 :, :]], axis=-1
    )


def piece_front(
    zx_pre,
    bc_pre,
    dt_raw,
    rim_rows,
    conv_w,
    conv_b,
    dt_bias,
    a_log,
    chan_mask,
    head_mask,
    keep_rows,
):
    z_gate = zx_pre[..., :E] * chan_mask
    pre_conv = jnp.concatenate([zx_pre[..., E:] * chan_mask, bc_pre], axis=-1)
    padded = jnp.concatenate([rim_rows * keep_rows[:, None, None], pre_conv], axis=1)
    conv_out = conv_b + padded[:, 0:BLOCK, :] * conv_w[:, 0]
    for offset in range(1, KCONV):
        conv_out = conv_out + padded[:, offset : offset + BLOCK, :] * conv_w[:, offset]
    active = jax.nn.silu(conv_out)
    x_conv = low(active[..., :E] * chan_mask)
    b_conv = low(active[..., E : E + N])
    c_conv = low(active[..., E + N :])
    dt_step = jax.nn.softplus(dt_raw + dt_bias) * head_mask
    log_step = -jnp.exp(a_log) * dt_step
    return (z_gate, x_conv, b_conv, c_conv, dt_step, log_step)


def block_state(x_conv, b_conv, dt_step, log_step):
    cumulative = jnp.cumsum(log_step, axis=1)
    to_end = jnp.exp(cumulative[:, -1:, :] - cumulative) * dt_step
    weighted = low(x_conv.reshape(x_conv.shape[0], BLOCK, H, HEAD_DIM) * to_end[..., None])
    state_sum = jnp.einsum("lqhp,lqn->lhpn", weighted, b_conv, precision=highest)
    return (state_sum, cumulative[:, -1, :])


def piece_mix(
    z_gate, x_conv, b_conv, c_conv, dt_step, log_step, state_in, d_skip, gate_gain, chan_count
):
    lane_count = x_conv.shape[0]
    cumulative = jnp.cumsum(log_step, axis=1)
    cum_heads = jnp.swapaxes(cumulative, 1, 2)
    causal = jnp.arange(BLOCK)[:, None] >= jnp.arange(BLOCK)[None, :]
    spread = cum_heads[:, :, :, None] - cum_heads[:, :, None, :]
    decays = jnp.where(causal, jnp.exp(jnp.where(causal, spread, 0.0)), 0.0)
    inner_cb = jnp.einsum("lqn,lsn->lqs", c_conv, b_conv, precision=highest)
    scores = low(inner_cb[:, None] * decays * jnp.swapaxes(dt_step, 1, 2)[:, :, None, :])
    x_heads = x_conv.reshape(lane_count, BLOCK, H, HEAD_DIM)
    within = jnp.einsum("lhqs,lshp->lqhp", scores, x_heads, precision=highest)
    carried = (
        jnp.einsum("lqn,lhpn->lqhp", c_conv, state_in, precision=highest)
        * jnp.exp(cumulative)[..., None]
    )
    mixed_sum = low_back(within + carried) + d_skip[:, None] * x_heads
    gated_rows = mixed_sum.reshape(lane_count, BLOCK, E) * jax.nn.silu(z_gate)
    mean_square = jnp.sum(gated_rows * gated_rows, axis=-1, keepdims=True) / chan_count
    return low(gated_rows * lax.rsqrt(mean_square + epsilon) * gate_gain)


def mix_lanes(lane_inputs, d_skip, gate_gain, chan_count):

    def one_lane(pieces):
        lane_gate, lane_xconv, lane_bconv, lane_cconv, lane_step, lane_decay, lane_state = pieces
        return piece_mix(
            lane_gate[None],
            lane_xconv[None],
            lane_bconv[None],
            lane_cconv[None],
            lane_step[None],
            lane_decay[None],
            lane_state[None],
            d_skip,
            gate_gain,
            chan_count,
        )[0]

    return lax.map(one_lane, lane_inputs)


def mix_back_lanes(lane_inputs, mixed_grad, d_skip, gate_gain, chan_count):

    def lane_mix(z_gate, x_conv, b_conv, c_conv, dt_step, log_step, state_in, skip_coef, gain_coef):
        return piece_mix(
            z_gate[None],
            x_conv[None],
            b_conv[None],
            c_conv[None],
            dt_step[None],
            log_step[None],
            state_in[None],
            skip_coef,
            gain_coef,
            chan_count,
        )[0]

    def one_lane(pieces):
        (
            lane_gate,
            lane_xconv,
            lane_bconv,
            lane_cconv,
            lane_step,
            lane_decay,
            lane_state,
            lane_grad,
        ) = pieces
        unused, pull_lane = jax.vjp(
            lane_mix,
            lane_gate,
            lane_xconv,
            lane_bconv,
            lane_cconv,
            lane_step,
            lane_decay,
            lane_state,
            d_skip,
            gate_gain,
        )
        return pull_lane(lane_grad)

    lane_grads = lax.map(one_lane, lane_inputs + (mixed_grad,))
    return (lane_grads[:7], jnp.sum(lane_grads[7], axis=0), jnp.sum(lane_grads[8], axis=0))


def chain_combine(earlier, latter):
    return (earlier[0] * latter[0], latter[0][:, :, None, None] * earlier[1] + latter[1])


def share_out(out_grad):
    return lax.psum_scatter(out_grad, "seq", scatter_dimension=0, tiled=True)


def contract_rows(left, right):
    return lax.dot_general(
        left, right, (((0,), (0,)), ((), ())), preferred_element_type=jnp.float32
    )


def contract_cols(left, right):
    return lax.dot_general(
        left, right, (((1,), (1,)), ((), ())), preferred_element_type=jnp.float32
    )


def rows_body(
    tokens,
    cotangent,
    starts,
    valid,
    norm_gain,
    w_zx,
    w_bc,
    w_dt,
    conv_w,
    conv_b,
    dt_bias,
    a_log,
    d_skip,
    gate_gain,
    w_out,
):
    lane_count = starts.shape[1]
    width_index = lax.axis_index("width")
    shift_bits = lax.axis_size("width") - 1 - width_index
    active_heads = jnp.right_shift(jnp.int32(H), shift_bits)
    chan_mask = (jnp.arange(E) // HEAD_DIM < active_heads).astype(jnp.float32)
    head_mask = (jnp.arange(H) < active_heads).astype(jnp.float32)
    chan_count = (active_heads * HEAD_DIM).astype(jnp.float32)
    keep_rows = 1.0 - starts[0].astype(jnp.float32)
    row_mask = (jnp.arange(BLOCK)[None, :] < valid[0][:, None]).astype(jnp.float32).reshape(-1, 1)
    x_rows = tokens.astype(jnp.float32)
    normed, norm_back = jax.vjp(rms_front, x_rows, norm_gain)
    normed_low = normed.astype(jnp.bfloat16)
    zx_full, bc_full, dt_full, out_full = (
        lax.all_gather(w_zx, "seq", axis=0, tiled=True),
        lax.all_gather(w_bc, "seq", axis=0, tiled=True),
        lax.all_gather(w_dt, "seq", axis=0, tiled=True),
        lax.all_gather(w_out, "seq", axis=0, tiled=True),
    )
    zx_pre = jnp.dot(normed_low, zx_full, preferred_element_type=jnp.float32).reshape(
        lane_count, BLOCK, 2 * E
    )
    bc_pre = jnp.dot(normed_low, bc_full, preferred_element_type=jnp.float32).reshape(
        lane_count, BLOCK, 2 * N
    )
    dt_raw = jnp.dot(normed_low, dt_full, preferred_element_type=jnp.float32).reshape(
        lane_count, BLOCK, H
    )
    rim_rows = passed_along(rim_of(zx_pre, bc_pre, chan_mask), "seq", 1)
    front_fn = partial(piece_front, chan_mask=chan_mask, head_mask=head_mask, keep_rows=keep_rows)
    front_out, front_back = jax.vjp(
        front_fn, zx_pre, bc_pre, dt_raw, rim_rows, conv_w, conv_b, dt_bias, a_log
    )
    z_gate, x_conv, b_conv, c_conv, dt_step, log_step = front_out
    (state_sum, log_total), state_back = jax.vjp(block_state, x_conv, b_conv, dt_step, log_step)
    carry_rate = jnp.exp(log_total) * keep_rows[:, None]
    identity = (jnp.ones_like(carry_rate), jnp.zeros_like(state_sum))
    prefix_pair = carried_in((carry_rate, state_sum), "seq", chain_combine, identity, False)
    state_in = prefix_pair[1] * keep_rows[:, None, None, None]
    lane_inputs = (z_gate, x_conv, b_conv, c_conv, dt_step, log_step, state_in)
    mixed_low = mix_lanes(lane_inputs, d_skip, gate_gain, chan_count)
    mixed_flat = mixed_low.reshape(-1, E).astype(jnp.bfloat16)
    branch = jnp.dot(mixed_flat, out_full, preferred_element_type=jnp.float32)
    output = (x_rows + row_mask * branch).astype(jnp.bfloat16)
    cot_rows = cotangent.astype(jnp.float32)
    branch_grad = (cot_rows * row_mask).astype(jnp.bfloat16)
    out_grad = contract_rows(mixed_flat, branch_grad)
    mixed_grad = contract_cols(branch_grad, out_full).reshape(lane_count, BLOCK, E)
    lane_grads, grad_skip, grad_gain = mix_back_lanes(
        lane_inputs, mixed_grad, d_skip, gate_gain, chan_count
    )
    grad_gate, grad_x, grad_b, grad_c, grad_dt, grad_log, grad_state = lane_grads
    later_pair = carried_in(
        (carry_rate, grad_state * keep_rows[:, None, None, None]),
        "seq",
        chain_combine,
        identity,
        True,
    )
    later_grad = later_pair[1]
    grad_total = jnp.exp(log_total) * jnp.sum(later_grad * state_in, axis=(2, 3))
    grad_x_more, grad_b_more, grad_dt_more, grad_log_more = state_back((later_grad, grad_total))
    grad_zx, grad_bc, grad_dtraw, grad_rim, grad_convw, grad_convb, grad_dtbias, grad_alog = (
        front_back(
            (
                grad_gate,
                grad_x + grad_x_more,
                grad_b + grad_b_more,
                grad_c,
                grad_dt + grad_dt_more,
                grad_log + grad_log_more,
            )
        )
    )
    rim_grad = passed_along(grad_rim.astype(jnp.bfloat16), "seq", -1).astype(grad_rim.dtype)
    grad_zx = grad_zx.at[:, BLOCK - KCONV + 1 :, E:].add(rim_grad[..., :E] * chan_mask)
    grad_bc = grad_bc.at[:, BLOCK - KCONV + 1 :, :].add(rim_grad[..., E:])
    zx_low = grad_zx.reshape(-1, 2 * E).astype(jnp.bfloat16)
    bc_low = grad_bc.reshape(-1, 2 * N).astype(jnp.bfloat16)
    dt_low = grad_dtraw.reshape(-1, H).astype(jnp.bfloat16)
    zx_weight_grad = contract_rows(normed_low, zx_low)
    bc_weight_grad = contract_rows(normed_low, bc_low)
    dt_weight_grad = contract_rows(normed_low, dt_low)
    normed_grad = (
        contract_cols(zx_low, zx_full)
        + contract_cols(bc_low, bc_full)
        + contract_cols(dt_low, dt_full)
    )
    grad_x_rows, grad_norm = norm_back(normed_grad)
    input_grad = cot_rows + grad_x_rows
    out_shard = share_out(out_grad)
    row_shards = (
        lax.psum_scatter(grad_norm, "seq", scatter_dimension=0, tiled=True),
        lax.psum_scatter(zx_weight_grad, "seq", scatter_dimension=0, tiled=True),
        lax.psum_scatter(bc_weight_grad, "seq", scatter_dimension=0, tiled=True),
        lax.psum_scatter(dt_weight_grad, "seq", scatter_dimension=0, tiled=True),
        lax.psum_scatter(grad_convw, "seq", scatter_dimension=0, tiled=True),
        lax.psum_scatter(grad_convb, "seq", scatter_dimension=0, tiled=True),
        lax.psum_scatter(grad_dtbias, "seq", scatter_dimension=0, tiled=True),
        lax.psum_scatter(grad_alog, "seq", scatter_dimension=0, tiled=True),
        lax.psum_scatter(grad_skip, "seq", scatter_dimension=0, tiled=True),
        lax.psum_scatter(grad_gain, "seq", scatter_dimension=0, tiled=True),
    )
    summed = lax.psum(
        (
            row_shards[0],
            row_shards[1],
            row_shards[2],
            row_shards[3],
            row_shards[4],
            row_shards[5],
            row_shards[6],
            row_shards[7],
            row_shards[8],
            row_shards[9],
            out_shard,
        ),
        "width",
    )
    return (
        output,
        input_grad,
        summed[0],
        summed[1],
        summed[2],
        summed[3],
        summed[4],
        summed[5],
        summed[6],
        summed[7],
        summed[8],
        summed[9],
        summed[10],
    )


def solution(mesh):
    in_specs = (
        P(("width", "seq"), None),
        P(("width", "seq"), None),
        P(("width", "seq"), None),
        P(("width", "seq"), None),
        P(),
        P("seq", None),
        P("seq", None),
        P("seq", None),
        P(),
        P(),
        P(),
        P(),
        P(),
        P(),
        P("seq", None),
    )
    out_specs = (
        P(("width", "seq"), None),
        P(("width", "seq"), None),
        P("seq"),
        P("seq", None),
        P("seq", None),
        P("seq", None),
        P("seq", None),
        P("seq"),
        P("seq"),
        P("seq"),
        P("seq"),
        P("seq"),
        P("seq", None),
    )
    body = heads_body if H % (2 * mesh.shape["seq"]) == 0 else rows_body
    return jax.shard_map(body, mesh=mesh, in_specs=in_specs, out_specs=out_specs, check_vma=False)
```

```python
from functools import partial

import jax
import jax.numpy as jnp
from jax import lax
from jax.experimental import pallas as pl
from jax.experimental.pallas import tpu as pltpu
from jax.sharding import PartitionSpec as P
import numpy as np

H = 64
HEAD_DIM = 64
N = 128
KCONV = 4
BLOCK = 128
E = 4096
SUB = 8

epsilon = 1e-05
highest = lax.Precision.HIGHEST
f32 = jnp.float32
bf16 = jnp.bfloat16

NN = ((1,), (0,))
NT = ((1,), (1,))
TN = ((0,), (0,))


def mm(left, right, dims=NN, precision=None):
    return lax.dot_general(left, right, (dims, ((), ())), precision=precision, preferred_element_type=f32)


def split2(value):
    high = value.astype(bf16)
    return high, (value - high.astype(f32)).astype(bf16)


def mm_right(left, right, dims=NN):
    high, low = split2(right)
    return mm(left, high, dims) + mm(left, low, dims)


def mm_left(left, right, dims=NN):
    high, low = split2(left)
    return mm(high, right, dims) + mm(low, right, dims)


def softplus(v):
    small = jnp.exp(-jnp.abs(v))
    log1p = jnp.where(small < 1e-4, small - 0.5 * small * small, jnp.log(1.0 + small))
    return jnp.maximum(v, 0.0) + log1p


def sigmoid(v):
    return 0.5 + 0.5 * jnp.tanh(0.5 * v)


def grids():
    row = lax.broadcasted_iota(jnp.int32, (BLOCK, BLOCK), 0)
    col = lax.broadcasted_iota(jnp.int32, (BLOCK, BLOCK), 1)
    return row, col


def halves(pair, lane):
    zero = jnp.zeros_like(pair)
    return jnp.where(lane < HEAD_DIM, pair, zero), jnp.where(lane < HEAD_DIM, zero, pair)


def decay_of(cum, cum_t, head, causal):
    return jnp.exp(jnp.where(causal, cum[:, head : head + 1] - cum_t[head : head + 1, :], -1e30))


TAP, BIAS, SKIP, GAIN, MASK = 0, 4, 5, 6, 7
DT_BIAS, NEG_A, HEAD_MASK = 0, 1, 2


def forward_block(
    keep_row, zx_ref, chan_ref, bc_par_ref, head_ref, spread,
    conv_ref, mix_ref, bc_ref, step_ref, state_ref, tail_ref,
    state, tail_x, tail_b, pad_x, pad_b,
    *, lane, heads,
):
    width = heads * HEAD_DIM
    row, col = grids()
    causal = row >= col
    tril = causal.astype(f32)
    rows = pl.ds(lane * BLOCK, BLOCK)
    keep = jnp.concatenate([keep_row] * (width // BLOCK), axis=1)
    keep_b = jnp.concatenate([keep_row] * (2 * N // BLOCK), axis=1)

    pre = zx_ref[rows, width : 2 * width]
    before = tail_x[lane] * keep
    pad_x[lane, 0:SUB] = before
    pad_x[lane, SUB:] = pre
    tail_ref[lane] = before
    tail_x[lane] = pre[BLOCK - SUB :, :]
    conv = chan_ref[BIAS : BIAS + 1, :]
    for k in range(KCONV):
        conv = conv + pad_x[lane, SUB - KCONV + 1 + k : SUB - KCONV + 1 + k + BLOCK, :] * chan_ref[k : k + 1, :]
    conv_ref[rows, :] = conv
    x_low = (conv * sigmoid(conv) * chan_ref[MASK : MASK + 1, :]).astype(bf16)

    pre_b = zx_ref[rows, 2 * width + BLOCK :]
    pad_b[lane, 0:SUB] = tail_b[lane] * keep_b
    pad_b[lane, SUB:] = pre_b
    tail_b[lane] = pre_b[BLOCK - SUB :, :]
    conv_b = bc_par_ref[BIAS : BIAS + 1, :]
    for k in range(KCONV):
        conv_b = conv_b + pad_b[lane, SUB - KCONV + 1 + k : SUB - KCONV + 1 + k + BLOCK, :] * bc_par_ref[k : k + 1, :]
    bc_low = (conv_b * sigmoid(conv_b)).astype(bf16)
    bc_ref[rows, :] = bc_low
    b_low, c_low = bc_low[:, :N], bc_low[:, N:]

    raw = zx_ref[rows, 2 * width : 2 * width + BLOCK] + head_ref[DT_BIAS : DT_BIAS + 1, :]
    dt = softplus(raw) * head_ref[HEAD_MASK : HEAD_MASK + 1, :]
    cum = mm(tril, head_ref[NEG_A : NEG_A + 1, :] * dt, precision=highest)
    step_ref[rows, :BLOCK] = cum
    step_ref[rows, BLOCK:] = dt
    cum_t, dt_t = cum.T, dt.T
    last = cum[BLOCK - 1 :, :]
    carry_x = mm_left(jnp.exp(cum), spread)
    end_x = mm_left(jnp.exp(last - cum) * dt, spread)
    last_x = carry_x[BLOCK - 1 :, :]

    inner = mm(c_low, b_low, NT)
    parts = []
    for j in range(heads // 2):
        pair = x_low[:, 2 * HEAD_DIM * j : 2 * HEAD_DIM * (j + 1)]
        scores = [
            (inner * decay_of(cum, cum_t, h, causal) * dt_t[h : h + 1, :]).astype(bf16)
            for h in (2 * j, 2 * j + 1)
        ]
        parts.append(mm(jnp.concatenate(scores, axis=1), jnp.concatenate(halves(pair, col), axis=0)))
    within = jnp.concatenate(parts, axis=1)

    state_in = state[lane] * keep
    state_ref[lane] = state_in
    carried = mm_right(c_low, state_in) * carry_x
    x_f = x_low.astype(f32)
    mix_ref[rows, :] = within + carried + chan_ref[SKIP : SKIP + 1, :] * x_f
    weighted = (x_f * end_x).astype(bf16)
    state[lane] = last_x * state_in + mm(b_low, weighted, TN)


def backward_kernel(
    start_ref, zx_ref, grad_ref, chan_ref, head_ref, spread_ref,
    conv_ref, mix_ref, bc_ref, step_ref, state_ref, tail_ref, scale_ref,
    dzx_ref, dbc_ref, dchan_ref, dhead_ref,
    state_grad, next_conv, pad_x, pad_d,
    *, lanes, heads,
):
    lap = pl.program_id(0)
    width = heads * HEAD_DIM
    row, col = grids()
    causal = row >= col
    triu = (col >= row).astype(f32)
    spread = spread_ref[...]

    @pl.when(lap == 0)
    def _():
        state_grad[...] = jnp.zeros_like(state_grad)
        next_conv[...] = jnp.zeros_like(next_conv)
        dchan_ref[...] = jnp.zeros_like(dchan_ref)
        dhead_ref[...] = jnp.zeros_like(dhead_ref)

    def total(value):
        return jnp.sum(value, axis=0, keepdims=True)

    for lane in range(lanes):
        rows = pl.ds(lane * BLOCK, BLOCK)
        keep = 1.0 - jnp.concatenate([start_ref[0, lane : lane + 1, :]] * (width // BLOCK), axis=1)
        z = zx_ref[rows, :width]
        conv = conv_ref[rows, :]
        mixed = mix_ref[rows, :]
        grad = grad_ref[rows, :]
        gain = chan_ref[GAIN : GAIN + 1, :]
        skip = chan_ref[SKIP : SKIP + 1, :]
        rate = scale_ref[rows, 0:1]
        pull = scale_ref[rows, 1:2]
        gate = sigmoid(z)
        silu = z * gate
        gated = mixed * silu
        dgated = grad * gain * rate - gated * pull
        dzx_ref[rows, :width] = (dgated * mixed * (gate * (1.0 + z * (1.0 - gate)))).astype(bf16)
        dmixed = dgated * silu
        act = sigmoid(conv)
        x_low = (conv * act * chan_ref[MASK : MASK + 1, :]).astype(bf16)
        x_f = x_low.astype(f32)
        dchan_ref[GAIN : GAIN + 1, :] += total(grad * gated * rate)
        dchan_ref[SKIP : SKIP + 1, :] += total(dmixed * x_f)
        dlow = dmixed.astype(bf16)
        dlow_f = dlow.astype(f32)

        b_low, c_low = bc_ref[rows, :N], bc_ref[rows, N:]
        cum, dt = step_ref[rows, :BLOCK], step_ref[rows, BLOCK:]
        cum_t, dt_t = cum.T, dt.T
        last = cum[BLOCK - 1 :, :]
        to_last = jnp.exp(last - cum)
        carry_x = mm_left(jnp.exp(cum), spread)
        end_x = mm_left(to_last * dt, spread)
        last_x = carry_x[BLOCK - 1 :, :]

        inner = mm(c_low, b_low, NT)
        dinner = jnp.zeros((BLOCK, BLOCK), f32)
        parts, dt_rows = [], []
        for j in range(heads // 2):
            lanes_j = slice(2 * HEAD_DIM * j, 2 * HEAD_DIM * (j + 1))
            pair, dpair = x_low[:, lanes_j], dlow[:, lanes_j]
            dstack = jnp.concatenate(halves(dpair, col), axis=0)
            dscores = mm(dstack, pair, NT)
            scores = []
            for i, h in enumerate((2 * j, 2 * j + 1)):
                decay = decay_of(cum, cum_t, h, causal)
                step = dt_t[h : h + 1, :]
                scores.append((inner * decay * step).astype(bf16))
                part = dscores[i * BLOCK : (i + 1) * BLOCK] * decay
                dinner = dinner + part * step
                dt_rows.append(total(part * inner))
            parts.append(mm(jnp.concatenate(scores, axis=0), dstack, TN))
        dx_within = jnp.concatenate(parts, axis=1)
        dt_rows.append(jnp.zeros((BLOCK - heads, BLOCK), f32))
        ddt_within = jnp.concatenate(dt_rows, axis=0).T

        state_in = state_ref[0, lane]
        sgrad = state_grad[lane]
        in_high, in_low = split2(state_in)
        sg_high, sg_low = split2(sgrad)
        dcarry = dlow_f * carry_x
        dc_high, dc_low = split2(dcarry)
        di_high, di_low = split2(dinner)
        dc = mm(dc_high, in_high, NT) + mm(dc_high, in_low, NT) + mm(dc_low, in_high, NT)
        dc = dc + mm(di_high, b_low) + mm(di_low, b_low)
        weighted = (x_f * end_x).astype(bf16)
        db = mm(weighted, sg_high, NT) + mm(weighted, sg_low, NT)
        db = db + mm(di_high, c_low, TN) + mm(di_low, c_low, TN)
        dbc_ref[:N, rows] = db.T.astype(bf16)
        dbc_ref[N:, rows] = dc.T.astype(bf16)
        dweighted = mm(b_low, sg_high)
        dx = dx_within + dweighted * end_x
        dcum = mm_left(dlow_f * (mixed - skip * x_f) - x_f * dx, spread, NT)
        dend = mm((dweighted * x_f).astype(bf16), spread, NT)
        touch = jnp.broadcast_to(total(sgrad * state_in), (SUB, width))
        dlast = total(dend * to_last * dt) + jnp.exp(last) * mm_left(touch, spread, NT)[0:1]
        dlog = mm(triu, dcum, precision=highest) + dlast
        neg_a = head_ref[NEG_A : NEG_A + 1, :]
        ddt = ddt_within + dend * to_last + dlog * neg_a
        raw = zx_ref[rows, 2 * width : 2 * width + BLOCK] + head_ref[DT_BIAS : DT_BIAS + 1, :]
        draw = ddt * sigmoid(raw) * head_ref[HEAD_MASK : HEAD_MASK + 1, :]
        dzx_ref[rows, 2 * width :] = draw.astype(bf16)
        dhead_ref[0:1, :] += total(draw)
        dhead_ref[1:2, :] += total(dlog * neg_a * dt)
        state_grad[lane] = keep * (mm(c_low, dc_high, TN) + last_x * sgrad)

        dx = dx + skip * dmixed
        dconv = dx * chan_ref[MASK : MASK + 1, :] * (act * (1.0 + conv * (1.0 - act)))
        pad_d[lane, :BLOCK] = dconv
        pad_d[lane, BLOCK:] = next_conv[lane]
        next_conv[lane] = dconv[:SUB] * keep
        pad_x[lane, :SUB] = tail_ref[0, lane]
        pad_x[lane, SUB:] = zx_ref[rows, width : 2 * width]
        dpre = jnp.zeros((BLOCK, width), f32)
        for k in range(KCONV):
            dpre = dpre + pad_d[lane, KCONV - 1 - k : KCONV - 1 - k + BLOCK, :] * chan_ref[k : k + 1, :]
            dchan_ref[k : k + 1, :] += total(dconv * pad_x[lane, SUB - KCONV + 1 + k : SUB - KCONV + 1 + k + BLOCK, :])
        dchan_ref[BIAS : BIAS + 1, :] += total(dconv)
        dzx_ref[rows, width : 2 * width] = dpre.astype(bf16)


def run_backward(starts, zx, grad, chan, head, spread, conv, mix, bc, step_arr, state, tail, scale, lanes, heads):
    rows, width = grad.shape
    step = lanes * BLOCK
    blocks = rows // step
    by_block = lambda cols: pl.BlockSpec((step, cols), lambda c: (blocks - 1 - c, 0))
    whole = lambda a: pl.BlockSpec(a.shape, lambda c: (0,) * a.ndim)
    fixed = lambda shape: pl.BlockSpec(shape, lambda c: (0,) * len(shape))
    per_lane = lambda r, cols: pl.BlockSpec((1, lanes, r, cols), lambda c: (blocks - 1 - c, 0, 0, 0))
    return pl.pallas_call(
        partial(backward_kernel, lanes=lanes, heads=heads),
        grid=(blocks,),
        in_specs=[
            pl.BlockSpec((1, SUB, BLOCK), lambda c: (blocks - 1 - c, 0, 0)), by_block(2 * width + BLOCK), by_block(width),
            whole(chan), whole(head), whole(spread),
            by_block(width), by_block(width), by_block(2 * N), by_block(2 * BLOCK),
            per_lane(N, width), per_lane(SUB, width), by_block(BLOCK),
        ],
        out_specs=[
            by_block(2 * width + BLOCK), pl.BlockSpec((2 * N, step), lambda c: (0, blocks - 1 - c)),
            fixed((SUB, width)), fixed((SUB, BLOCK)),
        ],
        out_shape=[
            jax.ShapeDtypeStruct((rows, 2 * width + BLOCK), bf16),
            jax.ShapeDtypeStruct((2 * N, rows), bf16), jax.ShapeDtypeStruct((SUB, width), f32),
            jax.ShapeDtypeStruct((SUB, BLOCK), f32),
        ],
        scratch_shapes=[
            pltpu.VMEM((lanes, N, width), f32), pltpu.VMEM((lanes, SUB, width), f32),
            pltpu.VMEM((lanes, BLOCK + SUB, width), f32), pltpu.VMEM((lanes, BLOCK + SUB, width), f32),
        ],
        compiler_params=pltpu.CompilerParams(vmem_limit_bytes=62 << 20, dimension_semantics=("arbitrary",)),
        cost_estimate=pl.CostEstimate(flops=rows * width * 6144, bytes_accessed=rows * width * 40, transcendentals=rows * width * 6),
        name="mix_backward",
    )(starts, zx, grad, chan, head, spread, conv, mix, bc, step_arr, state, tail, scale)


MESH = pl.DeviceIdType.MESH


def greet(others):
    for other in others:
        pl.semaphore_signal(pltpu.get_barrier_semaphore(), inc=1, device_id=other, device_id_type=MESH)


def met(others):
    pl.semaphore_wait(pltpu.get_barrier_semaphore(), len(others))


def remote(src, dst, send, recv, device):
    return pltpu.make_async_remote_copy(
        src_ref=src, dst_ref=dst, send_sem=send, recv_sem=recv, device_id=device, device_id_type=MESH
    )


PARTS = 2


def part_of(ref, i):
    rows = ref.shape[0] // PARTS
    return ref.at[pl.ds(i * rows, rows)]


class Rows:
    def __init__(self, own_ref, all_ref, sems, peers):
        self.own, self.all, self.sems, self.peers = own_ref, all_ref, sems, peers
        self.width, self.place = lax.axis_index("width"), lax.axis_index("seq")
        self.chips, self.chip = peers // 2, self.place // 2

    def hop(self, ref, s, step, by, i):
        send, recv = self.sems[0 if by > 0 else 2], self.sems[1 if by > 0 else 3]
        device = (self.width, jnp.clip(self.place + 2 * by, 0, self.peers - 1))
        return remote(part_of(ref, i), part_of(self.all.at[s], i), send.at[step, i], recv.at[step, i], device)

    def over(self, ref, s, slot, i):
        device = (self.width, jnp.bitwise_xor(self.place, 1))
        send, recv = self.sems[4].at[slot, i], self.sems[5].at[slot, i]
        return remote(part_of(ref, i), part_of(self.all.at[s], i), send, recv, device)

    def inside(self, by):
        return self.chip + 1 < self.chips if by > 0 else self.chip > 0

    def reached(self, by, step):
        return self.chip >= step if by > 0 else self.chip + step < self.chips

    def source(self, by, step):
        return jnp.clip(self.place - 2 * by * step, 0, self.peers - 1)

    def keep(self):
        return pltpu.make_async_copy(self.own, self.all.at[self.place], self.sems[6])

    def start(self):
        for i in range(PARTS):
            for by in (1, -1):
                @pl.when(self.inside(by))
                def _():
                    self.hop(self.own, self.place, 0, by, i).start()
        self.keep().start()
        for copy in self.mate(1, 0):
            copy.start()

    def pass_on(self, step):
        for i in range(PARTS):
            for by in (1, -1):
                @pl.when(self.reached(by, step))
                def _():
                    s = self.source(by, step)
                    ref = self.all.at[s]
                    self.hop(ref, s, step - 1, by, i).wait_recv()

                    @pl.when(self.inside(by))
                    def _():
                        self.hop(ref, s, step, by, i).start()
                    self.over(ref, s, 2 * step - (by > 0), i).start()

    def mate(self, by, step):
        if not step:
            return [self.over(self.own, self.place, 0, i) for i in range(PARTS)]
        s = self.source(by, step)
        return [self.over(self.all.at[s], s, 2 * step - (by > 0), i) for i in range(PARTS)]

    def arrived(self):
        self.keep().wait()
        for copy in self.mate(1, 0):
            copy.wait_recv()
        for step in range(1, self.chips):
            for by in (1, -1):
                @pl.when(self.reached(by, step))
                def _():
                    for copy in self.mate(by, step):
                        copy.wait_recv()

    def sent(self):
        for step in range(self.chips):
            for by in (1, -1):
                @pl.when(self.inside(by) & self.reached(by, step))
                def _():
                    s = self.source(by, step)
                    for i in range(PARTS):
                        self.hop(self.all.at[s], s, step, by, i).wait_send()
        for copy in self.mate(1, 0):
            copy.wait_send()
        for step in range(1, self.chips):
            for by in (1, -1):
                @pl.when(self.reached(by, step))
                def _():
                    for copy in self.mate(by, step):
                        copy.wait_send()


ROW_SEMS = 7


def row_sems(chips):
    dma = pltpu.SemaphoreType.DMA
    return [dma((chips, PARTS))] * 4 + [dma((2 * chips, PARTS))] * 2 + [dma(())]


def front_kernel(
    valid_ref, start_ref, x_ref, cot_ref, norm_gain_ref, bc_ref, dt_ref, taps_ref, bias_ref, dtb_ref, alog_ref, skip_ref,
    gain_ref, spread_ref, zx_ref, wout_ref,
    w_ref, rows_ref, grads_ref, starts_ref, chan_ref, head_ref, bc_par,
    out_zx, out_mix, out_grad, out_scale, out_q0, out_q1, out_q2, out_q3, out_up, out_down, out_mine, out_conv, out_bc, out_step, out_state, out_tail,
    w_v, rows_v, starts_v, wout_v, own_v, grad_v, third_v, start_v, part_got,
    z_v, mix_v, scale_v, low_v, zx_v, mgrad_v, conv_v, bc_v, step_v, state_v, tail_v, bgrad_v, up, down, wout_grad, sums, sums_got,
    state, tail_x, tail_b, pad_x, pad_b,
    w_send, w_recv, st_send, st_recv, own_sem, wide_send, wide_recv, in_sem, out_sem, slot_sem, grad_sem, part_send, part_recv, branch_sem,
    up_send, up_recv, down_send, down_recv, sum_send, sum_recv, *sems,
    peers, widths, lanes, heads,
):
    width, place = lax.axis_index("width"), lax.axis_index("seq")
    chips = peers // 2
    chans = heads * HEAD_DIM
    quarter = zx_ref.shape[0] // widths
    ring = [lax.rem(place + by, peers) for by in range(1, peers)]
    cross = [jnp.bitwise_xor(width, m) for m in range(1, widths)]
    others = [(width, s) for s in ring] + [(w, place) for w in cross]
    greet(others)

    x = x_ref[...].astype(f32)
    own_v[...] = (x * lax.rsqrt(jnp.mean(x * x, axis=-1, keepdims=True) + epsilon) * norm_gain_ref[...]).astype(bf16)
    row = lax.broadcasted_iota(jnp.int32, (BLOCK, 1), 0)
    sub = lax.broadcasted_iota(jnp.int32, (SUB, BLOCK), 0)
    tile = jnp.zeros((SUB, BLOCK), f32)
    for lane in range(lanes):
        at = slice(lane * BLOCK, (lane + 1) * BLOCK)
        mask = (row < valid_ref[0, lane]).astype(f32)
        grad_v[at, :] = (cot_ref[at, :].astype(f32) * mask).astype(bf16)
        tile = jnp.where(sub == lane, start_ref[0, lane].astype(f32), tile)
    start_v[...] = tile
    bc, dt = bc_ref[...].astype(f32), dt_ref[...].astype(f32).T
    share = bc.shape[1] // peers
    rest = jnp.zeros((bc.shape[0], BLOCK - share - heads), f32)
    for s in range(peers):
        columns = [dt[:, s * heads : (s + 1) * heads], bc[:, s * share : (s + 1) * share], rest]
        third_v[s] = jnp.concatenate(columns, axis=1).astype(bf16)
    met(others)

    mine = pl.ds(pl.multiple_of(width * quarter, quarter), quarter)
    rows = Rows(own_v, rows_ref, sems[:ROW_SEMS], peers)
    grads = Rows(grad_v, grads_ref, sems[ROW_SEMS:], peers)

    def columns_of(half, s):
        return pl.ds(pl.multiple_of(half * peers * chans + s * chans, 128), chans)

    wide = 2 * chans
    spots = [pl.ds(0, chans), pl.ds(chans, chans), pl.ds(wide, BLOCK), pl.ds(wide + BLOCK, 2 * N)]

    def parts(s):
        return [zx_ref.at[mine, columns_of(0, s)], zx_ref.at[mine, columns_of(1, s)], third_v.at[s, mine], bc_ref.at[mine]]

    pushes = []
    for i, s in enumerate(ring):
        for k, (part, spot) in enumerate(zip(parts(s), spots)):
            pushes.append(remote(part, w_ref.at[place, width, :, spot], w_send.at[k, i], w_recv.at[k, i], (width, s)))
        pushes.append(remote(start_v, starts_ref.at[place], st_send.at[i], st_recv.at[i], (width, s)))
    for push in pushes:
        push.start()
    keeps = [
        pltpu.make_async_copy(part, w_ref.at[place, width, :, spot], own_sem.at[k])
        for k, (part, spot) in enumerate(zip(parts(place), spots))
    ]
    keeps.append(pltpu.make_async_copy(start_v, starts_ref.at[place], own_sem.at[4]))
    for keep in keeps:
        keep.start()
    rows.start()

    active = jnp.right_shift(jnp.int32(H), widths - 1 - width)
    first = place * heads
    here = columns_of(0, place)
    spread = spread_ref[...]
    pick_row = lax.broadcasted_iota(jnp.int32, (H, BLOCK), 0)
    pick_lane = lax.broadcasted_iota(jnp.int32, (H, BLOCK), 1)
    chosen = ((pick_row == pick_lane + first) & (pick_lane < heads)).astype(f32)
    per_head = jnp.concatenate(
        [dtb_ref[...], -jnp.exp(alog_ref[...]), jnp.ones((1, H), f32), skip_ref[...], jnp.zeros((SUB - 4, H), f32)], axis=0
    )
    per_head = mm(per_head, chosen, precision=highest)
    head_lane = lax.broadcasted_iota(jnp.int32, (SUB, BLOCK), 1)
    head_ref[...] = jnp.where((sub == HEAD_MASK) & (head_lane + first >= active), 0.0, per_head)
    on_chans = mm(head_ref[...], spread.astype(f32), precision=highest)
    chan_ref[...] = jnp.concatenate(
        [taps_ref[:, here], bias_ref[:, here], on_chans[3:4], gain_ref[:, here], on_chans[HEAD_MASK : HEAD_MASK + 1]], axis=0
    )
    bc_par[...] = jnp.concatenate(
        [taps_ref[:, E:], bias_ref[:, E:], jnp.zeros((SUB - KCONV - 1, 2 * N), f32)], axis=0
    )

    for push in pushes:
        push.wait_recv()
    for keep in keeps:
        keep.wait()
    shares = [
        remote(w_ref.at[:, width], w_ref.at[:, width], wide_send.at[m], wide_recv.at[m], (w, place)) for m, w in enumerate(cross)
    ]
    for copy in shares:
        copy.start()
    for step in range(1, chips - 1):
        rows.pass_on(step)
    grads.start()
    for copy in shares:
        copy.wait_recv()
    in_w = pltpu.make_async_copy(w_ref, w_v, own_sem.at[0])
    in_starts = pltpu.make_async_copy(starts_ref, starts_v, own_sem.at[1])
    in_wout = pltpu.make_async_copy(wout_ref, wout_v, own_sem.at[2])
    for copy in (in_w, in_starts, in_wout):
        copy.start()
    rows.pass_on(chips - 1)
    rows.arrived()

    def load(src, s):
        return pltpu.make_async_copy(src.at[s], rows_v.at[s], in_sem.at[s])

    for c in range(peers):
        load(rows_ref, c).start()
    for array in (state, tail_x, tail_b):
        array[...] = jnp.zeros_like(array)
    for copy in (in_w, in_starts, in_wout):
        copy.wait()

    def out_copy(k, src, dst, c):
        return pltpu.make_async_copy(src.at[c], dst.at[c], out_sem.at[k, c])

    slots = [
        (zx_v, out_zx), (conv_v, out_conv), (bc_v, out_bc), (step_v, out_step), (state_v, out_state), (tail_v, out_tail)
    ]

    def slot_copies(c):
        slot = lax.rem(c, 2)
        return [pltpu.make_async_copy(src.at[slot], dst.at[c], slot_sem.at[k, slot]) for k, (src, dst) in enumerate(slots)]

    def compute(begin, end):
        @pl.loop(begin, end)
        def _(c):
            load(rows_ref, c).wait()

            @pl.when(c >= 2)
            def _():
                for copy in slot_copies(c - 2):
                    copy.wait()
            weights = w_v[...].reshape(w_v.shape[0] * w_v.shape[1] * w_v.shape[2], w_v.shape[3])
            slot = lax.rem(c, 2)
            zx = mm(rows_v[c], weights)
            zx_v[slot] = zx
            z_v[c] = zx[:, :chans]
            for lane in range(lanes):
                forward_block(
                    1.0 - starts_v[c, lane : lane + 1, :], zx_v.at[slot], chan_ref, bc_par, head_ref, spread_ref[...],
                    conv_v.at[slot], mix_v.at[c], bc_v.at[slot], step_v.at[slot], state_v.at[slot], tail_v.at[slot],
                    state, tail_x, tail_b, pad_x, pad_b, lane=lane, heads=heads,
                )
            out_copy(0, mix_v, out_mix, c).start()
            for copy in slot_copies(c):
                copy.start()
            gated = gated_of(c)
            square = mm_right(jnp.ones((SUB, chans), bf16), gated * gated, NT)
            for lane in range(lanes):
                sums[0, pl.ds(c * lanes + lane, 1), :] = square[:1, lane * BLOCK : (lane + 1) * BLOCK]

    def gated_of(c):
        z = z_v[c]
        return mix_v[c] * (z * sigmoid(z))

    core = lax.rem(place, 2)

    def give(k):
        copies = [
            remote(sums.at[k], sums_got.at[k, i], sum_send.at[k, i], sum_recv.at[k, i], (width, s)) for i, s in enumerate(ring)
        ]
        for copy in copies:
            copy.start()
        return copies

    def whole(k, copies):
        total = sums[k]
        for i, copy in enumerate(copies):
            copy.wait_recv()
            total = total + sums_got[k, i]
        return total

    def by_time(value):
        return jnp.concatenate([value, jnp.zeros((BLOCK - lanes * peers, BLOCK), f32)], axis=0).T

    def load_grad(s, slot):
        return pltpu.make_async_copy(grads_ref.at[s], bgrad_v.at[slot], in_sem.at[slot])

    def grad_out(s, slot):
        return pltpu.make_async_copy(mgrad_v.at[slot], out_grad.at[s], grad_sem.at[slot])

    def mix_grads(q, first):
        for slot in range(2):
            load_grad(2 * q + slot, slot).start()
        for slot in range(2):
            s = 2 * q + slot
            load_grad(s, slot).wait()
            if not first:
                grad_out(s, slot).wait()
            grad = mm(bgrad_v[slot], wout_v[...], NT)
            mgrad_v[slot] = grad
            grad_out(s, slot).start()
            pulled = mm_right(jnp.ones((SUB, chans), bf16), grad * chan_ref[GAIN : GAIN + 1, :] * gated_of(s), NT)
            for lane in range(lanes):
                sums[1, pl.ds(s * lanes + lane, 1), :] = pulled[:1, lane * BLOCK : (lane + 1) * BLOCK]
        rows_q = low_v[pl.ds(2 * q, 2)].reshape(2 * low_v.shape[1], chans)
        both = bgrad_v[...].reshape(2 * bgrad_v.shape[1], bgrad_v.shape[2])
        part = mm(rows_q, both, TN)
        wout_grad[...] = part if first else wout_grad[...] + part

    def mine(q):
        return rows_v.at[2 * q + core]

    def part_over(q):
        return remote(
            rows_v.at[2 * q + 1 - core], part_got.at[q], part_send.at[q], part_recv.at[q], (width, jnp.bitwise_xor(place, 1))
        )

    def part_sum(q):
        part_over(q).wait_recv()
        add_into(mine(q), [part_got.at[q]], rows_v.shape[1])

    def sends(by, step):
        far = chips - step
        return unit_chip + far < chips if by > 0 else unit_chip >= far

    def later(by):
        return unit_chip > 0 if by > 0 else unit_chip + 1 < chips

    unit_chip = place // 2

    def branch_hop(src, by, step, i):
        buffer, send, recv = (up, up_send, up_recv) if by > 0 else (down, down_send, down_recv)
        return remote(
            part_of(src, i), part_of(buffer.at[step - 1], i), send.at[step - 1, i], recv.at[step - 1, i],
            (width, jnp.clip(place + 2 * by, 0, peers - 1)),
        )

    def branch_stage(by, step):
        return (up if by > 0 else down).at[step - 2]

    def branch_hops(step):
        for i in range(PARTS):
            for by in (1, -1):
                owner = jnp.clip(unit_chip + by * (chips - step), 0, chips - 1)
                last = step == chips - 1

                def direct():
                    branch_hop(mine(owner), by, step, i).start()

                def relayed():
                    stage = branch_stage(by, step)
                    branch_hop(stage, by, step - 1, i).wait_recv()
                    add_into(part_of(stage, i), [part_of(mine(owner), i)], rows_v.shape[1] // PARTS)
                    if not last:
                        branch_hop(stage, by, step, i).start()

                if step == 1:
                    pl.when(sends(by, step))(direct)
                    continue
                if not last:
                    pl.when(sends(by, step) & jnp.logical_not(later(by)))(direct)
                pl.when(sends(by, step) & later(by))(relayed)

    def branch_out(k, src):
        return pltpu.make_async_copy(src, (out_mine, out_up, out_down)[k], branch_sem.at[k])

    def branch_outs(act):
        act(branch_out(0, mine(unit_chip)))
        for k, by in ((1, 1), (2, -1)):
            owner = jnp.clip(unit_chip + by, 0, chips - 1)

            @pl.when(later(by))
            def _():
                act(branch_out(k, branch_stage(by, chips - 1)))

            @pl.when(jnp.logical_not(later(by)))
            def _():
                act(branch_out(k, mine(owner)))

    compute(0, peers)
    squares = give(0)
    grads.pass_on(1)

    def mates_here(step):
        if not step:
            for copy in grads.mate(1, 0):
                copy.wait_recv()
        for by in (1, -1):
            if step:
                @pl.when(grads.reached(by, step))
                def _():
                    for copy in grads.mate(by, step):
                        copy.wait_recv()

    def at_distance(step):
        for by in (1, -1):
            @pl.when(grads.reached(by, step))
            def _():
                mix_grads(grads.source(by, step) // 2, False)

    @pl.loop(0, chips)
    def _(i):
        q = jnp.where(unit_chip < chips // 2, chips - 1 - i, i)
        for c in (2 * q + 1 - core, 2 * q + core):
            low = (gated_of(c) * chan_ref[GAIN : GAIN + 1, :]).astype(bf16)
            rows_v[c] = mm(low, wout_v[...]).astype(bf16)
        part_over(q).start()

    for q in range(chips):
        part_sum(q)
    branch_hops(1)
    count = (active * HEAD_DIM).astype(f32)
    rate = lax.rsqrt(whole(0, squares) / count + epsilon)
    rate_t = by_time(rate)
    lane_at = lax.broadcasted_iota(jnp.int32, (BLOCK, BLOCK), 1)
    spots_of = [(c, slice(lane * BLOCK, (lane + 1) * BLOCK)) for c in range(peers) for lane in range(lanes)]
    for i, (c, at) in enumerate(spots_of):
        scale_v[c, at, :] = jnp.where(lane_at == 0, rate_t[:, i : i + 1], 0.0)

    @pl.loop(0, peers)
    def _(c):
        low_v[c] = (gated_of(c) * scale_v[c, :, 0:1] * chan_ref[GAIN : GAIN + 1, :]).astype(bf16)

    grads.pass_on(2)
    grads.keep().wait()
    mates_here(0)
    mix_grads(unit_chip, True)
    mates_here(1)
    at_distance(1)
    for step in range(2, chips - 1):
        branch_hops(step)
        mates_here(step)
        at_distance(step)
    grads.pass_on(chips - 1)
    mates_here(chips - 1)
    at_distance(chips - 1)
    crosses = give(1)
    bgrad_v[...] = wout_grad[...].astype(bf16).reshape(bgrad_v.shape)
    wout_rows = chans // widths
    per_block = bgrad_v.shape[1] // wout_rows

    def wout_quarter(m):
        j = jnp.bitwise_xor(width, m)
        rows_j = pl.ds(pl.multiple_of(lax.rem(j, per_block) * wout_rows, 16), wout_rows)
        return bgrad_v.at[j // per_block, rows_j]

    wout_out = [
        pltpu.make_async_copy(wout_quarter(m), dst, own_sem.at[m]) for m, dst in enumerate((out_q0, out_q1, out_q2, out_q3))
    ]
    for copy in wout_out:
        copy.start()
    branch_hops(chips - 1)
    branch_outs(lambda copy: copy.start())
    pull_t = by_time(rate * rate * rate * whole(1, crosses) / count)
    for i, (c, at) in enumerate(spots_of):
        scale_v[c, at, :] = jnp.where(lane_at == 1, pull_t[:, i : i + 1], scale_v[c, at, :])
    for c in range(peers):
        out_copy(1, scale_v, out_scale, c).start()

    for copy in shares + pushes + squares + crosses:
        copy.wait_send()
    rows.sent()
    grads.sent()
    for c in (peers - 2, peers - 1):
        for copy in slot_copies(c):
            copy.wait()

    @pl.loop(0, peers)
    def _(c):
        for k, (src, dst) in enumerate([(mix_v, out_mix), (scale_v, out_scale)]):
            out_copy(k, src, dst, c).wait()

    for q in range(chips):
        part_over(q).wait_send()
    for step in range(1, chips - 1):
        for by in (1, -1):
            @pl.when(sends(by, step))
            def _():
                for i in range(PARTS):
                    branch_hop(mine(0), by, step, i).wait_send()
    for slot in range(2):
        grad_out(slot, slot).wait()
    for copy in wout_out:
        copy.wait()
    branch_outs(lambda copy: copy.wait())


def front(valid, starts, tokens, cotangent, norm_gain, w_bc, w_dt, taps, bias, dt_bias, a_log, d_skip, gate_gain, spread, w_zx, w_out):
    peers, widths = lax.axis_size("seq"), lax.axis_size("width")
    own, model = tokens.shape
    lanes = starts.shape[1]
    quarter = own // widths
    chans = w_out.shape[0]
    heads = chans // HEAD_DIM
    cols = 2 * chans + BLOCK + 2 * N
    dma = pltpu.SemaphoreType.DMA
    anywhere, vmem = pl.BlockSpec(memory_space=pl.ANY), pl.BlockSpec(memory_space=pltpu.VMEM)
    smem = pl.BlockSpec(memory_space=pltpu.SMEM)
    w_all = ((peers, widths, quarter, cols), bf16)
    rows_all = ((peers, own, model), bf16)
    part_all = ((peers // 2, own, model), bf16)
    starts_all = ((peers, SUB, BLOCK), f32)
    per_chan, low = ((peers, own, chans), f32), ((peers, own, chans), bf16)
    block = ((own, model), bf16)
    streamed = [
        ((own, cols), f32), ((own, chans), f32), ((own, chans), f32), ((own, 2 * N), bf16), ((own, 2 * BLOCK), f32),
        ((lanes, N, chans), f32), ((lanes, SUB, chans), f32),
    ]
    scale = ((peers, own, BLOCK), f32)
    of = lambda count, a: ((count,) + a[0], a[1])
    outs = [w_all, rows_all, rows_all, starts_all, ((SUB, chans), f32), ((SUB, BLOCK), f32), ((SUB, 2 * N), f32)]
    outs += [of(peers, streamed[0]), per_chan, per_chan, scale, *[((chans // widths, model), bf16)] * 4, block, block, block]
    outs += [of(peers, a) for a in streamed[2:]]
    scratch = [w_all, rows_all, starts_all, ((chans, model), bf16), ((own, model), bf16), ((own, model), bf16)]
    scratch += [((peers, own, BLOCK), bf16), ((SUB, BLOCK), f32), part_all, per_chan, per_chan, scale, low]
    scratch += [of(2, a) for a in streamed]
    scratch += [of(2, block)] * 3 + [((chans, model), f32)]
    scratch += [((2, peers * lanes, BLOCK), f32), ((2, peers - 1, peers * lanes, BLOCK), f32)]
    scratch += [((lanes, N, chans), f32), ((lanes, SUB, chans), f32), ((lanes, SUB, 2 * N), f32)]
    scratch += [((lanes, BLOCK + SUB, chans), f32), ((lanes, BLOCK + SUB, 2 * N), f32)]
    return pl.pallas_call(
        partial(front_kernel, peers=peers, widths=widths, lanes=lanes, heads=heads),
        in_specs=[smem] * 2 + [vmem] * 12 + [anywhere] * 2,
        out_specs=[anywhere] * 4 + [vmem] * 3 + [anywhere] * 16,
        out_shape=[jax.ShapeDtypeStruct(*a) for a in outs],
        scratch_shapes=[
            *[pltpu.VMEM(*a) for a in scratch],
            dma((4, peers - 1)), dma((4, peers - 1)), dma((peers - 1,)), dma((peers - 1,)),
            dma((5,)), dma((widths - 1,)), dma((widths - 1,)), dma((peers,)), dma((2, peers)), dma((6, 2)), dma((2,)),
            dma((peers // 2,)), dma((peers // 2,)), dma((3,)), *[dma((2, PARTS))] * 4,
            dma((2, peers - 1)), dma((2, peers - 1)),
            *row_sems(peers // 2), *row_sems(peers // 2),
        ],
        compiler_params=pltpu.CompilerParams(collective_id=1, has_side_effects=True, vmem_limit_bytes=62 << 20),
        name="front",
    )(valid, starts, tokens, cotangent, norm_gain, w_bc, w_dt, taps, bias, dt_bias, a_log, d_skip, gate_gain, spread, w_zx, w_out)


ROWS_AT_ONCE = 16


def add_into(dst, others, rows):
    @pl.loop(0, rows // ROWS_AT_ONCE)
    def _(i):
        at = pl.ds(pl.multiple_of(i * ROWS_AT_ONCE, ROWS_AT_ONCE), ROWS_AT_ONCE)
        value = dst[at].astype(f32)
        for other in others:
            value = value + other[at].astype(f32)
        dst[at] = value.astype(dst.dtype)


def bc_back(dbc, pre, par_ref, keep, keep_next):
    chans, times = pre.shape
    in_block = lax.rem(lax.broadcasted_iota(jnp.int32, (chans, times), 1), BLOCK)
    conv = jnp.broadcast_to(par_ref[:, BIAS : BIAS + 1], (chans, times))
    shifted = []
    for j in range(KCONV):
        moved = pre
        if j:
            moved = jnp.where(in_block >= j, pltpu.roll(pre, j, 1), keep * pltpu.roll(pre, BLOCK + j, 1))
        shifted.append(moved)
        conv = conv + moved * par_ref[:, KCONV - 1 - j : KCONV - j]
    act = sigmoid(conv)
    dconv = dbc * (act * (1.0 + conv * (1.0 - act)))
    dpre = dconv * par_ref[:, KCONV - 1 : KCONV]
    lane = lax.broadcasted_iota(jnp.int32, (chans, BLOCK), 1)
    dpar = jnp.where(lane == BIAS, jnp.sum(dconv, axis=1, keepdims=True), 0.0)
    for j in range(KCONV):
        dpar = dpar + jnp.where(lane == KCONV - 1 - j, jnp.sum(dconv * shifted[j], axis=1, keepdims=True), 0.0)
        if j:
            back = jnp.where(
                in_block < BLOCK - j, pltpu.roll(dconv, times - j, 1), keep_next * pltpu.roll(dconv, times - BLOCK - j, 1)
            )
            dpre = dpre + back * par_ref[:, KCONV - 1 - j : KCONV - j]
    return dpre, dpar


def scatter_kernel(
    valid_ref, got_ref, zx_ref, dzx_ref, w_ref, normed_ref, wide_ref, scale_ref, par_ref, start_ref, dchan_ref, dhead_ref,
    x_ref, branch_ref, above_ref, below_ref,
    output_ref, rows_ref, out_ref, out_third_ref,
    got_v, pre_v, dz_v, w_v, normed_v, third_t, third_g, par_t, rate_v,
    mine, to_mate, from_core, up, down, own0, own1, own2, got0, got1, got2, piece0, piece1, piece2,
    load_sem, core_send, core_recv, up_send, up_recv, down_send, down_recv,
    own_sem, q_send, q_recv, p_send, p_recv, o_send, o_recv,
    *, peers, widths, heads,
):
    width, place = lax.axis_index("width"), lax.axis_index("seq")
    chips = peers // 2
    chip, core = place // 2, lax.rem(place, 2)
    mate = (width, jnp.bitwise_xor(place, 1))
    ring = [lax.rem(place + by, peers) for by in range(1, peers)]
    cross = [jnp.bitwise_xor(width, m) for m in range(1, widths)]
    others = [(width, s) for s in ring] + [(w, place) for w in cross]
    greet(others)
    half = wide_ref.shape[3] // 2
    wide = 2 * half
    own = mine.shape[1]
    share, times = got_v.shape[1], got_v.shape[2]
    loads = [
        pltpu.make_async_copy(src, dst, load_sem.at[k])
        for k, (src, dst) in enumerate([
            (got_ref, got_v), (zx_ref.at[:, :, wide : wide + BLOCK], pre_v), (dzx_ref, dz_v), (w_ref, w_v), (normed_ref, normed_v),
            (scale_ref.at[place], rate_v),
        ])
    ]
    for load in loads:
        load.start()
    met(others)

    strip = third_g.shape[0] // widths
    lanes_of = lambda s: pl.ds(pl.multiple_of(s * own, BLOCK), own)
    strip_of = lambda w: pl.ds(pl.multiple_of(w * strip, 16), strip)
    sets = [
        (lambda w: wide_ref.at[:, w, :, 0:half], own0, got0, lambda s: own0.at[s], piece0,
         lambda w, at: out_ref.at[at, w, :, 0:half]),
        (lambda w: wide_ref.at[:, w, :, half:wide], own1, got1, lambda s: own1.at[s], piece1,
         lambda w, at: out_ref.at[at, w, :, half:wide]),
        (lambda w: third_g.at[strip_of(w)], own2, got2, lambda s: own2.at[:, lanes_of(s)], piece2,
         lambda w, at: out_third_ref.at[at, w]),
    ]
    own_in, to_width = [None] * 3, [None] * 3

    def begin(k):
        part, kept, arrived = sets[k][:3]
        own_in[k] = pltpu.make_async_copy(part(width), kept, own_sem.at[0, k])
        to_width[k] = [
            remote(part(w), arrived.at[m], q_send.at[k, m], q_recv.at[k, m], (w, place)) for m, w in enumerate(cross)
        ]
        for copy in [own_in[k]] + to_width[k]:
            copy.start()

    begin(0)
    begin(1)

    def flow(by):
        return (up, up_send, up_recv) if by > 0 else (down, down_send, down_recv)

    def sends(by, step):
        far = chips - step
        return chip + far < chips if by > 0 else chip >= far

    def later(by):
        return chip > 0 if by > 0 else chip + 1 < chips

    def hop(src, by, step, i):
        buffer, send, recv = flow(by)
        return remote(
            part_of(src, i), part_of(buffer.at[step - 1], i), send.at[step - 1, i], recv.at[step - 1, i],
            (width, jnp.clip(place + 2 * by, 0, peers - 1)),
        )

    def staged(by, step):
        return flow(by)[0].at[step - 2]

    def run_hops(step):
        for i in range(PARTS):
            for by in (1, -1):
                owner = jnp.clip(chip + by * (chips - step), 0, chips - 1)

                def direct():
                    hop(mine.at[owner], by, step, i).start()

                def relayed():
                    stage = staged(by, step)
                    hop(stage, by, step - 1, i).wait_recv()
                    add_into(part_of(stage, i), [part_of(mine.at[owner], i)], own // PARTS)
                    hop(stage, by, step, i).start()

                if step == 1:
                    pl.when(sends(by, step))(direct)
                else:
                    pl.when(sends(by, step) & jnp.logical_not(later(by)))(direct)
                    pl.when(sends(by, step) & later(by))(relayed)

    to_owner, to_all, kept_piece = [None] * 3, [None] * 3, [None] * 3

    def exchange(k):
        part, kept, arrived, piece_of, piece, out = sets[k]
        own_in[k].wait()
        for copy in to_width[k]:
            copy.wait_recv()
        if kept.ndim == 3:
            for s in range(peers):
                add_into(kept.at[s], [arrived.at[m, s] for m in range(widths - 1)], kept.shape[1])
        else:
            add_into(kept, [arrived.at[m] for m in range(widths - 1)], kept.shape[0])
        to_owner[k] = [
            remote(piece_of(s), piece.at[place], p_send.at[k, i], p_recv.at[k, i], (width, s)) for i, s in enumerate(ring)
        ]
        kept_piece[k] = pltpu.make_async_copy(piece_of(place), piece.at[place], own_sem.at[1, k])
        for copy in to_owner[k] + [kept_piece[k]]:
            copy.start()

    everything, relays = pl.ds(0, peers), [None] * 3
    over_x, over_y = jnp.bitwise_xor(width, 1), jnp.bitwise_xor(width, 2)

    def spread(k):
        piece, out = sets[k][4:]
        for copy in to_owner[k]:
            copy.wait_recv()
        kept_piece[k].wait()
        to_all[k] = [
            remote(piece, out(width, everything), o_send.at[k, i], o_recv.at[k, i], (w, place)) for i, w in enumerate((over_x, over_y))
        ]
        to_all[k].append(pltpu.make_async_copy(piece, out(width, everything), own_sem.at[2, k]))
        for copy in to_all[k]:
            copy.start()

    def relay(k):
        out = sets[k][5]
        relays[k] = []
        for i, (origin, target) in enumerate(((over_x, over_y), (over_y, over_x))):
            to_all[k][i].wait_recv()
            rows = out(origin, pl.ds(i * peers // 2, peers // 2))
            relays[k].append(remote(rows, rows, o_send.at[k, 2 + i], o_recv.at[k, 2 + i], (target, place)))
            relays[k][i].start()

    for load in loads[:3]:
        load.wait()
    dbc = got_v[0].astype(f32)
    for s in range(1, peers):
        dbc = dbc + got_v[s].astype(f32)
    block_rows = pre_v.shape[1]
    spots = [(c, slice(l * BLOCK, (l + 1) * BLOCK)) for c in range(peers) for l in range(block_rows // BLOCK)]
    pre = jnp.concatenate([pre_v[c, at, :].T[heads : heads + share] for c, at in spots], axis=1)
    par = jnp.concatenate([par_ref[...], jnp.zeros((BLOCK - SUB, 2 * N), f32)], axis=0)
    for i in range(2 * N // BLOCK):
        par_t[i * BLOCK : (i + 1) * BLOCK, :] = par[:, i * BLOCK : (i + 1) * BLOCK].T
    keep = [1.0 - start_ref[c, l : l + 1, :] for c in range(peers) for l in range(block_rows // BLOCK)]
    keep_next = keep[block_rows // BLOCK :] + [jnp.zeros((1, BLOCK), f32)] * (block_rows // BLOCK)
    own_par = par_t.at[pl.ds(pl.multiple_of(place * share, SUB), share)]
    dpre, dpar = bc_back(dbc, pre, own_par, jnp.concatenate(keep, axis=1), jnp.concatenate(keep_next, axis=1))
    for i, (c, at) in enumerate(spots):
        tile = jnp.concatenate(
            [
                dz_v[c, at, wide:].astype(f32).T[:heads], dpre[:, i * BLOCK : (i + 1) * BLOCK],
                jnp.zeros((BLOCK - heads - share, BLOCK), f32),
            ],
            axis=0,
        )
        third_t[:, i * BLOCK : (i + 1) * BLOCK] = tile.astype(bf16)
        dz_v[c, at, wide:] = tile.T.astype(bf16)
    loads[3].wait()

    def partial_rows(s):
        weights = w_v[...].reshape(w_v.shape[0] * w_v.shape[1] * w_v.shape[2], w_v.shape[3])
        return mm(dz_v[s], weights[:, : wide + BLOCK], NT).astype(bf16)

    def order(i):
        return jnp.where(chip < chips // 2, chips - 1 - i, i)

    def over(q):
        return remote(to_mate.at[q], from_core.at[q], core_send.at[q], core_recv.at[q], mate)

    def whole_sum(q):
        over(q).wait_recv()
        add_into(mine.at[q], [from_core.at[q]], own)

    for i in range(chips):
        q = order(i)
        to_mate[q] = partial_rows(2 * q + 1 - core)
        over(q).start()
        mine[q] = partial_rows(2 * q + core)
        if i > 1:
            whole_sum(order(i - 1))
        if not i:
            whole_sum(q)
            run_hops(1)
    whole_sum(order(chips - 1))

    loads[4].wait()
    small_at = heads + share
    chans = dchan_ref.shape[1]
    more_rows = jnp.concatenate([dhead_ref[0:1], dhead_ref[1:2], jnp.zeros((1, chans - 2 * BLOCK), f32)], axis=1)
    small = jnp.concatenate([dchan_ref[: SUB - 1], more_rows], axis=0)
    small = jnp.concatenate([small[:, i : i + own] for i in range(0, chans, own)], axis=0)
    used = small_at + small.shape[0]
    par_rows = jnp.concatenate([dpar, jnp.zeros((BLOCK - share, BLOCK), f32)], axis=0).T[:SUB]
    par_rows = jnp.concatenate([par_rows, jnp.zeros((SUB, own - BLOCK), f32)], axis=1)
    grads = mm(third_t[...], normed_v[...].reshape(times, normed_v.shape[2]))
    tail = [jnp.zeros((third_g.shape[0] - used - SUB, third_g.shape[1]), f32)] if third_g.shape[0] > used + SUB else []
    third_g[...] = jnp.concatenate(
        [grads[:small_at], jnp.concatenate([small] * peers, axis=1), jnp.concatenate([par_rows] * peers, axis=1), *tail], axis=0
    ).astype(bf16)
    begin(2)

    exchange(0)
    if chips > 2:
        run_hops(2)
    spread(0)
    exchange(1)
    exchange(2)
    for step in range(3, chips):
        run_hops(step)
    relay(0)
    spread(1)
    spread(2)
    relay(1)
    relay(2)

    for by in (1, -1):
        @pl.when(later(by))
        def _():
            buffer = flow(by)[0].at[chips - 2]
            for i in range(PARTS):
                hop(buffer, by, chips - 1, i).wait_recv()
                add_into(part_of(mine.at[chip], i), [part_of(buffer, i)], own // PARTS)

    rows_ref[...] = mine[chip]
    loads[5].wait()
    for lane in range(block_rows // BLOCK):
        @pl.loop(0, BLOCK // ROWS_AT_ONCE)
        def _(i):
            at = pl.ds(pl.multiple_of(lane * BLOCK + i * ROWS_AT_ONCE, ROWS_AT_ONCE), ROWS_AT_ONCE)
            row = lax.broadcasted_iota(jnp.int32, (ROWS_AT_ONCE, 1), 0) + i * ROWS_AT_ONCE
            mask = (row < valid_ref[0, lane]).astype(f32)
            branch = branch_ref[at, :].astype(f32) + above_ref[at, :].astype(f32) + below_ref[at, :].astype(f32)
            output_ref[at, :] = (x_ref[at, :].astype(f32) + mask * rate_v[at, 0:1] * branch).astype(bf16)

    for step in range(1, chips):
        for by in (1, -1):
            @pl.when(sends(by, step))
            def _():
                for i in range(PARTS):
                    hop(mine.at[0], by, step, i).wait_send()
    for q in range(chips):
        over(q).wait_send()
    for k in range(len(sets)):
        for copy in to_width[k] + to_owner[k] + to_all[k][:2]:
            copy.wait_send()
        to_all[k][2].wait()
        for copy in relays[k]:
            copy.wait()


def scattered_out(
    valid, got, zx, dzx, weights, normed, wide, scale, par, starts, dchan, dhead, x_rows, branch, above, below, heads
):
    peers, widths = lax.axis_size("seq"), lax.axis_size("width")
    chips = peers // 2
    dma = pltpu.SemaphoreType.DMA
    anywhere = pl.BlockSpec(memory_space=pl.ANY)
    vmem = pl.BlockSpec(memory_space=pltpu.VMEM)
    own, model = normed.shape[0] // peers, normed.shape[1]
    half = wide.shape[3] // 2
    small_rows = SUB * dchan.shape[1] // own
    strips = -(-(heads + got.shape[1] + small_rows + SUB) // (16 * widths)) * 16 * widths
    pieces = [(peers, wide.shape[2], half), (peers, wide.shape[2], half), (peers, strips // widths, own)]
    kept = pieces[:2] + [(strips // widths, model)]
    block = (own, model)
    zx, dzx, normed, scale = [a.reshape(peers, own, a.shape[1]) for a in (zx, dzx, normed, scale)]
    return pl.pallas_call(
        partial(scatter_kernel, peers=peers, widths=widths, heads=heads),
        in_specs=[pl.BlockSpec(memory_space=pltpu.SMEM)] + [anywhere] * 7 + [vmem] * 8,
        out_specs=[vmem, vmem, anywhere, anywhere],
        out_shape=[
            jax.ShapeDtypeStruct(block, bf16), jax.ShapeDtypeStruct(block, bf16), jax.ShapeDtypeStruct(wide.shape, bf16),
            jax.ShapeDtypeStruct((peers, widths, strips // widths, own), bf16),
        ],
        scratch_shapes=[
            pltpu.VMEM(got.shape, bf16), pltpu.VMEM((peers, own, BLOCK), f32), pltpu.VMEM(dzx.shape, bf16),
            pltpu.VMEM(weights.shape, bf16), pltpu.VMEM(normed.shape, bf16),
            pltpu.VMEM((BLOCK, peers * own), bf16), pltpu.VMEM((strips, model), bf16), pltpu.VMEM((2 * N, BLOCK), f32),
            pltpu.VMEM((own, BLOCK), f32),
            *[pltpu.VMEM((chips,) + block, bf16)] * 3, *[pltpu.VMEM((chips - 1,) + block, bf16)] * 2,
            *[pltpu.VMEM(a, bf16) for a in kept],
            *[pltpu.VMEM((widths - 1,) + a, bf16) for a in kept],
            *[pltpu.VMEM(a, bf16) for a in pieces],
            dma((6,)), dma((chips,)), dma((chips,)),
            *[dma((chips - 1, PARTS))] * 4,
            dma((3, 3)), dma((3, widths - 1)), dma((3, widths - 1)), dma((3, peers - 1)), dma((3, peers - 1)),
            dma((3, widths)), dma((3, widths)),
        ],
        compiler_params=pltpu.CompilerParams(collective_id=2, has_side_effects=True, vmem_limit_bytes=62 << 20),
        name="scatter_out",
    )(valid, got, zx, dzx, weights, normed, wide, scale, par, starts, dchan, dhead, x_rows, branch, above, below)


def laid_kernel(
    in_ref, third_ref, w_ref, bc_ref, dt_ref, rows_ref, x_ref, cot_ref, norm_gain_ref,
    out_ref, out_bc_ref, out_dt_ref, norm_ref, out_rows_ref, sums,
    *, heads, share,
):
    peers, rows, wide = in_ref.shape[0], in_ref.shape[2], in_ref.shape[3]
    chans = wide // 2
    step = pl.program_id(0)

    @pl.when(step == 0)
    def _():
        third = [
            jnp.concatenate([third_ref[s, q].astype(f32) for q in range(third_ref.shape[1])], axis=0) for s in range(peers)
        ]
        dt = jnp.concatenate([t[:heads] for t in third], axis=0)
        bc = jnp.concatenate([t[heads : heads + share] for t in third], axis=0)
        out_dt_ref[...] = dt
        out_bc_ref[...] = bc.T
        norm_ref[...] = jnp.sum(dt * dt_ref[...].astype(f32), axis=0, keepdims=True)
        norm_ref[...] += jnp.sum(bc * bc_ref[...].astype(f32).T, axis=0, keepdims=True)

    lane = jnp.zeros((rows, BLOCK), f32)
    for s in range(peers):
        for half in (0, 1):
            at = (half * peers + s) * chans
            value = in_ref[s, 0, :, half * chans : (half + 1) * chans].astype(f32)
            out_ref[:, at : at + chans] = value
            value = value * w_ref[:, at : at + chans].astype(f32)
            for j in range(chans // BLOCK):
                lane = lane + value[:, j * BLOCK : (j + 1) * BLOCK]
    x = x_ref[...].astype(f32)
    rate = lax.rsqrt(jnp.mean(x * x, axis=-1, keepdims=True) + epsilon)
    unit = x * rate
    pulled = rows_ref[...].astype(f32) * norm_gain_ref[...]
    inner = jnp.mean(pulled * unit, axis=-1, keepdims=True)
    out_rows_ref[...] = cot_ref[...].astype(f32) + rate * (pulled - unit * inner)
    sums[pl.ds(pl.multiple_of(step * rows, SUB), rows), :] = lane

    @pl.when(step == pl.num_programs(0) - 1)
    def _():
        own = sums.shape[0]
        gain = norm_gain_ref[:, pl.ds(pl.multiple_of(lax.axis_index("seq") * own, BLOCK), own)]
        by_row = [jnp.sum(sums[i : i + BLOCK, :].T, axis=0, keepdims=True) for i in range(0, own, BLOCK)]
        norm_ref[...] = (norm_ref[...] + jnp.concatenate(by_row, axis=1)) / gain


def laid_out(wide, third, w_zx, w_bc, w_dt, normed_grad, x_rows, cotangent, norm_gain, heads):
    peers, widths, quarter, cols = wide.shape
    rows = widths * quarter
    cut = quarter
    share = w_bc.shape[1] // peers
    by_rows = lambda a: pl.BlockSpec((cut, a.shape[1]), lambda i: (i, 0))
    whole = lambda a: pl.BlockSpec(a.shape, lambda i: (0,) * len(a.shape))
    by_piece = pl.BlockSpec((peers, 1, cut, cols), lambda i: (0, i, 0, 0))
    norm = jax.ShapeDtypeStruct((1, rows), f32)
    shapes = [jax.ShapeDtypeStruct(a.shape, f32) for a in (w_zx, w_bc, w_dt, norm, x_rows)]
    return pl.pallas_call(
        partial(laid_kernel, heads=heads, share=share),
        grid=(widths,),
        in_specs=[
            by_piece, whole(third), by_rows(w_zx), whole(w_bc), whole(w_dt),
            by_rows(normed_grad), by_rows(x_rows), by_rows(cotangent), whole(norm_gain),
        ],
        out_specs=[by_rows(w_zx), whole(w_bc), whole(w_dt), whole(norm), by_rows(x_rows)],
        out_shape=shapes,
        scratch_shapes=[pltpu.VMEM((rows, BLOCK), f32)],
        compiler_params=pltpu.CompilerParams(vmem_limit_bytes=62 << 20),
        name="lay_out",
    )(wide, third, w_zx, w_bc, w_dt, normed_grad, x_rows, cotangent, norm_gain)


def crossed(value, axis, mask):
    return lax.ppermute(value, axis, [(i, i ^ mask) for i in range(lax.axis_size(axis))])


def pick(value, index):
    return lax.dynamic_index_in_dim(value, index, 0, False)


def quarters_back(total):
    widths = lax.axis_size("width")
    return [total] + [crossed(total, "width", m) for m in range(1, widths)]


def quarters_joined(pieces):
    width = lax.axis_index("width")
    stacked = jnp.stack(pieces)
    whole = jnp.stack([pick(stacked, jnp.bitwise_xor(width, j)) for j in range(len(pieces))])
    return whole.reshape((-1,) + whole.shape[2:]).astype(f32)


def heads_body(
    tokens, cotangent, starts, valid, norm_gain, w_zx, w_bc, w_dt, conv_w, conv_b, dt_bias, a_log, d_skip, gate_gain, w_out
):
    peers = lax.axis_size("seq")
    widths = lax.axis_size("width")
    place = lax.axis_index("seq")
    lanes = starts.shape[1]
    heads = H // peers
    chans = heads * HEAD_DIM
    own, model = tokens.shape
    rows = own * peers
    first = place * heads
    share = 2 * N // peers
    used = heads + share
    spread = jnp.asarray(np.arange(chans)[None, :] // HEAD_DIM == np.arange(BLOCK)[:, None], bf16)
    weights, normed, bgrad, starts_all, chan, head, bc_par, *computed = front(
        valid, starts, tokens, cotangent, norm_gain[None], w_bc, w_dt.T, conv_w.T, conv_b[None], dt_bias[None], a_log[None],
        d_skip[None], gate_gain[None], spread, w_zx, w_out,
    )
    normed, bgrad = normed.reshape(rows, model), bgrad.reshape(rows, model)
    zx, mix, mixed_grad, scale = [a.reshape(rows, a.shape[-1]) for a in computed[:4]]
    out_parts = computed[4:8]
    up, down, branch = computed[8:11]
    conv, bc, steps = [a.reshape(rows, a.shape[-1]) for a in computed[11:14]]
    state, tail = computed[14:]
    above = lax.ppermute(up, "seq", [(i, i + 2) for i in range(peers - 2)])
    below = lax.ppermute(down, "seq", [(i + 2, i) for i in range(peers - 2)])
    out_quarters = [out_parts[0]] + [crossed(out_parts[m], "width", m) for m in range(1, widths)]
    dzx, dbc, dchan, dhead = run_backward(
        starts_all, zx, mixed_grad, chan, head, spread, conv, mix, bc, steps, state, tail, scale, lanes, heads
    )
    dzx, dbc, out_quarters = lax.optimization_barrier((dzx, dbc, out_quarters))
    out_pieces = quarters_back(sum(q.astype(f32) for q in out_quarters).astype(bf16))

    got = lax.all_to_all(dbc.reshape(peers, share, rows), "seq", 0, 0, tiled=True)

    wide = mm(normed, dzx[:, : 2 * chans], TN).astype(bf16)
    wide, out_pieces = lax.optimization_barrier((wide, out_pieces))
    out_grad = quarters_joined(out_pieces)
    got, out_grad = lax.optimization_barrier((got, out_grad))
    output, normed_grad, wide, third = scattered_out(
        valid, got, zx, dzx, weights, normed, wide.reshape(peers, widths, own // widths, -1), scale, bc_par, starts_all, dchan,
        dhead, tokens, branch, above, below, heads,
    )
    grad_zx, grad_bc, grad_dt, grad_norm, input_grad = laid_out(
        wide, third, w_zx, w_bc, w_dt.T, normed_grad, tokens, cotangent, norm_gain[None], heads
    )
    grad_dt = grad_dt.T
    grad_norm = grad_norm[0]
    third = third.reshape(peers, -1, own).astype(f32)
    small_rows = SUB * chans // own
    small = third[:, used : used + small_rows].reshape(peers, chans // own, SUB, own).transpose(2, 0, 1, 3).reshape(SUB, peers, chans)
    of_bc = third[:, used + small_rows : used + small_rows + KCONV + 1, :share].transpose(1, 0, 2).reshape(KCONV + 1, 2 * N)
    of_conv = jnp.concatenate([small[: KCONV + 1].reshape(KCONV + 1, E), of_bc], axis=1)
    mine = lambda a, axis: lax.dynamic_slice_in_dim(a, place * (a.shape[axis] // peers), a.shape[axis] // peers, axis)
    of_conv = mine(of_conv, 1)
    grad_taps, grad_bias = of_conv[:KCONV].T, of_conv[BIAS]
    kept = pick(small.transpose(1, 0, 2), place)
    grad_gain, grad_skip = kept[GAIN], jnp.sum(kept[SKIP].reshape(heads, HEAD_DIM), axis=1)
    grad_dtb, grad_alog = kept[SUB - 1, :heads], kept[SUB - 1, BLOCK : BLOCK + heads]
    return (
        output, input_grad, grad_norm, grad_zx, grad_bc, grad_dt, grad_taps, grad_bias, grad_dtb, grad_alog, grad_skip,
        grad_gain, out_grad,
    )


def passed_along(array, axis, by):
    peers = lax.axis_size(axis)
    pairs = [(i, i + by) for i in range(peers) if 0 <= i + by < peers]
    return lax.ppermute(array, axis, pairs)


def carried_in(part, axis, combine, identity, reverse):
    count = lax.axis_size(axis)
    place = lax.axis_index(axis)
    at = count - 1 - place if reverse else place
    by = -1 if reverse else 1
    state = jax.tree.map(lambda a, e: jnp.zeros_like(a) + jnp.asarray(e, a.dtype), part, identity)

    def one(lap, state):
        sent = combine(state, part)
        got = jax.tree.map(lambda a: passed_along(a, axis, by), sent)
        return jax.tree.map(lambda old, new: jnp.where(at == lap + 1, new, old), state, got)

    return lax.fori_loop(0, count - 1, one, state)


def round_value(v):
    return lax.optimization_barrier(v.astype(jnp.bfloat16)).astype(jnp.float32)


def keep_round(v):
    return (round_value(v), None)


def pass_grad(kept, grad):
    return (grad,)


def same_value(v):
    return v


def keep_same(v):
    return (v, None)


def round_grad(kept, grad):
    return (round_value(grad),)


def low(v):
    wrapped = jax.custom_vjp(round_value)
    wrapped.defvjp(keep_round, pass_grad)
    return wrapped(v)


def low_back(v):
    wrapped = jax.custom_vjp(same_value)
    wrapped.defvjp(keep_same, round_grad)
    return wrapped(v)


def rms_front(x_rows, norm_gain):
    mean_square = jnp.mean(x_rows * x_rows, axis=-1, keepdims=True)
    return x_rows * lax.rsqrt(mean_square + epsilon) * norm_gain


def rim_of(zx_pre, bc_pre, chan_mask):
    return jnp.concatenate(
        [zx_pre[:, BLOCK - KCONV + 1 :, E:] * chan_mask, bc_pre[:, BLOCK - KCONV + 1 :, :]], axis=-1
    )


def piece_front(
    zx_pre,
    bc_pre,
    dt_raw,
    rim_rows,
    conv_w,
    conv_b,
    dt_bias,
    a_log,
    chan_mask,
    head_mask,
    keep_rows,
):
    z_gate = zx_pre[..., :E] * chan_mask
    pre_conv = jnp.concatenate([zx_pre[..., E:] * chan_mask, bc_pre], axis=-1)
    padded = jnp.concatenate([rim_rows * keep_rows[:, None, None], pre_conv], axis=1)
    conv_out = conv_b + padded[:, 0:BLOCK, :] * conv_w[:, 0]
    for offset in range(1, KCONV):
        conv_out = conv_out + padded[:, offset : offset + BLOCK, :] * conv_w[:, offset]
    active = jax.nn.silu(conv_out)
    x_conv = low(active[..., :E] * chan_mask)
    b_conv = low(active[..., E : E + N])
    c_conv = low(active[..., E + N :])
    dt_step = jax.nn.softplus(dt_raw + dt_bias) * head_mask
    log_step = -jnp.exp(a_log) * dt_step
    return (z_gate, x_conv, b_conv, c_conv, dt_step, log_step)


def block_state(x_conv, b_conv, dt_step, log_step):
    cumulative = jnp.cumsum(log_step, axis=1)
    to_end = jnp.exp(cumulative[:, -1:, :] - cumulative) * dt_step
    weighted = low(x_conv.reshape(x_conv.shape[0], BLOCK, H, HEAD_DIM) * to_end[..., None])
    state_sum = jnp.einsum("lqhp,lqn->lhpn", weighted, b_conv, precision=highest)
    return (state_sum, cumulative[:, -1, :])


def piece_mix(
    z_gate, x_conv, b_conv, c_conv, dt_step, log_step, state_in, d_skip, gate_gain, chan_count
):
    lane_count = x_conv.shape[0]
    cumulative = jnp.cumsum(log_step, axis=1)
    cum_heads = jnp.swapaxes(cumulative, 1, 2)
    causal = jnp.arange(BLOCK)[:, None] >= jnp.arange(BLOCK)[None, :]
    spread = cum_heads[:, :, :, None] - cum_heads[:, :, None, :]
    decays = jnp.where(causal, jnp.exp(jnp.where(causal, spread, 0.0)), 0.0)
    inner_cb = jnp.einsum("lqn,lsn->lqs", c_conv, b_conv, precision=highest)
    scores = low(inner_cb[:, None] * decays * jnp.swapaxes(dt_step, 1, 2)[:, :, None, :])
    x_heads = x_conv.reshape(lane_count, BLOCK, H, HEAD_DIM)
    within = jnp.einsum("lhqs,lshp->lqhp", scores, x_heads, precision=highest)
    carried = (
        jnp.einsum("lqn,lhpn->lqhp", c_conv, state_in, precision=highest)
        * jnp.exp(cumulative)[..., None]
    )
    mixed_sum = low_back(within + carried) + d_skip[:, None] * x_heads
    gated_rows = mixed_sum.reshape(lane_count, BLOCK, E) * jax.nn.silu(z_gate)
    mean_square = jnp.sum(gated_rows * gated_rows, axis=-1, keepdims=True) / chan_count
    return low(gated_rows * lax.rsqrt(mean_square + epsilon) * gate_gain)


def mix_lanes(lane_inputs, d_skip, gate_gain, chan_count):

    def one_lane(pieces):
        lane_gate, lane_xconv, lane_bconv, lane_cconv, lane_step, lane_decay, lane_state = pieces
        return piece_mix(
            lane_gate[None],
            lane_xconv[None],
            lane_bconv[None],
            lane_cconv[None],
            lane_step[None],
            lane_decay[None],
            lane_state[None],
            d_skip,
            gate_gain,
            chan_count,
        )[0]

    return lax.map(one_lane, lane_inputs)


def mix_back_lanes(lane_inputs, mixed_grad, d_skip, gate_gain, chan_count):

    def lane_mix(z_gate, x_conv, b_conv, c_conv, dt_step, log_step, state_in, skip_coef, gain_coef):
        return piece_mix(
            z_gate[None],
            x_conv[None],
            b_conv[None],
            c_conv[None],
            dt_step[None],
            log_step[None],
            state_in[None],
            skip_coef,
            gain_coef,
            chan_count,
        )[0]

    def one_lane(pieces):
        (
            lane_gate,
            lane_xconv,
            lane_bconv,
            lane_cconv,
            lane_step,
            lane_decay,
            lane_state,
            lane_grad,
        ) = pieces
        unused, pull_lane = jax.vjp(
            lane_mix,
            lane_gate,
            lane_xconv,
            lane_bconv,
            lane_cconv,
            lane_step,
            lane_decay,
            lane_state,
            d_skip,
            gate_gain,
        )
        return pull_lane(lane_grad)

    lane_grads = lax.map(one_lane, lane_inputs + (mixed_grad,))
    return (lane_grads[:7], jnp.sum(lane_grads[7], axis=0), jnp.sum(lane_grads[8], axis=0))


def chain_combine(earlier, latter):
    return (earlier[0] * latter[0], latter[0][:, :, None, None] * earlier[1] + latter[1])


def share_out(out_grad):
    return lax.psum_scatter(out_grad, "seq", scatter_dimension=0, tiled=True)


def contract_rows(left, right):
    return lax.dot_general(
        left, right, (((0,), (0,)), ((), ())), preferred_element_type=jnp.float32
    )


def contract_cols(left, right):
    return lax.dot_general(
        left, right, (((1,), (1,)), ((), ())), preferred_element_type=jnp.float32
    )


def rows_body(
    tokens,
    cotangent,
    starts,
    valid,
    norm_gain,
    w_zx,
    w_bc,
    w_dt,
    conv_w,
    conv_b,
    dt_bias,
    a_log,
    d_skip,
    gate_gain,
    w_out,
):
    lane_count = starts.shape[1]
    width_index = lax.axis_index("width")
    shift_bits = lax.axis_size("width") - 1 - width_index
    active_heads = jnp.right_shift(jnp.int32(H), shift_bits)
    chan_mask = (jnp.arange(E) // HEAD_DIM < active_heads).astype(jnp.float32)
    head_mask = (jnp.arange(H) < active_heads).astype(jnp.float32)
    chan_count = (active_heads * HEAD_DIM).astype(jnp.float32)
    keep_rows = 1.0 - starts[0].astype(jnp.float32)
    row_mask = (jnp.arange(BLOCK)[None, :] < valid[0][:, None]).astype(jnp.float32).reshape(-1, 1)
    x_rows = tokens.astype(jnp.float32)
    normed, norm_back = jax.vjp(rms_front, x_rows, norm_gain)
    normed_low = normed.astype(jnp.bfloat16)
    zx_full, bc_full, dt_full, out_full = (
        lax.all_gather(w_zx, "seq", axis=0, tiled=True),
        lax.all_gather(w_bc, "seq", axis=0, tiled=True),
        lax.all_gather(w_dt, "seq", axis=0, tiled=True),
        lax.all_gather(w_out, "seq", axis=0, tiled=True),
    )
    zx_pre = jnp.dot(normed_low, zx_full, preferred_element_type=jnp.float32).reshape(
        lane_count, BLOCK, 2 * E
    )
    bc_pre = jnp.dot(normed_low, bc_full, preferred_element_type=jnp.float32).reshape(
        lane_count, BLOCK, 2 * N
    )
    dt_raw = jnp.dot(normed_low, dt_full, preferred_element_type=jnp.float32).reshape(
        lane_count, BLOCK, H
    )
    rim_rows = passed_along(rim_of(zx_pre, bc_pre, chan_mask), "seq", 1)
    front_fn = partial(piece_front, chan_mask=chan_mask, head_mask=head_mask, keep_rows=keep_rows)
    front_out, front_back = jax.vjp(
        front_fn, zx_pre, bc_pre, dt_raw, rim_rows, conv_w, conv_b, dt_bias, a_log
    )
    z_gate, x_conv, b_conv, c_conv, dt_step, log_step = front_out
    (state_sum, log_total), state_back = jax.vjp(block_state, x_conv, b_conv, dt_step, log_step)
    carry_rate = jnp.exp(log_total) * keep_rows[:, None]
    identity = (jnp.ones_like(carry_rate), jnp.zeros_like(state_sum))
    prefix_pair = carried_in((carry_rate, state_sum), "seq", chain_combine, identity, False)
    state_in = prefix_pair[1] * keep_rows[:, None, None, None]
    lane_inputs = (z_gate, x_conv, b_conv, c_conv, dt_step, log_step, state_in)
    mixed_low = mix_lanes(lane_inputs, d_skip, gate_gain, chan_count)
    mixed_flat = mixed_low.reshape(-1, E).astype(jnp.bfloat16)
    branch = jnp.dot(mixed_flat, out_full, preferred_element_type=jnp.float32)
    output = (x_rows + row_mask * branch).astype(jnp.bfloat16)
    cot_rows = cotangent.astype(jnp.float32)
    branch_grad = (cot_rows * row_mask).astype(jnp.bfloat16)
    out_grad = contract_rows(mixed_flat, branch_grad)
    mixed_grad = contract_cols(branch_grad, out_full).reshape(lane_count, BLOCK, E)
    lane_grads, grad_skip, grad_gain = mix_back_lanes(
        lane_inputs, mixed_grad, d_skip, gate_gain, chan_count
    )
    grad_gate, grad_x, grad_b, grad_c, grad_dt, grad_log, grad_state = lane_grads
    later_pair = carried_in(
        (carry_rate, grad_state * keep_rows[:, None, None, None]),
        "seq",
        chain_combine,
        identity,
        True,
    )
    later_grad = later_pair[1]
    grad_total = jnp.exp(log_total) * jnp.sum(later_grad * state_in, axis=(2, 3))
    grad_x_more, grad_b_more, grad_dt_more, grad_log_more = state_back((later_grad, grad_total))
    grad_zx, grad_bc, grad_dtraw, grad_rim, grad_convw, grad_convb, grad_dtbias, grad_alog = (
        front_back(
            (
                grad_gate,
                grad_x + grad_x_more,
                grad_b + grad_b_more,
                grad_c,
                grad_dt + grad_dt_more,
                grad_log + grad_log_more,
            )
        )
    )
    rim_grad = passed_along(grad_rim.astype(jnp.bfloat16), "seq", -1).astype(grad_rim.dtype)
    grad_zx = grad_zx.at[:, BLOCK - KCONV + 1 :, E:].add(rim_grad[..., :E] * chan_mask)
    grad_bc = grad_bc.at[:, BLOCK - KCONV + 1 :, :].add(rim_grad[..., E:])
    zx_low = grad_zx.reshape(-1, 2 * E).astype(jnp.bfloat16)
    bc_low = grad_bc.reshape(-1, 2 * N).astype(jnp.bfloat16)
    dt_low = grad_dtraw.reshape(-1, H).astype(jnp.bfloat16)
    zx_weight_grad = contract_rows(normed_low, zx_low)
    bc_weight_grad = contract_rows(normed_low, bc_low)
    dt_weight_grad = contract_rows(normed_low, dt_low)
    normed_grad = (
        contract_cols(zx_low, zx_full)
        + contract_cols(bc_low, bc_full)
        + contract_cols(dt_low, dt_full)
    )
    grad_x_rows, grad_norm = norm_back(normed_grad)
    input_grad = cot_rows + grad_x_rows
    out_shard = share_out(out_grad)
    row_shards = (
        lax.psum_scatter(grad_norm, "seq", scatter_dimension=0, tiled=True),
        lax.psum_scatter(zx_weight_grad, "seq", scatter_dimension=0, tiled=True),
        lax.psum_scatter(bc_weight_grad, "seq", scatter_dimension=0, tiled=True),
        lax.psum_scatter(dt_weight_grad, "seq", scatter_dimension=0, tiled=True),
        lax.psum_scatter(grad_convw, "seq", scatter_dimension=0, tiled=True),
        lax.psum_scatter(grad_convb, "seq", scatter_dimension=0, tiled=True),
        lax.psum_scatter(grad_dtbias, "seq", scatter_dimension=0, tiled=True),
        lax.psum_scatter(grad_alog, "seq", scatter_dimension=0, tiled=True),
        lax.psum_scatter(grad_skip, "seq", scatter_dimension=0, tiled=True),
        lax.psum_scatter(grad_gain, "seq", scatter_dimension=0, tiled=True),
    )
    summed = lax.psum(
        (
            row_shards[0],
            row_shards[1],
            row_shards[2],
            row_shards[3],
            row_shards[4],
            row_shards[5],
            row_shards[6],
            row_shards[7],
            row_shards[8],
            row_shards[9],
            out_shard,
        ),
        "width",
    )
    return (
        output,
        input_grad,
        summed[0],
        summed[1],
        summed[2],
        summed[3],
        summed[4],
        summed[5],
        summed[6],
        summed[7],
        summed[8],
        summed[9],
        summed[10],
    )


def solution(mesh):
    in_specs = (
        P(("width", "seq"), None),
        P(("width", "seq"), None),
        P(("width", "seq"), None),
        P(("width", "seq"), None),
        P(),
        P("seq", None),
        P("seq", None),
        P("seq", None),
        P(),
        P(),
        P(),
        P(),
        P(),
        P(),
        P("seq", None),
    )
    out_specs = (
        P(("width", "seq"), None),
        P(("width", "seq"), None),
        P("seq"),
        P("seq", None),
        P("seq", None),
        P("seq", None),
        P("seq", None),
        P("seq"),
        P("seq"),
        P("seq"),
        P("seq"),
        P("seq"),
        P("seq", None),
    )
    body = heads_body if mesh.shape["width"] == 4 and H % (2 * mesh.shape["seq"]) == 0 else rows_body
    return jax.shard_map(body, mesh=mesh, in_specs=in_specs, out_specs=out_specs, check_vma=False)
```

```python
from functools import partial

import jax
import jax.numpy as jnp
from jax import lax
from jax.experimental import pallas as pl
from jax.experimental.pallas import tpu as pltpu
from jax.sharding import PartitionSpec as P
import numpy as np

H = 64
HEAD_DIM = 64
N = 128
KCONV = 4
BLOCK = 128
E = 4096
SUB = 8

epsilon = 1e-05
highest = lax.Precision.HIGHEST
f32 = jnp.float32
bf16 = jnp.bfloat16

NN = ((1,), (0,))
NT = ((1,), (1,))
TN = ((0,), (0,))


def mm(left, right, dims=NN, precision=None):
    return lax.dot_general(left, right, (dims, ((), ())), precision=precision, preferred_element_type=f32)


def split2(value):
    high = value.astype(bf16)
    return high, (value - high.astype(f32)).astype(bf16)


def mm_right(left, right, dims=NN):
    high, low = split2(right)
    return mm(left, high, dims) + mm(left, low, dims)


def mm_left(left, right, dims=NN):
    high, low = split2(left)
    return mm(high, right, dims) + mm(low, right, dims)


def softplus(v):
    small = jnp.exp(-jnp.abs(v))
    log1p = jnp.where(small < 1e-4, small - 0.5 * small * small, jnp.log(1.0 + small))
    return jnp.maximum(v, 0.0) + log1p


def sigmoid(v):
    return 0.5 + 0.5 * jnp.tanh(0.5 * v)


def grids():
    row = lax.broadcasted_iota(jnp.int32, (BLOCK, BLOCK), 0)
    col = lax.broadcasted_iota(jnp.int32, (BLOCK, BLOCK), 1)
    return row, col


def halves(pair, lane):
    zero = jnp.zeros_like(pair)
    return jnp.where(lane < HEAD_DIM, pair, zero), jnp.where(lane < HEAD_DIM, zero, pair)


def decay_of(cum, cum_t, head, causal):
    return jnp.exp(jnp.where(causal, cum[:, head : head + 1] - cum_t[head : head + 1, :], -1e30))


TAP, BIAS, SKIP, GAIN, MASK = 0, 4, 5, 6, 7
DT_BIAS, NEG_A, HEAD_MASK = 0, 1, 2


def forward_block(
    keep_row, zx_ref, chan_ref, bc_par_ref, head_ref, spread,
    conv_ref, mix_ref, bc_ref, step_ref, state_ref, tail_ref,
    state, tail_x, tail_b, pad_x, pad_b,
    *, lane, heads,
):
    width = heads * HEAD_DIM
    row, col = grids()
    causal = row >= col
    tril = causal.astype(f32)
    rows = pl.ds(lane * BLOCK, BLOCK)
    keep = jnp.concatenate([keep_row] * (width // BLOCK), axis=1)
    keep_b = jnp.concatenate([keep_row] * (2 * N // BLOCK), axis=1)

    pre = zx_ref[rows, width : 2 * width]
    before = tail_x[lane] * keep
    pad_x[lane, 0:SUB] = before
    pad_x[lane, SUB:] = pre
    tail_ref[lane] = before
    tail_x[lane] = pre[BLOCK - SUB :, :]
    conv = chan_ref[BIAS : BIAS + 1, :]
    for k in range(KCONV):
        conv = conv + pad_x[lane, SUB - KCONV + 1 + k : SUB - KCONV + 1 + k + BLOCK, :] * chan_ref[k : k + 1, :]
    conv_ref[rows, :] = conv
    x_low = (conv * sigmoid(conv) * chan_ref[MASK : MASK + 1, :]).astype(bf16)

    pre_b = zx_ref[rows, 2 * width + BLOCK :]
    pad_b[lane, 0:SUB] = tail_b[lane] * keep_b
    pad_b[lane, SUB:] = pre_b
    tail_b[lane] = pre_b[BLOCK - SUB :, :]
    conv_b = bc_par_ref[BIAS : BIAS + 1, :]
    for k in range(KCONV):
        conv_b = conv_b + pad_b[lane, SUB - KCONV + 1 + k : SUB - KCONV + 1 + k + BLOCK, :] * bc_par_ref[k : k + 1, :]
    bc_low = (conv_b * sigmoid(conv_b)).astype(bf16)
    bc_ref[rows, :] = bc_low
    b_low, c_low = bc_low[:, :N], bc_low[:, N:]

    raw = zx_ref[rows, 2 * width : 2 * width + BLOCK] + head_ref[DT_BIAS : DT_BIAS + 1, :]
    dt = softplus(raw) * head_ref[HEAD_MASK : HEAD_MASK + 1, :]
    cum = mm(tril, head_ref[NEG_A : NEG_A + 1, :] * dt, precision=highest)
    step_ref[rows, :BLOCK] = cum
    step_ref[rows, BLOCK:] = dt
    cum_t, dt_t = cum.T, dt.T
    last = cum[BLOCK - 1 :, :]
    carry_x = mm_left(jnp.exp(cum), spread)
    end_x = mm_left(jnp.exp(last - cum) * dt, spread)
    last_x = carry_x[BLOCK - 1 :, :]

    inner = mm(c_low, b_low, NT)
    parts = []
    for j in range(heads // 2):
        pair = x_low[:, 2 * HEAD_DIM * j : 2 * HEAD_DIM * (j + 1)]
        scores = [
            (inner * decay_of(cum, cum_t, h, causal) * dt_t[h : h + 1, :]).astype(bf16)
            for h in (2 * j, 2 * j + 1)
        ]
        parts.append(mm(jnp.concatenate(scores, axis=1), jnp.concatenate(halves(pair, col), axis=0)))
    within = jnp.concatenate(parts, axis=1)

    state_in = state[lane] * keep
    state_ref[lane] = state_in
    carried = mm_right(c_low, state_in) * carry_x
    x_f = x_low.astype(f32)
    mix_ref[rows, :] = within + carried + chan_ref[SKIP : SKIP + 1, :] * x_f
    weighted = (x_f * end_x).astype(bf16)
    state[lane] = last_x * state_in + mm(b_low, weighted, TN)


def backward_kernel(
    start_ref, zx_ref, grad_ref, chan_ref, head_ref, spread_ref,
    conv_ref, mix_ref, bc_ref, step_ref, state_ref, tail_ref, scale_ref,
    dzx_ref, dbc_ref, dchan_ref, dhead_ref,
    state_grad, next_conv, pad_x, pad_d,
    *, lanes, heads,
):
    lap = pl.program_id(0)
    width = heads * HEAD_DIM
    row, col = grids()
    causal = row >= col
    triu = (col >= row).astype(f32)
    spread = spread_ref[...]

    @pl.when(lap == 0)
    def _():
        state_grad[...] = jnp.zeros_like(state_grad)
        next_conv[...] = jnp.zeros_like(next_conv)
        dchan_ref[...] = jnp.zeros_like(dchan_ref)
        dhead_ref[...] = jnp.zeros_like(dhead_ref)

    def total(value):
        return jnp.sum(value, axis=0, keepdims=True)

    for lane in range(lanes):
        rows = pl.ds(lane * BLOCK, BLOCK)
        keep = 1.0 - jnp.concatenate([start_ref[0, lane : lane + 1, :]] * (width // BLOCK), axis=1)
        z = zx_ref[rows, :width]
        conv = conv_ref[rows, :]
        mixed = mix_ref[rows, :]
        grad = grad_ref[rows, :]
        gain = chan_ref[GAIN : GAIN + 1, :]
        skip = chan_ref[SKIP : SKIP + 1, :]
        rate = scale_ref[rows, 0:1]
        pull = scale_ref[rows, 1:2]
        gate = sigmoid(z)
        silu = z * gate
        gated = mixed * silu
        dgated = grad * gain * rate - gated * pull
        dzx_ref[rows, :width] = (dgated * mixed * (gate * (1.0 + z * (1.0 - gate)))).astype(bf16)
        dmixed = dgated * silu
        act = sigmoid(conv)
        x_low = (conv * act * chan_ref[MASK : MASK + 1, :]).astype(bf16)
        x_f = x_low.astype(f32)
        dchan_ref[GAIN : GAIN + 1, :] += total(grad * gated * rate)
        dchan_ref[SKIP : SKIP + 1, :] += total(dmixed * x_f)
        dlow = dmixed.astype(bf16)
        dlow_f = dlow.astype(f32)

        b_low, c_low = bc_ref[rows, :N], bc_ref[rows, N:]
        cum, dt = step_ref[rows, :BLOCK], step_ref[rows, BLOCK:]
        cum_t, dt_t = cum.T, dt.T
        last = cum[BLOCK - 1 :, :]
        to_last = jnp.exp(last - cum)
        carry_x = mm_left(jnp.exp(cum), spread)
        end_x = mm_left(to_last * dt, spread)
        last_x = carry_x[BLOCK - 1 :, :]

        inner = mm(c_low, b_low, NT)
        dinner = jnp.zeros((BLOCK, BLOCK), f32)
        parts, dt_rows = [], []
        for j in range(heads // 2):
            lanes_j = slice(2 * HEAD_DIM * j, 2 * HEAD_DIM * (j + 1))
            pair, dpair = x_low[:, lanes_j], dlow[:, lanes_j]
            dstack = jnp.concatenate(halves(dpair, col), axis=0)
            dscores = mm(dstack, pair, NT)
            scores = []
            for i, h in enumerate((2 * j, 2 * j + 1)):
                decay = decay_of(cum, cum_t, h, causal)
                step = dt_t[h : h + 1, :]
                scores.append((inner * decay * step).astype(bf16))
                part = dscores[i * BLOCK : (i + 1) * BLOCK] * decay
                dinner = dinner + part * step
                dt_rows.append(total(part * inner))
            parts.append(mm(jnp.concatenate(scores, axis=0), dstack, TN))
        dx_within = jnp.concatenate(parts, axis=1)
        dt_rows.append(jnp.zeros((BLOCK - heads, BLOCK), f32))
        ddt_within = jnp.concatenate(dt_rows, axis=0).T

        state_in = state_ref[0, lane]
        sgrad = state_grad[lane]
        in_high, sg_high = state_in.astype(bf16), sgrad.astype(bf16)
        dcarry = dlow_f * carry_x
        dc_high = dcarry.astype(bf16)
        di_high, di_low = split2(dinner)
        dc = mm(dc_high, in_high, NT)
        dc = dc + mm(di_high, b_low) + mm(di_low, b_low)
        weighted = (x_f * end_x).astype(bf16)
        db = mm(weighted, sg_high, NT)
        db = db + mm(di_high, c_low, TN) + mm(di_low, c_low, TN)
        dbc_ref[:N, rows] = db.T.astype(bf16)
        dbc_ref[N:, rows] = dc.T.astype(bf16)
        dweighted = mm(b_low, sg_high)
        dx = dx_within + dweighted * end_x
        dcum = mm_left(dlow_f * (mixed - skip * x_f) - x_f * dx, spread, NT)
        dend = mm((dweighted * x_f).astype(bf16), spread, NT)
        touch = jnp.broadcast_to(total(sgrad * state_in), (SUB, width))
        dlast = total(dend * to_last * dt) + jnp.exp(last) * mm_left(touch, spread, NT)[0:1]
        dlog = mm(triu, dcum, precision=highest) + dlast
        neg_a = head_ref[NEG_A : NEG_A + 1, :]
        ddt = ddt_within + dend * to_last + dlog * neg_a
        raw = zx_ref[rows, 2 * width : 2 * width + BLOCK] + head_ref[DT_BIAS : DT_BIAS + 1, :]
        draw = ddt * sigmoid(raw) * head_ref[HEAD_MASK : HEAD_MASK + 1, :]
        dzx_ref[rows, 2 * width :] = draw.astype(bf16)
        dhead_ref[0:1, :] += total(draw)
        dhead_ref[1:2, :] += total(dlog * neg_a * dt)
        state_grad[lane] = keep * (mm(c_low, dc_high, TN) + last_x * sgrad)

        dx = dx + skip * dmixed
        dconv = dx * chan_ref[MASK : MASK + 1, :] * (act * (1.0 + conv * (1.0 - act)))
        pad_d[lane, :BLOCK] = dconv
        pad_d[lane, BLOCK:] = next_conv[lane]
        next_conv[lane] = dconv[:SUB] * keep
        pad_x[lane, :SUB] = tail_ref[0, lane]
        pad_x[lane, SUB:] = zx_ref[rows, width : 2 * width]
        dpre = jnp.zeros((BLOCK, width), f32)
        for k in range(KCONV):
            dpre = dpre + pad_d[lane, KCONV - 1 - k : KCONV - 1 - k + BLOCK, :] * chan_ref[k : k + 1, :]
            dchan_ref[k : k + 1, :] += total(dconv * pad_x[lane, SUB - KCONV + 1 + k : SUB - KCONV + 1 + k + BLOCK, :])
        dchan_ref[BIAS : BIAS + 1, :] += total(dconv)
        dzx_ref[rows, width : 2 * width] = dpre.astype(bf16)


def run_backward(starts, zx, grad, chan, head, spread, conv, mix, bc, step_arr, state, tail, scale, lanes, heads):
    rows, width = grad.shape
    step = lanes * BLOCK
    blocks = rows // step
    by_block = lambda cols: pl.BlockSpec((step, cols), lambda c: (blocks - 1 - c, 0))
    whole = lambda a: pl.BlockSpec(a.shape, lambda c: (0,) * a.ndim)
    fixed = lambda shape: pl.BlockSpec(shape, lambda c: (0,) * len(shape))
    per_lane = lambda r, cols: pl.BlockSpec((1, lanes, r, cols), lambda c: (blocks - 1 - c, 0, 0, 0))
    return pl.pallas_call(
        partial(backward_kernel, lanes=lanes, heads=heads),
        grid=(blocks,),
        in_specs=[
            pl.BlockSpec((1, SUB, BLOCK), lambda c: (blocks - 1 - c, 0, 0)), by_block(2 * width + BLOCK), by_block(width),
            whole(chan), whole(head), whole(spread),
            by_block(width), by_block(width), by_block(2 * N), by_block(2 * BLOCK),
            per_lane(N, width), per_lane(SUB, width), by_block(BLOCK),
        ],
        out_specs=[
            by_block(2 * width + BLOCK), pl.BlockSpec((2 * N, step), lambda c: (0, blocks - 1 - c)),
            fixed((SUB, width)), fixed((SUB, BLOCK)),
        ],
        out_shape=[
            jax.ShapeDtypeStruct((rows, 2 * width + BLOCK), bf16),
            jax.ShapeDtypeStruct((2 * N, rows), bf16), jax.ShapeDtypeStruct((SUB, width), f32),
            jax.ShapeDtypeStruct((SUB, BLOCK), f32),
        ],
        scratch_shapes=[
            pltpu.VMEM((lanes, N, width), f32), pltpu.VMEM((lanes, SUB, width), f32),
            pltpu.VMEM((lanes, BLOCK + SUB, width), f32), pltpu.VMEM((lanes, BLOCK + SUB, width), f32),
        ],
        compiler_params=pltpu.CompilerParams(vmem_limit_bytes=62 << 20, dimension_semantics=("arbitrary",)),
        cost_estimate=pl.CostEstimate(flops=rows * width * 6144, bytes_accessed=rows * width * 40, transcendentals=rows * width * 6),
        name="mix_backward",
    )(starts, zx, grad, chan, head, spread, conv, mix, bc, step_arr, state, tail, scale)


MESH = pl.DeviceIdType.MESH


def greet(others):
    for other in others:
        pl.semaphore_signal(pltpu.get_barrier_semaphore(), inc=1, device_id=other, device_id_type=MESH)


def met(others):
    pl.semaphore_wait(pltpu.get_barrier_semaphore(), len(others))


def remote(src, dst, send, recv, device):
    return pltpu.make_async_remote_copy(
        src_ref=src, dst_ref=dst, send_sem=send, recv_sem=recv, device_id=device, device_id_type=MESH
    )


PARTS = 2


def part_of(ref, i):
    rows = ref.shape[0] // PARTS
    return ref.at[pl.ds(i * rows, rows)]


class Rows:
    def __init__(self, own_ref, all_ref, sems, peers):
        self.own, self.all, self.sems, self.peers = own_ref, all_ref, sems, peers
        self.width, self.place = lax.axis_index("width"), lax.axis_index("seq")
        self.chips, self.chip = peers // 2, self.place // 2

    def hop(self, ref, s, step, by, i):
        send, recv = self.sems[0 if by > 0 else 2], self.sems[1 if by > 0 else 3]
        device = (self.width, jnp.clip(self.place + 2 * by, 0, self.peers - 1))
        return remote(part_of(ref, i), part_of(self.all.at[s], i), send.at[step, i], recv.at[step, i], device)

    def over(self, ref, s, slot, i):
        device = (self.width, jnp.bitwise_xor(self.place, 1))
        send, recv = self.sems[4].at[slot, i], self.sems[5].at[slot, i]
        return remote(part_of(ref, i), part_of(self.all.at[s], i), send, recv, device)

    def inside(self, by):
        return self.chip + 1 < self.chips if by > 0 else self.chip > 0

    def reached(self, by, step):
        return self.chip >= step if by > 0 else self.chip + step < self.chips

    def source(self, by, step):
        return jnp.clip(self.place - 2 * by * step, 0, self.peers - 1)

    def keep(self):
        return pltpu.make_async_copy(self.own, self.all.at[self.place], self.sems[6])

    def start(self):
        for i in range(PARTS):
            for by in (1, -1):
                @pl.when(self.inside(by))
                def _():
                    self.hop(self.own, self.place, 0, by, i).start()
        self.keep().start()
        for copy in self.mate(1, 0):
            copy.start()

    def pass_on(self, step):
        for i in range(PARTS):
            for by in (1, -1):
                @pl.when(self.reached(by, step))
                def _():
                    s = self.source(by, step)
                    ref = self.all.at[s]
                    self.hop(ref, s, step - 1, by, i).wait_recv()

                    @pl.when(self.inside(by))
                    def _():
                        self.hop(ref, s, step, by, i).start()
                    self.over(ref, s, 2 * step - (by > 0), i).start()

    def mate(self, by, step):
        if not step:
            return [self.over(self.own, self.place, 0, i) for i in range(PARTS)]
        s = self.source(by, step)
        return [self.over(self.all.at[s], s, 2 * step - (by > 0), i) for i in range(PARTS)]

    def arrived(self):
        self.keep().wait()
        for copy in self.mate(1, 0):
            copy.wait_recv()
        for step in range(1, self.chips):
            for by in (1, -1):
                @pl.when(self.reached(by, step))
                def _():
                    for copy in self.mate(by, step):
                        copy.wait_recv()

    def sent(self):
        for step in range(self.chips):
            for by in (1, -1):
                @pl.when(self.inside(by) & self.reached(by, step))
                def _():
                    s = self.source(by, step)
                    for i in range(PARTS):
                        self.hop(self.all.at[s], s, step, by, i).wait_send()
        for copy in self.mate(1, 0):
            copy.wait_send()
        for step in range(1, self.chips):
            for by in (1, -1):
                @pl.when(self.reached(by, step))
                def _():
                    for copy in self.mate(by, step):
                        copy.wait_send()


ROW_SEMS = 7


def row_sems(chips):
    dma = pltpu.SemaphoreType.DMA
    return [dma((chips, PARTS))] * 4 + [dma((2 * chips, PARTS))] * 2 + [dma(())]


def front_kernel(
    valid_ref, start_ref, x_ref, cot_ref, norm_gain_ref, bc_ref, dt_ref, taps_ref, bias_ref, dtb_ref, alog_ref, skip_ref,
    gain_ref, spread_ref, zx_ref, wout_ref,
    w_ref, rows_ref, grads_ref, starts_ref, chan_ref, head_ref, bc_par,
    out_zx, out_mix, out_grad, out_scale, out_q0, out_q1, out_q2, out_q3, out_up, out_down, out_mine, out_conv, out_bc, out_step, out_state, out_tail,
    w_v, rows_v, starts_v, wout_v, own_v, grad_v, third_v, start_v, part_got,
    z_v, mix_v, scale_v, low_v, zx_v, mgrad_v, conv_v, bc_v, step_v, state_v, tail_v, bgrad_v, up, down, wout_grad, sums, sums_got,
    state, tail_x, tail_b, pad_x, pad_b,
    w_send, w_recv, st_send, st_recv, own_sem, wide_send, wide_recv, in_sem, out_sem, slot_sem, grad_sem, part_send, part_recv, branch_sem,
    up_send, up_recv, down_send, down_recv, sum_send, sum_recv, *sems,
    peers, widths, lanes, heads,
):
    width, place = lax.axis_index("width"), lax.axis_index("seq")
    chips = peers // 2
    chans = heads * HEAD_DIM
    quarter = zx_ref.shape[0] // widths
    ring = [lax.rem(place + by, peers) for by in range(1, peers)]
    cross = [jnp.bitwise_xor(width, m) for m in range(1, widths)]
    others = [(width, s) for s in ring] + [(w, place) for w in cross]
    greet(others)

    x = x_ref[...].astype(f32)
    own_v[...] = (x * lax.rsqrt(jnp.mean(x * x, axis=-1, keepdims=True) + epsilon) * norm_gain_ref[...]).astype(bf16)
    row = lax.broadcasted_iota(jnp.int32, (BLOCK, 1), 0)
    sub = lax.broadcasted_iota(jnp.int32, (SUB, BLOCK), 0)
    tile = jnp.zeros((SUB, BLOCK), f32)
    for lane in range(lanes):
        at = slice(lane * BLOCK, (lane + 1) * BLOCK)
        mask = (row < valid_ref[0, lane]).astype(f32)
        grad_v[at, :] = (cot_ref[at, :].astype(f32) * mask).astype(bf16)
        tile = jnp.where(sub == lane, start_ref[0, lane].astype(f32), tile)
    start_v[...] = tile
    bc, dt = bc_ref[...].astype(f32), dt_ref[...].astype(f32).T
    share = bc.shape[1] // peers
    rest = jnp.zeros((bc.shape[0], BLOCK - share - heads), f32)
    for s in range(peers):
        columns = [dt[:, s * heads : (s + 1) * heads], bc[:, s * share : (s + 1) * share], rest]
        third_v[s] = jnp.concatenate(columns, axis=1).astype(bf16)
    met(others)

    mine = pl.ds(pl.multiple_of(width * quarter, quarter), quarter)
    rows = Rows(own_v, rows_ref, sems[:ROW_SEMS], peers)
    grads = Rows(grad_v, grads_ref, sems[ROW_SEMS:], peers)

    def columns_of(half, s):
        return pl.ds(pl.multiple_of(half * peers * chans + s * chans, 128), chans)

    wide = 2 * chans
    spots = [pl.ds(0, chans), pl.ds(chans, chans), pl.ds(wide, BLOCK), pl.ds(wide + BLOCK, 2 * N)]

    def parts(s):
        return [zx_ref.at[mine, columns_of(0, s)], zx_ref.at[mine, columns_of(1, s)], third_v.at[s, mine], bc_ref.at[mine]]

    pushes = []
    for i, s in enumerate(ring):
        for k, (part, spot) in enumerate(zip(parts(s), spots)):
            pushes.append(remote(part, w_ref.at[place, width, :, spot], w_send.at[k, i], w_recv.at[k, i], (width, s)))
        pushes.append(remote(start_v, starts_ref.at[place], st_send.at[i], st_recv.at[i], (width, s)))
    for push in pushes:
        push.start()
    keeps = [
        pltpu.make_async_copy(part, w_ref.at[place, width, :, spot], own_sem.at[k])
        for k, (part, spot) in enumerate(zip(parts(place), spots))
    ]
    keeps.append(pltpu.make_async_copy(start_v, starts_ref.at[place], own_sem.at[4]))
    for keep in keeps:
        keep.start()
    rows.start()

    active = jnp.right_shift(jnp.int32(H), widths - 1 - width)
    first = place * heads
    here = columns_of(0, place)
    spread = spread_ref[...]
    pick_row = lax.broadcasted_iota(jnp.int32, (H, BLOCK), 0)
    pick_lane = lax.broadcasted_iota(jnp.int32, (H, BLOCK), 1)
    chosen = ((pick_row == pick_lane + first) & (pick_lane < heads)).astype(f32)
    per_head = jnp.concatenate(
        [dtb_ref[...], -jnp.exp(alog_ref[...]), jnp.ones((1, H), f32), skip_ref[...], jnp.zeros((SUB - 4, H), f32)], axis=0
    )
    per_head = mm(per_head, chosen, precision=highest)
    head_lane = lax.broadcasted_iota(jnp.int32, (SUB, BLOCK), 1)
    head_ref[...] = jnp.where((sub == HEAD_MASK) & (head_lane + first >= active), 0.0, per_head)
    on_chans = mm(head_ref[...], spread.astype(f32), precision=highest)
    bias_rows = bias_ref[pl.ds(place * (chans // BLOCK), chans // BLOCK), :]
    bias_here = jnp.concatenate([bias_rows[i : i + 1] for i in range(chans // BLOCK)], axis=1)
    bias_bc = jnp.concatenate([bias_ref[i : i + 1, :] for i in range(E // BLOCK, (E + 2 * N) // BLOCK)], axis=1)
    chan_ref[...] = jnp.concatenate(
        [taps_ref[:, here], bias_here, on_chans[3:4], gain_ref[:, here], on_chans[HEAD_MASK : HEAD_MASK + 1]], axis=0
    )
    bc_par[...] = jnp.concatenate(
        [taps_ref[:, E:], bias_bc, jnp.zeros((SUB - KCONV - 1, 2 * N), f32)], axis=0
    )

    for push in pushes:
        push.wait_recv()
    for keep in keeps:
        keep.wait()
    shares = [
        remote(w_ref.at[:, width], w_ref.at[:, width], wide_send.at[m], wide_recv.at[m], (w, place)) for m, w in enumerate(cross)
    ]
    for copy in shares:
        copy.start()
    for step in range(1, chips - 1):
        rows.pass_on(step)
    grads.start()
    for copy in shares:
        copy.wait_recv()
    in_w = pltpu.make_async_copy(w_ref, w_v, own_sem.at[0])
    in_starts = pltpu.make_async_copy(starts_ref, starts_v, own_sem.at[1])
    in_wout = pltpu.make_async_copy(wout_ref, wout_v, own_sem.at[2])
    for copy in (in_w, in_starts, in_wout):
        copy.start()
    rows.pass_on(chips - 1)
    rows.arrived()

    def load(src, s):
        return pltpu.make_async_copy(src.at[s], rows_v.at[s], in_sem.at[s])

    for c in range(peers):
        load(rows_ref, c).start()
    for array in (state, tail_x, tail_b):
        array[...] = jnp.zeros_like(array)
    for copy in (in_w, in_starts, in_wout):
        copy.wait()

    def out_copy(k, src, dst, c):
        return pltpu.make_async_copy(src.at[c], dst.at[c], out_sem.at[k, c])

    slots = [
        (zx_v, out_zx), (conv_v, out_conv), (bc_v, out_bc), (step_v, out_step), (state_v, out_state), (tail_v, out_tail)
    ]

    def slot_copies(c):
        slot = lax.rem(c, 2)
        return [pltpu.make_async_copy(src.at[slot], dst.at[c], slot_sem.at[k, slot]) for k, (src, dst) in enumerate(slots)]

    def compute(begin, end):
        @pl.loop(begin, end)
        def _(c):
            load(rows_ref, c).wait()

            @pl.when(c >= 2)
            def _():
                for copy in slot_copies(c - 2):
                    copy.wait()
            weights = w_v[...].reshape(w_v.shape[0] * w_v.shape[1] * w_v.shape[2], w_v.shape[3])
            slot = lax.rem(c, 2)
            zx = mm(rows_v[c], weights)
            zx_v[slot] = zx
            z_v[c] = zx[:, :chans]
            for lane in range(lanes):
                forward_block(
                    1.0 - starts_v[c, lane : lane + 1, :], zx_v.at[slot], chan_ref, bc_par, head_ref, spread_ref[...],
                    conv_v.at[slot], mix_v.at[c], bc_v.at[slot], step_v.at[slot], state_v.at[slot], tail_v.at[slot],
                    state, tail_x, tail_b, pad_x, pad_b, lane=lane, heads=heads,
                )
            out_copy(0, mix_v, out_mix, c).start()
            for copy in slot_copies(c):
                copy.start()
            gated = gated_of(c)
            square = mm_right(jnp.ones((SUB, chans), bf16), gated * gated, NT)
            for lane in range(lanes):
                sums[0, pl.ds(c * lanes + lane, 1), :] = square[:1, lane * BLOCK : (lane + 1) * BLOCK]

    def gated_of(c):
        z = z_v[c]
        return mix_v[c] * (z * sigmoid(z))

    core = lax.rem(place, 2)

    def give(k):
        copies = [
            remote(sums.at[k], sums_got.at[k, i], sum_send.at[k, i], sum_recv.at[k, i], (width, s)) for i, s in enumerate(ring)
        ]
        for copy in copies:
            copy.start()
        return copies

    def whole(k, copies):
        total = sums[k]
        for i, copy in enumerate(copies):
            copy.wait_recv()
            total = total + sums_got[k, i]
        return total

    def by_time(value):
        return jnp.concatenate([value, jnp.zeros((BLOCK - lanes * peers, BLOCK), f32)], axis=0).T

    def load_grad(s, slot):
        return pltpu.make_async_copy(grads_ref.at[s], bgrad_v.at[slot], in_sem.at[slot])

    def grad_out(s, slot):
        return pltpu.make_async_copy(mgrad_v.at[slot], out_grad.at[s], grad_sem.at[slot])

    def mix_grads(q, first, begun=False):
        for slot in (1 - core,) if begun else range(2):
            load_grad(2 * q + slot, slot).start()
        for slot in range(2):
            s = 2 * q + slot
            load_grad(s, slot).wait()
            if not first:
                grad_out(s, slot).wait()
            grad = mm(bgrad_v[slot], wout_v[...], NT)
            mgrad_v[slot] = grad
            grad_out(s, slot).start()
            pulled = mm_right(jnp.ones((SUB, chans), bf16), grad * chan_ref[GAIN : GAIN + 1, :] * gated_of(s), NT)
            for lane in range(lanes):
                sums[1, pl.ds(s * lanes + lane, 1), :] = pulled[:1, lane * BLOCK : (lane + 1) * BLOCK]
        rows_q = low_v[pl.ds(2 * q, 2)].reshape(2 * low_v.shape[1], chans)
        both = bgrad_v[...].reshape(2 * bgrad_v.shape[1], bgrad_v.shape[2])
        part = mm(rows_q, both, TN)
        wout_grad[...] = part if first else wout_grad[...] + part

    def mine(q):
        return rows_v.at[2 * q + core]

    def part_over(q):
        return remote(
            rows_v.at[2 * q + 1 - core], part_got.at[q], part_send.at[q], part_recv.at[q], (width, jnp.bitwise_xor(place, 1))
        )

    def part_sum(q):
        part_over(q).wait_recv()
        add_into(mine(q), [part_got.at[q]], rows_v.shape[1])

    def sends(by, step):
        far = chips - step
        return unit_chip + far < chips if by > 0 else unit_chip >= far

    def later(by):
        return unit_chip > 0 if by > 0 else unit_chip + 1 < chips

    unit_chip = place // 2

    def branch_hop(src, by, step, i):
        buffer, send, recv = (up, up_send, up_recv) if by > 0 else (down, down_send, down_recv)
        return remote(
            part_of(src, i), part_of(buffer.at[step - 1], i), send.at[step - 1, i], recv.at[step - 1, i],
            (width, jnp.clip(place + 2 * by, 0, peers - 1)),
        )

    def branch_stage(by, step):
        return (up if by > 0 else down).at[step - 2]

    def branch_hops(step):
        for i in range(PARTS):
            for by in (1, -1):
                owner = jnp.clip(unit_chip + by * (chips - step), 0, chips - 1)
                last = step == chips - 1

                def direct():
                    branch_hop(mine(owner), by, step, i).start()

                def relayed():
                    stage = branch_stage(by, step)
                    branch_hop(stage, by, step - 1, i).wait_recv()
                    add_into(part_of(stage, i), [part_of(mine(owner), i)], rows_v.shape[1] // PARTS)
                    if not last:
                        branch_hop(stage, by, step, i).start()

                if step == 1:
                    pl.when(sends(by, step))(direct)
                    continue
                if not last:
                    pl.when(sends(by, step) & jnp.logical_not(later(by)))(direct)
                pl.when(sends(by, step) & later(by))(relayed)

    def branch_out(k, src):
        return pltpu.make_async_copy(src, (out_mine, out_up, out_down)[k], branch_sem.at[k])

    def branch_outs(act):
        act(branch_out(0, mine(unit_chip)))
        for k, by in ((1, 1), (2, -1)):
            owner = jnp.clip(unit_chip + by, 0, chips - 1)

            @pl.when(later(by))
            def _():
                act(branch_out(k, branch_stage(by, chips - 1)))

            @pl.when(jnp.logical_not(later(by)))
            def _():
                act(branch_out(k, mine(owner)))

    compute(0, peers)
    squares = give(0)
    grads.pass_on(1)

    def mates_here(step):
        if not step:
            for copy in grads.mate(1, 0):
                copy.wait_recv()
        for by in (1, -1):
            if step:
                @pl.when(grads.reached(by, step))
                def _():
                    for copy in grads.mate(by, step):
                        copy.wait_recv()

    def at_distance(step, begun=False):
        for by in (1, -1):
            @pl.when(grads.reached(by, step))
            def _():
                mix_grads(grads.source(by, step) // 2, False, begun)

    @pl.loop(0, chips)
    def _(i):
        q = jnp.where(unit_chip < chips // 2, chips - 1 - i, i)
        for c in (2 * q + 1 - core, 2 * q + core):
            low = (gated_of(c) * chan_ref[GAIN : GAIN + 1, :]).astype(bf16)
            rows_v[c] = mm(low, wout_v[...]).astype(bf16)
        part_over(q).start()

    for q in range(chips):
        part_sum(q)
    branch_hops(1)
    count = (active * HEAD_DIM).astype(f32)
    rate = lax.rsqrt(whole(0, squares) / count + epsilon)
    rate_t = by_time(rate)
    lane_at = lax.broadcasted_iota(jnp.int32, (BLOCK, BLOCK), 1)
    spots_of = [(c, slice(lane * BLOCK, (lane + 1) * BLOCK)) for c in range(peers) for lane in range(lanes)]
    for i, (c, at) in enumerate(spots_of):
        scale_v[c, at, :] = jnp.where(lane_at == 0, rate_t[:, i : i + 1], 0.0)

    @pl.loop(0, peers)
    def _(c):
        low_v[c] = (gated_of(c) * scale_v[c, :, 0:1] * chan_ref[GAIN : GAIN + 1, :]).astype(bf16)

    grads.pass_on(2)
    grads.keep().wait()
    mates_here(0)
    mix_grads(unit_chip, True)
    mates_here(1)
    at_distance(1)
    for step in range(2, chips - 1):
        branch_hops(step)
        mates_here(step)
        at_distance(step)
    grads.pass_on(chips - 1)
    for by in (1, -1):
        @pl.when(grads.reached(by, chips - 1))
        def _():
            load_grad(grads.source(by, chips - 1), core).start()
    mates_here(chips - 1)
    at_distance(chips - 1, True)
    crosses = give(1)
    bgrad_v[...] = wout_grad[...].astype(bf16).reshape(bgrad_v.shape)
    wout_rows = chans // widths
    per_block = bgrad_v.shape[1] // wout_rows

    def wout_quarter(m):
        j = jnp.bitwise_xor(width, m)
        rows_j = pl.ds(pl.multiple_of(lax.rem(j, per_block) * wout_rows, 16), wout_rows)
        return bgrad_v.at[j // per_block, rows_j]

    wout_out = [
        pltpu.make_async_copy(wout_quarter(m), dst, own_sem.at[m]) for m, dst in enumerate((out_q0, out_q1, out_q2, out_q3))
    ]
    for copy in wout_out:
        copy.start()
    branch_hops(chips - 1)
    branch_outs(lambda copy: copy.start())
    pull_t = by_time(rate * rate * rate * whole(1, crosses) / count)
    for i, (c, at) in enumerate(spots_of):
        scale_v[c, at, :] = jnp.where(lane_at == 1, pull_t[:, i : i + 1], scale_v[c, at, :])
    for c in range(peers):
        out_copy(1, scale_v, out_scale, c).start()

    for copy in shares + pushes + squares + crosses:
        copy.wait_send()
    rows.sent()
    grads.sent()
    for c in (peers - 2, peers - 1):
        for copy in slot_copies(c):
            copy.wait()

    @pl.loop(0, peers)
    def _(c):
        for k, (src, dst) in enumerate([(mix_v, out_mix), (scale_v, out_scale)]):
            out_copy(k, src, dst, c).wait()

    for q in range(chips):
        part_over(q).wait_send()
    for step in range(1, chips - 1):
        for by in (1, -1):
            @pl.when(sends(by, step))
            def _():
                for i in range(PARTS):
                    branch_hop(mine(0), by, step, i).wait_send()
    for slot in range(2):
        grad_out(slot, slot).wait()
    for copy in wout_out:
        copy.wait()
    branch_outs(lambda copy: copy.wait())


def front(valid, starts, tokens, cotangent, norm_gain, w_bc, w_dt, taps, bias, dt_bias, a_log, d_skip, gate_gain, spread, w_zx, w_out):
    peers, widths = lax.axis_size("seq"), lax.axis_size("width")
    own, model = tokens.shape
    lanes = starts.shape[1]
    quarter = own // widths
    chans = w_out.shape[0]
    heads = chans // HEAD_DIM
    cols = 2 * chans + BLOCK + 2 * N
    dma = pltpu.SemaphoreType.DMA
    anywhere, vmem = pl.BlockSpec(memory_space=pl.ANY), pl.BlockSpec(memory_space=pltpu.VMEM)
    smem = pl.BlockSpec(memory_space=pltpu.SMEM)
    w_all = ((peers, widths, quarter, cols), bf16)
    rows_all = ((peers, own, model), bf16)
    part_all = ((peers // 2, own, model), bf16)
    starts_all = ((peers, SUB, BLOCK), f32)
    per_chan, low = ((peers, own, chans), f32), ((peers, own, chans), bf16)
    block = ((own, model), bf16)
    streamed = [
        ((own, cols), f32), ((own, chans), f32), ((own, chans), f32), ((own, 2 * N), bf16), ((own, 2 * BLOCK), f32),
        ((lanes, N, chans), f32), ((lanes, SUB, chans), f32),
    ]
    scale = ((peers, own, BLOCK), f32)
    of = lambda count, a: ((count,) + a[0], a[1])
    outs = [w_all, rows_all, rows_all, starts_all, ((SUB, chans), f32), ((SUB, BLOCK), f32), ((SUB, 2 * N), f32)]
    outs += [of(peers, streamed[0]), per_chan, per_chan, scale, *[((chans // widths, model), bf16)] * 4, block, block, block]
    outs += [of(peers, a) for a in streamed[2:]]
    scratch = [w_all, rows_all, starts_all, ((chans, model), bf16), ((own, model), bf16), ((own, model), bf16)]
    scratch += [((peers, own, BLOCK), bf16), ((SUB, BLOCK), f32), part_all, per_chan, per_chan, scale, low]
    scratch += [of(2, a) for a in streamed]
    scratch += [of(2, block)] * 3 + [((chans, model), f32)]
    scratch += [((2, peers * lanes, BLOCK), f32), ((2, peers - 1, peers * lanes, BLOCK), f32)]
    scratch += [((lanes, N, chans), f32), ((lanes, SUB, chans), f32), ((lanes, SUB, 2 * N), f32)]
    scratch += [((lanes, BLOCK + SUB, chans), f32), ((lanes, BLOCK + SUB, 2 * N), f32)]
    return pl.pallas_call(
        partial(front_kernel, peers=peers, widths=widths, lanes=lanes, heads=heads),
        in_specs=[smem] * 2 + [vmem] * 12 + [anywhere] * 2,
        out_specs=[anywhere] * 4 + [vmem] * 3 + [anywhere] * 16,
        out_shape=[jax.ShapeDtypeStruct(*a) for a in outs],
        scratch_shapes=[
            *[pltpu.VMEM(*a) for a in scratch],
            dma((4, peers - 1)), dma((4, peers - 1)), dma((peers - 1,)), dma((peers - 1,)),
            dma((5,)), dma((widths - 1,)), dma((widths - 1,)), dma((peers,)), dma((2, peers)), dma((6, 2)), dma((2,)),
            dma((peers // 2,)), dma((peers // 2,)), dma((3,)), *[dma((2, PARTS))] * 4,
            dma((2, peers - 1)), dma((2, peers - 1)),
            *row_sems(peers // 2), *row_sems(peers // 2),
        ],
        compiler_params=pltpu.CompilerParams(collective_id=1, has_side_effects=True, vmem_limit_bytes=62 << 20),
        name="front",
    )(valid, starts, tokens, cotangent, norm_gain, w_bc, w_dt, taps, bias, dt_bias, a_log, d_skip, gate_gain, spread, w_zx, w_out)


ROWS_AT_ONCE = 16


def add_into(dst, others, rows):
    @pl.loop(0, rows // ROWS_AT_ONCE)
    def _(i):
        at = pl.ds(pl.multiple_of(i * ROWS_AT_ONCE, ROWS_AT_ONCE), ROWS_AT_ONCE)
        value = dst[at].astype(f32)
        for other in others:
            value = value + other[at].astype(f32)
        dst[at] = value.astype(dst.dtype)


def bc_back(dbc, pre, par_ref, keep, keep_next):
    chans, times = pre.shape
    in_block = lax.rem(lax.broadcasted_iota(jnp.int32, (chans, times), 1), BLOCK)
    conv = jnp.broadcast_to(par_ref[:, BIAS : BIAS + 1], (chans, times))
    shifted = []
    for j in range(KCONV):
        moved = pre
        if j:
            moved = jnp.where(in_block >= j, pltpu.roll(pre, j, 1), keep * pltpu.roll(pre, BLOCK + j, 1))
        shifted.append(moved)
        conv = conv + moved * par_ref[:, KCONV - 1 - j : KCONV - j]
    act = sigmoid(conv)
    dconv = dbc * (act * (1.0 + conv * (1.0 - act)))
    dpre = dconv * par_ref[:, KCONV - 1 : KCONV]
    lane = lax.broadcasted_iota(jnp.int32, (chans, BLOCK), 1)
    dpar = jnp.where(lane == BIAS, jnp.sum(dconv, axis=1, keepdims=True), 0.0)
    for j in range(KCONV):
        dpar = dpar + jnp.where(lane == KCONV - 1 - j, jnp.sum(dconv * shifted[j], axis=1, keepdims=True), 0.0)
        if j:
            back = jnp.where(
                in_block < BLOCK - j, pltpu.roll(dconv, times - j, 1), keep_next * pltpu.roll(dconv, times - BLOCK - j, 1)
            )
            dpre = dpre + back * par_ref[:, KCONV - 1 - j : KCONV - j]
    return dpre, dpar


def scatter_kernel(
    valid_ref, got_ref, zx_ref, dzx_ref, w_ref, normed_ref, wide_ref, scale_ref, par_ref, start_ref, dchan_ref, dhead_ref,
    x_ref, branch_ref, above_ref, below_ref,
    output_ref, rows_ref, out_ref, out_third_ref,
    got_v, pre_v, dz_v, w_v, normed_v, third_t, third_g, par_t, rate_v,
    mine, to_mate, from_core, up, down, own0, own1, own2, got0, got1, got2, piece0, piece1, piece2,
    load_sem, core_send, core_recv, up_send, up_recv, down_send, down_recv,
    own_sem, q_send, q_recv, p_send, p_recv, o_send, o_recv,
    *, peers, widths, heads,
):
    width, place = lax.axis_index("width"), lax.axis_index("seq")
    chips = peers // 2
    chip, core = place // 2, lax.rem(place, 2)
    mate = (width, jnp.bitwise_xor(place, 1))
    ring = [lax.rem(place + by, peers) for by in range(1, peers)]
    cross = [jnp.bitwise_xor(width, m) for m in range(1, widths)]
    others = [(width, s) for s in ring] + [(w, place) for w in cross]
    greet(others)
    half = wide_ref.shape[3] // 2
    wide = 2 * half
    own = mine.shape[1]
    share, times = got_v.shape[1], got_v.shape[2]
    loads = [
        pltpu.make_async_copy(src, dst, load_sem.at[k])
        for k, (src, dst) in enumerate([
            (got_ref, got_v), (zx_ref.at[:, :, wide : wide + BLOCK], pre_v), (dzx_ref, dz_v), (w_ref, w_v), (normed_ref, normed_v),
            (scale_ref.at[place], rate_v),
        ])
    ]
    for load in loads:
        load.start()
    met(others)

    strip = third_g.shape[0] // widths
    lanes_of = lambda s: pl.ds(pl.multiple_of(s * own, BLOCK), own)
    strip_of = lambda w: pl.ds(pl.multiple_of(w * strip, 16), strip)
    sets = [
        (lambda w: wide_ref.at[:, w, :, 0:half], own0, got0, lambda s: own0.at[s], piece0,
         lambda w, at: out_ref.at[at, w, :, 0:half]),
        (lambda w: wide_ref.at[:, w, :, half:wide], own1, got1, lambda s: own1.at[s], piece1,
         lambda w, at: out_ref.at[at, w, :, half:wide]),
        (lambda w: third_g.at[strip_of(w)], own2, got2, lambda s: own2.at[:, lanes_of(s)], piece2,
         lambda w, at: out_third_ref.at[at, w]),
    ]
    own_in, to_width = [None] * 3, [None] * 3

    def begin(k):
        part, kept, arrived = sets[k][:3]
        own_in[k] = pltpu.make_async_copy(part(width), kept, own_sem.at[0, k])
        to_width[k] = [
            remote(part(w), arrived.at[m], q_send.at[k, m], q_recv.at[k, m], (w, place)) for m, w in enumerate(cross)
        ]
        for copy in [own_in[k]] + to_width[k]:
            copy.start()

    begin(0)
    begin(1)

    def flow(by):
        return (up, up_send, up_recv) if by > 0 else (down, down_send, down_recv)

    def sends(by, step):
        far = chips - step
        return chip + far < chips if by > 0 else chip >= far

    def later(by):
        return chip > 0 if by > 0 else chip + 1 < chips

    def hop(src, by, step, i):
        buffer, send, recv = flow(by)
        return remote(
            part_of(src, i), part_of(buffer.at[step - 1], i), send.at[step - 1, i], recv.at[step - 1, i],
            (width, jnp.clip(place + 2 * by, 0, peers - 1)),
        )

    def staged(by, step):
        return flow(by)[0].at[step - 2]

    def run_hops(step):
        for i in range(PARTS):
            for by in (1, -1):
                owner = jnp.clip(chip + by * (chips - step), 0, chips - 1)

                def direct():
                    hop(mine.at[owner], by, step, i).start()

                def relayed():
                    stage = staged(by, step)
                    hop(stage, by, step - 1, i).wait_recv()
                    add_into(part_of(stage, i), [part_of(mine.at[owner], i)], own // PARTS)
                    hop(stage, by, step, i).start()

                if step == 1:
                    pl.when(sends(by, step))(direct)
                else:
                    pl.when(sends(by, step) & jnp.logical_not(later(by)))(direct)
                    pl.when(sends(by, step) & later(by))(relayed)

    to_owner, to_all, kept_piece = [None] * 3, [None] * 3, [None] * 3

    def exchange(k):
        part, kept, arrived, piece_of, piece, out = sets[k]
        own_in[k].wait()
        for copy in to_width[k]:
            copy.wait_recv()
        if kept.ndim == 3:
            for s in range(peers):
                add_into(kept.at[s], [arrived.at[m, s] for m in range(widths - 1)], kept.shape[1])
        else:
            add_into(kept, [arrived.at[m] for m in range(widths - 1)], kept.shape[0])
        to_owner[k] = [
            remote(piece_of(s), piece.at[place], p_send.at[k, i], p_recv.at[k, i], (width, s)) for i, s in enumerate(ring)
        ]
        kept_piece[k] = pltpu.make_async_copy(piece_of(place), piece.at[place], own_sem.at[1, k])
        for copy in to_owner[k] + [kept_piece[k]]:
            copy.start()

    everything, relays = pl.ds(0, peers), [None] * 3
    over_x, over_y = jnp.bitwise_xor(width, 1), jnp.bitwise_xor(width, 2)

    def spread(k):
        piece, out = sets[k][4:]
        for copy in to_owner[k]:
            copy.wait_recv()
        kept_piece[k].wait()
        to_all[k] = [
            remote(piece, out(width, everything), o_send.at[k, i], o_recv.at[k, i], (w, place)) for i, w in enumerate((over_x, over_y))
        ]
        to_all[k].append(pltpu.make_async_copy(piece, out(width, everything), own_sem.at[2, k]))
        for copy in to_all[k]:
            copy.start()

    def relay(k):
        out = sets[k][5]
        relays[k] = []
        for i, (origin, target) in enumerate(((over_x, over_y), (over_y, over_x))):
            to_all[k][i].wait_recv()
            rows = out(origin, pl.ds(i * peers // 2, peers // 2))
            relays[k].append(remote(rows, rows, o_send.at[k, 2 + i], o_recv.at[k, 2 + i], (target, place)))
            relays[k][i].start()

    for load in loads[:3]:
        load.wait()
    dbc = got_v[0].astype(f32)
    for s in range(1, peers):
        dbc = dbc + got_v[s].astype(f32)
    block_rows = pre_v.shape[1]
    spots = [(c, slice(l * BLOCK, (l + 1) * BLOCK)) for c in range(peers) for l in range(block_rows // BLOCK)]
    pre = jnp.concatenate([pre_v[c, at, :].T[heads : heads + share] for c, at in spots], axis=1)
    par = jnp.concatenate([par_ref[...], jnp.zeros((BLOCK - SUB, 2 * N), f32)], axis=0)
    for i in range(2 * N // BLOCK):
        par_t[i * BLOCK : (i + 1) * BLOCK, :] = par[:, i * BLOCK : (i + 1) * BLOCK].T
    keep = [1.0 - start_ref[c, l : l + 1, :] for c in range(peers) for l in range(block_rows // BLOCK)]
    keep_next = keep[block_rows // BLOCK :] + [jnp.zeros((1, BLOCK), f32)] * (block_rows // BLOCK)
    own_par = par_t.at[pl.ds(pl.multiple_of(place * share, SUB), share)]
    dpre, dpar = bc_back(dbc, pre, own_par, jnp.concatenate(keep, axis=1), jnp.concatenate(keep_next, axis=1))
    for i, (c, at) in enumerate(spots):
        tile = jnp.concatenate(
            [
                dz_v[c, at, wide:].astype(f32).T[:heads], dpre[:, i * BLOCK : (i + 1) * BLOCK],
                jnp.zeros((BLOCK - heads - share, BLOCK), f32),
            ],
            axis=0,
        )
        third_t[:, i * BLOCK : (i + 1) * BLOCK] = tile.astype(bf16)
        dz_v[c, at, wide:] = tile.T.astype(bf16)
    loads[3].wait()

    def partial_rows(s):
        weights = w_v[...].reshape(w_v.shape[0] * w_v.shape[1] * w_v.shape[2], w_v.shape[3])
        return mm(dz_v[s], weights[:, : wide + BLOCK], NT).astype(bf16)

    def order(i):
        return jnp.where(chip < chips // 2, chips - 1 - i, i)

    def over(q):
        return remote(to_mate.at[q], from_core.at[q], core_send.at[q], core_recv.at[q], mate)

    def whole_sum(q):
        over(q).wait_recv()
        add_into(mine.at[q], [from_core.at[q]], own)

    for i in range(chips):
        q = order(i)
        to_mate[q] = partial_rows(2 * q + 1 - core)
        over(q).start()
        mine[q] = partial_rows(2 * q + core)
        if i > 1:
            whole_sum(order(i - 1))
        if not i:
            whole_sum(q)
            run_hops(1)
    whole_sum(order(chips - 1))

    loads[4].wait()
    small_at = heads + share
    chans = dchan_ref.shape[1]
    more_rows = jnp.concatenate([dhead_ref[0:1], dhead_ref[1:2], jnp.zeros((1, chans - 2 * BLOCK), f32)], axis=1)
    small = jnp.concatenate([dchan_ref[: SUB - 1], more_rows], axis=0)
    small = jnp.concatenate([small[:, i : i + own] for i in range(0, chans, own)], axis=0)
    used = small_at + small.shape[0]
    par_rows = jnp.concatenate([dpar, jnp.zeros((BLOCK - share, BLOCK), f32)], axis=0).T[:SUB]
    par_rows = jnp.concatenate([par_rows, jnp.zeros((SUB, own - BLOCK), f32)], axis=1)
    grads = mm(third_t[...], normed_v[...].reshape(times, normed_v.shape[2]))
    tail = [jnp.zeros((third_g.shape[0] - used - SUB, third_g.shape[1]), f32)] if third_g.shape[0] > used + SUB else []
    third_g[...] = jnp.concatenate(
        [grads[:small_at], jnp.concatenate([small] * peers, axis=1), jnp.concatenate([par_rows] * peers, axis=1), *tail], axis=0
    ).astype(bf16)
    begin(2)

    exchange(0)
    if chips > 2:
        run_hops(2)
    spread(0)
    exchange(1)
    exchange(2)
    for step in range(3, chips):
        run_hops(step)
    relay(0)
    spread(1)
    spread(2)
    relay(1)
    relay(2)

    for by in (1, -1):
        @pl.when(later(by))
        def _():
            buffer = flow(by)[0].at[chips - 2]
            for i in range(PARTS):
                hop(buffer, by, chips - 1, i).wait_recv()
                add_into(part_of(mine.at[chip], i), [part_of(buffer, i)], own // PARTS)

    rows_ref[...] = mine[chip]
    loads[5].wait()
    for lane in range(block_rows // BLOCK):
        @pl.loop(0, BLOCK // ROWS_AT_ONCE)
        def _(i):
            at = pl.ds(pl.multiple_of(lane * BLOCK + i * ROWS_AT_ONCE, ROWS_AT_ONCE), ROWS_AT_ONCE)
            row = lax.broadcasted_iota(jnp.int32, (ROWS_AT_ONCE, 1), 0) + i * ROWS_AT_ONCE
            mask = (row < valid_ref[0, lane]).astype(f32)
            branch = branch_ref[at, :].astype(f32) + above_ref[at, :].astype(f32) + below_ref[at, :].astype(f32)
            output_ref[at, :] = (x_ref[at, :].astype(f32) + mask * rate_v[at, 0:1] * branch).astype(bf16)

    for step in range(1, chips):
        for by in (1, -1):
            @pl.when(sends(by, step))
            def _():
                for i in range(PARTS):
                    hop(mine.at[0], by, step, i).wait_send()
    for q in range(chips):
        over(q).wait_send()
    for k in range(len(sets)):
        for copy in to_width[k] + to_owner[k] + to_all[k][:2]:
            copy.wait_send()
        to_all[k][2].wait()
        for copy in relays[k]:
            copy.wait()


def scattered_out(
    valid, got, zx, dzx, weights, normed, wide, scale, par, starts, dchan, dhead, x_rows, branch, above, below, heads
):
    peers, widths = lax.axis_size("seq"), lax.axis_size("width")
    chips = peers // 2
    dma = pltpu.SemaphoreType.DMA
    anywhere = pl.BlockSpec(memory_space=pl.ANY)
    vmem = pl.BlockSpec(memory_space=pltpu.VMEM)
    own, model = normed.shape[0] // peers, normed.shape[1]
    half = wide.shape[3] // 2
    small_rows = SUB * dchan.shape[1] // own
    strips = -(-(heads + got.shape[1] + small_rows + SUB) // (16 * widths)) * 16 * widths
    pieces = [(peers, wide.shape[2], half), (peers, wide.shape[2], half), (peers, strips // widths, own)]
    kept = pieces[:2] + [(strips // widths, model)]
    block = (own, model)
    zx, dzx, normed, scale = [a.reshape(peers, own, a.shape[1]) for a in (zx, dzx, normed, scale)]
    return pl.pallas_call(
        partial(scatter_kernel, peers=peers, widths=widths, heads=heads),
        in_specs=[pl.BlockSpec(memory_space=pltpu.SMEM)] + [anywhere] * 7 + [vmem] * 8,
        out_specs=[vmem, vmem, anywhere, anywhere],
        out_shape=[
            jax.ShapeDtypeStruct(block, bf16), jax.ShapeDtypeStruct(block, bf16), jax.ShapeDtypeStruct(wide.shape, bf16),
            jax.ShapeDtypeStruct((peers, widths, strips // widths, own), bf16),
        ],
        scratch_shapes=[
            pltpu.VMEM(got.shape, bf16), pltpu.VMEM((peers, own, BLOCK), f32), pltpu.VMEM(dzx.shape, bf16),
            pltpu.VMEM(weights.shape, bf16), pltpu.VMEM(normed.shape, bf16),
            pltpu.VMEM((BLOCK, peers * own), bf16), pltpu.VMEM((strips, model), bf16), pltpu.VMEM((2 * N, BLOCK), f32),
            pltpu.VMEM((own, BLOCK), f32),
            *[pltpu.VMEM((chips,) + block, bf16)] * 3, *[pltpu.VMEM((chips - 1,) + block, bf16)] * 2,
            *[pltpu.VMEM(a, bf16) for a in kept],
            *[pltpu.VMEM((widths - 1,) + a, bf16) for a in kept],
            *[pltpu.VMEM(a, bf16) for a in pieces],
            dma((6,)), dma((chips,)), dma((chips,)),
            *[dma((chips - 1, PARTS))] * 4,
            dma((3, 3)), dma((3, widths - 1)), dma((3, widths - 1)), dma((3, peers - 1)), dma((3, peers - 1)),
            dma((3, widths)), dma((3, widths)),
        ],
        compiler_params=pltpu.CompilerParams(collective_id=2, has_side_effects=True, vmem_limit_bytes=62 << 20),
        name="scatter_out",
    )(valid, got, zx, dzx, weights, normed, wide, scale, par, starts, dchan, dhead, x_rows, branch, above, below)


def laid_kernel(
    in_ref, third_ref, w_ref, bc_ref, dt_ref, rows_ref, x_ref, cot_ref, norm_gain_ref,
    out_ref, out_bc_ref, out_dt_ref, norm_ref, out_rows_ref, sums,
    *, heads, share,
):
    peers, rows, wide = in_ref.shape[0], in_ref.shape[2], in_ref.shape[3]
    chans = wide // 2
    step = pl.program_id(0)

    @pl.when(step == 0)
    def _():
        third = [
            jnp.concatenate([third_ref[s, q].astype(f32) for q in range(third_ref.shape[1])], axis=0) for s in range(peers)
        ]
        dt = jnp.concatenate([t[:heads] for t in third], axis=0)
        bc = jnp.concatenate([t[heads : heads + share] for t in third], axis=0)
        out_dt_ref[...] = dt
        out_bc_ref[...] = bc.T
        norm_ref[...] = jnp.sum(dt * dt_ref[...].astype(f32), axis=0, keepdims=True)
        norm_ref[...] += jnp.sum(bc * bc_ref[...].astype(f32).T, axis=0, keepdims=True)

    lane = jnp.zeros((rows, BLOCK), f32)
    for s in range(peers):
        for half in (0, 1):
            at = (half * peers + s) * chans
            value = in_ref[s, 0, :, half * chans : (half + 1) * chans].astype(f32)
            out_ref[:, at : at + chans] = value
            value = value * w_ref[:, at : at + chans].astype(f32)
            for j in range(chans // BLOCK):
                lane = lane + value[:, j * BLOCK : (j + 1) * BLOCK]
    x = x_ref[...].astype(f32)
    rate = lax.rsqrt(jnp.mean(x * x, axis=-1, keepdims=True) + epsilon)
    unit = x * rate
    pulled = rows_ref[...].astype(f32) * norm_gain_ref[...]
    inner = jnp.mean(pulled * unit, axis=-1, keepdims=True)
    out_rows_ref[...] = cot_ref[...].astype(f32) + rate * (pulled - unit * inner)
    sums[pl.ds(pl.multiple_of(step * rows, SUB), rows), :] = lane

    @pl.when(step == pl.num_programs(0) - 1)
    def _():
        own = sums.shape[0]
        gain = norm_gain_ref[:, pl.ds(pl.multiple_of(lax.axis_index("seq") * own, BLOCK), own)]
        by_row = [jnp.sum(sums[i : i + BLOCK, :].T, axis=0, keepdims=True) for i in range(0, own, BLOCK)]
        norm_ref[...] = (norm_ref[...] + jnp.concatenate(by_row, axis=1)) / gain


def laid_out(wide, third, w_zx, w_bc, w_dt, normed_grad, x_rows, cotangent, norm_gain, heads):
    peers, widths, quarter, cols = wide.shape
    rows = widths * quarter
    cut = quarter
    share = w_bc.shape[1] // peers
    by_rows = lambda a: pl.BlockSpec((cut, a.shape[1]), lambda i: (i, 0))
    whole = lambda a: pl.BlockSpec(a.shape, lambda i: (0,) * len(a.shape))
    by_piece = pl.BlockSpec((peers, 1, cut, cols), lambda i: (0, i, 0, 0))
    norm = jax.ShapeDtypeStruct((1, rows), f32)
    shapes = [jax.ShapeDtypeStruct(a.shape, f32) for a in (w_zx, w_bc, w_dt, norm, x_rows)]
    return pl.pallas_call(
        partial(laid_kernel, heads=heads, share=share),
        grid=(widths,),
        in_specs=[
            by_piece, whole(third), by_rows(w_zx), whole(w_bc), whole(w_dt),
            by_rows(normed_grad), by_rows(x_rows), by_rows(cotangent), whole(norm_gain),
        ],
        out_specs=[by_rows(w_zx), whole(w_bc), whole(w_dt), whole(norm), by_rows(x_rows)],
        out_shape=shapes,
        scratch_shapes=[pltpu.VMEM((rows, BLOCK), f32)],
        compiler_params=pltpu.CompilerParams(vmem_limit_bytes=62 << 20),
        name="lay_out",
    )(wide, third, w_zx, w_bc, w_dt, normed_grad, x_rows, cotangent, norm_gain)


def crossed(value, axis, mask):
    return lax.ppermute(value, axis, [(i, i ^ mask) for i in range(lax.axis_size(axis))])


def pick(value, index):
    return lax.dynamic_index_in_dim(value, index, 0, False)


def quarters_back(total):
    widths = lax.axis_size("width")
    return [total] + [crossed(total, "width", m) for m in range(1, widths)]


def quarters_joined(pieces):
    width = lax.axis_index("width")
    stacked = jnp.stack(pieces)
    whole = jnp.stack([pick(stacked, jnp.bitwise_xor(width, j)) for j in range(len(pieces))])
    return whole.reshape((-1,) + whole.shape[2:]).astype(f32)


def heads_body(
    tokens, cotangent, starts, valid, norm_gain, w_zx, w_bc, w_dt, conv_w, conv_b, dt_bias, a_log, d_skip, gate_gain, w_out
):
    peers = lax.axis_size("seq")
    widths = lax.axis_size("width")
    place = lax.axis_index("seq")
    lanes = starts.shape[1]
    heads = H // peers
    chans = heads * HEAD_DIM
    own, model = tokens.shape
    rows = own * peers
    first = place * heads
    share = 2 * N // peers
    used = heads + share
    spread = jnp.asarray(np.arange(chans)[None, :] // HEAD_DIM == np.arange(BLOCK)[:, None], bf16)
    weights, normed, bgrad, starts_all, chan, head, bc_par, *computed = front(
        valid, starts, tokens, cotangent, norm_gain[None], w_bc, w_dt.T, conv_w.T, conv_b.reshape(-1, BLOCK), dt_bias[None], a_log[None],
        d_skip[None], gate_gain[None], spread, w_zx, w_out,
    )
    normed, bgrad = normed.reshape(rows, model), bgrad.reshape(rows, model)
    zx, mix, mixed_grad, scale = [a.reshape(rows, a.shape[-1]) for a in computed[:4]]
    out_parts = computed[4:8]
    up, down, branch = computed[8:11]
    conv, bc, steps = [a.reshape(rows, a.shape[-1]) for a in computed[11:14]]
    state, tail = computed[14:]
    above = lax.ppermute(up, "seq", [(i, i + 2) for i in range(peers - 2)])
    below = lax.ppermute(down, "seq", [(i + 2, i) for i in range(peers - 2)])
    out_quarters = [out_parts[0]] + [crossed(out_parts[m], "width", m) for m in range(1, widths)]
    dzx, dbc, dchan, dhead = run_backward(
        starts_all, zx, mixed_grad, chan, head, spread, conv, mix, bc, steps, state, tail, scale, lanes, heads
    )
    dzx, dbc, out_quarters = lax.optimization_barrier((dzx, dbc, out_quarters))
    out_pieces = quarters_back(sum(q.astype(f32) for q in out_quarters).astype(bf16))

    got = lax.all_to_all(dbc.reshape(peers, share, rows), "seq", 0, 0, tiled=True)

    wide = mm(normed, dzx[:, : 2 * chans], TN).astype(bf16)
    wide, out_pieces = lax.optimization_barrier((wide, out_pieces))
    out_grad = quarters_joined(out_pieces)
    got, out_grad = lax.optimization_barrier((got, out_grad))
    output, normed_grad, wide, third = scattered_out(
        valid, got, zx, dzx, weights, normed, wide.reshape(peers, widths, own // widths, -1), scale, bc_par, starts_all, dchan,
        dhead, tokens, branch, above, below, heads,
    )
    grad_zx, grad_bc, grad_dt, grad_norm, input_grad = laid_out(
        wide, third, w_zx, w_bc, w_dt.T, normed_grad, tokens, cotangent, norm_gain[None], heads
    )
    grad_dt = grad_dt.T
    grad_norm = grad_norm[0]
    third = third.reshape(peers, -1, own).astype(f32)
    small_rows = SUB * chans // own
    small = third[:, used : used + small_rows].reshape(peers, chans // own, SUB, own).transpose(2, 0, 1, 3).reshape(SUB, peers, chans)
    of_bc = third[:, used + small_rows : used + small_rows + KCONV + 1, :share].transpose(1, 0, 2).reshape(KCONV + 1, 2 * N)
    of_conv = jnp.concatenate([small[: KCONV + 1].reshape(KCONV + 1, E), of_bc], axis=1)
    mine = lambda a, axis: lax.dynamic_slice_in_dim(a, place * (a.shape[axis] // peers), a.shape[axis] // peers, axis)
    of_conv = mine(of_conv, 1)
    grad_taps, grad_bias = of_conv[:KCONV].T, of_conv[BIAS]
    kept = pick(small.transpose(1, 0, 2), place)
    grad_gain, grad_skip = kept[GAIN], jnp.sum(kept[SKIP].reshape(heads, HEAD_DIM), axis=1)
    grad_dtb, grad_alog = kept[SUB - 1, :heads], kept[SUB - 1, BLOCK : BLOCK + heads]
    return (
        output, input_grad, grad_norm, grad_zx, grad_bc, grad_dt, grad_taps, grad_bias, grad_dtb, grad_alog, grad_skip,
        grad_gain, out_grad,
    )


def passed_along(array, axis, by):
    peers = lax.axis_size(axis)
    pairs = [(i, i + by) for i in range(peers) if 0 <= i + by < peers]
    return lax.ppermute(array, axis, pairs)


def carried_in(part, axis, combine, identity, reverse):
    count = lax.axis_size(axis)
    place = lax.axis_index(axis)
    at = count - 1 - place if reverse else place
    by = -1 if reverse else 1
    state = jax.tree.map(lambda a, e: jnp.zeros_like(a) + jnp.asarray(e, a.dtype), part, identity)

    def one(lap, state):
        sent = combine(state, part)
        got = jax.tree.map(lambda a: passed_along(a, axis, by), sent)
        return jax.tree.map(lambda old, new: jnp.where(at == lap + 1, new, old), state, got)

    return lax.fori_loop(0, count - 1, one, state)


def round_value(v):
    return lax.optimization_barrier(v.astype(jnp.bfloat16)).astype(jnp.float32)


def keep_round(v):
    return (round_value(v), None)


def pass_grad(kept, grad):
    return (grad,)


def same_value(v):
    return v


def keep_same(v):
    return (v, None)


def round_grad(kept, grad):
    return (round_value(grad),)


def low(v):
    wrapped = jax.custom_vjp(round_value)
    wrapped.defvjp(keep_round, pass_grad)
    return wrapped(v)


def low_back(v):
    wrapped = jax.custom_vjp(same_value)
    wrapped.defvjp(keep_same, round_grad)
    return wrapped(v)


def rms_front(x_rows, norm_gain):
    mean_square = jnp.mean(x_rows * x_rows, axis=-1, keepdims=True)
    return x_rows * lax.rsqrt(mean_square + epsilon) * norm_gain


def rim_of(zx_pre, bc_pre, chan_mask):
    return jnp.concatenate(
        [zx_pre[:, BLOCK - KCONV + 1 :, E:] * chan_mask, bc_pre[:, BLOCK - KCONV + 1 :, :]], axis=-1
    )


def piece_front(
    zx_pre,
    bc_pre,
    dt_raw,
    rim_rows,
    conv_w,
    conv_b,
    dt_bias,
    a_log,
    chan_mask,
    head_mask,
    keep_rows,
):
    z_gate = zx_pre[..., :E] * chan_mask
    pre_conv = jnp.concatenate([zx_pre[..., E:] * chan_mask, bc_pre], axis=-1)
    padded = jnp.concatenate([rim_rows * keep_rows[:, None, None], pre_conv], axis=1)
    conv_out = conv_b + padded[:, 0:BLOCK, :] * conv_w[:, 0]
    for offset in range(1, KCONV):
        conv_out = conv_out + padded[:, offset : offset + BLOCK, :] * conv_w[:, offset]
    active = jax.nn.silu(conv_out)
    x_conv = low(active[..., :E] * chan_mask)
    b_conv = low(active[..., E : E + N])
    c_conv = low(active[..., E + N :])
    dt_step = jax.nn.softplus(dt_raw + dt_bias) * head_mask
    log_step = -jnp.exp(a_log) * dt_step
    return (z_gate, x_conv, b_conv, c_conv, dt_step, log_step)


def block_state(x_conv, b_conv, dt_step, log_step):
    cumulative = jnp.cumsum(log_step, axis=1)
    to_end = jnp.exp(cumulative[:, -1:, :] - cumulative) * dt_step
    weighted = low(x_conv.reshape(x_conv.shape[0], BLOCK, H, HEAD_DIM) * to_end[..., None])
    state_sum = jnp.einsum("lqhp,lqn->lhpn", weighted, b_conv, precision=highest)
    return (state_sum, cumulative[:, -1, :])


def piece_mix(
    z_gate, x_conv, b_conv, c_conv, dt_step, log_step, state_in, d_skip, gate_gain, chan_count
):
    lane_count = x_conv.shape[0]
    cumulative = jnp.cumsum(log_step, axis=1)
    cum_heads = jnp.swapaxes(cumulative, 1, 2)
    causal = jnp.arange(BLOCK)[:, None] >= jnp.arange(BLOCK)[None, :]
    spread = cum_heads[:, :, :, None] - cum_heads[:, :, None, :]
    decays = jnp.where(causal, jnp.exp(jnp.where(causal, spread, 0.0)), 0.0)
    inner_cb = jnp.einsum("lqn,lsn->lqs", c_conv, b_conv, precision=highest)
    scores = low(inner_cb[:, None] * decays * jnp.swapaxes(dt_step, 1, 2)[:, :, None, :])
    x_heads = x_conv.reshape(lane_count, BLOCK, H, HEAD_DIM)
    within = jnp.einsum("lhqs,lshp->lqhp", scores, x_heads, precision=highest)
    carried = (
        jnp.einsum("lqn,lhpn->lqhp", c_conv, state_in, precision=highest)
        * jnp.exp(cumulative)[..., None]
    )
    mixed_sum = low_back(within + carried) + d_skip[:, None] * x_heads
    gated_rows = mixed_sum.reshape(lane_count, BLOCK, E) * jax.nn.silu(z_gate)
    mean_square = jnp.sum(gated_rows * gated_rows, axis=-1, keepdims=True) / chan_count
    return low(gated_rows * lax.rsqrt(mean_square + epsilon) * gate_gain)


def mix_lanes(lane_inputs, d_skip, gate_gain, chan_count):

    def one_lane(pieces):
        lane_gate, lane_xconv, lane_bconv, lane_cconv, lane_step, lane_decay, lane_state = pieces
        return piece_mix(
            lane_gate[None],
            lane_xconv[None],
            lane_bconv[None],
            lane_cconv[None],
            lane_step[None],
            lane_decay[None],
            lane_state[None],
            d_skip,
            gate_gain,
            chan_count,
        )[0]

    return lax.map(one_lane, lane_inputs)


def mix_back_lanes(lane_inputs, mixed_grad, d_skip, gate_gain, chan_count):

    def lane_mix(z_gate, x_conv, b_conv, c_conv, dt_step, log_step, state_in, skip_coef, gain_coef):
        return piece_mix(
            z_gate[None],
            x_conv[None],
            b_conv[None],
            c_conv[None],
            dt_step[None],
            log_step[None],
            state_in[None],
            skip_coef,
            gain_coef,
            chan_count,
        )[0]

    def one_lane(pieces):
        (
            lane_gate,
            lane_xconv,
            lane_bconv,
            lane_cconv,
            lane_step,
            lane_decay,
            lane_state,
            lane_grad,
        ) = pieces
        unused, pull_lane = jax.vjp(
            lane_mix,
            lane_gate,
            lane_xconv,
            lane_bconv,
            lane_cconv,
            lane_step,
            lane_decay,
            lane_state,
            d_skip,
            gate_gain,
        )
        return pull_lane(lane_grad)

    lane_grads = lax.map(one_lane, lane_inputs + (mixed_grad,))
    return (lane_grads[:7], jnp.sum(lane_grads[7], axis=0), jnp.sum(lane_grads[8], axis=0))


def chain_combine(earlier, latter):
    return (earlier[0] * latter[0], latter[0][:, :, None, None] * earlier[1] + latter[1])


def share_out(out_grad):
    return lax.psum_scatter(out_grad, "seq", scatter_dimension=0, tiled=True)


def contract_rows(left, right):
    return lax.dot_general(
        left, right, (((0,), (0,)), ((), ())), preferred_element_type=jnp.float32
    )


def contract_cols(left, right):
    return lax.dot_general(
        left, right, (((1,), (1,)), ((), ())), preferred_element_type=jnp.float32
    )


def rows_body(
    tokens,
    cotangent,
    starts,
    valid,
    norm_gain,
    w_zx,
    w_bc,
    w_dt,
    conv_w,
    conv_b,
    dt_bias,
    a_log,
    d_skip,
    gate_gain,
    w_out,
):
    lane_count = starts.shape[1]
    width_index = lax.axis_index("width")
    shift_bits = lax.axis_size("width") - 1 - width_index
    active_heads = jnp.right_shift(jnp.int32(H), shift_bits)
    chan_mask = (jnp.arange(E) // HEAD_DIM < active_heads).astype(jnp.float32)
    head_mask = (jnp.arange(H) < active_heads).astype(jnp.float32)
    chan_count = (active_heads * HEAD_DIM).astype(jnp.float32)
    keep_rows = 1.0 - starts[0].astype(jnp.float32)
    row_mask = (jnp.arange(BLOCK)[None, :] < valid[0][:, None]).astype(jnp.float32).reshape(-1, 1)
    x_rows = tokens.astype(jnp.float32)
    normed, norm_back = jax.vjp(rms_front, x_rows, norm_gain)
    normed_low = normed.astype(jnp.bfloat16)
    zx_full, bc_full, dt_full, out_full = (
        lax.all_gather(w_zx, "seq", axis=0, tiled=True),
        lax.all_gather(w_bc, "seq", axis=0, tiled=True),
        lax.all_gather(w_dt, "seq", axis=0, tiled=True),
        lax.all_gather(w_out, "seq", axis=0, tiled=True),
    )
    zx_pre = jnp.dot(normed_low, zx_full, preferred_element_type=jnp.float32).reshape(
        lane_count, BLOCK, 2 * E
    )
    bc_pre = jnp.dot(normed_low, bc_full, preferred_element_type=jnp.float32).reshape(
        lane_count, BLOCK, 2 * N
    )
    dt_raw = jnp.dot(normed_low, dt_full, preferred_element_type=jnp.float32).reshape(
        lane_count, BLOCK, H
    )
    rim_rows = passed_along(rim_of(zx_pre, bc_pre, chan_mask), "seq", 1)
    front_fn = partial(piece_front, chan_mask=chan_mask, head_mask=head_mask, keep_rows=keep_rows)
    front_out, front_back = jax.vjp(
        front_fn, zx_pre, bc_pre, dt_raw, rim_rows, conv_w, conv_b, dt_bias, a_log
    )
    z_gate, x_conv, b_conv, c_conv, dt_step, log_step = front_out
    (state_sum, log_total), state_back = jax.vjp(block_state, x_conv, b_conv, dt_step, log_step)
    carry_rate = jnp.exp(log_total) * keep_rows[:, None]
    identity = (jnp.ones_like(carry_rate), jnp.zeros_like(state_sum))
    prefix_pair = carried_in((carry_rate, state_sum), "seq", chain_combine, identity, False)
    state_in = prefix_pair[1] * keep_rows[:, None, None, None]
    lane_inputs = (z_gate, x_conv, b_conv, c_conv, dt_step, log_step, state_in)
    mixed_low = mix_lanes(lane_inputs, d_skip, gate_gain, chan_count)
    mixed_flat = mixed_low.reshape(-1, E).astype(jnp.bfloat16)
    branch = jnp.dot(mixed_flat, out_full, preferred_element_type=jnp.float32)
    output = (x_rows + row_mask * branch).astype(jnp.bfloat16)
    cot_rows = cotangent.astype(jnp.float32)
    branch_grad = (cot_rows * row_mask).astype(jnp.bfloat16)
    out_grad = contract_rows(mixed_flat, branch_grad)
    mixed_grad = contract_cols(branch_grad, out_full).reshape(lane_count, BLOCK, E)
    lane_grads, grad_skip, grad_gain = mix_back_lanes(
        lane_inputs, mixed_grad, d_skip, gate_gain, chan_count
    )
    grad_gate, grad_x, grad_b, grad_c, grad_dt, grad_log, grad_state = lane_grads
    later_pair = carried_in(
        (carry_rate, grad_state * keep_rows[:, None, None, None]),
        "seq",
        chain_combine,
        identity,
        True,
    )
    later_grad = later_pair[1]
    grad_total = jnp.exp(log_total) * jnp.sum(later_grad * state_in, axis=(2, 3))
    grad_x_more, grad_b_more, grad_dt_more, grad_log_more = state_back((later_grad, grad_total))
    grad_zx, grad_bc, grad_dtraw, grad_rim, grad_convw, grad_convb, grad_dtbias, grad_alog = (
        front_back(
            (
                grad_gate,
                grad_x + grad_x_more,
                grad_b + grad_b_more,
                grad_c,
                grad_dt + grad_dt_more,
                grad_log + grad_log_more,
            )
        )
    )
    rim_grad = passed_along(grad_rim.astype(jnp.bfloat16), "seq", -1).astype(grad_rim.dtype)
    grad_zx = grad_zx.at[:, BLOCK - KCONV + 1 :, E:].add(rim_grad[..., :E] * chan_mask)
    grad_bc = grad_bc.at[:, BLOCK - KCONV + 1 :, :].add(rim_grad[..., E:])
    zx_low = grad_zx.reshape(-1, 2 * E).astype(jnp.bfloat16)
    bc_low = grad_bc.reshape(-1, 2 * N).astype(jnp.bfloat16)
    dt_low = grad_dtraw.reshape(-1, H).astype(jnp.bfloat16)
    zx_weight_grad = contract_rows(normed_low, zx_low)
    bc_weight_grad = contract_rows(normed_low, bc_low)
    dt_weight_grad = contract_rows(normed_low, dt_low)
    normed_grad = (
        contract_cols(zx_low, zx_full)
        + contract_cols(bc_low, bc_full)
        + contract_cols(dt_low, dt_full)
    )
    grad_x_rows, grad_norm = norm_back(normed_grad)
    input_grad = cot_rows + grad_x_rows
    out_shard = share_out(out_grad)
    row_shards = (
        lax.psum_scatter(grad_norm, "seq", scatter_dimension=0, tiled=True),
        lax.psum_scatter(zx_weight_grad, "seq", scatter_dimension=0, tiled=True),
        lax.psum_scatter(bc_weight_grad, "seq", scatter_dimension=0, tiled=True),
        lax.psum_scatter(dt_weight_grad, "seq", scatter_dimension=0, tiled=True),
        lax.psum_scatter(grad_convw, "seq", scatter_dimension=0, tiled=True),
        lax.psum_scatter(grad_convb, "seq", scatter_dimension=0, tiled=True),
        lax.psum_scatter(grad_dtbias, "seq", scatter_dimension=0, tiled=True),
        lax.psum_scatter(grad_alog, "seq", scatter_dimension=0, tiled=True),
        lax.psum_scatter(grad_skip, "seq", scatter_dimension=0, tiled=True),
        lax.psum_scatter(grad_gain, "seq", scatter_dimension=0, tiled=True),
    )
    summed = lax.psum(
        (
            row_shards[0],
            row_shards[1],
            row_shards[2],
            row_shards[3],
            row_shards[4],
            row_shards[5],
            row_shards[6],
            row_shards[7],
            row_shards[8],
            row_shards[9],
            out_shard,
        ),
        "width",
    )
    return (
        output,
        input_grad,
        summed[0],
        summed[1],
        summed[2],
        summed[3],
        summed[4],
        summed[5],
        summed[6],
        summed[7],
        summed[8],
        summed[9],
        summed[10],
    )


def solution(mesh):
    in_specs = (
        P(("width", "seq"), None),
        P(("width", "seq"), None),
        P(("width", "seq"), None),
        P(("width", "seq"), None),
        P(),
        P("seq", None),
        P("seq", None),
        P("seq", None),
        P(),
        P(),
        P(),
        P(),
        P(),
        P(),
        P("seq", None),
    )
    out_specs = (
        P(("width", "seq"), None),
        P(("width", "seq"), None),
        P("seq"),
        P("seq", None),
        P("seq", None),
        P("seq", None),
        P("seq", None),
        P("seq"),
        P("seq"),
        P("seq"),
        P("seq"),
        P("seq"),
        P("seq", None),
    )
    body = heads_body if mesh.shape["width"] == 4 and H % (2 * mesh.shape["seq"]) == 0 else rows_body
    return jax.shard_map(body, mesh=mesh, in_specs=in_specs, out_specs=out_specs, check_vma=False)
```
